32 devices in a mesh: dp: 4 (over x, core), ctx: 8 (over z, y).
Axes of the slice: x: 2, y: 2, z: 4, core: 2. Of those that a mesh axis runs over, the one named last changes fastest.
Arguments:
- tokens: bfloat16 [8, 1024, 2048], P('dp', 'ctx'), may hold values from -6 to 6
- cotangent: bfloat16 [8, 1024, 2048], P('dp', 'ctx'), may hold values from -6 to 6
- block_order: int32 [16], replicated, may hold values from 0 to 15, as said below
- attention_in: float32 [2048, 3072], P(('dp', 'ctx')), may hold values from -0.125 to 0.125
- attention_out: float32 [2048, 2048], P(('dp', 'ctx')), may hold values from -0.75 to 0.75
- gate_up: float32 [2048, 16384], P(('dp', 'ctx')), may hold values from -0.125 to 0.125
- down_matrix: float32 [8192, 2048], P(('dp', 'ctx')), may hold values from -0.0625 to 0.0625
- gains: float32 [2, 2048], P(None, ('dp', 'ctx')), may hold values from 0.5 to 1.5
- mean_attention_in: float32 [2048, 3072], P(('dp', 'ctx')), may hold values from -32 to 32
- mean_attention_out: float32 [2048, 2048], P(('dp', 'ctx')), may hold values from -12 to 12
- mean_gate_up: float32 [2048, 16384], P(('dp', 'ctx')), may hold values from -16 to 16
- mean_down: float32 [8192, 2048], P(('dp', 'ctx')), may hold values from -32 to 32
- mean_gains: float32 [2, 2048], P(None, ('dp', 'ctx')), may hold values from -64 to 64
- square_attention_in: float32 [2048, 3072], P(('dp', 'ctx')), may hold values from 108.1344 to 430.8992
- square_attention_out: float32 [2048, 2048], P(('dp', 'ctx')), may hold values from 17.2032 to 68.8128
- square_gate_up: float32 [2048, 16384], P(('dp', 'ctx')), may hold values from 38.5024 to 155.648
- square_down: float32 [8192, 2048], P(('dp', 'ctx')), may hold values from 155.648 to 622.592
- square_gains: float32 [2, 2048], P(None, ('dp', 'ctx')), may hold values from 430.8992 to 1720.32
Outputs:
- block_out: bfloat16 [8, 1024, 2048], P('dp', 'ctx')
- tokens_grad: float32 [8, 1024, 2048], P('dp', 'ctx')
- new_mean_attention_in: float32 [2048, 3072], P(('dp', 'ctx'))
- new_square_attention_in: float32 [2048, 3072], P(('dp', 'ctx'))
- new_attention_in: float32 [2048, 3072], P(('dp', 'ctx'))
- new_mean_attention_out: float32 [2048, 2048], P(('dp', 'ctx'))
- new_square_attention_out: float32 [2048, 2048], P(('dp', 'ctx'))
- new_attention_out: float32 [2048, 2048], P(('dp', 'ctx'))
- new_mean_gate_up: float32 [2048, 16384], P(('dp', 'ctx'))
- new_square_gate_up: float32 [2048, 16384], P(('dp', 'ctx'))
- new_gate_up: float32 [2048, 16384], P(('dp', 'ctx'))
- new_mean_down: float32 [8192, 2048], P(('dp', 'ctx'))
- new_square_down: float32 [8192, 2048], P(('dp', 'ctx'))
- new_down_matrix: float32 [8192, 2048], P(('dp', 'ctx'))
- new_mean_gains: float32 [2, 2048], P(None, ('dp', 'ctx'))
- new_square_gains: float32 [2, 2048], P(None, ('dp', 'ctx'))
- new_gains: float32 [2, 2048], P(None, ('dp', 'ctx'))
The draws below stay inside these ranges and needn't reach their ends.
Inputs may be any that keep to these rules, and one draw needn't show every extreme that they name: `block_order`: a permutation; the two entries 2c and 2c+1 of each device c sum to 15.
All inputs are finite; a program needn't handle non-finite values.
Results may differ from the reference program's by a relative error of at most 0.024.
Values may be sent and summed in bfloat16 or wider, within the bound.
A program may use at most 512 MiB of HBM per device.

```python
import math
import jax
import jax.numpy as jnp
from jax import lax

D = 2048
HEADS = 32
KV_HEADS = 8
HEAD = 64
FF = 8192
TPS = 128
STEP = 5
SEQS = 8
LEN = 1024
N_CTX = 8


def draw_block_order(key, part):
    key = jax.random.fold_in(key, 7)
    pair_count = LEN // TPS
    lower = jax.random.permutation(key, pair_count).astype(jnp.int32)
    upper = (2 * pair_count - 1 - lower).astype(jnp.int32)
    return jnp.stack([lower, upper], 1).reshape(2 * pair_count).astype(jnp.int32)


def block_levels(key, dims, cuts, smallest, largest):
    def one(dim, blocks):
        steps = jax.random.uniform(jax.random.fold_in(jax.random.fold_in(key, 6), dim), (blocks,), jnp.float32, smallest / len(cuts), largest / len(cuts))
        return jnp.repeat(jnp.exp(steps), dims[dim] // blocks).reshape((-1,) + (1,) * (len(dims) - dim - 1))

    gain = one(*cuts[0])
    for cut in cuts[1:]:
        gain = gain * one(*cut)
    return gain


def gaussian(key, shape, width, most, cuts=(), kind=jnp.bfloat16):
    array = jax.random.normal(key, shape, jnp.float32) * width
    if len(cuts) > 0:
        array = block_levels(key, shape, cuts, -0.22, 0.18) * array
    return jnp.clip(array, min=-most, max=most).astype(kind)


def setup_inputs(seed: int = 0) -> dict:
    splits = jax.random.split(jax.random.key(seed), 19)
    tokens = gaussian(splits[0], (SEQS, LEN, D), 1.0, 6.0, ((0, 4), (1, 8)))
    cotangent = gaussian(splits[1], (SEQS, LEN, D), 1.0, 6.0, ((0, 4), (1, 8)))
    block_order = draw_block_order(jax.random.fold_in(splits[18], 71), 0)
    attention_in = gaussian(splits[3], (D, (HEADS + 2 * KV_HEADS) * HEAD), D ** -0.5, 0.125, ((0, 32),), jnp.float32)
    attention_out = gaussian(splits[4], (HEADS * HEAD, D), (HEADS * HEAD // 32) ** -0.5, 0.75, ((0, 32),), jnp.float32)
    gate_up = gaussian(splits[5], (D, 2 * FF), D ** -0.5, 0.125, ((0, 32),), jnp.float32)
    down_matrix = gaussian(splits[6], (FF, D), FF ** -0.5, 0.0625, ((0, 32),), jnp.float32)
    gains = jnp.clip(1.0 + 0.1 * jax.random.normal(splits[7], (2, D), jnp.float32), 0.5, 1.5)
    mean_attention_in = gaussian(splits[8], (D, (HEADS + 2 * KV_HEADS) * HEAD), (0.056 * (SEQS * LEN) ** 0.5), 32.0, ((0, 32),), jnp.float32)
    mean_attention_out = gaussian(splits[9], (HEADS * HEAD, D), (0.022 * (SEQS * LEN) ** 0.5), 12.0, ((0, 32),), jnp.float32)
    mean_gate_up = gaussian(splits[10], (D, 2 * FF), (0.033 * (SEQS * LEN) ** 0.5), 16.0, ((0, 32),), jnp.float32)
    mean_down = gaussian(splits[11], (FF, D), (0.067 * (SEQS * LEN) ** 0.5), 32.0, ((0, 32),), jnp.float32)
    mean_gains = gaussian(splits[12], (2, D), (0.111 * (SEQS * LEN) ** 0.5), 64.0, ((1, 32),), jnp.float32)
    square_attention_in = jnp.clip(jnp.exp(math.log(430.8992) - 1.3824993 * jax.random.uniform(splits[13], (D, (HEADS + 2 * KV_HEADS) * HEAD), jnp.float32) ** block_levels(splits[13], (D, (HEADS + 2 * KV_HEADS) * HEAD), ((0, 32),), -0.2, 0.2)), 108.1344, 430.8992)
    square_attention_out = jnp.clip(jnp.exp(math.log(68.8128) - 1.3862944 * jax.random.uniform(splits[14], (HEADS * HEAD, D), jnp.float32) ** block_levels(splits[14], (HEADS * HEAD, D), ((0, 32),), -0.2, 0.2)), 17.2032, 68.8128)
    square_gate_up = jnp.clip(jnp.exp(math.log(155.648) - 1.3968765 * jax.random.uniform(splits[15], (D, 2 * FF), jnp.float32) ** block_levels(splits[15], (D, 2 * FF), ((0, 32),), -0.2, 0.2)), 38.5024, 155.648)
    square_down = jnp.clip(jnp.exp(math.log(622.592) - 1.3862944 * jax.random.uniform(splits[16], (FF, D), jnp.float32) ** block_levels(splits[16], (FF, D), ((0, 32),), -0.2, 0.2)), 155.648, 622.592)
    square_gains = jnp.clip(jnp.exp(math.log(1720.32) - 1.3843914 * jax.random.uniform(splits[17], (2, D), jnp.float32) ** block_levels(splits[17], (2, D), ((1, 32),), -0.2, 0.2)), 430.8992, 1720.32)
    return dict(tokens=tokens, cotangent=cotangent, block_order=block_order, attention_in=attention_in, attention_out=attention_out, gate_up=gate_up, down_matrix=down_matrix, gains=gains, mean_attention_in=mean_attention_in, mean_attention_out=mean_attention_out, mean_gate_up=mean_gate_up, mean_down=mean_down, mean_gains=mean_gains, square_attention_in=square_attention_in, square_attention_out=square_attention_out, square_gate_up=square_gate_up, square_down=square_down, square_gains=square_gains)


norm_eps = 1e-05
rope_base = 500000.0
beta_one = 0.9
beta_two = 0.95
gain_rate = 1.25
input_boost = 2.5
weight_decay = 0.1
adam_eps = 1e-08
masked_score = -1e+30

@jax.custom_vjp
def low(v):
    return lax.optimization_barrier(v.astype(jnp.bfloat16)).astype(jnp.float32)

@jax.custom_vjp
def low_back(v):
    return v

def low_keep(v):
    return (low(v), None)

def low_pass(kept, grad):
    return (grad,)

def back_keep(v):
    return (v, None)

def back_low(kept, grad):
    return (low(grad),)
low.defvjp(low_keep, low_pass)
low_back.defvjp(back_keep, back_low)

def rotary_tables(positions, head_width):
    half_width = head_width // 2
    frequency = rope_base ** (-(jnp.arange(half_width, dtype=jnp.float32) * 2.0 / head_width))
    angles = positions.astype(jnp.float32)[:, None] * frequency[None, :]
    angles = jnp.concatenate([angles, angles], 1)
    return (jnp.cos(angles), jnp.sin(angles))

def swap_halves(values):
    half_width = values.shape[-1] // 2
    return jnp.concatenate([-values[..., half_width:], values[..., :half_width]], -1)

def rotate(values, cosine, sine_table):
    return values * cosine + swap_halves(values) * sine_table

def norm_apply(values, gain_row):
    factor = lax.rsqrt(lax.optimization_barrier(jnp.mean(values * values, -1, keepdims=True)) + norm_eps)
    return values * factor * gain_row

def product(left_side, right_side):
    return jnp.dot(left_side, right_side, precision=lax.Precision.HIGHEST, preferred_element_type=jnp.float32)

def adam_update(weight, gradient, first_moment, second_moment, step_rate, decay_rate):
    first_new = beta_one * first_moment + (1.0 - beta_one) * gradient
    second_new = beta_two * second_moment + (1.0 - beta_two) * gradient * gradient
    update = first_new / (1.0 - beta_one ** STEP) / (jnp.sqrt(second_new / (1.0 - beta_two ** STEP)) + adam_eps)
    return (first_new, second_new, weight - step_rate * (update + decay_rate * weight))

def reference(tokens, cotangent, block_order, attention_in, attention_out, gate_up, down_matrix, gains, mean_attention_in, mean_attention_out, mean_gate_up, mean_down, mean_gains, square_attention_in, square_attention_out, square_gate_up, square_down, square_gains):
    length = TPS * N_CTX
    half_rows = TPS // 2
    group_size = HEADS // KV_HEADS
    query_cols = HEADS * HEAD
    key_cols = KV_HEADS * HEAD
    score_scale = HEAD ** (-0.5)
    block_rows = min(512, length)
    row_place = jnp.arange(length, dtype=jnp.int32)
    positions = (block_order[row_place // half_rows] * half_rows + row_place % half_rows).astype(jnp.int32)
    cosine, sine_table = rotary_tables(positions, HEAD)
    cos_rows = cosine[:, None, :]
    sin_rows = sine_table[:, None, :]
    block_starts = jnp.arange(length // block_rows, dtype=jnp.int32) * block_rows

    def one_layer(sequence, parameters):
        gain_all, project_in, project_out, gate_up_w, down_w = parameters
        input_one = low(norm_apply(sequence, gain_all[0]))
        projected = low_back(product(input_one, project_in))
        query_rows = low(rotate(projected[:, :query_cols].reshape(length, HEADS, HEAD), cos_rows, sin_rows))
        query_rows = query_rows.reshape(length, KV_HEADS, group_size, HEAD)
        key_rows = low(rotate(projected[:, query_cols:query_cols + key_cols].reshape(length, KV_HEADS, HEAD), cos_rows, sin_rows))
        value_rows = low(projected[:, query_cols + key_cols:].reshape(length, KV_HEADS, HEAD))

        def attend_block(block_start):
            query_block = lax.dynamic_slice_in_dim(query_rows, block_start, block_rows, 0)
            place_block = lax.dynamic_slice_in_dim(positions, block_start, block_rows, 0)
            scores = jnp.einsum('qkgd,tkd->kgqt', query_block, key_rows, precision=lax.Precision.HIGHEST) * score_scale
            scores = low_back(scores)
            allowed = positions[None, :] <= place_block[:, None]
            scores = jnp.where(allowed, scores, masked_score)
            weights = jax.nn.softmax(scores, -1)
            return jnp.einsum('kgqt,tkd->qkgd', low(weights), value_rows, precision=lax.Precision.HIGHEST)
        attended = lax.map(jax.checkpoint(attend_block), block_starts).reshape(length, query_cols)
        attended = low_back(low(attended))
        residual = sequence + low_back(product(attended, project_out))
        input_two = low(norm_apply(residual, gain_all[1]))
        gate_both = low_back(product(input_two, gate_up_w))
        hidden = low(jax.nn.silu(gate_both[:, :FF]) * gate_both[:, FF:])
        return residual + product(hidden, down_w)

    def forward(all_tokens, parameters):
        rounded = tuple((low(entry) for entry in parameters))

        def one_sequence(loop_carry, sequence):
            return (loop_carry, one_layer(sequence, rounded))
        _, outputs = lax.scan(jax.checkpoint(one_sequence), jnp.zeros((), jnp.float32), all_tokens)
        return outputs
    parameters = (gains, attention_in, attention_out, gate_up, down_matrix)
    all_tokens = tokens.astype(jnp.float32)
    outputs, pull_back = jax.vjp(forward, all_tokens, parameters)
    tokens_grad, gradients = pull_back(cotangent.astype(jnp.float32))
    grad_gains, grad_in, grad_out, grad_gate_up, grad_down = gradients
    new_in = adam_update(attention_in, grad_in, mean_attention_in, square_attention_in, input_boost * D ** (-0.5), weight_decay)
    new_out = adam_update(attention_out, grad_out, mean_attention_out, square_attention_out, (HEADS * HEAD // 32) ** (-0.5), weight_decay)
    new_gate = adam_update(gate_up, grad_gate_up, mean_gate_up, square_gate_up, D ** (-0.5), weight_decay)
    new_down = adam_update(down_matrix, grad_down, mean_down, square_down, FF ** (-0.5), weight_decay)
    new_gain = adam_update(gains, grad_gains, mean_gains, square_gains, gain_rate, 0.0)
    return (outputs.astype(jnp.bfloat16), tokens_grad, new_in[0], new_in[1], new_in[2], new_out[0], new_out[1], new_out[2], new_gate[0], new_gate[1], new_gate[2], new_down[0], new_down[1], new_down[2], new_gain[0], new_gain[1], new_gain[2])
```

```python
import functools

import jax
import jax.numpy as jnp
from jax import lax
from jax.experimental import pallas as pl
from jax.experimental.pallas import tpu as pltpu
from jax.sharding import PartitionSpec as P

D = 2048
HEADS = 32
KV_HEADS = 8
HEAD = 64
FF = 8192
STEP = 5


norm_eps = 1e-05
rope_base = 500000.0
beta_one = 0.9
beta_two = 0.95
gain_rate = 1.25
input_boost = 2.5
weight_decay = 0.1
adam_eps = 1e-08
masked_score = -1e30


def rotary_tables(positions, head_width):
    half_width = head_width // 2
    frequency = rope_base ** (-(jnp.arange(half_width, dtype=jnp.float32) * 2.0 / head_width))
    angles = positions.astype(jnp.float32)[:, None] * frequency[None, :]
    angles = jnp.concatenate([angles, angles], 1)
    return (jnp.cos(angles), jnp.sin(angles))


def swap_halves(values):
    half_width = values.shape[-1] // 2
    return jnp.concatenate([-values[..., half_width:], values[..., :half_width]], -1)


def rotate(values, cosine, sine_table):
    return values * cosine + swap_halves(values) * sine_table


def rotate_back(values, cosine, sine_table):
    return values * cosine - swap_halves(values) * sine_table


def norm_parts(values):
    factor = lax.rsqrt(jnp.mean(values * values, -1, keepdims=True) + norm_eps)
    return (values * factor, factor)


def norm_back(back_normed, normed, factor):
    return factor * (back_normed - normed * jnp.mean(back_normed * normed, -1, keepdims=True))


def local_places(order, device, shard_rows):
    half_rows = shard_rows // 2
    pair_start = lax.dynamic_slice_in_dim(order, device * 2, 2)
    local_rows = jnp.arange(shard_rows, dtype=jnp.int32)
    block_first = jnp.where(local_rows < half_rows, pair_start[0], pair_start[1])
    return block_first * half_rows + local_rows % half_rows


def adam_update(weight, gradient, first_moment, second_moment, step_rate, decay_rate):
    first_new = beta_one * first_moment + (1.0 - beta_one) * gradient
    second_new = beta_two * second_moment + (1.0 - beta_two) * gradient * gradient
    update = (
        first_new
        / (1.0 - beta_one**STEP)
        / (jnp.sqrt(second_new / (1.0 - beta_two**STEP)) + adam_eps)
    )
    return (first_new, second_new, weight - step_rate * (update + decay_rate * weight))


def swapped(values, by):
    return lax.ppermute(values, "dp", [(i, i ^ by) for i in range(4)])


def gather_dp(values):
    beside = swapped(values, 1)
    across = swapped(values, 2)
    corner = swapped(across, 1)
    return jnp.stack([values, beside, across, corner])


def scatter_dp(parts):
    low = parts.astype(jnp.bfloat16)
    beside = swapped(jnp.stack([low[1], low[3]]), 1).astype(jnp.float32)
    far = (parts[2] + beside[1]).astype(jnp.bfloat16)
    return parts[0] + beside[0] + swapped(far, 2).astype(jnp.float32)


def exchange_dp(pieces):
    mine = lax.axis_index("dp")
    slots = [lax.dynamic_index_in_dim(pieces, mine, 0, keepdims=False)]
    for by in (1, 2, 3):
        slots.append(swapped(lax.dynamic_index_in_dim(pieces, mine ^ by, 0, keepdims=False), by))
    slots = jnp.stack(slots)
    return jnp.stack(
        [lax.dynamic_index_in_dim(slots, mine ^ i, 0, keepdims=False) for i in range(4)]
    )


def to_owner_order(rows, shards):
    count, width = rows.shape
    return rows.reshape(count, 4, shards, -1).swapaxes(1, 2).reshape(count, width)


def from_owner_order(rows, shards):
    count, width = rows.shape
    return rows.reshape(count, shards, 4, -1).swapaxes(1, 2).reshape(count, width)


def dot_nn(a, b):
    return lax.dot_general(a, b, (((1,), (0,)), ((), ())), preferred_element_type=jnp.float32)


def dot_nt(a, b):
    return lax.dot_general(a, b, (((1,), (1,)), ((), ())), preferred_element_type=jnp.float32)


def dot_tn(a, b):
    return lax.dot_general(a, b, (((0,), (0,)), ((), ())), preferred_element_type=jnp.float32)


def causal_keep(tile):
    keys = lax.broadcasted_iota(jnp.int32, (tile, tile), 0)
    queries = lax.broadcasted_iota(jnp.int32, (tile, tile), 1)
    return keys <= queries


def sort_blocks(order_ref, source, target, blocks, rows):
    for i in range(blocks):
        start = pl.multiple_of(order_ref[i] * rows, rows)
        target[pl.ds(start, rows), :] = source[i * rows : (i + 1) * rows, :]


def unsort_blocks(order_ref, source, target, blocks, rows):
    for i in range(blocks):
        start = pl.multiple_of(order_ref[i] * rows, rows)
        target[i * rows : (i + 1) * rows, :] = source[pl.ds(start, rows), :]


def attend_kernel(
    q_heads, kv_heads, tile, order_ref, qkv_ref, out_ref, lse_ref, sorted_qkv, sorted_out
):
    length = qkv_ref.shape[0]
    blocks = order_ref.shape[0]
    rows = length // blocks
    group = q_heads // kv_heads
    q_cols, k_cols = q_heads * HEAD, kv_heads * HEAD
    scale = HEAD ** (-0.5)
    sort_blocks(order_ref, qkv_ref, sorted_qkv, blocks, rows)
    keep = causal_keep(tile)
    for kv in range(kv_heads):
        k_at = q_cols + kv * HEAD
        v_at = q_cols + k_cols + kv * HEAD

        def query_step(i, _):
            q_start = pl.multiple_of(i * tile, tile)
            queries = [
                sorted_qkv[pl.ds(q_start, tile), (kv * group + g) * HEAD :][:, :HEAD]
                for g in range(group)
            ]

            def key_tile(j, carry, masked):
                k_start = pl.multiple_of(j * tile, tile)
                keys = sorted_qkv[pl.ds(k_start, tile), k_at : k_at + HEAD]
                values = sorted_qkv[pl.ds(k_start, tile), v_at : v_at + HEAD]
                result = []
                for g in range(group):
                    peak, total, weighted = carry[g]
                    scores = dot_nt(keys, queries[g]) * scale
                    if masked:
                        scores = jnp.where(keep, scores, masked_score)
                    new_peak = jnp.maximum(peak, jnp.max(scores, 0, keepdims=True))
                    weights = jnp.exp(scores - new_peak)
                    shrink = jnp.exp(peak - new_peak)
                    total = total * shrink + jnp.sum(weights, 0, keepdims=True)
                    weighted = weighted * shrink + dot_tn(values, weights.astype(jnp.bfloat16))
                    result.append((new_peak, total, weighted))
                return tuple(result)

            start = tuple(
                (
                    jnp.full((1, tile), masked_score, jnp.float32),
                    jnp.zeros((1, tile), jnp.float32),
                    jnp.zeros((HEAD, tile), jnp.float32),
                )
                for _ in range(group)
            )
            carry = lax.fori_loop(0, i, lambda j, c: key_tile(j, c, False), start)
            carry = key_tile(i, carry, True)
            for g in range(group):
                head = kv * group + g
                peak, total, weighted = carry[g]
                lse_ref[head : head + 1, pl.ds(q_start, tile)] = peak + jnp.log(total)
                sorted_out[pl.ds(q_start, tile), head * HEAD : (head + 1) * HEAD] = (
                    (weighted / total).T.astype(jnp.bfloat16)
                )
            return 0

        lax.fori_loop(0, length // tile, query_step, 0)
    unsort_blocks(order_ref, sorted_out, out_ref, blocks, rows)


def attend_back_kernel(
    q_heads,
    kv_heads,
    tile,
    order_ref,
    qkv_ref,
    back_ref,
    lse_ref,
    out_ref,
    sorted_qkv,
    sorted_back,
    sorted_grad,
    delta_ref,
    dq_ref,
):
    length = qkv_ref.shape[0]
    blocks = order_ref.shape[0]
    rows = length // blocks
    group = q_heads // kv_heads
    q_cols, k_cols = q_heads * HEAD, kv_heads * HEAD
    scale = HEAD ** (-0.5)
    tiles = length // tile
    sort_blocks(order_ref, qkv_ref, sorted_qkv, blocks, rows)
    sort_blocks(order_ref, back_ref, sorted_back, blocks, rows)
    keep = causal_keep(tile)
    for kv in range(kv_heads):
        k_at = q_cols + kv * HEAD
        v_at = q_cols + k_cols + kv * HEAD

        def load(i, g):
            start = pl.multiple_of(i * tile, tile)
            head = kv * group + g
            cols = slice(head * HEAD, (head + 1) * HEAD)
            return (
                sorted_qkv[pl.ds(start, tile), cols],
                sorted_back[pl.ds(start, tile), cols],
                lse_ref[head : head + 1, pl.ds(start, tile)],
            )

        def load_kv(j):
            start = pl.multiple_of(j * tile, tile)
            return (
                sorted_qkv[pl.ds(start, tile), k_at : k_at + HEAD],
                sorted_qkv[pl.ds(start, tile), v_at : v_at + HEAD],
            )

        def tile_terms(keys, values, query, back, lse, masked):
            weights = jnp.exp(dot_nt(keys, query) * scale - lse)
            if masked:
                weights = jnp.where(keep, weights, 0.0)
            return weights, dot_nt(values, back)

        def delta_step(i, _):
            rows_i = [load(i, g) for g in range(group)]

            def one(j, carry, masked):
                keys, values = load_kv(j)
                result = []
                for g in range(group):
                    weights, back_weights = tile_terms(keys, values, *rows_i[g], masked)
                    result.append(carry[g] + jnp.sum(weights * back_weights, 0, keepdims=True))
                return tuple(result)

            carry = tuple(jnp.zeros((1, tile), jnp.float32) for _ in range(group))
            carry = lax.fori_loop(0, i, lambda j, c: one(j, c, False), carry)
            carry = one(i, carry, True)
            for g in range(group):
                delta_ref[g : g + 1, pl.ds(pl.multiple_of(i * tile, tile), tile)] = carry[g]
            return 0

        lax.fori_loop(0, tiles, delta_step, 0)
        dq_ref[...] = jnp.zeros_like(dq_ref)

        def key_step(j, _):
            keys, values = load_kv(j)

            def one(i, carry, masked):
                back_key, back_value = carry
                start = pl.multiple_of(i * tile, tile)
                for g in range(group):
                    query, back, lse = load(i, g)
                    weights, back_weights = tile_terms(keys, values, query, back, lse, masked)
                    delta = delta_ref[g : g + 1, pl.ds(start, tile)]
                    back_scores = (weights * (back_weights - delta)).astype(jnp.bfloat16)
                    back_key = back_key + dot_nn(back_scores, query)
                    back_value = back_value + dot_nn(weights.astype(jnp.bfloat16), back)
                    dq_ref[g * HEAD : (g + 1) * HEAD, pl.ds(start, tile)] += dot_tn(
                        keys, back_scores
                    )
                return back_key, back_value

            zero = jnp.zeros((tile, HEAD), jnp.float32)
            carry = one(j, (zero, zero), True)
            carry = lax.fori_loop(j + 1, tiles, lambda i, c: one(i, c, False), carry)
            start = pl.multiple_of(j * tile, tile)
            sorted_grad[pl.ds(start, tile), k_at : k_at + HEAD] = (carry[0] * scale).astype(
                jnp.bfloat16
            )
            sorted_grad[pl.ds(start, tile), v_at : v_at + HEAD] = carry[1].astype(jnp.bfloat16)
            return 0

        lax.fori_loop(0, tiles, key_step, 0)
        for g in range(group):
            head = kv * group + g
            sorted_grad[:, head * HEAD : (head + 1) * HEAD] = (
                (dq_ref[g * HEAD : (g + 1) * HEAD, :] * scale).T.astype(jnp.bfloat16)
            )
    unsort_blocks(order_ref, sorted_grad, out_ref, blocks, rows)


def attend(order, qkv, q_heads, kv_heads):
    length, cols = qkv.shape
    whole = pl.BlockSpec(memory_space=pltpu.VMEM)
    return pl.pallas_call(
        functools.partial(attend_kernel, q_heads, kv_heads, 256),
        out_shape=(
            jax.ShapeDtypeStruct((length, q_heads * HEAD), jnp.bfloat16),
            jax.ShapeDtypeStruct((q_heads, length), jnp.float32),
        ),
        in_specs=[pl.BlockSpec(memory_space=pltpu.SMEM), whole],
        out_specs=(whole, whole),
        scratch_shapes=[
            pltpu.VMEM((length, cols), jnp.bfloat16),
            pltpu.VMEM((length, q_heads * HEAD), jnp.bfloat16),
        ],
        compiler_params=pltpu.CompilerParams(vmem_limit_bytes=40 << 20),
        cost_estimate=pl.CostEstimate(
            flops=2 * length * length * q_heads * HEAD,
            bytes_accessed=4 * length * cols,
            transcendentals=length * length * q_heads // 2,
        ),
    )(order, qkv)


def attend_back(order, qkv, back, lse, q_heads, kv_heads):
    length, cols = qkv.shape
    group = q_heads // kv_heads
    whole = pl.BlockSpec(memory_space=pltpu.VMEM)
    return pl.pallas_call(
        functools.partial(attend_back_kernel, q_heads, kv_heads, 256),
        out_shape=jax.ShapeDtypeStruct((length, cols), jnp.bfloat16),
        in_specs=[pl.BlockSpec(memory_space=pltpu.SMEM), whole, whole, whole],
        out_specs=whole,
        scratch_shapes=[
            pltpu.VMEM((length, cols), jnp.bfloat16),
            pltpu.VMEM((length, q_heads * HEAD), jnp.bfloat16),
            pltpu.VMEM((length, cols), jnp.bfloat16),
            pltpu.VMEM((group, length), jnp.float32),
            pltpu.VMEM((group * HEAD, length), jnp.float32),
        ],
        compiler_params=pltpu.CompilerParams(vmem_limit_bytes=40 << 20),
        cost_estimate=pl.CostEstimate(
            flops=7 * length * length * q_heads * HEAD,
            bytes_accessed=6 * length * cols,
            transcendentals=length * length * q_heads // 2,
        ),
    )(order, qkv, back, lse)


def local(
    tokens,
    cotangent,
    block_order,
    attention_in,
    attention_out,
    gate_up,
    down_matrix,
    gains,
    mean_attention_in,
    mean_attention_out,
    mean_gate_up,
    mean_down,
    mean_gains,
    square_attention_in,
    square_attention_out,
    square_gate_up,
    square_down,
    square_gains,
):
    seq_count, shard_rows, width = tokens.shape
    shards = lax.axis_size("ctx")
    device = lax.axis_index("ctx")
    owned = attention_in.shape[0]
    hidden_units = gate_up.shape[1] // 2
    part_hidden = hidden_units // 4
    part_q = HEADS * HEAD // 4
    part_k = KV_HEADS * HEAD // 4
    part_cols = part_q + 2 * part_k
    count = seq_count * shard_rows
    seqs = 4 * seq_count
    splits = shards // seqs
    q_heads = HEADS // 4 // splits
    kv_heads = max(1, KV_HEADS // 4 // splits)

    tokens_all = gather_dp(to_owner_order(tokens.reshape(count, width), shards))
    back_all = gather_dp(cotangent.reshape(count, width)).reshape(4 * count, width)

    in_low = attention_in.astype(jnp.bfloat16)
    in_pieces = jnp.concatenate(
        [
            in_low[:, : 4 * part_q].reshape(owned, 4, part_q),
            in_low[:, 4 * part_q : 4 * (part_q + part_k)].reshape(owned, 4, part_k),
            in_low[:, 4 * (part_q + part_k) :].reshape(owned, 4, part_k),
        ],
        2,
    ).swapaxes(0, 1)
    in_part = exchange_dp(in_pieces).reshape(4 * owned, part_cols)
    gains_low = gains.astype(jnp.bfloat16)
    gains_part = exchange_dp(jnp.broadcast_to(gains_low, (4, 2, owned)))
    gains_row = jnp.pad(gains_part.reshape(-1), (0, 16 * part_cols - 8 * owned))
    in_gathered = lax.all_gather(
        jnp.concatenate([in_part, gains_row.reshape(16, part_cols)]), "ctx", axis=0
    )
    w_in = in_gathered[:, : 4 * owned].reshape(width, part_cols)
    gains_all = in_gathered[:, 4 * owned :].reshape(shards, -1)[:, : 8 * owned]
    gains_all = gains_all.reshape(shards, 4, 2, owned).astype(jnp.float32)
    gain_one_own = gains_all[:, :, 0].reshape(width)
    gain_one = gains_all[:, :, 0].swapaxes(0, 1).reshape(width)
    gain_two = gains_all[:, :, 1].swapaxes(0, 1).reshape(width)
    w_out = lax.all_gather(attention_out.astype(jnp.bfloat16), "ctx", axis=0, tiled=True)
    gate_pieces = (
        gate_up.astype(jnp.bfloat16)
        .reshape(owned, 2, 4, part_hidden)
        .transpose(2, 0, 1, 3)
        .reshape(4, owned, 2 * part_hidden)
    )
    gate_part_rows = exchange_dp(gate_pieces).reshape(4 * owned, 2 * part_hidden)
    w_gate = lax.all_gather(gate_part_rows, "ctx", axis=0, tiled=True)
    w_down = lax.all_gather(down_matrix.astype(jnp.bfloat16), "ctx", axis=0, tiled=True)

    normed_all, _ = norm_parts(tokens_all.reshape(4 * count, width).astype(jnp.float32))
    input_one = (normed_all * gain_one_own).astype(jnp.bfloat16)
    projected = dot_nn(input_one, w_in)
    cosine, sine_table = rotary_tables(local_places(block_order, device, shard_rows), HEAD)
    cos_rows = cosine[:, None, :]
    sin_rows = sine_table[:, None, :]

    def turned(values, how):
        shape = values.shape
        heads = values.reshape(seqs, shard_rows, -1, HEAD)
        return how(heads, cos_rows, sin_rows).reshape(shape)

    def to_sequences(q, k, v):
        parts = []
        for values, each in (
            (q, q_heads * HEAD),
            (k, kv_heads * HEAD),
            (v, kv_heads * HEAD),
        ):
            groups = values.shape[1] // each
            values = values.reshape(seqs, shard_rows, groups, each).swapaxes(1, 2)
            values = jnp.repeat(values, splits // groups, axis=1)
            parts.append(values.reshape(shards, shard_rows, each))
        sent = jnp.concatenate(parts, 2)
        return lax.all_to_all(sent, "ctx", 0, 0, tiled=True).reshape(shards * shard_rows, -1)

    def from_sequences(rows):
        got = lax.all_to_all(
            rows.reshape(shards, shard_rows, -1), "ctx", 0, 0, tiled=True
        ).reshape(seqs, splits, shard_rows, -1)
        return got

    low = jnp.bfloat16
    query = turned(projected[:, :part_q], rotate).astype(low)
    key = turned(projected[:, part_q : part_q + part_k], rotate).astype(low)
    value = projected[:, part_q + part_k :].astype(low)
    qkv = to_sequences(query, key, value)
    attended_seq, lse = attend(block_order, qkv, q_heads, kv_heads)
    attended = from_sequences(attended_seq).swapaxes(1, 2).reshape(4 * count, part_q)

    flat_rows = tokens.reshape(count, width).astype(jnp.float32)
    normed_one, factor_one = norm_parts(flat_rows)
    residual = flat_rows + scatter_dp(dot_nn(attended, w_out).reshape(4, count, width))
    normed_two, factor_two = norm_parts(residual)
    input_two_own = to_owner_order((normed_two * gain_two).astype(low), shards)
    input_two = gather_dp(input_two_own).reshape(4 * count, width)
    gate_both = dot_nn(input_two, w_gate)
    gate_part = gate_both[:, :part_hidden]
    up_part = gate_both[:, part_hidden:]
    sigmoid_gate = jax.nn.sigmoid(gate_part)
    active = gate_part * sigmoid_gate
    hidden = (active * up_part).astype(low)
    output_rows = residual + scatter_dp(dot_nn(hidden, w_down).reshape(4, count, width))
    block_out = output_rows.astype(low).reshape(seq_count, shard_rows, width)

    def summed(gradient):
        return lax.psum_scatter(
            gradient.astype(low), "ctx", scatter_dimension=0, tiled=True
        )

    down_sum = summed(dot_tn(hidden, back_all)).astype(jnp.float32)
    back_hidden = dot_nt(back_all, w_down)
    back_gate = back_hidden * up_part * sigmoid_gate * (1.0 + gate_part * (1.0 - sigmoid_gate))
    back_upper = back_hidden * active
    back_gate_up = jnp.concatenate([back_gate, back_upper], 1).astype(low)
    gate_sum = summed(dot_tn(input_two, back_gate_up))
    gate_sum = exchange_dp(gate_sum.reshape(4, owned, 2 * part_hidden))
    gate_sum = (
        gate_sum.reshape(4, owned, 2, part_hidden)
        .transpose(1, 2, 0, 3)
        .reshape(owned, 2 * hidden_units)
        .astype(jnp.float32)
    )
    back_input_two = from_owner_order(
        scatter_dp(dot_nt(back_gate_up, w_gate).reshape(4, count, width)), shards
    )
    grad_gain_two = jnp.sum(back_input_two * normed_two, 0)
    back_residual = cotangent.reshape(count, width).astype(jnp.float32) + norm_back(
        back_input_two * gain_two, normed_two, factor_two
    )
    back_residual_all = gather_dp(back_residual.astype(low)).reshape(4 * count, width)
    out_sum = summed(dot_tn(attended, back_residual_all)).astype(jnp.float32)
    back_attended = dot_nt(back_residual_all, w_out).astype(low)
    sent = back_attended.reshape(seqs, shard_rows, splits, -1).swapaxes(1, 2)
    back_seq = lax.all_to_all(
        sent.reshape(shards, shard_rows, -1), "ctx", 0, 0, tiled=True
    ).reshape(shards * shard_rows, -1)
    back_qkv = attend_back(block_order, qkv, back_seq, lse, q_heads, kv_heads)
    back_qkv = from_sequences(back_qkv).astype(jnp.float32)
    cut = q_heads * HEAD
    each = kv_heads * HEAD
    back_query = back_qkv[..., :cut].swapaxes(1, 2).reshape(4 * count, part_q)

    def shared(values):
        groups = part_k // each
        values = values.reshape(seqs, groups, splits // groups, shard_rows, each).sum(2)
        return values.swapaxes(1, 2).reshape(4 * count, part_k)

    back_key = shared(back_qkv[..., cut : cut + each])
    back_value = shared(back_qkv[..., cut + each :])
    back_projected = jnp.concatenate(
        [turned(back_query, rotate_back), turned(back_key, rotate_back), back_value], 1
    ).astype(low)
    back_input_one = from_owner_order(
        scatter_dp(dot_nt(back_projected, w_in).reshape(4, count, width)), shards
    )
    grad_gain_one = jnp.sum(back_input_one * normed_one, 0)
    tokens_grad = (
        back_residual + norm_back(back_input_one * gain_one, normed_one, factor_one)
    ).reshape(seq_count, shard_rows, width)
    grad_gains = jnp.stack([grad_gain_one, grad_gain_two]).reshape(2, 4, shards, owned)
    gains_rows = grad_gains.transpose(2, 1, 0, 3).reshape(shards, 8 * owned)
    gains_rows = jnp.pad(gains_rows, ((0, 0), (0, 16 * part_cols - 8 * owned)))
    grad_in = dot_tn(input_one, back_projected).reshape(shards, 4 * owned, part_cols)
    grad_in = jnp.concatenate([grad_in, gains_rows.reshape(shards, 16, part_cols)], 1)
    in_sum = summed(grad_in.reshape(-1, part_cols))
    gains_part = in_sum[4 * owned :].reshape(-1)[: 8 * owned].reshape(4, 2, owned)
    gains_sum = exchange_dp(gains_part).astype(jnp.float32).sum(0)
    in_sum = exchange_dp(in_sum[: 4 * owned].reshape(4, owned, part_cols))

    def columns(first, last):
        return in_sum[..., first:last].swapaxes(0, 1).reshape(owned, -1)

    in_sum = jnp.concatenate(
        [
            columns(0, part_q),
            columns(part_q, part_q + part_k),
            columns(part_q + part_k, part_cols),
        ],
        1,
    ).astype(jnp.float32)
    new_in = adam_update(
        attention_in,
        in_sum,
        mean_attention_in,
        square_attention_in,
        input_boost * D ** (-0.5),
        weight_decay,
    )
    new_out = adam_update(
        attention_out,
        out_sum,
        mean_attention_out,
        square_attention_out,
        (HEADS * HEAD // 32) ** (-0.5),
        weight_decay,
    )
    new_gate = adam_update(
        gate_up, gate_sum, mean_gate_up, square_gate_up, D ** (-0.5), weight_decay
    )
    new_down = adam_update(
        down_matrix, down_sum, mean_down, square_down, FF ** (-0.5), weight_decay
    )
    new_gain = adam_update(gains, gains_sum, mean_gains, square_gains, gain_rate, 0.0)
    return (
        block_out,
        tokens_grad,
        new_in[0],
        new_in[1],
        new_in[2],
        new_out[0],
        new_out[1],
        new_out[2],
        new_gate[0],
        new_gate[1],
        new_gate[2],
        new_down[0],
        new_down[1],
        new_down[2],
        new_gain[0],
        new_gain[1],
        new_gain[2],
    )


def solution(mesh):
    in_specs = (
        P("dp", "ctx", None),
        P("dp", "ctx", None),
        P(),
        P(("dp", "ctx"), None),
        P(("dp", "ctx"), None),
        P(("dp", "ctx"), None),
        P(("dp", "ctx"), None),
        P(None, ("dp", "ctx")),
        P(("dp", "ctx"), None),
        P(("dp", "ctx"), None),
        P(("dp", "ctx"), None),
        P(("dp", "ctx"), None),
        P(None, ("dp", "ctx")),
        P(("dp", "ctx"), None),
        P(("dp", "ctx"), None),
        P(("dp", "ctx"), None),
        P(("dp", "ctx"), None),
        P(None, ("dp", "ctx")),
    )
    out_specs = (
        P("dp", "ctx", None),
        P("dp", "ctx", None),
        P(("dp", "ctx"), None),
        P(("dp", "ctx"), None),
        P(("dp", "ctx"), None),
        P(("dp", "ctx"), None),
        P(("dp", "ctx"), None),
        P(("dp", "ctx"), None),
        P(("dp", "ctx"), None),
        P(("dp", "ctx"), None),
        P(("dp", "ctx"), None),
        P(("dp", "ctx"), None),
        P(("dp", "ctx"), None),
        P(("dp", "ctx"), None),
        P(None, ("dp", "ctx")),
        P(None, ("dp", "ctx")),
        P(None, ("dp", "ctx")),
    )
    return jax.shard_map(local, mesh=mesh, in_specs=in_specs, out_specs=out_specs, check_vma=False)
```

```python
import functools

import jax
import jax.numpy as jnp
from jax import lax
from jax.experimental import pallas as pl
from jax.experimental.pallas import tpu as pltpu
from jax.sharding import PartitionSpec as P

D = 2048
HEADS = 32
KV_HEADS = 8
HEAD = 64
FF = 8192
STEP = 5


norm_eps = 1e-05
rope_base = 500000.0
beta_one = 0.9
beta_two = 0.95
gain_rate = 1.25
input_boost = 2.5
weight_decay = 0.1
adam_eps = 1e-08
masked_score = -1e30


def rotary_tables(positions, head_width):
    half_width = head_width // 2
    frequency = rope_base ** (-(jnp.arange(half_width, dtype=jnp.float32) * 2.0 / head_width))
    angles = positions.astype(jnp.float32)[:, None] * frequency[None, :]
    angles = jnp.concatenate([angles, angles], 1)
    return (jnp.cos(angles), jnp.sin(angles))


def norm_parts(values):
    factor = lax.rsqrt(jnp.mean(values * values, -1, keepdims=True) + norm_eps)
    return (values * factor, factor)


def norm_back(back_normed, normed, factor):
    return factor * (back_normed - normed * jnp.mean(back_normed * normed, -1, keepdims=True))


def adam_update(weight, gradient, first_moment, second_moment, step_rate, decay_rate):
    first_new = beta_one * first_moment + (1.0 - beta_one) * gradient
    second_new = beta_two * second_moment + (1.0 - beta_two) * gradient * gradient
    update = (
        first_new
        / (1.0 - beta_one**STEP)
        / (jnp.sqrt(second_new / (1.0 - beta_two**STEP)) + adam_eps)
    )
    return (first_new, second_new, weight - step_rate * (update + decay_rate * weight))


def swapped(values, by):
    return lax.ppermute(values, "dp", [(i, i ^ by) for i in range(4)])


def gather_dp(values):
    beside = swapped(values, 1)
    across = swapped(values, 2)
    corner = swapped(across, 1)
    return jnp.stack([values, beside, across, corner])


def scatter_dp(parts):
    low = parts.astype(jnp.bfloat16)
    beside = swapped(jnp.stack([low[1], low[3]]), 1).astype(jnp.float32)
    far = (parts[2] + beside[1]).astype(jnp.bfloat16)
    return parts[0] + beside[0] + swapped(far, 2).astype(jnp.float32)


def exchange_dp(pieces):
    mine = lax.axis_index("dp")
    slots = [lax.dynamic_index_in_dim(pieces, mine, 0, keepdims=False)]
    for by in (1, 2, 3):
        slots.append(swapped(lax.dynamic_index_in_dim(pieces, mine ^ by, 0, keepdims=False), by))
    slots = jnp.stack(slots)
    return jnp.stack(
        [lax.dynamic_index_in_dim(slots, mine ^ i, 0, keepdims=False) for i in range(4)]
    )


def to_owner_order(rows, shards):
    count, width = rows.shape
    return rows.reshape(count, 4, shards, -1).swapaxes(1, 2).reshape(count, width)


def from_owner_order(rows, shards):
    count, width = rows.shape
    return rows.reshape(count, shards, 4, -1).swapaxes(1, 2).reshape(count, width)


def dot_nn(a, b):
    return lax.dot_general(a, b, (((1,), (0,)), ((), ())), preferred_element_type=jnp.float32)


def dot_nt(a, b):
    return lax.dot_general(a, b, (((1,), (1,)), ((), ())), preferred_element_type=jnp.float32)


def dot_tn(a, b):
    return lax.dot_general(a, b, (((0,), (0,)), ((), ())), preferred_element_type=jnp.float32)


def causal_keep(tile):
    keys = lax.broadcasted_iota(jnp.int32, (tile, tile), 0)
    queries = lax.broadcasted_iota(jnp.int32, (tile, tile), 1)
    return keys <= queries


def turn_group(values, cos, sin, forward):
    lanes = lax.broadcasted_iota(jnp.int32, values.shape, 1)
    other = jnp.where(
        lanes % HEAD < HEAD // 2,
        pltpu.roll(values, 2 * HEAD - HEAD // 2, 1),
        pltpu.roll(values, HEAD // 2, 1),
    )
    if forward:
        return values * cos + other * sin
    return values * cos - other * sin


def turn_columns(values, start, turned_cols, cos, sin, forward):
    if start >= turned_cols:
        return values
    turned = turn_group(values, cos, sin, forward)
    if start + 2 * HEAD <= turned_cols:
        return turned
    lanes = lax.broadcasted_iota(jnp.int32, values.shape, 1)
    return jnp.where(lanes < turned_cols - start, turned, values)


def attend_kernel(
    q_heads, kv_heads, tile, order_ref, qkv_ref, cos_ref, sin_ref, out_ref, lse_ref, kept_ref, made
):
    length, cols = qkv_ref.shape
    blocks = order_ref.shape[0]
    rows = length // blocks
    group = q_heads // kv_heads
    q_cols, k_cols = q_heads * HEAD, kv_heads * HEAD
    scale = HEAD ** (-0.5)

    def take_block(i, _):
        start = pl.multiple_of(order_ref[i] * rows, rows)
        source = pl.multiple_of(i * rows, rows)
        cos = cos_ref[pl.ds(start, rows), :]
        sin = sin_ref[pl.ds(start, rows), :]
        for c in range(0, cols, 2 * HEAD):
            values = qkv_ref[pl.ds(source, rows), c : c + 2 * HEAD]
            values = turn_columns(values, c, q_cols + k_cols, cos, sin, True)
            kept_ref[pl.ds(start, rows), c : c + 2 * HEAD] = values.astype(jnp.bfloat16)
        return 0

    lax.fori_loop(0, blocks, take_block, 0)
    keep = causal_keep(tile)
    for kv in range(kv_heads):
        k_at = q_cols + kv * HEAD
        v_at = q_cols + k_cols + kv * HEAD

        def query_step(i, _):
            q_start = pl.multiple_of(i * tile, tile)
            queries = [
                kept_ref[
                    pl.ds(q_start, tile), (kv * group + g) * HEAD : (kv * group + g + 1) * HEAD
                ]
                for g in range(group)
            ]

            def key_tile(j, carry, masked):
                k_start = pl.multiple_of(j * tile, tile)
                keys = kept_ref[pl.ds(k_start, tile), k_at : k_at + HEAD]
                values = kept_ref[pl.ds(k_start, tile), v_at : v_at + HEAD]
                result = []
                for g in range(group):
                    peak, total, weighted = carry[g]
                    scores = dot_nt(keys, queries[g]) * scale
                    if masked:
                        scores = jnp.where(keep, scores, masked_score)
                    new_peak = jnp.maximum(peak, jnp.max(scores, 0, keepdims=True))
                    weights = jnp.exp(scores - new_peak)
                    shrink = jnp.exp(peak - new_peak)
                    total = total * shrink + jnp.sum(weights, 0, keepdims=True)
                    weighted = weighted * shrink + dot_tn(values, weights.astype(jnp.bfloat16))
                    result.append((new_peak, total, weighted))
                return tuple(result)

            start = tuple(
                (
                    jnp.full((1, tile), masked_score, jnp.float32),
                    jnp.zeros((1, tile), jnp.float32),
                    jnp.zeros((HEAD, tile), jnp.float32),
                )
                for _ in range(group)
            )
            carry = lax.fori_loop(0, i, lambda j, c: key_tile(j, c, False), start)
            carry = key_tile(i, carry, True)
            for g in range(group):
                head = kv * group + g
                peak, total, weighted = carry[g]
                lse_ref[head : head + 1, pl.ds(q_start, tile)] = peak + jnp.log(total)
                made[pl.ds(q_start, tile), head * HEAD : (head + 1) * HEAD] = (
                    (weighted / total).T.astype(jnp.bfloat16)
                )
            return 0

        lax.fori_loop(0, length // tile, query_step, 0)

    def give_block(i, _):
        start = pl.multiple_of(order_ref[i] * rows, rows)
        target = pl.multiple_of(i * rows, rows)
        out_ref[pl.ds(target, rows), :] = made[pl.ds(start, rows), :]
        return 0

    lax.fori_loop(0, blocks, give_block, 0)


def attend_back_kernel(
    q_heads,
    kv_heads,
    tile,
    order_ref,
    kept_ref,
    back_ref,
    lse_ref,
    cos_ref,
    sin_ref,
    out_ref,
    back_sorted,
    grad,
    delta_ref,
    dq_ref,
):
    length, cols = kept_ref.shape
    blocks = order_ref.shape[0]
    rows = length // blocks
    group = q_heads // kv_heads
    q_cols, k_cols = q_heads * HEAD, kv_heads * HEAD
    scale = HEAD ** (-0.5)
    tiles = length // tile

    def take_block(i, _):
        start = pl.multiple_of(order_ref[i] * rows, rows)
        source = pl.multiple_of(i * rows, rows)
        back_sorted[pl.ds(start, rows), :] = back_ref[pl.ds(source, rows), :]
        return 0

    lax.fori_loop(0, blocks, take_block, 0)
    keep = causal_keep(tile)
    for kv in range(kv_heads):
        k_at = q_cols + kv * HEAD
        v_at = q_cols + k_cols + kv * HEAD

        def load(i, g):
            start = pl.multiple_of(i * tile, tile)
            head = kv * group + g
            at = slice(head * HEAD, (head + 1) * HEAD)
            return (
                kept_ref[pl.ds(start, tile), at],
                back_sorted[pl.ds(start, tile), at],
                lse_ref[head : head + 1, pl.ds(start, tile)],
            )

        def load_kv(j):
            start = pl.multiple_of(j * tile, tile)
            return (
                kept_ref[pl.ds(start, tile), k_at : k_at + HEAD],
                kept_ref[pl.ds(start, tile), v_at : v_at + HEAD],
            )

        def tile_terms(keys, values, query, back, lse, masked):
            weights = jnp.exp(dot_nt(keys, query) * scale - lse)
            if masked:
                weights = jnp.where(keep, weights, 0.0)
            return weights, dot_nt(values, back)

        def delta_step(i, _):
            rows_i = [load(i, g) for g in range(group)]

            def one(j, carry, masked):
                keys, values = load_kv(j)
                result = []
                for g in range(group):
                    weights, back_weights = tile_terms(keys, values, *rows_i[g], masked)
                    result.append(carry[g] + jnp.sum(weights * back_weights, 0, keepdims=True))
                return tuple(result)

            carry = tuple(jnp.zeros((1, tile), jnp.float32) for _ in range(group))
            carry = lax.fori_loop(0, i, lambda j, c: one(j, c, False), carry)
            carry = one(i, carry, True)
            for g in range(group):
                delta_ref[g : g + 1, pl.ds(pl.multiple_of(i * tile, tile), tile)] = carry[g]
            return 0

        lax.fori_loop(0, tiles, delta_step, 0)
        dq_ref[...] = jnp.zeros_like(dq_ref)

        def key_step(j, _):
            keys, values = load_kv(j)

            def one(i, carry, masked):
                back_key, back_value = carry
                start = pl.multiple_of(i * tile, tile)
                for g in range(group):
                    query, back, lse = load(i, g)
                    weights, back_weights = tile_terms(keys, values, query, back, lse, masked)
                    delta = delta_ref[g : g + 1, pl.ds(start, tile)]
                    back_scores = (weights * (back_weights - delta)).astype(jnp.bfloat16)
                    back_key = back_key + dot_nn(back_scores, query)
                    back_value = back_value + dot_nn(weights.astype(jnp.bfloat16), back)
                    dq_ref[g * HEAD : (g + 1) * HEAD, pl.ds(start, tile)] += dot_tn(
                        keys, back_scores
                    )
                return back_key, back_value

            zero = jnp.zeros((tile, HEAD), jnp.float32)
            carry = one(j, (zero, zero), True)
            carry = lax.fori_loop(j + 1, tiles, lambda i, c: one(i, c, False), carry)
            start = pl.multiple_of(j * tile, tile)
            grad[pl.ds(start, tile), k_at : k_at + HEAD] = carry[0] * scale
            grad[pl.ds(start, tile), v_at : v_at + HEAD] = carry[1]
            return 0

        lax.fori_loop(0, tiles, key_step, 0)
        for g in range(group):
            head = kv * group + g
            grad[:, head * HEAD : (head + 1) * HEAD] = (
                dq_ref[g * HEAD : (g + 1) * HEAD, :] * scale
            ).T

    def give_block(i, _):
        start = pl.multiple_of(order_ref[i] * rows, rows)
        target = pl.multiple_of(i * rows, rows)
        cos = cos_ref[pl.ds(start, rows), :]
        sin = sin_ref[pl.ds(start, rows), :]
        for c in range(0, cols, 2 * HEAD):
            values = grad[pl.ds(start, rows), c : c + 2 * HEAD]
            values = turn_columns(values, c, q_cols + k_cols, cos, sin, False)
            out_ref[pl.ds(target, rows), c : c + 2 * HEAD] = values.astype(jnp.bfloat16)
        return 0

    lax.fori_loop(0, blocks, give_block, 0)


def position_tables(length):
    cosine, sine_table = rotary_tables(jnp.arange(length, dtype=jnp.int32), HEAD)
    sign = jnp.where(jnp.arange(HEAD) < HEAD // 2, -1.0, 1.0)
    return jnp.tile(cosine, (1, 2)), jnp.tile(sine_table * sign, (1, 2))


def attend(order, qkv, tables, q_heads, kv_heads):
    length, cols = qkv.shape
    whole = pl.BlockSpec(memory_space=pltpu.VMEM)
    return pl.pallas_call(
        functools.partial(attend_kernel, q_heads, kv_heads, 256),
        out_shape=(
            jax.ShapeDtypeStruct((length, q_heads * HEAD), jnp.bfloat16),
            jax.ShapeDtypeStruct((q_heads, length), jnp.float32),
            jax.ShapeDtypeStruct((length, cols), jnp.bfloat16),
        ),
        in_specs=[pl.BlockSpec(memory_space=pltpu.SMEM), whole, whole, whole],
        out_specs=(whole, whole, whole),
        scratch_shapes=[pltpu.VMEM((length, q_heads * HEAD), jnp.bfloat16)],
        compiler_params=pltpu.CompilerParams(vmem_limit_bytes=40 << 20),
        cost_estimate=pl.CostEstimate(
            flops=2 * length * length * q_heads * HEAD,
            bytes_accessed=8 * length * cols,
            transcendentals=length * length * q_heads // 2,
        ),
    )(order, qkv, *tables)


def attend_back(order, kept, back, lse, tables, q_heads, kv_heads):
    length, cols = kept.shape
    group = q_heads // kv_heads
    whole = pl.BlockSpec(memory_space=pltpu.VMEM)
    return pl.pallas_call(
        functools.partial(attend_back_kernel, q_heads, kv_heads, 256),
        out_shape=jax.ShapeDtypeStruct((length, cols), jnp.bfloat16),
        in_specs=[pl.BlockSpec(memory_space=pltpu.SMEM)] + [whole] * 5,
        out_specs=whole,
        scratch_shapes=[
            pltpu.VMEM((length, q_heads * HEAD), jnp.bfloat16),
            pltpu.VMEM((length, cols), jnp.float32),
            pltpu.VMEM((group, length), jnp.float32),
            pltpu.VMEM((group * HEAD, length), jnp.float32),
        ],
        compiler_params=pltpu.CompilerParams(vmem_limit_bytes=40 << 20),
        cost_estimate=pl.CostEstimate(
            flops=7 * length * length * q_heads * HEAD,
            bytes_accessed=6 * length * cols,
            transcendentals=length * length * q_heads // 2,
        ),
    )(order, kept, back, lse, *tables)


def moved_pairs(shards, splits, second):
    pairs = []
    for source in range(4 * shards):
        group, place = divmod(source, shards)
        sequence = 2 * group + (place + second) % 2
        part = place // 2
        pairs.append((source, part % 4 * shards + sequence * splits + part // 4))
    return pairs


def to_sequences(values, shards, splits):
    place = lax.axis_index("ctx")
    got = [
        lax.ppermute(
            lax.dynamic_index_in_dim(values, (place + second) % 2, 0, keepdims=False),
            ("dp", "ctx"),
            moved_pairs(shards, splits, second),
        )
        for second in (0, 1)
    ]
    odd = (place // splits) % 2 == 1
    return jnp.stack([jnp.where(odd, got[1], got[0]), jnp.where(odd, got[0], got[1])])


def from_sequences(values, shards, splits):
    place = lax.axis_index("ctx")
    odd = (place // splits) % 2
    got = [
        lax.ppermute(
            lax.dynamic_index_in_dim(values, (odd + second) % 2, 0, keepdims=False),
            ("dp", "ctx"),
            [(b, a) for a, b in moved_pairs(shards, splits, second)],
        )
        for second in (0, 1)
    ]
    swap = place % 2 == 1
    return jnp.stack([jnp.where(swap, got[1], got[0]), jnp.where(swap, got[0], got[1])])


def local(
    tokens,
    cotangent,
    block_order,
    attention_in,
    attention_out,
    gate_up,
    down_matrix,
    gains,
    mean_attention_in,
    mean_attention_out,
    mean_gate_up,
    mean_down,
    mean_gains,
    square_attention_in,
    square_attention_out,
    square_gate_up,
    square_down,
    square_gains,
):
    seq_count, shard_rows, width = tokens.shape
    shards = lax.axis_size("ctx")
    mine = lax.axis_index("dp")
    low = jnp.bfloat16
    owned = attention_in.shape[0]
    hidden_units = gate_up.shape[1] // 2
    part_hidden = hidden_units // 4
    part_q = HEADS * HEAD // 4
    part_k = KV_HEADS * HEAD // 4
    part_cols = part_q + 2 * part_k
    count = seq_count * shard_rows
    length = shards * shard_rows
    splits = shards // (4 * seq_count)
    q_heads = HEADS // 4 // splits
    kv_heads = max(1, KV_HEADS // 4 // splits)

    x_low = to_sequences(tokens, shards, splits).reshape(count, width)
    tokens_all = gather_dp(to_owner_order(x_low, shards))
    cot_own = to_sequences(cotangent, shards, splits).reshape(count, width)
    back_all = gather_dp(cot_own).reshape(4 * count, width)

    in_low = attention_in.astype(low)
    in_pieces = jnp.concatenate(
        [
            in_low[:, : 4 * part_q].reshape(owned, 4, part_q),
            in_low[:, 4 * part_q : 4 * (part_q + part_k)].reshape(owned, 4, part_k),
            in_low[:, 4 * (part_q + part_k) :].reshape(owned, 4, part_k),
        ],
        2,
    ).swapaxes(0, 1)
    in_part = exchange_dp(in_pieces).reshape(4 * owned, part_cols)
    gains_part = exchange_dp(jnp.broadcast_to(gains.astype(low), (4, 2, owned)))
    gains_rows = jnp.pad(gains_part.reshape(-1), (0, 16 * part_cols - 8 * owned))
    out_low = jnp.pad(attention_out.astype(low), ((0, 0), (0, 3 * part_cols - width)))
    first_gathered = lax.all_gather(
        jnp.concatenate(
            [
                in_part,
                out_low[:, :part_cols],
                out_low[:, part_cols : 2 * part_cols],
                out_low[:, 2 * part_cols :],
                gains_rows.reshape(16, part_cols),
            ]
        ),
        "ctx",
        axis=0,
    )
    w_in = first_gathered[:, : 4 * owned].reshape(width, part_cols)
    w_out = jnp.concatenate(
        [
            first_gathered[:, (4 + i) * owned : (5 + i) * owned].reshape(part_q, part_cols)
            for i in range(3)
        ],
        1,
    )[:, :width]
    gains_all = first_gathered[:, 7 * owned :].reshape(shards, -1)[:, : 8 * owned]
    gains_all = gains_all.reshape(shards, 4, 2, owned).astype(jnp.float32)
    gain_one_own = gains_all[:, :, 0].reshape(width)
    gain_one = gains_all[:, :, 0].swapaxes(0, 1).reshape(width)
    gain_two = gains_all[:, :, 1].swapaxes(0, 1).reshape(width)
    gate_pieces = (
        gate_up.astype(low)
        .reshape(owned, 2, 4, part_hidden)
        .transpose(2, 0, 1, 3)
        .reshape(4, owned, 2 * part_hidden)
    )
    gate_rows = exchange_dp(gate_pieces).reshape(4 * owned, 2 * part_hidden)
    gate_rows, first_gathered = lax.optimization_barrier((gate_rows, first_gathered))
    w_gate = lax.all_gather(gate_rows, "ctx", axis=0, tiled=True)
    down_rows, _ = lax.optimization_barrier((down_matrix.astype(low), w_gate[:1, :1]))
    w_down = lax.all_gather(down_rows, "ctx", axis=0, tiled=True)

    normed_all, _ = norm_parts(tokens_all.reshape(4 * count, width).astype(jnp.float32))
    input_one = (normed_all * gain_one_own).astype(low)
    qkv = dot_nn(input_one, w_in)
    slot_order = block_order.reshape(splits, 4, -1)
    slot_order = jnp.stack(
        [lax.dynamic_index_in_dim(slot_order, mine ^ by, 1, keepdims=False) for by in range(4)], 1
    ).reshape(-1)
    tables = position_tables(length)
    groups = [[s * splits + g for g in range(splits)] for s in range(shards // splits)]

    def split_heads(values, widths, copies):
        parts = []
        start = 0
        for each, repeat in zip(widths, copies):
            kinds = splits // repeat
            piece = values[:, start : start + kinds * each].reshape(-1, kinds, each)
            parts.append(jnp.repeat(piece.swapaxes(0, 1), repeat, axis=0))
            start += kinds * each
        sent = jnp.concatenate(parts, 2)
        got = lax.all_to_all(sent, "ctx", 0, 0, axis_index_groups=groups, tiled=True)
        return got.reshape(length, -1)

    def join_heads(values):
        sent = values.reshape(splits, 4 * count, -1)
        return lax.all_to_all(sent, "ctx", 0, 0, axis_index_groups=groups, tiled=True)

    q_width, k_width = q_heads * HEAD, kv_heads * HEAD
    copies = splits * k_width // part_k
    if splits > 1:
        qkv = split_heads(qkv, (q_width, k_width, k_width), (1, copies, copies))
    attended, lse, kept = attend(slot_order, qkv, tables, q_heads, kv_heads)
    if splits > 1:
        attended = join_heads(attended).swapaxes(0, 1).reshape(4 * count, part_q)

    flat_rows = x_low.astype(jnp.float32)
    normed_one, factor_one = norm_parts(flat_rows)
    residual = flat_rows + scatter_dp(dot_nn(attended, w_out).reshape(4, count, width))
    normed_two, factor_two = norm_parts(residual)
    input_two_own = to_owner_order((normed_two * gain_two).astype(low), shards)
    input_two = gather_dp(input_two_own).reshape(4 * count, width)
    gate_both = dot_nn(input_two, w_gate)
    gate_part = gate_both[:, :part_hidden]
    up_part = gate_both[:, part_hidden:]
    sigmoid_gate = jax.nn.sigmoid(gate_part)
    active = gate_part * sigmoid_gate
    hidden = (active * up_part).astype(low)
    output_rows = residual + scatter_dp(dot_nn(hidden, w_down).reshape(4, count, width))
    block_out = from_sequences(
        output_rows.astype(low).reshape(seq_count, shard_rows, width), shards, splits
    )

    def summed(gradient):
        return lax.psum_scatter(gradient.astype(low), "ctx", scatter_dimension=0, tiled=True)

    down_low = summed(dot_tn(hidden, back_all))
    down_sum = down_low.astype(jnp.float32)
    back_hidden = dot_nt(back_all, w_down)
    back_gate = back_hidden * up_part * sigmoid_gate * (1.0 + gate_part * (1.0 - sigmoid_gate))
    back_upper = back_hidden * active
    back_gate_up = jnp.concatenate([back_gate, back_upper], 1).astype(low)
    gate_low = summed(dot_tn(input_two, back_gate_up))
    gate_sum = exchange_dp(gate_low.reshape(4, owned, 2 * part_hidden))
    gate_sum = (
        gate_sum.reshape(4, owned, 2, part_hidden)
        .transpose(1, 2, 0, 3)
        .reshape(owned, 2 * hidden_units)
        .astype(jnp.float32)
    )
    back_input_two = from_owner_order(
        scatter_dp(dot_nt(back_gate_up, w_gate).reshape(4, count, width)), shards
    )
    grad_gain_two = jnp.sum(back_input_two * normed_two, 0)
    back_residual = cot_own.astype(jnp.float32) + norm_back(
        back_input_two * gain_two, normed_two, factor_two
    )
    back_residual_all = gather_dp(back_residual.astype(low)).reshape(4 * count, width)
    grad_out = dot_tn(attended, back_residual_all).astype(low)
    back_attended = dot_nt(back_residual_all, w_out).astype(low)
    if splits > 1:
        back_attended = split_heads(back_attended, (q_width,), (1,))
    back_projected = attend_back(
        slot_order, kept, back_attended, lse, tables, q_heads, kv_heads
    )
    if splits > 1:
        back_projected = join_heads(back_projected).astype(jnp.float32)

        def shared(values):
            values = values.reshape(splits // copies, copies, 4 * count, k_width).sum(1)
            return values.swapaxes(0, 1).reshape(4 * count, part_k)

        back_projected = jnp.concatenate(
            [
                back_projected[..., :q_width].swapaxes(0, 1).reshape(4 * count, part_q),
                shared(back_projected[..., q_width : q_width + k_width]),
                shared(back_projected[..., q_width + k_width :]),
            ],
            1,
        ).astype(low)
    back_input_one = from_owner_order(
        scatter_dp(dot_nt(back_projected, w_in).reshape(4, count, width)), shards
    )
    grad_gain_one = jnp.sum(back_input_one * normed_one, 0)
    tokens_grad = back_residual + norm_back(back_input_one * gain_one, normed_one, factor_one)
    tokens_grad = from_sequences(
        tokens_grad.astype(low).reshape(seq_count, shard_rows, width), shards, splits
    ).astype(jnp.float32)
    grad_gains = jnp.stack([grad_gain_one, grad_gain_two]).reshape(2, 4, shards, owned)
    gains_rows = grad_gains.transpose(2, 1, 0, 3).reshape(shards, 8 * owned).astype(low)
    gains_rows = jnp.pad(gains_rows, ((0, 0), (0, 16 * part_cols - 8 * owned)))
    grad_in = dot_tn(input_one, back_projected).astype(low)
    grad_out = jnp.pad(grad_out, ((0, 0), (0, 3 * part_cols - width)))
    grad_out = grad_out.reshape(shards, owned, 3 * part_cols)
    last = jnp.concatenate(
        [
            grad_in.reshape(shards, 4 * owned, part_cols),
            grad_out[..., :part_cols],
            grad_out[..., part_cols : 2 * part_cols],
            grad_out[..., 2 * part_cols :],
            gains_rows.reshape(shards, 16, part_cols),
        ],
        1,
    ).reshape(-1, part_cols)
    last, _ = lax.optimization_barrier((last, gate_low[:1, :1]))
    last_sum = summed(last)
    gains_part = last_sum[7 * owned :].reshape(-1)[: 8 * owned].reshape(4, 2, owned)
    gains_sum = exchange_dp(gains_part).astype(jnp.float32).sum(0)
    in_sum = exchange_dp(last_sum[: 4 * owned].reshape(4, owned, part_cols))
    out_sum = jnp.concatenate(
        [last_sum[(4 + i) * owned : (5 + i) * owned] for i in range(3)], 1
    )[:, :width].astype(jnp.float32)

    def columns(first, last):
        return in_sum[..., first:last].swapaxes(0, 1).reshape(owned, -1)

    in_sum = jnp.concatenate(
        [
            columns(0, part_q),
            columns(part_q, part_q + part_k),
            columns(part_q + part_k, part_cols),
        ],
        1,
    ).astype(jnp.float32)
    new_in = adam_update(
        attention_in,
        in_sum,
        mean_attention_in,
        square_attention_in,
        input_boost * D ** (-0.5),
        weight_decay,
    )
    new_out = adam_update(
        attention_out,
        out_sum,
        mean_attention_out,
        square_attention_out,
        (HEADS * HEAD // 32) ** (-0.5),
        weight_decay,
    )
    new_gate = adam_update(
        gate_up, gate_sum, mean_gate_up, square_gate_up, D ** (-0.5), weight_decay
    )
    new_down = adam_update(
        down_matrix, down_sum, mean_down, square_down, FF ** (-0.5), weight_decay
    )
    new_gain = adam_update(gains, gains_sum, mean_gains, square_gains, gain_rate, 0.0)
    return (
        block_out,
        tokens_grad,
        new_in[0],
        new_in[1],
        new_in[2],
        new_out[0],
        new_out[1],
        new_out[2],
        new_gate[0],
        new_gate[1],
        new_gate[2],
        new_down[0],
        new_down[1],
        new_down[2],
        new_gain[0],
        new_gain[1],
        new_gain[2],
    )


def solution(mesh):
    in_specs = (
        P("dp", "ctx", None),
        P("dp", "ctx", None),
        P(),
        P(("dp", "ctx"), None),
        P(("dp", "ctx"), None),
        P(("dp", "ctx"), None),
        P(("dp", "ctx"), None),
        P(None, ("dp", "ctx")),
        P(("dp", "ctx"), None),
        P(("dp", "ctx"), None),
        P(("dp", "ctx"), None),
        P(("dp", "ctx"), None),
        P(None, ("dp", "ctx")),
        P(("dp", "ctx"), None),
        P(("dp", "ctx"), None),
        P(("dp", "ctx"), None),
        P(("dp", "ctx"), None),
        P(None, ("dp", "ctx")),
    )
    out_specs = (
        P("dp", "ctx", None),
        P("dp", "ctx", None),
        P(("dp", "ctx"), None),
        P(("dp", "ctx"), None),
        P(("dp", "ctx"), None),
        P(("dp", "ctx"), None),
        P(("dp", "ctx"), None),
        P(("dp", "ctx"), None),
        P(("dp", "ctx"), None),
        P(("dp", "ctx"), None),
        P(("dp", "ctx"), None),
        P(("dp", "ctx"), None),
        P(("dp", "ctx"), None),
        P(("dp", "ctx"), None),
        P(None, ("dp", "ctx")),
        P(None, ("dp", "ctx")),
        P(None, ("dp", "ctx")),
    )
    return jax.shard_map(local, mesh=mesh, in_specs=in_specs, out_specs=out_specs, check_vma=False)
```

```python
import functools

import jax
import jax.numpy as jnp
from jax import lax
from jax.experimental import pallas as pl
from jax.experimental.pallas import tpu as pltpu
from jax.sharding import PartitionSpec as P

D = 2048
HEADS = 32
KV_HEADS = 8
HEAD = 64
FF = 8192
STEP = 5


norm_eps = 1e-05
rope_base = 500000.0
beta_one = 0.9
beta_two = 0.95
gain_rate = 1.25
input_boost = 2.5
weight_decay = 0.1
adam_eps = 1e-08
masked_score = -1e30


def rotary_tables(positions, head_width):
    half_width = head_width // 2
    frequency = rope_base ** (-(jnp.arange(half_width, dtype=jnp.float32) * 2.0 / head_width))
    angles = positions.astype(jnp.float32)[:, None] * frequency[None, :]
    angles = jnp.concatenate([angles, angles], 1)
    return (jnp.cos(angles), jnp.sin(angles))


def norm_parts(values):
    factor = lax.rsqrt(jnp.mean(values * values, -1, keepdims=True) + norm_eps)
    return (values * factor, factor)


def norm_back(back_normed, normed, factor):
    return factor * (back_normed - normed * jnp.mean(back_normed * normed, -1, keepdims=True))


def adam_update(weight, gradient, first_moment, second_moment, step_rate, decay_rate):
    first_new = beta_one * first_moment + (1.0 - beta_one) * gradient
    second_new = beta_two * second_moment + (1.0 - beta_two) * gradient * gradient
    update = (
        first_new
        / (1.0 - beta_one**STEP)
        / (jnp.sqrt(second_new / (1.0 - beta_two**STEP)) + adam_eps)
    )
    return (first_new, second_new, weight - step_rate * (update + decay_rate * weight))


def swapped(values, by):
    return lax.ppermute(values, "dp", [(i, i ^ by) for i in range(4)])


def gather_dp(values):
    beside = swapped(values, 1)
    across = swapped(values, 2)
    corner = swapped(across, 1)
    return jnp.stack([values, beside, across, corner])


def scatter_dp(parts):
    low = parts.astype(jnp.bfloat16)
    beside = swapped(jnp.stack([low[1], low[3]]), 1).astype(jnp.float32)
    far = (parts[2] + beside[1]).astype(jnp.bfloat16)
    return parts[0] + beside[0] + swapped(far, 2).astype(jnp.float32)


def exchange_dp(pieces):
    mine = lax.axis_index("dp")
    slots = [lax.dynamic_index_in_dim(pieces, mine, 0, keepdims=False)]
    for by in (1, 2, 3):
        slots.append(swapped(lax.dynamic_index_in_dim(pieces, mine ^ by, 0, keepdims=False), by))
    slots = jnp.stack(slots)
    return jnp.stack(
        [lax.dynamic_index_in_dim(slots, mine ^ i, 0, keepdims=False) for i in range(4)]
    )


def to_owner_order(rows, shards):
    count, width = rows.shape
    return rows.reshape(count, 4, shards, -1).swapaxes(1, 2).reshape(count, width)


def from_owner_order(rows, shards):
    count, width = rows.shape
    return rows.reshape(count, shards, 4, -1).swapaxes(1, 2).reshape(count, width)


def dot_nn(a, b):
    return lax.dot_general(a, b, (((1,), (0,)), ((), ())), preferred_element_type=jnp.float32)


def dot_nt(a, b):
    return lax.dot_general(a, b, (((1,), (1,)), ((), ())), preferred_element_type=jnp.float32)


def dot_tn(a, b):
    return lax.dot_general(a, b, (((0,), (0,)), ((), ())), preferred_element_type=jnp.float32)


def causal_keep(tile):
    keys = lax.broadcasted_iota(jnp.int32, (tile, tile), 0)
    queries = lax.broadcasted_iota(jnp.int32, (tile, tile), 1)
    return keys <= queries


def turn_group(values, cos, sin, forward):
    lanes = lax.broadcasted_iota(jnp.int32, values.shape, 1)
    other = jnp.where(
        lanes % HEAD < HEAD // 2,
        pltpu.roll(values, 2 * HEAD - HEAD // 2, 1),
        pltpu.roll(values, HEAD // 2, 1),
    )
    if forward:
        return values * cos + other * sin
    return values * cos - other * sin


def turn_columns(values, start, turned_cols, cos, sin, forward):
    if start >= turned_cols:
        return values
    turned = turn_group(values, cos, sin, forward)
    if start + 2 * HEAD <= turned_cols:
        return turned
    lanes = lax.broadcasted_iota(jnp.int32, values.shape, 1)
    return jnp.where(lanes < turned_cols - start, turned, values)


def attend_kernel(
    q_heads, kv_heads, tile, order_ref, qkv_ref, cos_ref, sin_ref, out_ref, lse_ref, kept_ref, made
):
    length, cols = qkv_ref.shape
    blocks = order_ref.shape[0]
    rows = length // blocks
    group = q_heads // kv_heads
    q_cols, k_cols = q_heads * HEAD, kv_heads * HEAD
    scale = HEAD ** (-0.5)

    def take_block(i, _):
        start = pl.multiple_of(order_ref[i] * rows, rows)
        source = pl.multiple_of(i * rows, rows)
        cos = cos_ref[pl.ds(start, rows), :]
        sin = sin_ref[pl.ds(start, rows), :]
        for c in range(0, cols, 2 * HEAD):
            values = qkv_ref[pl.ds(source, rows), c : c + 2 * HEAD]
            values = turn_columns(values, c, q_cols + k_cols, cos, sin, True)
            kept_ref[pl.ds(start, rows), c : c + 2 * HEAD] = values.astype(jnp.bfloat16)
        return 0

    lax.fori_loop(0, blocks, take_block, 0)
    keep = causal_keep(tile)
    for kv in range(kv_heads):
        k_at = q_cols + kv * HEAD
        v_at = q_cols + k_cols + kv * HEAD

        def query_step(i, _):
            q_start = pl.multiple_of(i * tile, tile)
            queries = [
                kept_ref[
                    pl.ds(q_start, tile), (kv * group + g) * HEAD : (kv * group + g + 1) * HEAD
                ]
                for g in range(group)
            ]

            def key_tile(j, carry, masked):
                k_start = pl.multiple_of(j * tile, tile)
                keys = kept_ref[pl.ds(k_start, tile), k_at : k_at + HEAD]
                values = kept_ref[pl.ds(k_start, tile), v_at : v_at + HEAD]
                result = []
                for g in range(group):
                    peak, total, weighted = carry[g]
                    scores = dot_nt(keys, queries[g]) * scale
                    if masked:
                        scores = jnp.where(keep, scores, masked_score)
                    new_peak = jnp.maximum(peak, jnp.max(scores, 0, keepdims=True))
                    weights = jnp.exp(scores - new_peak)
                    shrink = jnp.exp(peak - new_peak)
                    total = total * shrink + jnp.sum(weights, 0, keepdims=True)
                    weighted = weighted * shrink + dot_tn(values, weights.astype(jnp.bfloat16))
                    result.append((new_peak, total, weighted))
                return tuple(result)

            start = tuple(
                (
                    jnp.full((1, tile), masked_score, jnp.float32),
                    jnp.zeros((1, tile), jnp.float32),
                    jnp.zeros((HEAD, tile), jnp.float32),
                )
                for _ in range(group)
            )
            carry = lax.fori_loop(0, i, lambda j, c: key_tile(j, c, False), start)
            carry = key_tile(i, carry, True)
            for g in range(group):
                head = kv * group + g
                peak, total, weighted = carry[g]
                lse_ref[head : head + 1, pl.ds(q_start, tile)] = peak + jnp.log(total)
                made[pl.ds(q_start, tile), head * HEAD : (head + 1) * HEAD] = (
                    (weighted / total).T.astype(jnp.bfloat16)
                )
            return 0

        lax.fori_loop(0, length // tile, query_step, 0)

    def give_block(i, _):
        start = pl.multiple_of(order_ref[i] * rows, rows)
        target = pl.multiple_of(i * rows, rows)
        out_ref[pl.ds(target, rows), :] = made[pl.ds(start, rows), :]
        return 0

    lax.fori_loop(0, blocks, give_block, 0)


def attend_back_kernel(
    q_heads,
    kv_heads,
    tile,
    order_ref,
    kept_ref,
    back_ref,
    lse_ref,
    cos_ref,
    sin_ref,
    out_ref,
    back_sorted,
    grad,
    delta_ref,
    dq_ref,
):
    length, cols = kept_ref.shape
    blocks = order_ref.shape[0]
    rows = length // blocks
    group = q_heads // kv_heads
    q_cols, k_cols = q_heads * HEAD, kv_heads * HEAD
    scale = HEAD ** (-0.5)
    tiles = length // tile

    def take_block(i, _):
        start = pl.multiple_of(order_ref[i] * rows, rows)
        source = pl.multiple_of(i * rows, rows)
        back_sorted[pl.ds(start, rows), :] = back_ref[pl.ds(source, rows), :]
        return 0

    lax.fori_loop(0, blocks, take_block, 0)
    keep = causal_keep(tile)
    for kv in range(kv_heads):
        k_at = q_cols + kv * HEAD
        v_at = q_cols + k_cols + kv * HEAD

        def load(i, g):
            start = pl.multiple_of(i * tile, tile)
            head = kv * group + g
            at = slice(head * HEAD, (head + 1) * HEAD)
            return (
                kept_ref[pl.ds(start, tile), at],
                back_sorted[pl.ds(start, tile), at],
                lse_ref[head : head + 1, pl.ds(start, tile)],
            )

        def load_kv(j):
            start = pl.multiple_of(j * tile, tile)
            return (
                kept_ref[pl.ds(start, tile), k_at : k_at + HEAD],
                kept_ref[pl.ds(start, tile), v_at : v_at + HEAD],
            )

        def tile_terms(keys, values, query, back, lse, masked):
            weights = jnp.exp(dot_nt(keys, query) * scale - lse)
            if masked:
                weights = jnp.where(keep, weights, 0.0)
            return weights, dot_nt(values, back)

        def delta_step(i, _):
            rows_i = [load(i, g) for g in range(group)]

            def one(j, carry, masked):
                keys, values = load_kv(j)
                result = []
                for g in range(group):
                    weights, back_weights = tile_terms(keys, values, *rows_i[g], masked)
                    result.append(carry[g] + jnp.sum(weights * back_weights, 0, keepdims=True))
                return tuple(result)

            carry = tuple(jnp.zeros((1, tile), jnp.float32) for _ in range(group))
            carry = lax.fori_loop(0, i, lambda j, c: one(j, c, False), carry)
            carry = one(i, carry, True)
            for g in range(group):
                delta_ref[g : g + 1, pl.ds(pl.multiple_of(i * tile, tile), tile)] = carry[g]
            return 0

        lax.fori_loop(0, tiles, delta_step, 0)
        dq_ref[...] = jnp.zeros_like(dq_ref)

        def key_step(j, _):
            keys, values = load_kv(j)

            def one(i, carry, masked):
                back_key, back_value = carry
                start = pl.multiple_of(i * tile, tile)
                for g in range(group):
                    query, back, lse = load(i, g)
                    weights, back_weights = tile_terms(keys, values, query, back, lse, masked)
                    delta = delta_ref[g : g + 1, pl.ds(start, tile)]
                    back_scores = (weights * (back_weights - delta)).astype(jnp.bfloat16)
                    back_key = back_key + dot_nn(back_scores, query)
                    back_value = back_value + dot_nn(weights.astype(jnp.bfloat16), back)
                    dq_ref[g * HEAD : (g + 1) * HEAD, pl.ds(start, tile)] += dot_tn(
                        keys, back_scores
                    )
                return back_key, back_value

            zero = jnp.zeros((tile, HEAD), jnp.float32)
            carry = one(j, (zero, zero), True)
            carry = lax.fori_loop(j + 1, tiles, lambda i, c: one(i, c, False), carry)
            start = pl.multiple_of(j * tile, tile)
            grad[pl.ds(start, tile), k_at : k_at + HEAD] = carry[0] * scale
            grad[pl.ds(start, tile), v_at : v_at + HEAD] = carry[1]
            return 0

        lax.fori_loop(0, tiles, key_step, 0)
        for g in range(group):
            head = kv * group + g
            grad[:, head * HEAD : (head + 1) * HEAD] = (
                dq_ref[g * HEAD : (g + 1) * HEAD, :] * scale
            ).T

    def give_block(i, _):
        start = pl.multiple_of(order_ref[i] * rows, rows)
        target = pl.multiple_of(i * rows, rows)
        cos = cos_ref[pl.ds(start, rows), :]
        sin = sin_ref[pl.ds(start, rows), :]
        for c in range(0, cols, 2 * HEAD):
            values = grad[pl.ds(start, rows), c : c + 2 * HEAD]
            values = turn_columns(values, c, q_cols + k_cols, cos, sin, False)
            out_ref[pl.ds(target, rows), c : c + 2 * HEAD] = values.astype(jnp.bfloat16)
        return 0

    lax.fori_loop(0, blocks, give_block, 0)


MESH = pl.DeviceIdType.MESH


def chunk_rows(rows, width, most):
    best = 16
    for size in range(16, rows + 1, 16):
        if rows % size == 0 and size * width <= most:
            best = size
    return best


def greet(peers):
    barrier = pltpu.get_barrier_semaphore()
    for peer in peers:
        pl.semaphore_signal(barrier, inc=1, device_id=peer, device_id_type=MESH)
    pl.semaphore_wait(barrier, len(peers))


def sum_kernel(shards, plans, *refs):
    count = len(plans)
    slow = shards // 2
    sources, totals = refs[:count], refs[count : 2 * count]
    scratch = refs[2 * count :]
    group = lax.axis_index("dp")
    place = lax.axis_index("ctx")
    half, slot = place % 2, place // 2
    pair = (group, place - half + 1 - half)
    owners = [(group, (slot ^ by) * 2 + half) for by in range(1, slow)]
    greet([pair] + owners)
    for piece in range(count):
        chunks, rows = plans[piece]
        source, total = sources[piece], totals[piece]
        landed, arrived, kept, sent = scratch[9 * piece : 9 * piece + 4]
        kept_sem, pair_send, pair_recv, own_send, own_recv = scratch[9 * piece + 4 : 9 * piece + 9]
        ahead = kept.shape[0]

        def window(c):
            return pl.ds(pl.multiple_of(c * rows, rows), rows)

        def to_pair(c):
            return pltpu.make_async_remote_copy(
                src_ref=source.at[:, 1 - half, window(c)],
                dst_ref=landed.at[c],
                send_sem=pair_send.at[c],
                recv_sem=pair_recv.at[c],
                device_id=pair,
                device_id_type=MESH,
            )

        def keep(c):
            return pltpu.make_async_copy(
                source.at[:, half, window(c)], kept.at[c % ahead], kept_sem.at[c % ahead]
            )

        def to_owner(c, by):
            return pltpu.make_async_remote_copy(
                src_ref=sent.at[c, by - 1],
                dst_ref=arrived.at[c, by - 1],
                send_sem=own_send.at[c, by - 1],
                recv_sem=own_recv.at[c, by - 1],
                device_id=owners[by - 1],
                device_id_type=MESH,
            )

        def start(c):
            to_pair(c).start()
            keep(c).start()

        def pass_on(c):
            keep(c).wait()
            to_pair(c).wait_recv()
            for by in range(1, slow):
                both = kept[c % ahead, slot ^ by].astype(jnp.float32) + landed[
                    c, slot ^ by
                ].astype(jnp.float32)
                sent[c, by - 1] = both.astype(jnp.bfloat16)
                to_owner(c, by).start()
            total[window(c), :] = kept[c % ahead, slot].astype(jnp.float32) + landed[
                c, slot
            ].astype(jnp.float32)

        def finish(c):
            value = total[window(c), :]
            for by in range(1, slow):
                to_owner(c, by).wait_recv()
                value = value + arrived[c, by - 1].astype(jnp.float32)
            total[window(c), :] = value

        for c in range(min(ahead, chunks)):
            start(c)

        def step(c, _):
            pass_on(c)

            @pl.when(c + ahead < chunks)
            def _():
                start(c + ahead)

            @pl.when(c > 0)
            def _():
                finish(c - 1)

            return 0

        lax.fori_loop(0, chunks, step, 0)
        finish(chunks - 1)

        def drain(c, _):
            to_pair(c).wait_send()
            for by in range(1, slow):
                to_owner(c, by).wait_send()
            return 0

        lax.fori_loop(0, chunks, drain, 0)


def sums_over_ctx(pieces, shards, identity):
    slow = shards // 2
    plans, scratch, shapes, views = [], [], [], []
    for piece in pieces:
        rows, width = piece.shape[0] // shards, piece.shape[1]
        size = chunk_rows(rows, width, 1 << 16)
        chunks = rows // size
        ahead = min(3, chunks)
        plans.append((chunks, size))
        views.append(piece.reshape(slow, 2, rows, width))
        shapes.append(jax.ShapeDtypeStruct((rows, width), jnp.float32))
        scratch += [
            pltpu.VMEM((chunks, slow, size, width), jnp.bfloat16),
            pltpu.VMEM((chunks, slow - 1, size, width), jnp.bfloat16),
            pltpu.VMEM((ahead, slow, size, width), jnp.bfloat16),
            pltpu.VMEM((chunks, slow - 1, size, width), jnp.bfloat16),
            pltpu.SemaphoreType.DMA((ahead,)),
            pltpu.SemaphoreType.DMA((chunks,)),
            pltpu.SemaphoreType.DMA((chunks,)),
            pltpu.SemaphoreType.DMA((chunks, slow - 1)),
            pltpu.SemaphoreType.DMA((chunks, slow - 1)),
        ]
    return pl.pallas_call(
        functools.partial(sum_kernel, shards, tuple(plans)),
        out_shape=tuple(shapes),
        in_specs=[pl.BlockSpec(memory_space=pl.ANY)] * len(pieces),
        out_specs=tuple(pl.BlockSpec(memory_space=pltpu.VMEM) for _ in pieces),
        scratch_shapes=scratch,
        compiler_params=pltpu.CompilerParams(
            collective_id=identity, has_side_effects=True, vmem_limit_bytes=56 << 20
        ),
    )(*views)


def position_tables(length):
    cosine, sine_table = rotary_tables(jnp.arange(length, dtype=jnp.int32), HEAD)
    sign = jnp.where(jnp.arange(HEAD) < HEAD // 2, -1.0, 1.0)
    return jnp.tile(cosine, (1, 2)), jnp.tile(sine_table * sign, (1, 2))


def attend(order, qkv, tables, q_heads, kv_heads):
    length, cols = qkv.shape
    whole = pl.BlockSpec(memory_space=pltpu.VMEM)
    return pl.pallas_call(
        functools.partial(attend_kernel, q_heads, kv_heads, 256),
        out_shape=(
            jax.ShapeDtypeStruct((length, q_heads * HEAD), jnp.bfloat16),
            jax.ShapeDtypeStruct((q_heads, length), jnp.float32),
            jax.ShapeDtypeStruct((length, cols), jnp.bfloat16),
        ),
        in_specs=[pl.BlockSpec(memory_space=pltpu.SMEM), whole, whole, whole],
        out_specs=(whole, whole, whole),
        scratch_shapes=[pltpu.VMEM((length, q_heads * HEAD), jnp.bfloat16)],
        compiler_params=pltpu.CompilerParams(vmem_limit_bytes=40 << 20),
        cost_estimate=pl.CostEstimate(
            flops=2 * length * length * q_heads * HEAD,
            bytes_accessed=8 * length * cols,
            transcendentals=length * length * q_heads // 2,
        ),
    )(order, qkv, *tables)


def attend_back(order, kept, back, lse, tables, q_heads, kv_heads):
    length, cols = kept.shape
    group = q_heads // kv_heads
    whole = pl.BlockSpec(memory_space=pltpu.VMEM)
    return pl.pallas_call(
        functools.partial(attend_back_kernel, q_heads, kv_heads, 256),
        out_shape=jax.ShapeDtypeStruct((length, cols), jnp.bfloat16),
        in_specs=[pl.BlockSpec(memory_space=pltpu.SMEM)] + [whole] * 5,
        out_specs=whole,
        scratch_shapes=[
            pltpu.VMEM((length, q_heads * HEAD), jnp.bfloat16),
            pltpu.VMEM((length, cols), jnp.float32),
            pltpu.VMEM((group, length), jnp.float32),
            pltpu.VMEM((group * HEAD, length), jnp.float32),
        ],
        compiler_params=pltpu.CompilerParams(vmem_limit_bytes=40 << 20),
        cost_estimate=pl.CostEstimate(
            flops=7 * length * length * q_heads * HEAD,
            bytes_accessed=6 * length * cols,
            transcendentals=length * length * q_heads // 2,
        ),
    )(order, kept, back, lse, *tables)


def part_owner(part):
    return part % 2 * 2 + part // 2


def moved_pairs(shards, splits, second):
    pairs = []
    for source in range(4 * shards):
        group, place = divmod(source, shards)
        sequence = 2 * group + (place + second) % 2
        part = place // 2
        pairs.append((source, part_owner(part % 4) * shards + sequence * splits + part // 4))
    return pairs


def to_sequences(values, shards, splits):
    place = lax.axis_index("ctx")
    got = [
        lax.ppermute(
            lax.dynamic_index_in_dim(values, (place + second) % 2, 0, keepdims=False),
            ("dp", "ctx"),
            moved_pairs(shards, splits, second),
        )
        for second in (0, 1)
    ]
    odd = (place // splits) % 2 == 1
    return jnp.stack([jnp.where(odd, got[1], got[0]), jnp.where(odd, got[0], got[1])])


def from_sequences(values, shards, splits):
    place = lax.axis_index("ctx")
    odd = (place // splits) % 2
    got = [
        lax.ppermute(
            lax.dynamic_index_in_dim(values, (odd + second) % 2, 0, keepdims=False),
            ("dp", "ctx"),
            [(b, a) for a, b in moved_pairs(shards, splits, second)],
        )
        for second in (0, 1)
    ]
    swap = place % 2 == 1
    return jnp.stack([jnp.where(swap, got[1], got[0]), jnp.where(swap, got[0], got[1])])


def local(
    tokens,
    cotangent,
    block_order,
    attention_in,
    attention_out,
    gate_up,
    down_matrix,
    gains,
    mean_attention_in,
    mean_attention_out,
    mean_gate_up,
    mean_down,
    mean_gains,
    square_attention_in,
    square_attention_out,
    square_gate_up,
    square_down,
    square_gains,
):
    seq_count, shard_rows, width = tokens.shape
    shards = lax.axis_size("ctx")
    mine = lax.axis_index("dp")
    low = jnp.bfloat16
    owned = attention_in.shape[0]
    hidden_units = gate_up.shape[1] // 2
    part_hidden = hidden_units // 4
    part_q = HEADS * HEAD // 4
    part_k = KV_HEADS * HEAD // 4
    part_cols = part_q + 2 * part_k
    count = seq_count * shard_rows
    length = shards * shard_rows
    splits = shards // (4 * seq_count)
    gain_rows = 16 + -(7 * owned + 16) % 32
    q_heads = HEADS // 4 // splits
    kv_heads = max(1, KV_HEADS // 4 // splits)

    both = to_sequences(jnp.concatenate([tokens, cotangent], 2), shards, splits)
    both = both.reshape(count, 2 * width)
    x_low = both[:, :width]
    cot_own = both[:, width:]
    tokens_all = gather_dp(to_owner_order(x_low, shards))
    back_all = gather_dp(cot_own).reshape(4 * count, width)

    in_low = (attention_in + 0.0 * both[0, 0].astype(jnp.float32)).astype(low)
    in_pieces = jnp.concatenate(
        [
            in_low[:, : 4 * part_q].reshape(owned, 4, part_q),
            in_low[:, 4 * part_q : 4 * (part_q + part_k)].reshape(owned, 4, part_k),
            in_low[:, 4 * (part_q + part_k) :].reshape(owned, 4, part_k),
        ],
        2,
    ).swapaxes(0, 1)
    in_part = exchange_dp(in_pieces).reshape(4 * owned, part_cols)
    gains_part = exchange_dp(jnp.broadcast_to(gains.astype(low), (4, 2, owned)))
    gains_rows = jnp.pad(gains_part.reshape(-1), (0, gain_rows * part_cols - 8 * owned))
    out_low = jnp.pad(attention_out.astype(low), ((0, 0), (0, 3 * part_cols - width)))
    first_gathered = lax.all_gather(
        jnp.concatenate(
            [
                in_part,
                out_low[:, :part_cols],
                out_low[:, part_cols : 2 * part_cols],
                out_low[:, 2 * part_cols :],
                gains_rows.reshape(gain_rows, part_cols),
            ]
        ),
        "ctx",
        axis=0,
    )
    w_in = first_gathered[:, : 4 * owned].reshape(width, part_cols)
    w_out = jnp.concatenate(
        [
            first_gathered[:, (4 + i) * owned : (5 + i) * owned].reshape(part_q, part_cols)
            for i in range(3)
        ],
        1,
    )[:, :width]
    gains_all = first_gathered[:, 7 * owned :].reshape(shards, -1)[:, : 8 * owned]
    gains_all = gains_all.reshape(shards, 4, 2, owned).astype(jnp.float32)
    gain_one_own = gains_all[:, :, 0].reshape(width)
    gain_one = gains_all[:, :, 0].swapaxes(0, 1).reshape(width)
    gain_two = gains_all[:, :, 1].swapaxes(0, 1).reshape(width)
    gate_pieces = (
        gate_up.astype(low)
        .reshape(owned, 2, 4, part_hidden)
        .transpose(2, 0, 1, 3)
        .reshape(4, owned, 2 * part_hidden)
    )
    gate_rows = exchange_dp(gate_pieces).reshape(4 * owned, 2 * part_hidden)
    gate_rows, first_gathered = lax.optimization_barrier((gate_rows, first_gathered))
    w_gate = lax.all_gather(gate_rows, "ctx", axis=0, tiled=True)
    down_rows, _ = lax.optimization_barrier((down_matrix.astype(low), w_gate[:1, :1]))
    w_down = lax.all_gather(down_rows, "ctx", axis=0, tiled=True)

    normed_all, _ = norm_parts(tokens_all.reshape(4 * count, width).astype(jnp.float32))
    input_one = (normed_all * gain_one_own).astype(low)
    qkv = dot_nn(input_one, w_in)
    slot_order = block_order.reshape(splits, 4, -1)
    slot_order = jnp.stack(
        [
            lax.dynamic_index_in_dim(slot_order, part_owner(mine ^ by), 1, keepdims=False)
            for by in range(4)
        ],
        1,
    ).reshape(-1)
    tables = position_tables(length)
    groups = [[s * splits + g for g in range(splits)] for s in range(shards // splits)]

    def split_heads(values, widths, copies):
        parts = []
        start = 0
        for each, repeat in zip(widths, copies):
            kinds = splits // repeat
            piece = values[:, start : start + kinds * each].reshape(-1, kinds, each)
            parts.append(jnp.repeat(piece.swapaxes(0, 1), repeat, axis=0))
            start += kinds * each
        sent = jnp.concatenate(parts, 2)
        got = lax.all_to_all(sent, "ctx", 0, 0, axis_index_groups=groups, tiled=True)
        return got.reshape(length, -1)

    def join_heads(values):
        sent = values.reshape(splits, 4 * count, -1)
        return lax.all_to_all(sent, "ctx", 0, 0, axis_index_groups=groups, tiled=True)

    q_width, k_width = q_heads * HEAD, kv_heads * HEAD
    copies = splits * k_width // part_k
    if splits > 1:
        qkv = split_heads(qkv, (q_width, k_width, k_width), (1, copies, copies))
    attended, lse, kept = attend(slot_order, qkv, tables, q_heads, kv_heads)
    if splits > 1:
        attended = join_heads(attended).swapaxes(0, 1).reshape(4 * count, part_q)

    flat_rows = x_low.astype(jnp.float32)
    normed_one, factor_one = norm_parts(flat_rows)
    residual = flat_rows + scatter_dp(dot_nn(attended, w_out).reshape(4, count, width))
    normed_two, factor_two = norm_parts(residual)
    input_two_own = to_owner_order((normed_two * gain_two).astype(low), shards)
    input_two = gather_dp(input_two_own).reshape(4 * count, width)
    gate_both = dot_nn(input_two, w_gate)
    gate_part = gate_both[:, :part_hidden]
    up_part = gate_both[:, part_hidden:]
    sigmoid_gate = jax.nn.sigmoid(gate_part)
    active = gate_part * sigmoid_gate
    hidden = (active * up_part).astype(low)
    output_rows = residual + scatter_dp(dot_nn(hidden, w_down).reshape(4, count, width))

    down_low = lax.psum_scatter(
        dot_tn(hidden, back_all).astype(low), "ctx", scatter_dimension=0, tiled=True
    )
    down_sum = down_low.astype(jnp.float32)
    back_hidden = dot_nt(back_all, w_down)
    back_gate = back_hidden * up_part * sigmoid_gate * (1.0 + gate_part * (1.0 - sigmoid_gate))
    back_upper = back_hidden * active
    back_gate_up = jnp.concatenate([back_gate, back_upper], 1).astype(low)
    grad_gate = dot_tn(input_two, back_gate_up).astype(low)
    back_input_two = from_owner_order(
        scatter_dp(dot_nt(back_gate_up, w_gate).reshape(4, count, width)), shards
    )
    grad_gain_two = jnp.sum(back_input_two * normed_two, 0)
    back_residual = cot_own.astype(jnp.float32) + norm_back(
        back_input_two * gain_two, normed_two, factor_two
    )
    back_residual_all = gather_dp(back_residual.astype(low)).reshape(4 * count, width)
    grad_out = dot_tn(attended, back_residual_all).astype(low)
    back_attended = dot_nt(back_residual_all, w_out).astype(low)
    if splits > 1:
        back_attended = split_heads(back_attended, (q_width,), (1,))
    back_projected = attend_back(
        slot_order, kept, back_attended, lse, tables, q_heads, kv_heads
    )
    if splits > 1:
        back_projected = join_heads(back_projected).astype(jnp.float32)

        def shared(values):
            values = values.reshape(splits // copies, copies, 4 * count, k_width).sum(1)
            return values.swapaxes(0, 1).reshape(4 * count, part_k)

        back_projected = jnp.concatenate(
            [
                back_projected[..., :q_width].swapaxes(0, 1).reshape(4 * count, part_q),
                shared(back_projected[..., q_width : q_width + k_width]),
                shared(back_projected[..., q_width + k_width :]),
            ],
            1,
        ).astype(low)
    back_input_one = from_owner_order(
        scatter_dp(dot_nt(back_projected, w_in).reshape(4, count, width)), shards
    )
    grad_gain_one = jnp.sum(back_input_one * normed_one, 0)
    tokens_grad = back_residual + norm_back(back_input_one * gain_one, normed_one, factor_one)
    both = jnp.concatenate([output_rows.astype(low), tokens_grad.astype(low)], 1)
    both = from_sequences(both.reshape(seq_count, shard_rows, 2 * width), shards, splits)
    block_out = both[..., :width]
    tokens_grad = both[..., width:].astype(jnp.float32)
    grad_gains = jnp.stack([grad_gain_one, grad_gain_two]).reshape(2, 4, shards, owned)
    gains_rows = grad_gains.transpose(2, 1, 0, 3).reshape(shards, 8 * owned).astype(low)
    gains_rows = jnp.pad(gains_rows, ((0, 0), (0, gain_rows * part_cols - 8 * owned)))
    grad_in = dot_tn(input_one, back_projected).astype(low)
    grad_out = jnp.pad(grad_out, ((0, 0), (0, 3 * part_cols - width)))
    grad_out = grad_out.reshape(shards, owned, 3 * part_cols)
    last = jnp.concatenate(
        [
            grad_in.reshape(shards, 4 * owned, part_cols),
            grad_out[..., :part_cols],
            grad_out[..., part_cols : 2 * part_cols],
            grad_out[..., 2 * part_cols :],
            gains_rows.reshape(shards, gain_rows, part_cols),
        ],
        1,
    ).reshape(-1, part_cols)
    gate_sum, last_sum = sums_over_ctx([grad_gate, last], shards, 1)
    gate_sum = exchange_dp(gate_sum.astype(low).reshape(4, owned, 2 * part_hidden))
    gate_sum = jnp.concatenate(
        [
            gate_sum[dp, :, side * part_hidden : (side + 1) * part_hidden]
            for side in range(2)
            for dp in range(4)
        ],
        1,
    ).astype(jnp.float32)
    last_sum = last_sum.astype(low)
    gains_part = last_sum[7 * owned :].reshape(-1)[: 8 * owned].reshape(4, 2, owned)
    gains_sum = exchange_dp(gains_part).astype(jnp.float32).sum(0)
    in_sum = exchange_dp(last_sum[: 4 * owned].reshape(4, owned, part_cols))
    out_sum = jnp.concatenate(
        [last_sum[(4 + i) * owned : (5 + i) * owned] for i in range(3)], 1
    )[:, :width].astype(jnp.float32)

    def columns(first, last):
        return in_sum[..., first:last].swapaxes(0, 1).reshape(owned, -1)

    in_sum = jnp.concatenate(
        [
            columns(0, part_q),
            columns(part_q, part_q + part_k),
            columns(part_q + part_k, part_cols),
        ],
        1,
    ).astype(jnp.float32)
    new_in = adam_update(
        attention_in,
        in_sum,
        mean_attention_in,
        square_attention_in,
        input_boost * D ** (-0.5),
        weight_decay,
    )
    new_out = adam_update(
        attention_out,
        out_sum,
        mean_attention_out,
        square_attention_out,
        (HEADS * HEAD // 32) ** (-0.5),
        weight_decay,
    )
    new_gate = adam_update(
        gate_up, gate_sum, mean_gate_up, square_gate_up, D ** (-0.5), weight_decay
    )
    new_down = adam_update(
        down_matrix, down_sum, mean_down, square_down, FF ** (-0.5), weight_decay
    )
    new_gain = adam_update(gains, gains_sum, mean_gains, square_gains, gain_rate, 0.0)
    return (
        block_out,
        tokens_grad,
        new_in[0],
        new_in[1],
        new_in[2],
        new_out[0],
        new_out[1],
        new_out[2],
        new_gate[0],
        new_gate[1],
        new_gate[2],
        new_down[0],
        new_down[1],
        new_down[2],
        new_gain[0],
        new_gain[1],
        new_gain[2],
    )


def solution(mesh):
    in_specs = (
        P("dp", "ctx", None),
        P("dp", "ctx", None),
        P(),
        P(("dp", "ctx"), None),
        P(("dp", "ctx"), None),
        P(("dp", "ctx"), None),
        P(("dp", "ctx"), None),
        P(None, ("dp", "ctx")),
        P(("dp", "ctx"), None),
        P(("dp", "ctx"), None),
        P(("dp", "ctx"), None),
        P(("dp", "ctx"), None),
        P(None, ("dp", "ctx")),
        P(("dp", "ctx"), None),
        P(("dp", "ctx"), None),
        P(("dp", "ctx"), None),
        P(("dp", "ctx"), None),
        P(None, ("dp", "ctx")),
    )
    out_specs = (
        P("dp", "ctx", None),
        P("dp", "ctx", None),
        P(("dp", "ctx"), None),
        P(("dp", "ctx"), None),
        P(("dp", "ctx"), None),
        P(("dp", "ctx"), None),
        P(("dp", "ctx"), None),
        P(("dp", "ctx"), None),
        P(("dp", "ctx"), None),
        P(("dp", "ctx"), None),
        P(("dp", "ctx"), None),
        P(("dp", "ctx"), None),
        P(("dp", "ctx"), None),
        P(("dp", "ctx"), None),
        P(None, ("dp", "ctx")),
        P(None, ("dp", "ctx")),
        P(None, ("dp", "ctx")),
    )
    return jax.shard_map(local, mesh=mesh, in_specs=in_specs, out_specs=out_specs, check_vma=False)
```

```python
import functools

import jax
import jax.numpy as jnp
from jax import lax
from jax.experimental import pallas as pl
from jax.experimental.pallas import tpu as pltpu
from jax.sharding import PartitionSpec as P

D = 2048
HEADS = 32
KV_HEADS = 8
HEAD = 64
FF = 8192
STEP = 5


norm_eps = 1e-05
rope_base = 500000.0
beta_one = 0.9
beta_two = 0.95
gain_rate = 1.25
input_boost = 2.5
weight_decay = 0.1
adam_eps = 1e-08
masked_score = -1e30


def rotary_tables(positions, head_width):
    half_width = head_width // 2
    frequency = rope_base ** (-(jnp.arange(half_width, dtype=jnp.float32) * 2.0 / head_width))
    angles = positions.astype(jnp.float32)[:, None] * frequency[None, :]
    angles = jnp.concatenate([angles, angles], 1)
    return (jnp.cos(angles), jnp.sin(angles))


def norm_parts(values):
    factor = lax.rsqrt(jnp.mean(values * values, -1, keepdims=True) + norm_eps)
    return (values * factor, factor)


def norm_back(back_normed, normed, factor):
    return factor * (back_normed - normed * jnp.mean(back_normed * normed, -1, keepdims=True))


def adam_update(weight, gradient, first_moment, second_moment, step_rate, decay_rate):
    first_new = beta_one * first_moment + (1.0 - beta_one) * gradient
    second_new = beta_two * second_moment + (1.0 - beta_two) * gradient * gradient
    update = (
        first_new
        / (1.0 - beta_one**STEP)
        / (jnp.sqrt(second_new / (1.0 - beta_two**STEP)) + adam_eps)
    )
    return (first_new, second_new, weight - step_rate * (update + decay_rate * weight))


def swapped(values, by):
    return lax.ppermute(values, "dp", [(i, i ^ by) for i in range(4)])


def gather_dp(values):
    beside = swapped(values, 1)
    across = swapped(values, 2)
    corner = swapped(across, 1)
    return jnp.stack([values, beside, across, corner])


def scatter_dp(parts):
    low = parts.astype(jnp.bfloat16)
    beside = swapped(jnp.stack([low[1], low[3]]), 1).astype(jnp.float32)
    far = (parts[2] + beside[1]).astype(jnp.bfloat16)
    return parts[0] + beside[0] + swapped(far, 2).astype(jnp.float32)


def exchange_dp(pieces):
    mine = lax.axis_index("dp")
    slots = [lax.dynamic_index_in_dim(pieces, mine, 0, keepdims=False)]
    for by in (1, 2, 3):
        slots.append(swapped(lax.dynamic_index_in_dim(pieces, mine ^ by, 0, keepdims=False), by))
    slots = jnp.stack(slots)
    return jnp.stack(
        [lax.dynamic_index_in_dim(slots, mine ^ i, 0, keepdims=False) for i in range(4)]
    )


def to_owner_order(rows, shards):
    count, width = rows.shape
    return rows.reshape(count, 4, shards, -1).swapaxes(1, 2).reshape(count, width)


def from_owner_order(rows, shards):
    count, width = rows.shape
    return rows.reshape(count, shards, 4, -1).swapaxes(1, 2).reshape(count, width)


def dot_nn(a, b):
    return lax.dot_general(a, b, (((1,), (0,)), ((), ())), preferred_element_type=jnp.float32)


def dot_nt(a, b):
    return lax.dot_general(a, b, (((1,), (1,)), ((), ())), preferred_element_type=jnp.float32)


def dot_tn(a, b):
    return lax.dot_general(a, b, (((0,), (0,)), ((), ())), preferred_element_type=jnp.float32)


def causal_keep(tile):
    keys = lax.broadcasted_iota(jnp.int32, (tile, tile), 0)
    queries = lax.broadcasted_iota(jnp.int32, (tile, tile), 1)
    return keys <= queries


def turn_group(values, cos, sin, forward):
    lanes = lax.broadcasted_iota(jnp.int32, values.shape, 1)
    other = jnp.where(
        lanes % HEAD < HEAD // 2,
        pltpu.roll(values, 2 * HEAD - HEAD // 2, 1),
        pltpu.roll(values, HEAD // 2, 1),
    )
    if forward:
        return values * cos + other * sin
    return values * cos - other * sin


def turn_columns(values, start, turned_cols, cos, sin, forward):
    if start >= turned_cols:
        return values
    turned = turn_group(values, cos, sin, forward)
    if start + 2 * HEAD <= turned_cols:
        return turned
    lanes = lax.broadcasted_iota(jnp.int32, values.shape, 1)
    return jnp.where(lanes < turned_cols - start, turned, values)


def attend_kernel(
    q_heads, kv_heads, tile, order_ref, qkv_ref, cos_ref, sin_ref, out_ref, lse_ref, kept_ref, made
):
    length, cols = qkv_ref.shape
    blocks = order_ref.shape[0]
    rows = length // blocks
    group = q_heads // kv_heads
    q_cols, k_cols = q_heads * HEAD, kv_heads * HEAD
    scale = HEAD ** (-0.5)

    def take_block(i, _):
        start = pl.multiple_of(order_ref[i] * rows, rows)
        source = pl.multiple_of(i * rows, rows)
        cos = cos_ref[pl.ds(start, rows), :]
        sin = sin_ref[pl.ds(start, rows), :]
        for c in range(0, cols, 2 * HEAD):
            values = qkv_ref[pl.ds(source, rows), c : c + 2 * HEAD]
            values = turn_columns(values, c, q_cols + k_cols, cos, sin, True)
            kept_ref[pl.ds(start, rows), c : c + 2 * HEAD] = values.astype(jnp.bfloat16)
        return 0

    lax.fori_loop(0, blocks, take_block, 0)
    keep = causal_keep(tile)
    for kv in range(kv_heads):
        k_at = q_cols + kv * HEAD
        v_at = q_cols + k_cols + kv * HEAD

        def query_step(i, _):
            q_start = pl.multiple_of(i * tile, tile)
            queries = [
                kept_ref[
                    pl.ds(q_start, tile), (kv * group + g) * HEAD : (kv * group + g + 1) * HEAD
                ]
                for g in range(group)
            ]

            def key_tile(j, carry, masked):
                k_start = pl.multiple_of(j * tile, tile)
                keys = kept_ref[pl.ds(k_start, tile), k_at : k_at + HEAD]
                values = kept_ref[pl.ds(k_start, tile), v_at : v_at + HEAD]
                result = []
                for g in range(group):
                    peak, total, weighted = carry[g]
                    scores = dot_nt(keys, queries[g]) * scale
                    if masked:
                        scores = jnp.where(keep, scores, masked_score)
                    new_peak = jnp.maximum(peak, jnp.max(scores, 0, keepdims=True))
                    weights = jnp.exp(scores - new_peak)
                    shrink = jnp.exp(peak - new_peak)
                    total = total * shrink + jnp.sum(weights, 0, keepdims=True)
                    weighted = weighted * shrink + dot_tn(values, weights.astype(jnp.bfloat16))
                    result.append((new_peak, total, weighted))
                return tuple(result)

            start = tuple(
                (
                    jnp.full((1, tile), masked_score, jnp.float32),
                    jnp.zeros((1, tile), jnp.float32),
                    jnp.zeros((HEAD, tile), jnp.float32),
                )
                for _ in range(group)
            )
            carry = lax.fori_loop(0, i, lambda j, c: key_tile(j, c, False), start)
            carry = key_tile(i, carry, True)
            for g in range(group):
                head = kv * group + g
                peak, total, weighted = carry[g]
                lse_ref[head : head + 1, pl.ds(q_start, tile)] = peak + jnp.log(total)
                made[pl.ds(q_start, tile), head * HEAD : (head + 1) * HEAD] = (
                    (weighted / total).T.astype(jnp.bfloat16)
                )
            return 0

        lax.fori_loop(0, length // tile, query_step, 0)

    def give_block(i, _):
        start = pl.multiple_of(order_ref[i] * rows, rows)
        target = pl.multiple_of(i * rows, rows)
        out_ref[pl.ds(target, rows), :] = made[pl.ds(start, rows), :]
        return 0

    lax.fori_loop(0, blocks, give_block, 0)


def attend_back_kernel(
    q_heads,
    kv_heads,
    tile,
    order_ref,
    kept_ref,
    back_ref,
    lse_ref,
    cos_ref,
    sin_ref,
    out_ref,
    back_sorted,
    grad,
    delta_ref,
    dq_ref,
):
    length, cols = kept_ref.shape
    blocks = order_ref.shape[0]
    rows = length // blocks
    group = q_heads // kv_heads
    q_cols, k_cols = q_heads * HEAD, kv_heads * HEAD
    scale = HEAD ** (-0.5)
    tiles = length // tile

    def take_block(i, _):
        start = pl.multiple_of(order_ref[i] * rows, rows)
        source = pl.multiple_of(i * rows, rows)
        back_sorted[pl.ds(start, rows), :] = back_ref[pl.ds(source, rows), :]
        return 0

    lax.fori_loop(0, blocks, take_block, 0)
    keep = causal_keep(tile)
    for kv in range(kv_heads):
        k_at = q_cols + kv * HEAD
        v_at = q_cols + k_cols + kv * HEAD

        def load(i, g):
            start = pl.multiple_of(i * tile, tile)
            head = kv * group + g
            at = slice(head * HEAD, (head + 1) * HEAD)
            return (
                kept_ref[pl.ds(start, tile), at],
                back_sorted[pl.ds(start, tile), at],
                lse_ref[head : head + 1, pl.ds(start, tile)],
            )

        def load_kv(j):
            start = pl.multiple_of(j * tile, tile)
            return (
                kept_ref[pl.ds(start, tile), k_at : k_at + HEAD],
                kept_ref[pl.ds(start, tile), v_at : v_at + HEAD],
            )

        def tile_terms(keys, values, query, back, lse, masked):
            weights = jnp.exp(dot_nt(keys, query) * scale - lse)
            if masked:
                weights = jnp.where(keep, weights, 0.0)
            return weights, dot_nt(values, back)

        def delta_step(i, _):
            rows_i = [load(i, g) for g in range(group)]

            def one(j, carry, masked):
                keys, values = load_kv(j)
                result = []
                for g in range(group):
                    weights, back_weights = tile_terms(keys, values, *rows_i[g], masked)
                    result.append(carry[g] + jnp.sum(weights * back_weights, 0, keepdims=True))
                return tuple(result)

            carry = tuple(jnp.zeros((1, tile), jnp.float32) for _ in range(group))
            carry = lax.fori_loop(0, i, lambda j, c: one(j, c, False), carry)
            carry = one(i, carry, True)
            for g in range(group):
                delta_ref[g : g + 1, pl.ds(pl.multiple_of(i * tile, tile), tile)] = carry[g]
            return 0

        lax.fori_loop(0, tiles, delta_step, 0)
        dq_ref[...] = jnp.zeros_like(dq_ref)

        def key_step(j, _):
            keys, values = load_kv(j)

            def one(i, carry, masked):
                back_key, back_value = carry
                start = pl.multiple_of(i * tile, tile)
                for g in range(group):
                    query, back, lse = load(i, g)
                    weights, back_weights = tile_terms(keys, values, query, back, lse, masked)
                    delta = delta_ref[g : g + 1, pl.ds(start, tile)]
                    back_scores = (weights * (back_weights - delta)).astype(jnp.bfloat16)
                    back_key = back_key + dot_nn(back_scores, query)
                    back_value = back_value + dot_nn(weights.astype(jnp.bfloat16), back)
                    dq_ref[g * HEAD : (g + 1) * HEAD, pl.ds(start, tile)] += dot_tn(
                        keys, back_scores
                    )
                return back_key, back_value

            zero = jnp.zeros((tile, HEAD), jnp.float32)
            carry = one(j, (zero, zero), True)
            carry = lax.fori_loop(j + 1, tiles, lambda i, c: one(i, c, False), carry)
            start = pl.multiple_of(j * tile, tile)
            grad[pl.ds(start, tile), k_at : k_at + HEAD] = carry[0] * scale
            grad[pl.ds(start, tile), v_at : v_at + HEAD] = carry[1]
            return 0

        lax.fori_loop(0, tiles, key_step, 0)
        for g in range(group):
            head = kv * group + g
            grad[:, head * HEAD : (head + 1) * HEAD] = (
                dq_ref[g * HEAD : (g + 1) * HEAD, :] * scale
            ).T

    def give_block(i, _):
        start = pl.multiple_of(order_ref[i] * rows, rows)
        target = pl.multiple_of(i * rows, rows)
        cos = cos_ref[pl.ds(start, rows), :]
        sin = sin_ref[pl.ds(start, rows), :]
        for c in range(0, cols, 2 * HEAD):
            values = grad[pl.ds(start, rows), c : c + 2 * HEAD]
            values = turn_columns(values, c, q_cols + k_cols, cos, sin, False)
            out_ref[pl.ds(target, rows), c : c + 2 * HEAD] = values.astype(jnp.bfloat16)
        return 0

    lax.fori_loop(0, blocks, give_block, 0)


MESH = pl.DeviceIdType.MESH


def part_owner(part):
    return part % 2 * 2 + part // 2


def sequence_target(group, place, second, splits):
    part = place // 2
    target = (part_owner(part % 4), (2 * group + second) * splits + part // 4)
    return target, place % 2


def token_target(group, place, half, splits):
    sequence = place // splits
    part = part_owner(group) + 4 * (place % splits)
    return (sequence // 2, 2 * part + half), sequence % 2


def chunk_rows(rows, width, most):
    best = 16
    for size in range(16, rows + 1, 16):
        if rows % size == 0 and size * width <= most:
            best = size
    return best


def remote(source, target, sems, device):
    return pltpu.make_async_remote_copy(
        src_ref=source,
        dst_ref=target,
        send_sem=sems[0],
        recv_sem=sems[1],
        device_id=device,
        device_id_type=MESH,
    )


def same(one, other):
    return jnp.logical_and(one[0] == other[0], one[1] == other[1])


def greet(me, peers, movers):
    barrier = pltpu.get_barrier_semaphore()
    for peer in peers:
        pl.semaphore_signal(barrier, inc=1, device_id=peer, device_id_type=MESH)
    expected = len(peers)
    for source, target in movers:

        @pl.when(jnp.logical_not(same(source, me)))
        def _():
            pl.semaphore_signal(barrier, inc=1, device_id=source, device_id_type=MESH)

        expected = expected + jnp.where(same(target, me), 0, 1)
    pl.semaphore_wait(barrier, expected)


def move_start(me, source, target, target_device, send, receive):
    here = same(target_device, me)

    @pl.when(here)
    def _():
        pltpu.make_async_copy(source, target, receive).start()

    @pl.when(jnp.logical_not(here))
    def _():
        remote(source, target, (send, receive), target_device).start()


def move_sent(me, source, target, target_device, send, receive):
    @pl.when(jnp.logical_not(same(target_device, me)))
    def _():
        remote(source, target, (send, receive), target_device).wait_send()


class Gathers:
    def __init__(self, me, shards, sems, jobs):
        self.group, self.place = me
        self.slow = shards // 2
        self.line = [(me[0], me[1] ^ (2 * by)) for by in range(1, self.slow)]
        self.pair = (me[0], me[1] ^ 1)
        self.line_send, self.line_recv, self.pair_send, self.pair_recv, self.own = sems
        self.jobs = jobs

    def to_line(self, job, by):
        source, target = self.jobs[job]
        sems = (self.line_send.at[job, by - 1], self.line_recv.at[job, by - 1])
        return remote(source, target(self.place), sems, self.line[by - 1])

    def to_pair(self, job, by):
        source, target = self.jobs[job]
        if by > 0:
            source = target(self.place ^ (2 * by))
        sems = (self.pair_send.at[job, by], self.pair_recv.at[job, by])
        return remote(source, target(self.place ^ (2 * by)), sems, self.pair)

    def to_own(self, job):
        source, target = self.jobs[job]
        return pltpu.make_async_copy(source, target(self.place), self.own.at[job])

    def start(self, job):
        self.to_pair(job, 0).start()
        for by in range(1, self.slow):
            self.to_line(job, by).start()
        self.to_own(job).start()

    def pass_on(self, job):
        for by in range(1, self.slow):
            self.to_line(job, by).wait_recv()
            self.to_pair(job, by).start()

    def finish(self, job):
        self.to_own(job).wait()
        for by in range(self.slow):
            self.to_pair(job, by).wait()
        for by in range(1, self.slow):
            self.to_line(job, by).wait_send()


class GroupGather:
    def __init__(self, me, rows, sems):
        group, place = me
        self.rows, self.sems = rows, sems
        self.beside, self.across = (group ^ 1, place), (group ^ 2, place)

    def hop(self, source, slot, device):
        sems = (self.sems.at[0, slot - 1], self.sems.at[1, slot - 1])
        return remote(self.rows.at[source], self.rows.at[slot], sems, device)

    def start(self):
        self.hop(0, 2, self.across).start()
        self.hop(0, 1, self.beside).start()

    def pass_on(self):
        self.hop(0, 2, self.across).wait_recv()
        self.hop(2, 3, self.beside).start()

    def finish(self):
        self.hop(0, 1, self.beside).wait()
        self.hop(2, 3, self.beside).wait()
        self.hop(0, 2, self.across).wait_send()


def first_kernel(shards, splits, tokens, pieces, out_own, gate_pieces, *refs):
    rows, in_all, out_all, gate_rows = refs[:4]
    held, move_send, move_recv, group_sems, piece_sems, gate_sems, own_sems = refs[4:11]
    gather_sems = refs[11:16]
    me = (lax.axis_index("dp"), lax.axis_index("ctx"))
    group, place = me
    slow = shards // 2
    peers = [(group ^ by, place) for by in (1, 2, 3)]
    jobs = [(held.at[t], lambda j, t=t: in_all.at[t, j]) for t in range(4)]
    jobs.append((out_own, lambda j: out_all.at[j]))
    gathers = Gathers(me, shards, gather_sems, jobs)
    movers = []
    for i in (0, 1):
        movers.append(
            (token_target(group, place, i, splits)[0], sequence_target(group, place, i, splits)[0])
        )
    greet(me, peers + gathers.line + [gathers.pair], movers)

    def piece(by):
        sems = (piece_sems.at[0, by - 1], piece_sems.at[1, by - 1])
        return remote(pieces.at[group ^ by], held.at[group], sems, peers[by - 1])

    def gate(by):
        sems = (gate_sems.at[0, by - 1], gate_sems.at[1, by - 1])
        return remote(gate_pieces.at[group ^ by], gate_rows.at[group], sems, peers[by - 1])

    def move(second):
        device, half = sequence_target(group, place, second, splits)
        return (
            me,
            tokens.at[second],
            rows.at[0, half],
            device,
            move_send.at[second],
            move_recv.at[half],
        )

    own_piece = pltpu.make_async_copy(pieces.at[group], held.at[group], own_sems.at[0])
    own_gate = pltpu.make_async_copy(gate_pieces.at[group], gate_rows.at[group], own_sems.at[1])
    for by in (1, 2, 3):
        piece(by).start()
    own_piece.start()
    for second in (0, 1):
        move_start(*move(second))
    own_piece.wait()
    for by in (1, 2, 3):
        piece(by).wait_recv()
    gathers.start(0)
    gathers.start(1)
    for half in (0, 1):
        pltpu.make_async_copy(tokens.at[0], rows.at[0, half], move_recv.at[half]).wait()
    spread = GroupGather(me, rows, group_sems)
    spread.start()
    for job in range(len(jobs)):
        gathers.pass_on(job)
        if job + 2 < len(jobs):
            gathers.start(job + 2)
        if job == 2:
            spread.pass_on()
            for by in (1, 2, 3):
                gate(by).start()
            own_gate.start()
    for job in range(len(jobs)):
        gathers.finish(job)
    spread.finish()
    own_gate.wait()
    for by in (1, 2, 3):
        piece(by).wait_send()
        gate(by).wait()
    for second in (0, 1):
        move_sent(*move(second))


def gather_scratch(jobs, shards):
    slow = shards // 2
    return [
        pltpu.SemaphoreType.DMA((jobs, slow - 1)),
        pltpu.SemaphoreType.DMA((jobs, slow - 1)),
        pltpu.SemaphoreType.DMA((jobs, slow)),
        pltpu.SemaphoreType.DMA((jobs, slow)),
        pltpu.SemaphoreType.DMA((jobs,)),
    ]


def first_exchange(tokens, pieces, out_own, gate_pieces, shards, splits, identity):
    low = jnp.bfloat16
    any_space = pl.BlockSpec(memory_space=pl.ANY)
    _, rows, width = pieces.shape
    return pl.pallas_call(
        functools.partial(first_kernel, shards, splits),
        out_shape=(
            jax.ShapeDtypeStruct((4,) + tokens.shape, low),
            jax.ShapeDtypeStruct((4, shards, rows, width), low),
            jax.ShapeDtypeStruct((shards,) + out_own.shape, low),
            jax.ShapeDtypeStruct(gate_pieces.shape, low),
        ),
        in_specs=[any_space] * 4,
        out_specs=(any_space,) * 4,
        scratch_shapes=[
            pltpu.VMEM(pieces.shape, low),
            pltpu.SemaphoreType.DMA((2,)),
            pltpu.SemaphoreType.DMA((2,)),
            pltpu.SemaphoreType.DMA((2, 3)),
            pltpu.SemaphoreType.DMA((2, 3)),
            pltpu.SemaphoreType.DMA((2, 3)),
            pltpu.SemaphoreType.DMA((2,)),
        ]
        + gather_scratch(5, shards),
        compiler_params=pltpu.CompilerParams(
            collective_id=identity, has_side_effects=True, vmem_limit_bytes=8 << 20
        ),
        cost_estimate=pl.CostEstimate(flops=0, bytes_accessed=200 << 20, transcendentals=0),
    )(tokens, pieces, out_own, gate_pieces)


def sum_kernel(shards, splits, plans, *refs):
    count = len(plans)
    slow = shards // 2
    moved = 2
    sources, made = refs[:count], refs[count : count + moved]
    totals = refs[count + moved : 2 * count + moved]
    brought = refs[2 * count + moved : 2 * count + 2 * moved]
    scratch = refs[2 * count + 2 * moved :]
    move_send, move_recv = scratch[:2]
    scratch = scratch[2:]
    me = (lax.axis_index("dp"), lax.axis_index("ctx"))
    group, place = me
    half, slot = place % 2, place // 2
    pair = (group, place ^ 1)
    owners = [(group, place ^ (2 * by)) for by in range(1, slow)]
    members = [(group ^ by, place) for by in (1, 2, 3)]
    movers = []
    for i in (0, 1):
        movers.append(
            (sequence_target(group, place, i, splits)[0], token_target(group, place, i, splits)[0])
        )
    greet(me, [pair] + owners + members, movers)

    def move(array, part):
        device, second = token_target(group, place, part, splits)
        return (
            me,
            made[array].at[part],
            brought[array].at[second],
            device,
            move_send.at[array, part],
            move_recv.at[array, second],
        )

    for array in range(moved):
        for part in (0, 1):
            move_start(*move(array, part))
    for piece in range(count):
        chunks, rows, per_member = plans[piece]
        source, total = sources[piece], totals[piece]
        landed, arrived, kept, sent, value_ref, done = scratch[13 * piece : 13 * piece + 6]
        kept_sem, pair_send, pair_recv, own_send, own_recv, last_send, last_recv = scratch[
            13 * piece + 6 : 13 * piece + 13
        ]
        ahead = kept.shape[0]

        def window(c):
            return pl.ds(pl.multiple_of(c * rows, rows), rows)

        def to_pair(c):
            return remote(
                source.at[:, 1 - half, window(c)],
                landed.at[c],
                (pair_send.at[c], pair_recv.at[c]),
                pair,
            )

        def keep(c):
            return pltpu.make_async_copy(
                source.at[:, half, window(c)], kept.at[c % ahead], kept_sem.at[c % ahead]
            )

        def to_owner(c, by):
            return remote(
                sent.at[c, by - 1],
                arrived.at[c, by - 1],
                (own_send.at[c, by - 1], own_recv.at[c, by - 1]),
                owners[by - 1],
            )

        def start(c):
            to_pair(c).start()
            keep(c).start()

        def pass_on(c):
            keep(c).wait()
            to_pair(c).wait_recv()
            for by in range(1, slow):
                both = kept[c % ahead, slot ^ by].astype(jnp.float32) + landed[
                    c, slot ^ by
                ].astype(jnp.float32)
                sent[c, by - 1] = both.astype(jnp.bfloat16)
                to_owner(c, by).start()
            value_ref[c % 2] = kept[c % ahead, slot].astype(jnp.float32) + landed[
                c, slot
            ].astype(jnp.float32)

        def finish(c):
            value = value_ref[c % 2]
            for by in range(1, slow):
                to_owner(c, by).wait_recv()
                value = value + arrived[c, by - 1].astype(jnp.float32)
            if per_member == 0:
                total[window(c), :] = value
                return
            done[c] = value.astype(jnp.bfloat16)
            member = c // per_member
            inner = pl.ds(pl.multiple_of(c % per_member * rows, rows), rows)

            @pl.when(member == group)
            def _():
                pltpu.make_async_copy(done.at[c], total.at[group, inner], last_send.at[c]).start()

            @pl.when(member != group)
            def _():
                sems = (last_send.at[c], last_recv.at[(group ^ member) * per_member + c % per_member])
                remote(done.at[c], total.at[group, inner], sems, (member, place)).start()

        for c in range(min(ahead, chunks)):
            start(c)

        def step(c, _):
            pass_on(c)

            @pl.when(c + ahead < chunks)
            def _():
                start(c + ahead)

            @pl.when(c > 0)
            def _():
                finish(c - 1)

            return 0

        lax.fori_loop(0, chunks, step, 0)
        finish(chunks - 1)

    for piece in range(count):
        chunks, rows, per_member = plans[piece]
        source, total = sources[piece], totals[piece]
        landed, arrived, kept, sent, value_ref, done = scratch[13 * piece : 13 * piece + 6]
        kept_sem, pair_send, pair_recv, own_send, own_recv, last_send, last_recv = scratch[
            13 * piece + 6 : 13 * piece + 13
        ]

        def drain(c, _):
            pltpu.make_async_copy(landed.at[c], landed.at[c], pair_send.at[c]).wait()
            for by in range(1, slow):
                pltpu.make_async_copy(
                    sent.at[c, by - 1], sent.at[c, by - 1], own_send.at[c, by - 1]
                ).wait()
            if per_member:
                pltpu.make_async_copy(done.at[c], done.at[c], last_send.at[c]).wait()
            return 0

        lax.fori_loop(0, chunks, drain, 0)
        if per_member:

            def receive(c, _):
                for by in (1, 2, 3):
                    pltpu.make_async_copy(
                        done.at[0], done.at[0], last_recv.at[by * per_member + c]
                    ).wait()
                return 0

            lax.fori_loop(0, per_member, receive, 0)
    for array in range(moved):
        for part in (0, 1):
            pltpu.make_async_copy(
                made[array].at[part], brought[array].at[part], move_recv.at[array, part]
            ).wait()
            move_sent(*move(array, part))


def sums_over_ctx(pieces, members, moved, shards, splits, identity):
    slow = shards // 2
    any_space = pl.BlockSpec(memory_space=pl.ANY)
    plans, shapes, views, spaces = [], [], [], []
    scratch = [pltpu.SemaphoreType.DMA((2, 2)), pltpu.SemaphoreType.DMA((2, 2))]
    for piece, spread in zip(pieces, members):
        rows, width = piece.shape[0] // shards, piece.shape[1]
        size = chunk_rows(rows // 4 if spread else rows, width, 1 << 16)
        chunks = rows // size
        ahead = min(3, chunks)
        plans.append((chunks, size, chunks // 4 if spread else 0))
        views.append(piece.reshape(slow, 2, rows, width))
        if spread:
            shapes.append(jax.ShapeDtypeStruct((4, rows // 4, width), jnp.bfloat16))
        else:
            shapes.append(jax.ShapeDtypeStruct((rows, width), jnp.float32))
        spaces.append(any_space if spread else pl.BlockSpec(memory_space=pltpu.VMEM))
        scratch += [
            pltpu.VMEM((chunks, slow, size, width), jnp.bfloat16),
            pltpu.VMEM((chunks, slow - 1, size, width), jnp.bfloat16),
            pltpu.VMEM((ahead, slow, size, width), jnp.bfloat16),
            pltpu.VMEM((chunks, slow - 1, size, width), jnp.bfloat16),
            pltpu.VMEM((2, size, width), jnp.float32),
            pltpu.VMEM((chunks if spread else 1, size, width), jnp.bfloat16),
            pltpu.SemaphoreType.DMA((ahead,)),
            pltpu.SemaphoreType.DMA((chunks,)),
            pltpu.SemaphoreType.DMA((chunks,)),
            pltpu.SemaphoreType.DMA((chunks, slow - 1)),
            pltpu.SemaphoreType.DMA((chunks, slow - 1)),
            pltpu.SemaphoreType.DMA((chunks,)),
            pltpu.SemaphoreType.DMA((chunks,)),
        ]
    return pl.pallas_call(
        functools.partial(sum_kernel, shards, splits, tuple(plans)),
        out_shape=tuple(shapes) + tuple(jax.ShapeDtypeStruct(m.shape, m.dtype) for m in moved),
        in_specs=[any_space] * (len(pieces) + 2),
        out_specs=tuple(spaces) + (any_space, any_space),
        scratch_shapes=scratch,
        compiler_params=pltpu.CompilerParams(
            collective_id=identity, has_side_effects=True, vmem_limit_bytes=56 << 20
        ),
        cost_estimate=pl.CostEstimate(
            flops=0,
            bytes_accessed=sum(20 * piece.size for piece in pieces),
            transcendentals=0,
        ),
    )(*views, *moved)


def position_tables(length):
    cosine, sine_table = rotary_tables(jnp.arange(length, dtype=jnp.int32), HEAD)
    sign = jnp.where(jnp.arange(HEAD) < HEAD // 2, -1.0, 1.0)
    return jnp.tile(cosine, (1, 2)), jnp.tile(sine_table * sign, (1, 2))


def attend(order, qkv, tables, q_heads, kv_heads):
    length, cols = qkv.shape
    whole = pl.BlockSpec(memory_space=pltpu.VMEM)
    return pl.pallas_call(
        functools.partial(attend_kernel, q_heads, kv_heads, 256),
        out_shape=(
            jax.ShapeDtypeStruct((length, q_heads * HEAD), jnp.bfloat16),
            jax.ShapeDtypeStruct((q_heads, length), jnp.float32),
            jax.ShapeDtypeStruct((length, cols), jnp.bfloat16),
        ),
        in_specs=[pl.BlockSpec(memory_space=pltpu.SMEM), whole, whole, whole],
        out_specs=(whole, whole, whole),
        scratch_shapes=[pltpu.VMEM((length, q_heads * HEAD), jnp.bfloat16)],
        compiler_params=pltpu.CompilerParams(vmem_limit_bytes=40 << 20),
        cost_estimate=pl.CostEstimate(
            flops=2 * length * length * q_heads * HEAD,
            bytes_accessed=8 * length * cols,
            transcendentals=length * length * q_heads // 2,
        ),
    )(order, qkv, *tables)


def attend_back(order, kept, back, lse, tables, q_heads, kv_heads):
    length, cols = kept.shape
    group = q_heads // kv_heads
    whole = pl.BlockSpec(memory_space=pltpu.VMEM)
    return pl.pallas_call(
        functools.partial(attend_back_kernel, q_heads, kv_heads, 256),
        out_shape=jax.ShapeDtypeStruct((length, cols), jnp.bfloat16),
        in_specs=[pl.BlockSpec(memory_space=pltpu.SMEM)] + [whole] * 5,
        out_specs=whole,
        scratch_shapes=[
            pltpu.VMEM((length, q_heads * HEAD), jnp.bfloat16),
            pltpu.VMEM((length, cols), jnp.float32),
            pltpu.VMEM((group, length), jnp.float32),
            pltpu.VMEM((group * HEAD, length), jnp.float32),
        ],
        compiler_params=pltpu.CompilerParams(vmem_limit_bytes=40 << 20),
        cost_estimate=pl.CostEstimate(
            flops=7 * length * length * q_heads * HEAD,
            bytes_accessed=6 * length * cols,
            transcendentals=length * length * q_heads // 2,
        ),
    )(order, kept, back, lse, *tables)


def moved_pairs(shards, splits, second):
    pairs = []
    for source in range(4 * shards):
        group, place = divmod(source, shards)
        sequence = 2 * group + (place + second) % 2
        part = place // 2
        pairs.append((source, part_owner(part % 4) * shards + sequence * splits + part // 4))
    return pairs


def to_sequences(values, shards, splits):
    place = lax.axis_index("ctx")
    got = [
        lax.ppermute(
            lax.dynamic_index_in_dim(values, (place + second) % 2, 0, keepdims=False),
            ("dp", "ctx"),
            moved_pairs(shards, splits, second),
        )
        for second in (0, 1)
    ]
    odd = (place // splits) % 2 == 1
    return jnp.stack([jnp.where(odd, got[1], got[0]), jnp.where(odd, got[0], got[1])])


def local(
    tokens,
    cotangent,
    block_order,
    attention_in,
    attention_out,
    gate_up,
    down_matrix,
    gains,
    mean_attention_in,
    mean_attention_out,
    mean_gate_up,
    mean_down,
    mean_gains,
    square_attention_in,
    square_attention_out,
    square_gate_up,
    square_down,
    square_gains,
):
    seq_count, shard_rows, width = tokens.shape
    shards = lax.axis_size("ctx")
    mine = lax.axis_index("dp")
    low = jnp.bfloat16
    owned = attention_in.shape[0]
    hidden_units = gate_up.shape[1] // 2
    part_hidden = hidden_units // 4
    part_q = HEADS * HEAD // 4
    part_k = KV_HEADS * HEAD // 4
    part_cols = part_q + 2 * part_k
    count = seq_count * shard_rows
    length = shards * shard_rows
    splits = shards // (4 * seq_count)
    q_heads = HEADS // 4 // splits
    kv_heads = max(1, KV_HEADS // 4 // splits)

    in_low = attention_in.astype(low)
    gains_row = jnp.pad(gains.astype(low).reshape(1, -1), ((0, 15), (0, part_cols - 2 * owned)))
    pieces = jnp.stack(
        [
            jnp.concatenate(
                [
                    jnp.concatenate(
                        [
                            in_low[:, i * part_q : (i + 1) * part_q],
                            in_low[:, 4 * part_q + i * part_k :][:, :part_k],
                            in_low[:, 4 * (part_q + part_k) + i * part_k :][:, :part_k],
                        ],
                        1,
                    ),
                    gains_row,
                ]
            )
            for i in range(4)
        ]
    )
    gate_low = gate_up.astype(low)
    gate_pieces = jnp.stack(
        [
            jnp.concatenate(
                [
                    gate_low[:, i * part_hidden : (i + 1) * part_hidden],
                    gate_low[:, hidden_units + i * part_hidden :][:, :part_hidden],
                ],
                1,
            )
            for i in range(4)
        ]
    )
    tokens_all, in_all, w_out, gate_rows = first_exchange(
        tokens, pieces, attention_out.astype(low), gate_pieces, shards, splits, 1
    )
    w_in = in_all[:, :, :owned].reshape(width, part_cols)
    w_out = w_out.reshape(part_q, width)
    gains_all = in_all[:, :, owned, : 2 * owned].reshape(4, shards, 2, owned)
    gains_all = gains_all.astype(jnp.float32).transpose(2, 0, 1, 3).reshape(2, width)
    gain_one, gain_two = gains_all[0], gains_all[1]
    x_low = tokens_all[0].reshape(count, width)
    cot_own = cotangent + 0.0 * x_low[0, 0]
    cot_own = to_sequences(cot_own, shards, splits).reshape(count, width)
    back_all = gather_dp(cot_own).reshape(4 * count, width)
    gate_rows = gate_rows.reshape(4 * owned, 2 * part_hidden)
    w_gate = lax.all_gather(gate_rows, "ctx", axis=0, tiled=True)
    w_down = lax.all_gather(down_matrix.astype(low), "ctx", axis=0, tiled=True)

    normed_all, _ = norm_parts(tokens_all.reshape(4 * count, width).astype(jnp.float32))
    input_one = (normed_all * gain_one).astype(low)
    qkv = dot_nn(input_one, w_in)
    slot_order = block_order.reshape(splits, 4, -1)
    slot_order = jnp.stack(
        [
            lax.dynamic_index_in_dim(slot_order, part_owner(mine ^ by), 1, keepdims=False)
            for by in range(4)
        ],
        1,
    ).reshape(-1)
    tables = position_tables(length)
    groups = [[s * splits + g for g in range(splits)] for s in range(shards // splits)]

    def split_heads(values, widths, copies):
        parts = []
        start = 0
        for each, repeat in zip(widths, copies):
            kinds = splits // repeat
            piece = values[:, start : start + kinds * each].reshape(-1, kinds, each)
            parts.append(jnp.repeat(piece.swapaxes(0, 1), repeat, axis=0))
            start += kinds * each
        sent = jnp.concatenate(parts, 2)
        got = lax.all_to_all(sent, "ctx", 0, 0, axis_index_groups=groups, tiled=True)
        return got.reshape(length, -1)

    def join_heads(values):
        sent = values.reshape(splits, 4 * count, -1)
        return lax.all_to_all(sent, "ctx", 0, 0, axis_index_groups=groups, tiled=True)

    q_width, k_width = q_heads * HEAD, kv_heads * HEAD
    copies = splits * k_width // part_k
    if splits > 1:
        qkv = split_heads(qkv, (q_width, k_width, k_width), (1, copies, copies))
    attended, lse, kept = attend(slot_order, qkv, tables, q_heads, kv_heads)
    if splits > 1:
        attended = join_heads(attended).swapaxes(0, 1).reshape(4 * count, part_q)

    flat_rows = x_low.astype(jnp.float32)
    normed_one, factor_one = norm_parts(flat_rows)
    residual = flat_rows + scatter_dp(dot_nn(attended, w_out).reshape(4, count, width))
    normed_two, factor_two = norm_parts(residual)
    input_two_own = to_owner_order((normed_two * gain_two).astype(low), shards)
    input_two = gather_dp(input_two_own).reshape(4 * count, width)
    gate_both = dot_nn(input_two, w_gate)
    gate_part = gate_both[:, :part_hidden]
    up_part = gate_both[:, part_hidden:]
    sigmoid_gate = jax.nn.sigmoid(gate_part)
    active = gate_part * sigmoid_gate
    hidden = (active * up_part).astype(low)
    output_rows = residual + scatter_dp(dot_nn(hidden, w_down).reshape(4, count, width))
    output_rows = output_rows.astype(low).reshape(seq_count, shard_rows, width)

    grad_down = dot_tn(hidden, back_all).astype(low)
    down_low = lax.psum_scatter(grad_down, "ctx", scatter_dimension=0, tiled=True)
    down_sum = down_low.astype(jnp.float32)
    early = 0.0 * grad_down[0, 0]
    back_hidden = dot_nt(back_all + early, w_down)
    back_gate = back_hidden * up_part * sigmoid_gate * (1.0 + gate_part * (1.0 - sigmoid_gate))
    back_upper = back_hidden * active
    back_gate_up = jnp.concatenate([back_gate, back_upper], 1).astype(low)
    grad_gate = dot_tn(input_two, back_gate_up[:, :part_hidden]).astype(low)
    grad_upper = dot_tn(input_two, back_gate_up[:, part_hidden:]).astype(low)
    gate_low = lax.psum_scatter(grad_gate, "ctx", scatter_dimension=0, tiled=True)
    gate_sum = exchange_dp(gate_low.reshape(4, owned, part_hidden))
    back_input_two = from_owner_order(
        scatter_dp(dot_nt(back_gate_up, w_gate).reshape(4, count, width)), shards
    )
    grad_gain_two = jnp.sum(back_input_two * normed_two, 0)
    back_residual = cot_own.astype(jnp.float32) + norm_back(
        back_input_two * gain_two, normed_two, factor_two
    )
    back_residual_all = gather_dp(back_residual.astype(low)).reshape(4 * count, width)
    grad_out = dot_tn(attended, back_residual_all).astype(low)
    back_attended = dot_nt(back_residual_all, w_out).astype(low)
    if splits > 1:
        back_attended = split_heads(back_attended, (q_width,), (1,))
    back_projected = attend_back(
        slot_order, kept, back_attended, lse, tables, q_heads, kv_heads
    )
    if splits > 1:
        back_projected = join_heads(back_projected).astype(jnp.float32)

        def shared(values):
            values = values.reshape(splits // copies, copies, 4 * count, k_width).sum(1)
            return values.swapaxes(0, 1).reshape(4 * count, part_k)

        back_projected = jnp.concatenate(
            [
                back_projected[..., :q_width].swapaxes(0, 1).reshape(4 * count, part_q),
                shared(back_projected[..., q_width : q_width + k_width]),
                shared(back_projected[..., q_width + k_width :]),
            ],
            1,
        ).astype(low)
    back_input_one = scatter_dp(dot_nt(back_projected, w_in).reshape(4, count, width))
    grad_gain_one = jnp.sum(back_input_one * normed_one, 0)
    tokens_grad = back_residual + norm_back(back_input_one * gain_one, normed_one, factor_one)
    tokens_grad = tokens_grad.astype(low).reshape(seq_count, shard_rows, width)
    grad_gains = jnp.stack([grad_gain_one, grad_gain_two]).reshape(2, 4, shards, owned)
    gains_rows = grad_gains.transpose(2, 1, 0, 3).reshape(shards, 4, 1, 2 * owned).astype(low)
    gains_rows = jnp.pad(gains_rows, ((0, 0), (0, 0), (0, 15), (0, part_cols - 2 * owned)))
    grad_in = dot_tn(input_one, back_projected).astype(low)
    grad_in = grad_in.reshape(4, shards, owned, part_cols).swapaxes(0, 1)
    grad_in = jnp.concatenate([grad_in, gains_rows], 2).reshape(-1, part_cols)
    upper_sum, out_sum, in_sum, block_out, tokens_grad = sums_over_ctx(
        [grad_upper, grad_out, grad_in],
        [True, False, True],
        [output_rows, tokens_grad],
        shards,
        splits,
        2,
    )
    tokens_grad = tokens_grad.astype(jnp.float32)
    gate_sum = jnp.concatenate(
        [side[dp] for side in (gate_sum, upper_sum) for dp in range(4)], 1
    ).astype(jnp.float32)
    gains_sum = in_sum[:, owned, : 2 * owned].reshape(4, 2, owned).astype(jnp.float32).sum(0)
    cuts = ((0, part_q), (part_q, part_q + part_k), (part_q + part_k, part_cols))
    in_sum = jnp.concatenate(
        [in_sum[dp, :owned, first:last] for first, last in cuts for dp in range(4)], 1
    ).astype(jnp.float32)
    new_in = adam_update(
        attention_in,
        in_sum,
        mean_attention_in,
        square_attention_in,
        input_boost * D ** (-0.5),
        weight_decay,
    )
    new_out = adam_update(
        attention_out,
        out_sum,
        mean_attention_out,
        square_attention_out,
        (HEADS * HEAD // 32) ** (-0.5),
        weight_decay,
    )
    new_gate = adam_update(
        gate_up, gate_sum, mean_gate_up, square_gate_up, D ** (-0.5), weight_decay
    )
    new_down = adam_update(
        down_matrix, down_sum, mean_down, square_down, FF ** (-0.5), weight_decay
    )
    new_gain = adam_update(gains, gains_sum, mean_gains, square_gains, gain_rate, 0.0)
    return (
        block_out,
        tokens_grad,
        new_in[0],
        new_in[1],
        new_in[2],
        new_out[0],
        new_out[1],
        new_out[2],
        new_gate[0],
        new_gate[1],
        new_gate[2],
        new_down[0],
        new_down[1],
        new_down[2],
        new_gain[0],
        new_gain[1],
        new_gain[2],
    )


def solution(mesh):
    in_specs = (
        P("dp", "ctx", None),
        P("dp", "ctx", None),
        P(),
        P(("dp", "ctx"), None),
        P(("dp", "ctx"), None),
        P(("dp", "ctx"), None),
        P(("dp", "ctx"), None),
        P(None, ("dp", "ctx")),
        P(("dp", "ctx"), None),
        P(("dp", "ctx"), None),
        P(("dp", "ctx"), None),
        P(("dp", "ctx"), None),
        P(None, ("dp", "ctx")),
        P(("dp", "ctx"), None),
        P(("dp", "ctx"), None),
        P(("dp", "ctx"), None),
        P(("dp", "ctx"), None),
        P(None, ("dp", "ctx")),
    )
    out_specs = (
        P("dp", "ctx", None),
        P("dp", "ctx", None),
        P(("dp", "ctx"), None),
        P(("dp", "ctx"), None),
        P(("dp", "ctx"), None),
        P(("dp", "ctx"), None),
        P(("dp", "ctx"), None),
        P(("dp", "ctx"), None),
        P(("dp", "ctx"), None),
        P(("dp", "ctx"), None),
        P(("dp", "ctx"), None),
        P(("dp", "ctx"), None),
        P(("dp", "ctx"), None),
        P(("dp", "ctx"), None),
        P(None, ("dp", "ctx")),
        P(None, ("dp", "ctx")),
        P(None, ("dp", "ctx")),
    )
    return jax.shard_map(local, mesh=mesh, in_specs=in_specs, out_specs=out_specs, check_vma=False)
```

```python
import functools

import jax
import jax.numpy as jnp
from jax import lax
from jax.experimental import pallas as pl
from jax.experimental.pallas import tpu as pltpu
from jax.sharding import PartitionSpec as P

D = 2048
HEADS = 32
KV_HEADS = 8
HEAD = 64
FF = 8192
STEP = 5


norm_eps = 1e-05
rope_base = 500000.0
beta_one = 0.9
beta_two = 0.95
gain_rate = 1.25
input_boost = 2.5
weight_decay = 0.1
adam_eps = 1e-08
masked_score = -1e30


def rotary_tables(positions, head_width):
    half_width = head_width // 2
    frequency = rope_base ** (-(jnp.arange(half_width, dtype=jnp.float32) * 2.0 / head_width))
    angles = positions.astype(jnp.float32)[:, None] * frequency[None, :]
    angles = jnp.concatenate([angles, angles], 1)
    return (jnp.cos(angles), jnp.sin(angles))


def norm_parts(values):
    factor = lax.rsqrt(jnp.mean(values * values, -1, keepdims=True) + norm_eps)
    return (values * factor, factor)


def norm_back(back_normed, normed, factor):
    return factor * (back_normed - normed * jnp.mean(back_normed * normed, -1, keepdims=True))


def adam_update(weight, gradient, first_moment, second_moment, step_rate, decay_rate):
    first_new = beta_one * first_moment + (1.0 - beta_one) * gradient
    second_new = beta_two * second_moment + (1.0 - beta_two) * gradient * gradient
    update = (
        first_new
        / (1.0 - beta_one**STEP)
        / (jnp.sqrt(second_new / (1.0 - beta_two**STEP)) + adam_eps)
    )
    return (first_new, second_new, weight - step_rate * (update + decay_rate * weight))


def swapped(values, by):
    shards = lax.axis_size("ctx")
    everyone = range(4 * shards)
    pairs = [(i, (i // shards ^ by[0]) * shards + (i % shards ^ by[1])) for i in everyone]
    return lax.ppermute(values, ("dp", "ctx"), pairs)


CORE, ACROSS, BESIDE = (1, 0), (2, 0), (0, 1)


def gather_group(values):
    half = values.shape[0] // 2
    one, two = values[:half], values[half:]
    one_across = swapped(one, ACROSS)
    two_beside = swapped(two, BESIDE)
    core = swapped(values, CORE)
    ones = swapped(jnp.stack([one, one_across]), BESIDE)
    twos = swapped(jnp.stack([two, two_beside]), ACROSS)
    others = jnp.stack(
        [
            jnp.concatenate([one_across, twos[0]]),
            jnp.concatenate([ones[0], two_beside]),
            jnp.concatenate([ones[1], twos[1]]),
        ]
    )
    cores = swapped(others, CORE)
    return jnp.stack(
        [values, core, others[0], cores[0], others[1], cores[1], others[2], cores[2]]
    ).reshape((2, 4) + values.shape)


def scatter_group(parts):
    low = jnp.bfloat16
    half = parts.shape[2] // 2
    wide = jnp.float32
    core = swapped(jnp.stack([parts[:, 1], parts[:, 3]], 1).astype(low), CORE)
    kept = jnp.stack([parts[:, 0], parts[:, 2]], 1) + core.astype(wide)
    one, two = kept[:, :, :half], kept[:, :, half:]
    ones = swapped(one[1].astype(low), BESIDE).astype(wide)
    twos = swapped(two[:, 1].astype(low), ACROSS).astype(wide)
    one_last = swapped((one[0, 1] + ones[1]).astype(low), ACROSS).astype(wide)
    two_last = swapped((two[1, 0] + twos[1]).astype(low), BESIDE).astype(wide)
    return jnp.concatenate([one[0, 0] + ones[0] + one_last, two[0, 0] + twos[0] + two_last])


def exchange_group(pieces):
    mine = 2 * lax.axis_index("dp") + lax.axis_index("ctx") % 2
    slots = [lax.dynamic_index_in_dim(pieces, mine, 0, keepdims=False)]
    for by in range(1, 8):
        piece = lax.dynamic_index_in_dim(pieces, mine ^ by, 0, keepdims=False)
        slots.append(swapped(piece, (by // 2, by % 2)))
    slots = jnp.stack(slots)
    return jnp.stack(
        [lax.dynamic_index_in_dim(slots, mine ^ i, 0, keepdims=False) for i in range(8)]
    )


def line_groups(shards):
    return [[2 * s + half for s in range(shards // 2)] for half in (0, 1)]


def gather_line(rows):
    return lax.all_gather(
        rows, "ctx", axis=0, tiled=True, axis_index_groups=line_groups(lax.axis_size("ctx"))
    )


def sum_line(gradient):
    return lax.psum_scatter(
        gradient,
        "ctx",
        scatter_dimension=0,
        tiled=True,
        axis_index_groups=line_groups(lax.axis_size("ctx")),
    )


def to_owner_order(rows, slow):
    count, width = rows.shape
    return rows.reshape(count, 4, slow, -1).swapaxes(1, 2).reshape(count, width)


def from_owner_order(rows, slow):
    count, width = rows.shape
    return rows.reshape(count, slow, 4, -1).swapaxes(1, 2).reshape(count, width)


def dot_nn(a, b):
    return lax.dot_general(a, b, (((1,), (0,)), ((), ())), preferred_element_type=jnp.float32)


def dot_nt(a, b):
    return lax.dot_general(a, b, (((1,), (1,)), ((), ())), preferred_element_type=jnp.float32)


def dot_tn(a, b):
    return lax.dot_general(a, b, (((0,), (0,)), ((), ())), preferred_element_type=jnp.float32)


def causal_keep(tile):
    keys = lax.broadcasted_iota(jnp.int32, (tile, tile), 0)
    queries = lax.broadcasted_iota(jnp.int32, (tile, tile), 1)
    return keys <= queries


def turn_group(values, cos, sin, forward):
    lanes = lax.broadcasted_iota(jnp.int32, values.shape, 1)
    other = jnp.where(
        lanes % HEAD < HEAD // 2,
        pltpu.roll(values, 2 * HEAD - HEAD // 2, 1),
        pltpu.roll(values, HEAD // 2, 1),
    )
    if forward:
        return values * cos + other * sin
    return values * cos - other * sin


def turn_columns(values, start, turned_cols, cos, sin, forward):
    if start >= turned_cols:
        return values
    turned = turn_group(values, cos, sin, forward)
    if start + 2 * HEAD <= turned_cols:
        return turned
    lanes = lax.broadcasted_iota(jnp.int32, values.shape, 1)
    return jnp.where(lanes < turned_cols - start, turned, values)


def attend_kernel(
    q_heads,
    kv_heads,
    tile,
    order_ref,
    all_qkv_ref,
    cos_ref,
    sin_ref,
    all_out_ref,
    all_lse_ref,
    all_kept_ref,
    made,
):
    for sequence in range(all_qkv_ref.shape[0]):
        attend_sequence(
            q_heads,
            kv_heads,
            tile,
            order_ref,
            all_qkv_ref.at[sequence],
            cos_ref,
            sin_ref,
            all_out_ref.at[sequence],
            all_lse_ref.at[sequence],
            all_kept_ref.at[sequence],
            made,
        )


def attend_sequence(
    q_heads, kv_heads, tile, order_ref, qkv_ref, cos_ref, sin_ref, out_ref, lse_ref, kept_ref, made
):
    length, cols = qkv_ref.shape
    blocks = order_ref.shape[0]
    rows = length // blocks
    group = q_heads // kv_heads
    q_cols, k_cols = q_heads * HEAD, kv_heads * HEAD
    scale = HEAD ** (-0.5)

    def take_block(i, _):
        start = pl.multiple_of(order_ref[i] * rows, rows)
        source = pl.multiple_of(i * rows, rows)
        cos = cos_ref[pl.ds(start, rows), :]
        sin = sin_ref[pl.ds(start, rows), :]
        for c in range(0, cols, 2 * HEAD):
            values = qkv_ref[pl.ds(source, rows), c : c + 2 * HEAD]
            values = turn_columns(values, c, q_cols + k_cols, cos, sin, True)
            kept_ref[pl.ds(start, rows), c : c + 2 * HEAD] = values.astype(jnp.bfloat16)
        return 0

    lax.fori_loop(0, blocks, take_block, 0)
    keep = causal_keep(tile)
    for kv in range(kv_heads):
        k_at = q_cols + kv * HEAD
        v_at = q_cols + k_cols + kv * HEAD

        def query_step(i, _):
            q_start = pl.multiple_of(i * tile, tile)
            queries = [
                kept_ref[
                    pl.ds(q_start, tile), (kv * group + g) * HEAD : (kv * group + g + 1) * HEAD
                ]
                for g in range(group)
            ]

            def key_tile(j, carry, masked):
                k_start = pl.multiple_of(j * tile, tile)
                keys = kept_ref[pl.ds(k_start, tile), k_at : k_at + HEAD]
                values = kept_ref[pl.ds(k_start, tile), v_at : v_at + HEAD]
                result = []
                for g in range(group):
                    peak, total, weighted = carry[g]
                    scores = dot_nt(keys, queries[g]) * scale
                    if masked:
                        scores = jnp.where(keep, scores, masked_score)
                    new_peak = jnp.maximum(peak, jnp.max(scores, 0, keepdims=True))
                    weights = jnp.exp(scores - new_peak)
                    shrink = jnp.exp(peak - new_peak)
                    total = total * shrink + jnp.sum(weights, 0, keepdims=True)
                    weighted = weighted * shrink + dot_tn(values, weights.astype(jnp.bfloat16))
                    result.append((new_peak, total, weighted))
                return tuple(result)

            start = tuple(
                (
                    jnp.full((1, tile), masked_score, jnp.float32),
                    jnp.zeros((1, tile), jnp.float32),
                    jnp.zeros((HEAD, tile), jnp.float32),
                )
                for _ in range(group)
            )
            carry = lax.fori_loop(0, i, lambda j, c: key_tile(j, c, False), start)
            carry = key_tile(i, carry, True)
            for g in range(group):
                head = kv * group + g
                peak, total, weighted = carry[g]
                lse_ref[head : head + 1, pl.ds(q_start, tile)] = peak + jnp.log(total)
                made[pl.ds(q_start, tile), head * HEAD : (head + 1) * HEAD] = (
                    (weighted / total).T.astype(jnp.bfloat16)
                )
            return 0

        lax.fori_loop(0, length // tile, query_step, 0)

    def give_block(i, _):
        start = pl.multiple_of(order_ref[i] * rows, rows)
        target = pl.multiple_of(i * rows, rows)
        out_ref[pl.ds(target, rows), :] = made[pl.ds(start, rows), :]
        return 0

    lax.fori_loop(0, blocks, give_block, 0)


def attend_back_kernel(
    q_heads,
    kv_heads,
    tile,
    order_ref,
    all_kept_ref,
    all_back_ref,
    all_lse_ref,
    cos_ref,
    sin_ref,
    all_out_ref,
    *scratch,
):
    for sequence in range(all_kept_ref.shape[0]):
        attend_back_sequence(
            q_heads,
            kv_heads,
            tile,
            order_ref,
            all_kept_ref.at[sequence],
            all_back_ref.at[sequence],
            all_lse_ref.at[sequence],
            cos_ref,
            sin_ref,
            all_out_ref.at[sequence],
            *scratch,
        )


def attend_back_sequence(
    q_heads,
    kv_heads,
    tile,
    order_ref,
    kept_ref,
    back_ref,
    lse_ref,
    cos_ref,
    sin_ref,
    out_ref,
    back_sorted,
    grad,
    delta_ref,
    dq_ref,
):
    length, cols = kept_ref.shape
    blocks = order_ref.shape[0]
    rows = length // blocks
    group = q_heads // kv_heads
    q_cols, k_cols = q_heads * HEAD, kv_heads * HEAD
    scale = HEAD ** (-0.5)
    tiles = length // tile

    def take_block(i, _):
        start = pl.multiple_of(order_ref[i] * rows, rows)
        source = pl.multiple_of(i * rows, rows)
        back_sorted[pl.ds(start, rows), :] = back_ref[pl.ds(source, rows), :]
        return 0

    lax.fori_loop(0, blocks, take_block, 0)
    keep = causal_keep(tile)
    for kv in range(kv_heads):
        k_at = q_cols + kv * HEAD
        v_at = q_cols + k_cols + kv * HEAD

        def load(i, g):
            start = pl.multiple_of(i * tile, tile)
            head = kv * group + g
            at = slice(head * HEAD, (head + 1) * HEAD)
            return (
                kept_ref[pl.ds(start, tile), at],
                back_sorted[pl.ds(start, tile), at],
                lse_ref[head : head + 1, pl.ds(start, tile)],
            )

        def load_kv(j):
            start = pl.multiple_of(j * tile, tile)
            return (
                kept_ref[pl.ds(start, tile), k_at : k_at + HEAD],
                kept_ref[pl.ds(start, tile), v_at : v_at + HEAD],
            )

        def tile_terms(keys, values, query, back, lse, masked):
            weights = jnp.exp(dot_nt(keys, query) * scale - lse)
            if masked:
                weights = jnp.where(keep, weights, 0.0)
            return weights, dot_nt(values, back)

        def delta_step(i, _):
            rows_i = [load(i, g) for g in range(group)]

            def one(j, carry, masked):
                keys, values = load_kv(j)
                result = []
                for g in range(group):
                    weights, back_weights = tile_terms(keys, values, *rows_i[g], masked)
                    result.append(carry[g] + jnp.sum(weights * back_weights, 0, keepdims=True))
                return tuple(result)

            carry = tuple(jnp.zeros((1, tile), jnp.float32) for _ in range(group))
            carry = lax.fori_loop(0, i, lambda j, c: one(j, c, False), carry)
            carry = one(i, carry, True)
            for g in range(group):
                delta_ref[g : g + 1, pl.ds(pl.multiple_of(i * tile, tile), tile)] = carry[g]
            return 0

        lax.fori_loop(0, tiles, delta_step, 0)
        dq_ref[...] = jnp.zeros_like(dq_ref)

        def key_step(j, _):
            keys, values = load_kv(j)

            def one(i, carry, masked):
                back_key, back_value = carry
                start = pl.multiple_of(i * tile, tile)
                for g in range(group):
                    query, back, lse = load(i, g)
                    weights, back_weights = tile_terms(keys, values, query, back, lse, masked)
                    delta = delta_ref[g : g + 1, pl.ds(start, tile)]
                    back_scores = (weights * (back_weights - delta)).astype(jnp.bfloat16)
                    back_key = back_key + dot_nn(back_scores, query)
                    back_value = back_value + dot_nn(weights.astype(jnp.bfloat16), back)
                    dq_ref[g * HEAD : (g + 1) * HEAD, pl.ds(start, tile)] += dot_tn(
                        keys, back_scores
                    )
                return back_key, back_value

            zero = jnp.zeros((tile, HEAD), jnp.float32)
            carry = one(j, (zero, zero), True)
            carry = lax.fori_loop(j + 1, tiles, lambda i, c: one(i, c, False), carry)
            start = pl.multiple_of(j * tile, tile)
            grad[pl.ds(start, tile), k_at : k_at + HEAD] = carry[0] * scale
            grad[pl.ds(start, tile), v_at : v_at + HEAD] = carry[1]
            return 0

        lax.fori_loop(0, tiles, key_step, 0)
        for g in range(group):
            head = kv * group + g
            grad[:, head * HEAD : (head + 1) * HEAD] = (
                dq_ref[g * HEAD : (g + 1) * HEAD, :] * scale
            ).T

    def give_block(i, _):
        start = pl.multiple_of(order_ref[i] * rows, rows)
        target = pl.multiple_of(i * rows, rows)
        cos = cos_ref[pl.ds(start, rows), :]
        sin = sin_ref[pl.ds(start, rows), :]
        for c in range(0, cols, 2 * HEAD):
            values = grad[pl.ds(start, rows), c : c + 2 * HEAD]
            values = turn_columns(values, c, q_cols + k_cols, cos, sin, False)
            out_ref[pl.ds(target, rows), c : c + 2 * HEAD] = values.astype(jnp.bfloat16)
        return 0

    lax.fori_loop(0, blocks, give_block, 0)


MESH = pl.DeviceIdType.MESH


def part_owner(part):
    return part % 2 * 2 + part // 2


def sequence_target(group, place, second, splits):
    part = place // 2
    target = (part_owner(part % 4), (2 * group + second) * splits + part // 4)
    return target, place % 2


def token_target(group, place, half, splits):
    sequence = place // splits
    part = part_owner(group) + 4 * (place % splits)
    return (sequence // 2, 2 * part + half), sequence % 2


def remote(source, target, sems, device):
    return pltpu.make_async_remote_copy(
        src_ref=source,
        dst_ref=target,
        send_sem=sems[0],
        recv_sem=sems[1],
        device_id=device,
        device_id_type=MESH,
    )


def same(one, other):
    return jnp.logical_and(one[0] == other[0], one[1] == other[1])


def greet(me, peers, movers):
    barrier = pltpu.get_barrier_semaphore()
    for peer in peers:
        pl.semaphore_signal(barrier, inc=1, device_id=peer, device_id_type=MESH)
    expected = len(peers)
    for source, target in movers:

        @pl.when(jnp.logical_not(same(source, me)))
        def _():
            pl.semaphore_signal(barrier, inc=1, device_id=source, device_id_type=MESH)

        expected = expected + jnp.where(same(target, me), 0, 1)
    pl.semaphore_wait(barrier, expected)


def move_start(me, source, target, target_device, send, receive):
    here = same(target_device, me)

    @pl.when(here)
    def _():
        pltpu.make_async_copy(source, target, receive).start()

    @pl.when(jnp.logical_not(here))
    def _():
        remote(source, target, (send, receive), target_device).start()


def move_sent(me, source, target, target_device, send, receive):
    @pl.when(jnp.logical_not(same(target_device, me)))
    def _():
        remote(source, target, (send, receive), target_device).wait_send()


def member(me, by):
    return (me[0] ^ (by // 2), me[1] ^ (by % 2))


def group_index(device):
    return 2 * device[0] + device[1] % 2


class GroupGather:
    def __init__(self, me, rows, sems):
        self.rows, self.sems = rows, sems
        self.core, self.across, self.beside = member(me, 2), member(me, 4), member(me, 1)

    def hop(self, index):
        rows, across, beside, core = self.rows, self.across, self.beside, self.core
        source, target, device = (
            (rows.at[0, 0, 0], rows.at[0, 2, 0], across),
            (rows.at[0, 0, 1], rows.at[1, 0, 1], beside),
            (rows.at[0, 0, 0], rows.at[1, 0, 0], beside),
            (rows.at[0, 0, 1], rows.at[0, 2, 1], across),
            (rows.at[0, 2, 0], rows.at[1, 2, 0], beside),
            (rows.at[1, 0, 1], rows.at[1, 2, 1], across),
            (rows.at[0, 0], rows.at[0, 1], core),
            (rows.at[0, 2], rows.at[0, 3], core),
            (rows.at[1, 0], rows.at[1, 1], core),
            (rows.at[1, 2], rows.at[1, 3], core),
        )[index]
        return remote(source, target, (self.sems.at[0, index], self.sems.at[1, index]), device)

    def start(self):
        for index in (0, 1, 2, 3, 6):
            self.hop(index).start()

    def pass_on(self):
        self.hop(0).wait_recv()
        self.hop(4).start()
        self.hop(1).wait_recv()
        self.hop(5).start()
        self.hop(3).wait_recv()
        self.hop(7).start()
        self.hop(2).wait_recv()
        self.hop(8).start()

    def finish(self):
        self.hop(4).wait_recv()
        self.hop(5).wait_recv()
        self.hop(9).start()
        for index in (6, 7, 8, 9):
            self.hop(index).wait_recv()
        for index in range(10):
            self.hop(index).wait_send()


def first_kernel(shards, splits, tokens, cot, pieces, out_own, gate_pieces, *refs):
    rows, cot_rows, in_all, out_all, gate_rows = refs[:5]
    held, move_send, move_recv, group_sems, piece_sems, gate_sems, own_sems = refs[5:12]
    in_sems, line_sems, pair_sems = refs[12:]
    me = (lax.axis_index("dp"), lax.axis_index("ctx"))
    group, place = me
    slow = shards // 2
    slot, half = place // 2, place % 2
    mine = group_index(me)
    line = [(group, place ^ (2 * by)) for by in range(1, slow)]
    pair = member(me, 1)
    movers = []
    for i in (0, 1):
        movers.append(
            (token_target(group, place, i, splits)[0], sequence_target(group, place, i, splits)[0])
        )
    greet(me, [member(me, by) for by in range(1, 8)] + line, movers)

    def piece(by):
        sems = (piece_sems.at[0, by - 1], piece_sems.at[1, by - 1])
        peer = member(me, by)
        index = group_index(peer)
        return remote(
            pieces.at[index // 2, index % 2], held.at[group, half], sems, peer
        )

    def gate(by):
        sems = (gate_sems.at[0, by - 1], gate_sems.at[1, by - 1])
        peer = member(me, by)
        return remote(gate_pieces.at[group_index(peer)], gate_rows.at[mine], sems, peer)

    def move(array, second):
        device, part = sequence_target(group, place, second, splits)
        source = (tokens, cot)[array].at[second]
        target = (rows.at[0, 0], cot_rows)[array].at[part]
        return me, source, target, device, move_send.at[array, second], move_recv.at[array, part]

    def in_line(by):
        sems = (in_sems.at[0, by - 1], in_sems.at[1, by - 1])
        return remote(held, in_all.at[:, slot], sems, line[by - 1])

    def out_line(by):
        sems = (line_sems.at[0, by - 1], line_sems.at[1, by - 1])
        return remote(out_own, out_all.at[place], sems, line[by - 1])

    def out_pair(by):
        block = place ^ (2 * by)
        source = out_own if by == 0 else out_all.at[block]
        sems = (pair_sems.at[0, by], pair_sems.at[1, by])
        return remote(source, out_all.at[block], sems, pair)

    own = [
        pltpu.make_async_copy(pieces.at[group, half], held.at[group, half], own_sems.at[0]),
        pltpu.make_async_copy(gate_pieces.at[mine], gate_rows.at[mine], own_sems.at[1]),
        pltpu.make_async_copy(out_own, out_all.at[place], own_sems.at[2]),
        pltpu.make_async_copy(held, in_all.at[:, slot], own_sems.at[3]),
    ]
    for by in range(1, 8):
        piece(by).start()
    own[0].start()
    for second in (0, 1):
        move_start(*move(0, second))
    own[0].wait()
    for by in range(1, 8):
        piece(by).wait_recv()
    for by in range(1, slow):
        in_line(by).start()
    own[3].start()
    for part in (0, 1):
        pltpu.make_async_copy(tokens.at[0], rows.at[0, 0, part], move_recv.at[0, part]).wait()
    spread = GroupGather(me, rows, group_sems)
    spread.start()
    out_pair(0).start()
    for by in range(1, slow):
        out_line(by).start()
    own[2].start()
    spread.pass_on()
    for by in range(1, slow):
        in_line(by).wait_recv()
    for second in (0, 1):
        move_start(*move(1, second))
    for by in range(1, 8):
        gate(by).start()
    own[1].start()
    for by in range(1, slow):
        out_line(by).wait_recv()
        out_pair(by).start()
    spread.finish()
    for part in (0, 1):
        pltpu.make_async_copy(cot.at[0], cot_rows.at[part], move_recv.at[1, part]).wait()
    for index in (1, 2, 3):
        own[index].wait()
    for by in range(1, 8):
        piece(by).wait_send()
        gate(by).wait()
    for by in range(1, slow):
        in_line(by).wait_send()
        out_line(by).wait_send()
    for by in range(slow):
        out_pair(by).wait()
    for array in (0, 1):
        for second in (0, 1):
            move_sent(*move(array, second))


def first_exchange(tokens, cot, pieces, out_own, gate_pieces, shards, splits, identity):
    low = jnp.bfloat16
    slow = shards // 2
    any_space = pl.BlockSpec(memory_space=pl.ANY)
    dma = pltpu.SemaphoreType.DMA
    rows, width = pieces.shape[2:]
    return pl.pallas_call(
        functools.partial(first_kernel, shards, splits),
        out_shape=(
            jax.ShapeDtypeStruct((2, 4) + tokens.shape, low),
            jax.ShapeDtypeStruct(cot.shape, low),
            jax.ShapeDtypeStruct((4, slow, 2, rows, width), low),
            jax.ShapeDtypeStruct((shards,) + out_own.shape, low),
            jax.ShapeDtypeStruct(gate_pieces.shape, low),
        ),
        in_specs=[any_space] * 5,
        out_specs=(any_space,) * 5,
        scratch_shapes=[
            pltpu.VMEM(pieces.shape, low),
            dma((2, 2)),
            dma((2, 2)),
            dma((2, 10)),
            dma((2, 7)),
            dma((2, 7)),
            dma((4,)),
            dma((2, slow - 1)),
            dma((2, slow - 1)),
            dma((2, slow)),
        ],
        compiler_params=pltpu.CompilerParams(
            collective_id=identity, has_side_effects=True, vmem_limit_bytes=8 << 20
        ),
        cost_estimate=pl.CostEstimate(flops=0, bytes_accessed=200 << 20, transcendentals=0),
    )(tokens, cot, pieces, out_own, gate_pieces)


def last_kernel(shards, splits, in_parts, out_parts, made_one, made_two, *refs):
    in_total, out_total, one, two = refs[:4]
    in_kept, in_arrived, in_done, out_kept, out_arrived, out_done = refs[4:10]
    move_send, move_recv, own_sems, in_sems, out_sems, piece_sems, home_sems = refs[10:]
    me = (lax.axis_index("dp"), lax.axis_index("ctx"))
    group, place = me
    slow = shards // 2
    slot, half = place // 2, place % 2
    mine = group_index(me)
    line = [(group, place ^ (2 * by)) for by in range(1, slow)]
    movers = []
    for i in (0, 1):
        movers.append(
            (sequence_target(group, place, i, splits)[0], token_target(group, place, i, splits)[0])
        )
    home = (group, half * slow + slot)
    movers.append(((group, place % slow * 2 + place // slow), home))
    greet(me, [member(me, by) for by in range(1, 8)] + line, movers)

    def move(array, part):
        device, second = token_target(group, place, part, splits)
        source = (made_one, made_two)[array].at[part]
        target = (one, two)[array].at[second]
        return me, source, target, device, move_send.at[array, part], move_recv.at[array, second]

    def in_line(by):
        sems = (in_sems.at[0, by - 1], in_sems.at[1, by - 1])
        return remote(in_parts.at[slot ^ by], in_arrived.at[by - 1], sems, line[by - 1])

    def out_line(by):
        sems = (out_sems.at[0, by - 1], out_sems.at[1, by - 1])
        return remote(out_parts.at[slot ^ by], out_arrived.at[by - 1], sems, line[by - 1])

    def piece(by):
        sems = (piece_sems.at[0, by - 1], piece_sems.at[1, by - 1])
        peer = member(me, by)
        return remote(in_done.at[group_index(peer)], in_total.at[mine], sems, peer)

    own = [
        pltpu.make_async_copy(in_parts.at[slot], in_kept, own_sems.at[0]),
        pltpu.make_async_copy(out_parts.at[slot], out_kept, own_sems.at[1]),
        pltpu.make_async_copy(in_done.at[mine], in_total.at[mine], own_sems.at[2]),
    ]
    for by in range(1, slow):
        in_line(by).start()
    for by in range(1, slow):
        out_line(by).start()
    own[0].start()
    own[1].start()
    for array in (0, 1):
        for part in (0, 1):
            move_start(*move(array, part))
    own[0].wait()
    value = in_kept[...].astype(jnp.float32)
    for by in range(1, slow):
        in_line(by).wait_recv()
        value = value + in_arrived[by - 1].astype(jnp.float32)
    in_done[...] = value.astype(jnp.bfloat16)
    for by in range(1, 8):
        piece(by).start()
    own[2].start()
    own[1].wait()
    value = out_kept[...].astype(jnp.float32)
    for by in range(1, slow):
        out_line(by).wait_recv()
        value = value + out_arrived[by - 1].astype(jnp.float32)
    out_done[...] = value.astype(jnp.bfloat16)
    to_home = (me, out_done, out_total, home, home_sems.at[0], home_sems.at[1])
    move_start(*to_home)
    pltpu.make_async_copy(out_done, out_total, home_sems.at[1]).wait()
    move_sent(*to_home)
    own[2].wait()
    for by in range(1, 8):
        piece(by).wait()
    for by in range(1, slow):
        in_line(by).wait_send()
        out_line(by).wait_send()
    for array in (0, 1):
        for part in (0, 1):
            pltpu.make_async_copy(
                (made_one, made_two)[array].at[part],
                (one, two)[array].at[part],
                move_recv.at[array, part],
            ).wait()
    for array in (0, 1):
        for part in (0, 1):
            move_sent(*move(array, part))


def last_sums(in_parts, out_parts, made, shards, splits, identity):
    low = jnp.bfloat16
    slow = shards // 2
    any_space = pl.BlockSpec(memory_space=pl.ANY)
    dma = pltpu.SemaphoreType.DMA
    return pl.pallas_call(
        functools.partial(last_kernel, shards, splits),
        out_shape=(
            jax.ShapeDtypeStruct(in_parts.shape[1:], low),
            jax.ShapeDtypeStruct(out_parts.shape[1:], low),
            jax.ShapeDtypeStruct(made[0].shape, low),
            jax.ShapeDtypeStruct(made[1].shape, low),
        ),
        in_specs=[any_space] * 4,
        out_specs=(any_space,) * 4,
        scratch_shapes=[
            pltpu.VMEM(in_parts.shape[1:], low),
            pltpu.VMEM((slow - 1,) + in_parts.shape[1:], low),
            pltpu.VMEM(in_parts.shape[1:], low),
            pltpu.VMEM(out_parts.shape[1:], low),
            pltpu.VMEM((slow - 1,) + out_parts.shape[1:], low),
            pltpu.VMEM(out_parts.shape[1:], low),
            dma((2, 2)),
            dma((2, 2)),
            dma((3,)),
            dma((2, slow - 1)),
            dma((2, slow - 1)),
            dma((2, 7)),
            dma((2,)),
        ],
        compiler_params=pltpu.CompilerParams(
            collective_id=identity, has_side_effects=True, vmem_limit_bytes=24 << 20
        ),
        cost_estimate=pl.CostEstimate(flops=0, bytes_accessed=150 << 20, transcendentals=0),
    )(in_parts, out_parts, *made)


def position_tables(length):
    cosine, sine_table = rotary_tables(jnp.arange(length, dtype=jnp.int32), HEAD)
    sign = jnp.where(jnp.arange(HEAD) < HEAD // 2, -1.0, 1.0)
    return jnp.tile(cosine, (1, 2)), jnp.tile(sine_table * sign, (1, 2))


def attend(order, qkv, tables, q_heads, kv_heads):
    seqs, length, cols = qkv.shape
    whole = pl.BlockSpec(memory_space=pltpu.VMEM)
    return pl.pallas_call(
        functools.partial(attend_kernel, q_heads, kv_heads, 256),
        out_shape=(
            jax.ShapeDtypeStruct((seqs, length, q_heads * HEAD), jnp.bfloat16),
            jax.ShapeDtypeStruct((seqs, q_heads, length), jnp.float32),
            jax.ShapeDtypeStruct((seqs, length, cols), jnp.bfloat16),
        ),
        in_specs=[pl.BlockSpec(memory_space=pltpu.SMEM), whole, whole, whole],
        out_specs=(whole, whole, whole),
        scratch_shapes=[pltpu.VMEM((length, q_heads * HEAD), jnp.bfloat16)],
        compiler_params=pltpu.CompilerParams(vmem_limit_bytes=40 << 20),
        cost_estimate=pl.CostEstimate(
            flops=2 * seqs * length * length * q_heads * HEAD,
            bytes_accessed=8 * seqs * length * cols,
            transcendentals=seqs * length * length * q_heads // 2,
        ),
    )(order, qkv, *tables)


def attend_back(order, kept, back, lse, tables, q_heads, kv_heads):
    seqs, length, cols = kept.shape
    group = q_heads // kv_heads
    whole = pl.BlockSpec(memory_space=pltpu.VMEM)
    return pl.pallas_call(
        functools.partial(attend_back_kernel, q_heads, kv_heads, 256),
        out_shape=jax.ShapeDtypeStruct((seqs, length, cols), jnp.bfloat16),
        in_specs=[pl.BlockSpec(memory_space=pltpu.SMEM)] + [whole] * 5,
        out_specs=whole,
        scratch_shapes=[
            pltpu.VMEM((length, q_heads * HEAD), jnp.bfloat16),
            pltpu.VMEM((length, cols), jnp.float32),
            pltpu.VMEM((group, length), jnp.float32),
            pltpu.VMEM((group * HEAD, length), jnp.float32),
        ],
        compiler_params=pltpu.CompilerParams(vmem_limit_bytes=40 << 20),
        cost_estimate=pl.CostEstimate(
            flops=7 * seqs * length * length * q_heads * HEAD,
            bytes_accessed=6 * seqs * length * cols,
            transcendentals=seqs * length * length * q_heads // 2,
        ),
    )(order, kept, back, lse, *tables)


def local(
    tokens,
    cotangent,
    block_order,
    attention_in,
    attention_out,
    gate_up,
    down_matrix,
    gains,
    mean_attention_in,
    mean_attention_out,
    mean_gate_up,
    mean_down,
    mean_gains,
    square_attention_in,
    square_attention_out,
    square_gate_up,
    square_down,
    square_gains,
):
    seq_count, shard_rows, width = tokens.shape
    shards = lax.axis_size("ctx")
    slow = shards // 2
    mine = lax.axis_index("dp")
    beside = lax.axis_index("ctx") % 2
    low = jnp.bfloat16
    owned = attention_in.shape[0]
    hidden_units = gate_up.shape[1] // 2
    part_hidden = hidden_units // 8
    units = down_matrix.shape[0]
    part_q = HEADS * HEAD // 8
    part_k = KV_HEADS * HEAD // 8
    part_cols = part_q + 2 * part_k
    count = seq_count * shard_rows
    together = 8 * count
    spread = shards // (4 * seq_count)
    splits = max(1, slow // 8)
    seqs = 2 // spread if spread < 2 else 1
    length = shards * shard_rows
    q_heads = HEADS // 8 // splits
    kv_heads = KV_HEADS // 8

    in_low = attention_in.astype(low)
    gains_row = jnp.pad(gains.astype(low).reshape(1, -1), ((0, 15), (0, part_cols - 2 * owned)))
    pieces = jnp.stack(
        [
            jnp.concatenate(
                [
                    jnp.concatenate(
                        [
                            in_low[:, i * part_q : (i + 1) * part_q],
                            in_low[:, 8 * part_q + i * part_k :][:, :part_k],
                            in_low[:, 8 * (part_q + part_k) + i * part_k :][:, :part_k],
                        ],
                        1,
                    ),
                    gains_row,
                ]
            )
            for i in range(8)
        ]
    ).reshape(4, 2, owned + 16, part_cols)
    gate_low = gate_up.astype(low)
    gate_pieces = jnp.stack(
        [
            jnp.concatenate(
                [
                    gate_low[:, side * hidden_units + (dp * shards + 2 * s + half) * units :][
                        :, :units
                    ]
                    for side in range(2)
                    for s in range(slow)
                ],
                1,
            )
            for dp in range(4)
            for half in range(2)
        ]
    )
    tokens_all, cot_own, in_all, out_all, gate_rows = first_exchange(
        tokens, cotangent, pieces, attention_out.astype(low), gate_pieces, shards, spread, 1
    )
    w_in = in_all[:, :, :, :owned].reshape(width, part_cols)
    w_out = lax.dynamic_slice_in_dim(out_all.reshape(-1, width), beside * part_q, part_q, 0)
    gains_all = in_all[:, :, :, owned, : 2 * owned].reshape(-1, 2, owned)
    gains_all = gains_all.astype(jnp.float32).swapaxes(0, 1).reshape(2, width)
    gain_one, gain_two = gains_all[0], gains_all[1]
    x_low = tokens_all[0, 0].reshape(count, width)
    cot_own = cot_own.reshape(count, width)
    back_all = gather_group(cot_own).reshape(together, width)
    w_gate = gather_line(gate_rows.reshape(8 * owned, 2 * part_hidden))
    w_down = gather_line((down_matrix + 0.0 * w_gate[0, 0].astype(jnp.float32)).astype(low))

    normed_all, _ = norm_parts(tokens_all.reshape(together, width).astype(jnp.float32))
    input_one = (normed_all * gain_one).astype(low)
    qkv = dot_nn(input_one, w_in)
    orders = block_order.reshape(2 * splits if spread > 1 else 1, 4, -1)
    slot_order = jnp.concatenate(
        [
            orders[(2 * s + (beside ^ i)) if spread > 1 else 0, part_owner(mine ^ j)]
            for s in range(splits)
            for i in range(2 // seqs)
            for j in range(4)
        ]
    )
    tables = position_tables(length)
    groups = [
        [2 * (s * splits + g) + half for g in range(splits)]
        for s in range(slow // splits)
        for half in (0, 1)
    ]

    def split_heads(values, widths, copies):
        parts = []
        start = 0
        for each, repeat in zip(widths, copies):
            kinds = splits // repeat
            piece = values[:, start : start + kinds * each].reshape(-1, kinds, each)
            parts.append(jnp.repeat(piece.swapaxes(0, 1), repeat, axis=0))
            start += kinds * each
        sent = jnp.concatenate(parts, 2)
        got = lax.all_to_all(sent, "ctx", 0, 0, axis_index_groups=groups, tiled=True)
        return got.reshape(length, -1)

    def join_heads(values):
        sent = values.reshape(splits, together, -1)
        return lax.all_to_all(sent, "ctx", 0, 0, axis_index_groups=groups, tiled=True)

    q_width, k_width = q_heads * HEAD, kv_heads * HEAD
    if splits > 1:
        qkv = split_heads(qkv, (q_width, k_width, k_width), (1, splits, splits))
    qkv = qkv.reshape(seqs, length, -1)
    attended, lse, kept = attend(slot_order, qkv, tables, q_heads, kv_heads)
    if splits > 1:
        attended = join_heads(attended).swapaxes(0, 1)
    attended = attended.reshape(together, part_q)

    def grouped(values):
        return scatter_group(values.reshape(2, 4, count, width))

    flat_rows = x_low.astype(jnp.float32)
    normed_one, factor_one = norm_parts(flat_rows)
    residual = flat_rows + grouped(dot_nn(attended, w_out))
    normed_two, factor_two = norm_parts(residual)
    input_two_own = to_owner_order((normed_two * gain_two).astype(low), slow)
    input_two = gather_group(input_two_own).reshape(together, width)
    gate_both = dot_nn(input_two, w_gate)
    gate_part = gate_both[:, :part_hidden]
    up_part = gate_both[:, part_hidden:]
    sigmoid_gate = jax.nn.sigmoid(gate_part)
    active = gate_part * sigmoid_gate
    hidden = (active * up_part).astype(low)
    output_rows = residual + grouped(dot_nn(hidden, w_down))
    output_rows = output_rows.astype(low).reshape(seq_count, shard_rows, width)
    grad_down = dot_tn(hidden, back_all) + 0.0 * w_down[0, 0].astype(jnp.float32)
    down_low = sum_line(grad_down.astype(low))
    down_sum = down_low.astype(jnp.float32)
    back_hidden = dot_nt(back_all, w_down)
    back_gate = back_hidden * up_part * sigmoid_gate * (1.0 + gate_part * (1.0 - sigmoid_gate))
    back_upper = back_hidden * active
    back_gate_up = jnp.concatenate([back_gate, back_upper], 1).astype(low)
    gate_sum = exchange_group(
        sum_line(dot_tn(input_two, back_gate_up).astype(low)).reshape(8, owned, 2 * part_hidden)
    )
    gate_sum = (
        gate_sum.reshape(4, 2, owned, 2, slow, units)
        .transpose(2, 3, 0, 4, 1, 5)
        .reshape(owned, 2 * hidden_units)
        .astype(jnp.float32)
    )
    back_input_two = from_owner_order(grouped(dot_nt(back_gate_up, w_gate)), slow)
    grad_gain_two = jnp.sum(back_input_two * normed_two, 0)
    back_residual = cot_own.astype(jnp.float32) + norm_back(
        back_input_two * gain_two, normed_two, factor_two
    )
    back_residual_all = gather_group(back_residual.astype(low)).reshape(together, width)
    grad_out = dot_tn(attended, back_residual_all).astype(low)
    back_attended = dot_nt(back_residual_all, w_out).astype(low)
    if splits > 1:
        back_attended = split_heads(back_attended, (q_width,), (1,))
    back_projected = attend_back(
        slot_order, kept, back_attended.reshape(seqs, length, -1), lse, tables, q_heads, kv_heads
    )
    if splits > 1:
        back_projected = join_heads(back_projected).astype(jnp.float32)
        back_projected = jnp.concatenate(
            [
                back_projected[..., :q_width].swapaxes(0, 1).reshape(together, part_q),
                back_projected[..., q_width:].sum(0),
            ],
            1,
        ).astype(low)
    back_projected = back_projected.reshape(together, part_cols)
    back_input_one = grouped(dot_nt(back_projected, w_in))
    grad_gain_one = jnp.sum(back_input_one * normed_one, 0)
    tokens_grad = back_residual + norm_back(back_input_one * gain_one, normed_one, factor_one)
    tokens_grad = tokens_grad.astype(low).reshape(seq_count, shard_rows, width)
    grad_gains = jnp.stack([grad_gain_one, grad_gain_two]).reshape(2, 4, slow, 2, owned)
    gains_rows = grad_gains.transpose(2, 1, 3, 0, 4).reshape(slow, 8, 1, 2 * owned).astype(low)
    gains_rows = jnp.pad(gains_rows, ((0, 0), (0, 0), (0, 15), (0, part_cols - 2 * owned)))
    grad_in = dot_tn(input_one, back_projected).astype(low)
    grad_in = grad_in.reshape(4, slow, 2 * owned, part_cols).swapaxes(0, 1)
    grad_in = grad_in.reshape(slow, 8, owned, part_cols)
    in_sum, out_sum, block_out, tokens_grad = last_sums(
        jnp.concatenate([grad_in, gains_rows], 2),
        grad_out.reshape(slow, owned, width),
        [output_rows, tokens_grad],
        shards,
        spread,
        2,
    )
    tokens_grad = tokens_grad.astype(jnp.float32)
    out_sum = out_sum.astype(jnp.float32)
    gains_sum = in_sum[:, owned, : 2 * owned].reshape(8, 2, owned).astype(jnp.float32).sum(0)
    cuts = ((0, part_q), (part_q, part_q + part_k), (part_q + part_k, part_cols))
    in_sum = jnp.concatenate(
        [in_sum[i, :owned, first:last] for first, last in cuts for i in range(8)], 1
    ).astype(jnp.float32)
    new_in = adam_update(
        attention_in,
        in_sum,
        mean_attention_in,
        square_attention_in,
        input_boost * D ** (-0.5),
        weight_decay,
    )
    new_out = adam_update(
        attention_out,
        out_sum,
        mean_attention_out,
        square_attention_out,
        (HEADS * HEAD // 32) ** (-0.5),
        weight_decay,
    )
    new_gate = adam_update(
        gate_up, gate_sum, mean_gate_up, square_gate_up, D ** (-0.5), weight_decay
    )
    new_down = adam_update(
        down_matrix, down_sum, mean_down, square_down, FF ** (-0.5), weight_decay
    )
    new_gain = adam_update(gains, gains_sum, mean_gains, square_gains, gain_rate, 0.0)
    return (
        block_out,
        tokens_grad,
        new_in[0],
        new_in[1],
        new_in[2],
        new_out[0],
        new_out[1],
        new_out[2],
        new_gate[0],
        new_gate[1],
        new_gate[2],
        new_down[0],
        new_down[1],
        new_down[2],
        new_gain[0],
        new_gain[1],
        new_gain[2],
    )


def solution(mesh):
    in_specs = (
        P("dp", "ctx", None),
        P("dp", "ctx", None),
        P(),
        P(("dp", "ctx"), None),
        P(("dp", "ctx"), None),
        P(("dp", "ctx"), None),
        P(("dp", "ctx"), None),
        P(None, ("dp", "ctx")),
        P(("dp", "ctx"), None),
        P(("dp", "ctx"), None),
        P(("dp", "ctx"), None),
        P(("dp", "ctx"), None),
        P(None, ("dp", "ctx")),
        P(("dp", "ctx"), None),
        P(("dp", "ctx"), None),
        P(("dp", "ctx"), None),
        P(("dp", "ctx"), None),
        P(None, ("dp", "ctx")),
    )
    out_specs = (
        P("dp", "ctx", None),
        P("dp", "ctx", None),
        P(("dp", "ctx"), None),
        P(("dp", "ctx"), None),
        P(("dp", "ctx"), None),
        P(("dp", "ctx"), None),
        P(("dp", "ctx"), None),
        P(("dp", "ctx"), None),
        P(("dp", "ctx"), None),
        P(("dp", "ctx"), None),
        P(("dp", "ctx"), None),
        P(("dp", "ctx"), None),
        P(("dp", "ctx"), None),
        P(("dp", "ctx"), None),
        P(None, ("dp", "ctx")),
        P(None, ("dp", "ctx")),
        P(None, ("dp", "ctx")),
    )
    return jax.shard_map(local, mesh=mesh, in_specs=in_specs, out_specs=out_specs, check_vma=False)
```

```python
import functools

import jax
import jax.numpy as jnp
from jax import lax
from jax.experimental import pallas as pl
from jax.experimental.pallas import tpu as pltpu
from jax.sharding import PartitionSpec as P

D = 2048
HEADS = 32
KV_HEADS = 8
HEAD = 64
FF = 8192
STEP = 5


norm_eps = 1e-05
rope_base = 500000.0
beta_one = 0.9
beta_two = 0.95
gain_rate = 1.25
input_boost = 2.5
weight_decay = 0.1
adam_eps = 1e-08
masked_score = -1e30


def rotary_tables(positions, head_width):
    half_width = head_width // 2
    frequency = rope_base ** (-(jnp.arange(half_width, dtype=jnp.float32) * 2.0 / head_width))
    angles = positions.astype(jnp.float32)[:, None] * frequency[None, :]
    angles = jnp.concatenate([angles, angles], 1)
    return (jnp.cos(angles), jnp.sin(angles))


def norm_parts(values):
    factor = lax.rsqrt(jnp.mean(values * values, -1, keepdims=True) + norm_eps)
    return (values * factor, factor)


def norm_back(back_normed, normed, factor):
    return factor * (back_normed - normed * jnp.mean(back_normed * normed, -1, keepdims=True))


def adam_update(weight, gradient, first_moment, second_moment, step_rate, decay_rate):
    first_new = beta_one * first_moment + (1.0 - beta_one) * gradient
    second_new = beta_two * second_moment + (1.0 - beta_two) * gradient * gradient
    update = (
        first_new
        / (1.0 - beta_one**STEP)
        / (jnp.sqrt(second_new / (1.0 - beta_two**STEP)) + adam_eps)
    )
    return (first_new, second_new, weight - step_rate * (update + decay_rate * weight))


def swapped(values, by):
    shards = lax.axis_size("ctx")
    everyone = range(4 * shards)
    pairs = [(i, (i // shards ^ by[0]) * shards + (i % shards ^ by[1])) for i in everyone]
    return lax.ppermute(values, ("dp", "ctx"), pairs)


CORE, ACROSS, BESIDE = (1, 0), (2, 0), (0, 1)


def gather_group(values):
    half = values.shape[0] // 2
    one, two = values[:half], values[half:]
    one_across = swapped(one, ACROSS)
    two_beside = swapped(two, BESIDE)
    core = swapped(values, CORE)
    ones = swapped(jnp.stack([one, one_across]), BESIDE)
    twos = swapped(jnp.stack([two, two_beside]), ACROSS)
    others = jnp.stack(
        [
            jnp.concatenate([one_across, twos[0]]),
            jnp.concatenate([ones[0], two_beside]),
            jnp.concatenate([ones[1], twos[1]]),
        ]
    )
    cores = swapped(others, CORE)
    return jnp.stack(
        [values, core, others[0], cores[0], others[1], cores[1], others[2], cores[2]]
    ).reshape((2, 4) + values.shape)


def scatter_group(parts):
    low = jnp.bfloat16
    half = parts.shape[2] // 2
    wide = jnp.float32
    core = swapped(jnp.stack([parts[:, 1], parts[:, 3]], 1).astype(low), CORE)
    kept = jnp.stack([parts[:, 0], parts[:, 2]], 1) + core.astype(wide)
    one, two = kept[:, :, :half], kept[:, :, half:]
    ones = swapped(one[1].astype(low), BESIDE).astype(wide)
    twos = swapped(two[:, 1].astype(low), ACROSS).astype(wide)
    one_last = swapped((one[0, 1] + ones[1]).astype(low), ACROSS).astype(wide)
    two_last = swapped((two[1, 0] + twos[1]).astype(low), BESIDE).astype(wide)
    return jnp.concatenate([one[0, 0] + ones[0] + one_last, two[0, 0] + twos[0] + two_last])


def line_groups(shards):
    return [[2 * s + half for s in range(shards // 2)] for half in (0, 1)]


def gather_line(rows):
    return lax.all_gather(
        rows, "ctx", axis=0, tiled=True, axis_index_groups=line_groups(lax.axis_size("ctx"))
    )


def sum_line(gradient):
    return lax.psum_scatter(
        gradient,
        "ctx",
        scatter_dimension=0,
        tiled=True,
        axis_index_groups=line_groups(lax.axis_size("ctx")),
    )


def dot_nn(a, b):
    return lax.dot_general(a, b, (((1,), (0,)), ((), ())), preferred_element_type=jnp.float32)


def dot_nt(a, b):
    return lax.dot_general(a, b, (((1,), (1,)), ((), ())), preferred_element_type=jnp.float32)


def dot_tn(a, b):
    return lax.dot_general(a, b, (((0,), (0,)), ((), ())), preferred_element_type=jnp.float32)


def causal_keep(tile):
    keys = lax.broadcasted_iota(jnp.int32, (tile, tile), 0)
    queries = lax.broadcasted_iota(jnp.int32, (tile, tile), 1)
    return keys <= queries


def turn_group(values, cos, sin, forward):
    lanes = lax.broadcasted_iota(jnp.int32, values.shape, 1)
    other = jnp.where(
        lanes % HEAD < HEAD // 2,
        pltpu.roll(values, 2 * HEAD - HEAD // 2, 1),
        pltpu.roll(values, HEAD // 2, 1),
    )
    if forward:
        return values * cos + other * sin
    return values * cos - other * sin


def turn_columns(values, start, turned_cols, cos, sin, forward):
    if start >= turned_cols:
        return values
    turned = turn_group(values, cos, sin, forward)
    if start + 2 * HEAD <= turned_cols:
        return turned
    lanes = lax.broadcasted_iota(jnp.int32, values.shape, 1)
    return jnp.where(lanes < turned_cols - start, turned, values)


def attend_kernel(
    q_heads,
    kv_heads,
    tile,
    order_ref,
    all_qkv_ref,
    cos_ref,
    sin_ref,
    all_out_ref,
    all_lse_ref,
    all_kept_ref,
    made,
):
    for sequence in range(all_qkv_ref.shape[0]):
        attend_sequence(
            q_heads,
            kv_heads,
            tile,
            order_ref,
            all_qkv_ref.at[sequence],
            cos_ref,
            sin_ref,
            all_out_ref.at[sequence],
            all_lse_ref.at[sequence],
            all_kept_ref.at[sequence],
            made,
        )


def attend_sequence(
    q_heads, kv_heads, tile, order_ref, qkv_ref, cos_ref, sin_ref, out_ref, lse_ref, kept_ref, made
):
    length, cols = qkv_ref.shape
    blocks = order_ref.shape[0]
    rows = length // blocks
    group = q_heads // kv_heads
    q_cols, k_cols = q_heads * HEAD, kv_heads * HEAD
    scale = HEAD ** (-0.5)

    def take_block(i, _):
        start = pl.multiple_of(order_ref[i] * rows, rows)
        source = pl.multiple_of(i * rows, rows)
        cos = cos_ref[pl.ds(start, rows), :]
        sin = sin_ref[pl.ds(start, rows), :]
        for c in range(0, cols, 2 * HEAD):
            values = qkv_ref[pl.ds(source, rows), c : c + 2 * HEAD]
            values = turn_columns(values, c, q_cols + k_cols, cos, sin, True)
            kept_ref[pl.ds(start, rows), c : c + 2 * HEAD] = values.astype(jnp.bfloat16)
        return 0

    lax.fori_loop(0, blocks, take_block, 0)
    keep = causal_keep(tile)
    for kv in range(kv_heads):
        k_at = q_cols + kv * HEAD
        v_at = q_cols + k_cols + kv * HEAD

        def query_step(i, _):
            q_start = pl.multiple_of(i * tile, tile)
            queries = [
                kept_ref[
                    pl.ds(q_start, tile), (kv * group + g) * HEAD : (kv * group + g + 1) * HEAD
                ]
                for g in range(group)
            ]

            def key_tile(j, carry, masked):
                k_start = pl.multiple_of(j * tile, tile)
                keys = kept_ref[pl.ds(k_start, tile), k_at : k_at + HEAD]
                values = kept_ref[pl.ds(k_start, tile), v_at : v_at + HEAD]
                result = []
                for g in range(group):
                    peak, total, weighted = carry[g]
                    scores = dot_nt(keys, queries[g]) * scale
                    if masked:
                        scores = jnp.where(keep, scores, masked_score)
                    new_peak = jnp.maximum(peak, jnp.max(scores, 0, keepdims=True))
                    weights = jnp.exp(scores - new_peak)
                    shrink = jnp.exp(peak - new_peak)
                    total = total * shrink + jnp.sum(weights, 0, keepdims=True)
                    weighted = weighted * shrink + dot_tn(values, weights.astype(jnp.bfloat16))
                    result.append((new_peak, total, weighted))
                return tuple(result)

            start = tuple(
                (
                    jnp.full((1, tile), masked_score, jnp.float32),
                    jnp.zeros((1, tile), jnp.float32),
                    jnp.zeros((HEAD, tile), jnp.float32),
                )
                for _ in range(group)
            )
            carry = lax.fori_loop(0, i, lambda j, c: key_tile(j, c, False), start)
            carry = key_tile(i, carry, True)
            for g in range(group):
                head = kv * group + g
                peak, total, weighted = carry[g]
                lse_ref[head : head + 1, pl.ds(q_start, tile)] = peak + jnp.log(total)
                made[pl.ds(q_start, tile), head * HEAD : (head + 1) * HEAD] = (
                    (weighted / total).T.astype(jnp.bfloat16)
                )
            return 0

        lax.fori_loop(0, length // tile, query_step, 0)

    def give_block(i, _):
        start = pl.multiple_of(order_ref[i] * rows, rows)
        target = pl.multiple_of(i * rows, rows)
        out_ref[pl.ds(target, rows), :] = made[pl.ds(start, rows), :]
        return 0

    lax.fori_loop(0, blocks, give_block, 0)


def attend_back_kernel(
    q_heads,
    kv_heads,
    tile,
    order_ref,
    all_kept_ref,
    all_back_ref,
    all_lse_ref,
    cos_ref,
    sin_ref,
    all_out_ref,
    *scratch,
):
    for sequence in range(all_kept_ref.shape[0]):
        attend_back_sequence(
            q_heads,
            kv_heads,
            tile,
            order_ref,
            all_kept_ref.at[sequence],
            all_back_ref.at[sequence],
            all_lse_ref.at[sequence],
            cos_ref,
            sin_ref,
            all_out_ref.at[sequence],
            *scratch,
        )


def attend_back_sequence(
    q_heads,
    kv_heads,
    tile,
    order_ref,
    kept_ref,
    back_ref,
    lse_ref,
    cos_ref,
    sin_ref,
    out_ref,
    back_sorted,
    grad,
    delta_ref,
    dq_ref,
):
    length, cols = kept_ref.shape
    blocks = order_ref.shape[0]
    rows = length // blocks
    group = q_heads // kv_heads
    q_cols, k_cols = q_heads * HEAD, kv_heads * HEAD
    scale = HEAD ** (-0.5)
    tiles = length // tile

    def take_block(i, _):
        start = pl.multiple_of(order_ref[i] * rows, rows)
        source = pl.multiple_of(i * rows, rows)
        back_sorted[pl.ds(start, rows), :] = back_ref[pl.ds(source, rows), :]
        return 0

    lax.fori_loop(0, blocks, take_block, 0)
    keep = causal_keep(tile)
    for kv in range(kv_heads):
        k_at = q_cols + kv * HEAD
        v_at = q_cols + k_cols + kv * HEAD

        def load(i, g):
            start = pl.multiple_of(i * tile, tile)
            head = kv * group + g
            at = slice(head * HEAD, (head + 1) * HEAD)
            return (
                kept_ref[pl.ds(start, tile), at],
                back_sorted[pl.ds(start, tile), at],
                lse_ref[head : head + 1, pl.ds(start, tile)],
            )

        def load_kv(j):
            start = pl.multiple_of(j * tile, tile)
            return (
                kept_ref[pl.ds(start, tile), k_at : k_at + HEAD],
                kept_ref[pl.ds(start, tile), v_at : v_at + HEAD],
            )

        def tile_terms(keys, values, query, back, lse, masked):
            weights = jnp.exp(dot_nt(keys, query) * scale - lse)
            if masked:
                weights = jnp.where(keep, weights, 0.0)
            return weights, dot_nt(values, back)

        def delta_step(i, _):
            rows_i = [load(i, g) for g in range(group)]

            def one(j, carry, masked):
                keys, values = load_kv(j)
                result = []
                for g in range(group):
                    weights, back_weights = tile_terms(keys, values, *rows_i[g], masked)
                    result.append(carry[g] + jnp.sum(weights * back_weights, 0, keepdims=True))
                return tuple(result)

            carry = tuple(jnp.zeros((1, tile), jnp.float32) for _ in range(group))
            carry = lax.fori_loop(0, i, lambda j, c: one(j, c, False), carry)
            carry = one(i, carry, True)
            for g in range(group):
                delta_ref[g : g + 1, pl.ds(pl.multiple_of(i * tile, tile), tile)] = carry[g]
            return 0

        lax.fori_loop(0, tiles, delta_step, 0)
        dq_ref[...] = jnp.zeros_like(dq_ref)

        def key_step(j, _):
            keys, values = load_kv(j)

            def one(i, carry, masked):
                back_key, back_value = carry
                start = pl.multiple_of(i * tile, tile)
                for g in range(group):
                    query, back, lse = load(i, g)
                    weights, back_weights = tile_terms(keys, values, query, back, lse, masked)
                    delta = delta_ref[g : g + 1, pl.ds(start, tile)]
                    back_scores = (weights * (back_weights - delta)).astype(jnp.bfloat16)
                    back_key = back_key + dot_nn(back_scores, query)
                    back_value = back_value + dot_nn(weights.astype(jnp.bfloat16), back)
                    dq_ref[g * HEAD : (g + 1) * HEAD, pl.ds(start, tile)] += dot_tn(
                        keys, back_scores
                    )
                return back_key, back_value

            zero = jnp.zeros((tile, HEAD), jnp.float32)
            carry = one(j, (zero, zero), True)
            carry = lax.fori_loop(j + 1, tiles, lambda i, c: one(i, c, False), carry)
            start = pl.multiple_of(j * tile, tile)
            grad[pl.ds(start, tile), k_at : k_at + HEAD] = carry[0] * scale
            grad[pl.ds(start, tile), v_at : v_at + HEAD] = carry[1]
            return 0

        lax.fori_loop(0, tiles, key_step, 0)
        for g in range(group):
            head = kv * group + g
            grad[:, head * HEAD : (head + 1) * HEAD] = (
                dq_ref[g * HEAD : (g + 1) * HEAD, :] * scale
            ).T

    def give_block(i, _):
        start = pl.multiple_of(order_ref[i] * rows, rows)
        target = pl.multiple_of(i * rows, rows)
        cos = cos_ref[pl.ds(start, rows), :]
        sin = sin_ref[pl.ds(start, rows), :]
        for c in range(0, cols, 2 * HEAD):
            values = grad[pl.ds(start, rows), c : c + 2 * HEAD]
            values = turn_columns(values, c, q_cols + k_cols, cos, sin, False)
            out_ref[pl.ds(target, rows), c : c + 2 * HEAD] = values.astype(jnp.bfloat16)
        return 0

    lax.fori_loop(0, blocks, give_block, 0)


MESH = pl.DeviceIdType.MESH


def part_owner(part):
    return part % 2 * 2 + part // 2


def sequence_target(group, place, second, splits):
    part = place // 2
    target = (part_owner(part % 4), (2 * group + second) * splits + part // 4)
    return target, place % 2


def token_target(group, place, half, splits):
    sequence = place // splits
    part = part_owner(group) + 4 * (place % splits)
    return (sequence // 2, 2 * part + half), sequence % 2


def remote(source, target, sems, device):
    return pltpu.make_async_remote_copy(
        src_ref=source,
        dst_ref=target,
        send_sem=sems[0],
        recv_sem=sems[1],
        device_id=device,
        device_id_type=MESH,
    )


def same(one, other):
    return jnp.logical_and(one[0] == other[0], one[1] == other[1])


def greet(me, peers, movers):
    barrier = pltpu.get_barrier_semaphore()
    for peer in peers:
        pl.semaphore_signal(barrier, inc=1, device_id=peer, device_id_type=MESH)
    expected = len(peers)
    for source, target in movers:

        @pl.when(jnp.logical_not(same(source, me)))
        def _():
            pl.semaphore_signal(barrier, inc=1, device_id=source, device_id_type=MESH)

        expected = expected + jnp.where(same(target, me), 0, 1)
    pl.semaphore_wait(barrier, expected)


def move_start(me, source, target, target_device, send, receive):
    here = same(target_device, me)

    @pl.when(here)
    def _():
        pltpu.make_async_copy(source, target, receive).start()

    @pl.when(jnp.logical_not(here))
    def _():
        remote(source, target, (send, receive), target_device).start()


def move_sent(me, source, target, target_device, send, receive):
    @pl.when(jnp.logical_not(same(target_device, me)))
    def _():
        remote(source, target, (send, receive), target_device).wait_send()


def member(me, by):
    return (me[0] ^ (by // 2), me[1] ^ (by % 2))


def group_index(device):
    return 2 * device[0] + device[1] % 2


class GroupExchange:
    def __init__(self, me, pieces, got, sems):
        self.me, self.pieces, self.got, self.sems = me, pieces, got, sems

    def hop(self, by):
        peer = member(self.me, by)
        sems = (self.sems.at[0, by - 1], self.sems.at[1, by - 1])
        return remote(
            self.pieces.at[group_index(peer)], self.got.at[group_index(self.me)], sems, peer
        )

    def own(self):
        mine = group_index(self.me)
        return pltpu.make_async_copy(self.pieces.at[mine], self.got.at[mine], self.sems.at[0, 7])

    def start(self):
        for by in range(1, 8):
            self.hop(by).start()
        self.own().start()

    def finish(self):
        self.own().wait()
        for by in range(1, 8):
            self.hop(by).wait()


class GroupGather:
    def __init__(self, me, rows, sems, own, window):
        self.rows, self.sems, self.own, self.window = rows, sems, own, window
        self.core, self.across, self.beside = member(me, 2), member(me, 4), member(me, 1)

    def hop(self, index):
        across, beside, core = self.across, self.beside, self.core
        source, i, j, half, device = (
            (None, 0, 2, 0, across),
            (None, 1, 0, 1, beside),
            (None, 1, 0, 0, beside),
            (None, 0, 2, 1, across),
            ((0, 2), 1, 2, 0, beside),
            ((1, 0), 1, 2, 1, across),
            (None, 0, 1, slice(0, 2), core),
            ((0, 2), 0, 3, slice(0, 2), core),
            ((1, 0), 1, 1, slice(0, 2), core),
            ((1, 2), 1, 3, slice(0, 2), core),
        )[index]
        if source is None:
            source = self.own.at[half, self.window]
        else:
            source = self.rows.at[source[0], source[1], half, self.window]
        target = self.rows.at[i, j, half, self.window]
        return remote(source, target, (self.sems.at[0, index], self.sems.at[1, index]), device)

    def start(self):
        for index in (0, 1, 2, 3, 6):
            self.hop(index).start()

    def pass_on(self):
        self.hop(0).wait_recv()
        self.hop(4).start()
        self.hop(1).wait_recv()
        self.hop(5).start()
        self.hop(3).wait_recv()
        self.hop(7).start()
        self.hop(2).wait_recv()
        self.hop(8).start()

    def finish(self):
        self.hop(4).wait_recv()
        self.hop(5).wait_recv()
        self.hop(9).start()
        for index in (6, 7, 8, 9):
            self.hop(index).wait_recv()
        for index in range(10):
            self.hop(index).wait_send()


def first_kernel(shards, splits, tokens, cot, held, out_own, *refs):
    rows, cot_rows, in_all, out_all = refs[:4]
    move_send, move_recv, group_sems, own_sems, in_sems, line_sems, pair_sems = refs[4:]
    me = (lax.axis_index("dp"), lax.axis_index("ctx"))
    group, place = me
    slow = shards // 2
    slot, half = place // 2, place % 2
    line = [(group, place ^ (2 * by)) for by in range(1, slow)]
    pair = member(me, 1)
    movers = []
    for i in (0, 1):
        movers.append(
            (token_target(group, place, i, splits)[0], sequence_target(group, place, i, splits)[0])
        )
    greet(me, [member(me, by) for by in (1, 2, 4)] + line, movers)

    def move(array, second):
        device, part = sequence_target(group, place, second, splits)
        source = (tokens, cot)[array].at[second]
        target = (rows.at[0, 0], cot_rows)[array].at[part]
        return me, source, target, device, move_send.at[array, second], move_recv.at[array, part]

    def in_line(by):
        sems = (in_sems.at[0, by - 1], in_sems.at[1, by - 1])
        return remote(held, in_all.at[:, slot], sems, line[by - 1])

    def out_line(by):
        sems = (line_sems.at[0, by - 1], line_sems.at[1, by - 1])
        return remote(out_own, out_all.at[place], sems, line[by - 1])

    def out_pair(by):
        block = place ^ (2 * by)
        source = out_own if by == 0 else out_all.at[block]
        sems = (pair_sems.at[0, by], pair_sems.at[1, by])
        return remote(source, out_all.at[block], sems, pair)

    own_in = pltpu.make_async_copy(held, in_all.at[:, slot], own_sems.at[0])
    own_out = pltpu.make_async_copy(out_own, out_all.at[place], own_sems.at[1])
    for second in (0, 1):
        move_start(*move(0, second))
    for by in range(1, slow):
        in_line(by).start()
    own_in.start()
    for part in (0, 1):
        pltpu.make_async_copy(tokens.at[0], rows.at[0, 0, part], move_recv.at[0, part]).wait()
    spread = GroupGather(me, rows, group_sems, rows.at[0, 0], slice(0, tokens.shape[1]))
    spread.start()
    for by in range(1, slow):
        out_line(by).start()
    own_out.start()
    spread.pass_on()
    out_pair(0).start()
    for by in range(1, slow):
        in_line(by).wait_recv()
    for second in (0, 1):
        move_start(*move(1, second))
    for by in range(1, slow):
        out_line(by).wait_recv()
        out_pair(by).start()
    spread.finish()
    for part in (0, 1):
        pltpu.make_async_copy(cot.at[0], cot_rows.at[part], move_recv.at[1, part]).wait()
    own_in.wait()
    own_out.wait()
    for by in range(1, slow):
        in_line(by).wait_send()
        out_line(by).wait_send()
    for by in range(slow):
        out_pair(by).wait()
    for array in (0, 1):
        for second in (0, 1):
            move_sent(*move(array, second))


def first_exchange(tokens, cot, pieces, out_own, shards, splits, identity):
    low = jnp.bfloat16
    slow = shards // 2
    any_space = pl.BlockSpec(memory_space=pl.ANY)
    dma = pltpu.SemaphoreType.DMA
    rows, width = pieces.shape[2:]
    return pl.pallas_call(
        functools.partial(first_kernel, shards, splits),
        out_shape=(
            jax.ShapeDtypeStruct((2, 4) + tokens.shape, low),
            jax.ShapeDtypeStruct(cot.shape, low),
            jax.ShapeDtypeStruct((4, slow, 2, rows, width), low),
            jax.ShapeDtypeStruct((shards,) + out_own.shape, low),
        ),
        in_specs=[any_space] * 4,
        out_specs=(any_space,) * 4,
        scratch_shapes=[
            dma((2, 2)),
            dma((2, 2)),
            dma((2, 10)),
            dma((2,)),
            dma((2, slow - 1)),
            dma((2, slow - 1)),
            dma((2, slow)),
        ],
        compiler_params=pltpu.CompilerParams(
            collective_id=identity, has_side_effects=True, vmem_limit_bytes=8 << 20
        ),
        cost_estimate=pl.CostEstimate(flops=0, bytes_accessed=200 << 20, transcendentals=0),
    )(tokens, cot, pieces, out_own)


def last_kernel(shards, splits, in_parts, out_parts, made_one, made_two, gate_parts, *refs):
    in_total, out_total, one, two, gate_total = refs[:5]
    in_kept, in_arrived, in_done, out_kept, out_arrived, out_done = refs[5:11]
    move_send, move_recv, own_sems, in_sems, out_sems, piece_sems, home_sems, gate_sems = refs[11:]
    me = (lax.axis_index("dp"), lax.axis_index("ctx"))
    group, place = me
    slow = shards // 2
    slot, half = place // 2, place % 2
    line = [(group, place ^ (2 * by)) for by in range(1, slow)]
    movers = []
    for i in (0, 1):
        movers.append(
            (sequence_target(group, place, i, splits)[0], token_target(group, place, i, splits)[0])
        )
    home = (group, half * slow + slot)
    movers.append(((group, place % slow * 2 + place // slow), home))
    greet(me, [member(me, by) for by in range(1, 8)] + line, movers)

    def move(array, part):
        device, second = token_target(group, place, part, splits)
        source = (made_one, made_two)[array].at[part]
        target = (one, two)[array].at[second]
        return me, source, target, device, move_send.at[array, part], move_recv.at[array, second]

    def in_line(by):
        sems = (in_sems.at[0, by - 1], in_sems.at[1, by - 1])
        return remote(in_parts.at[slot ^ by], in_arrived.at[by - 1], sems, line[by - 1])

    def out_line(by):
        sems = (out_sems.at[0, by - 1], out_sems.at[1, by - 1])
        return remote(out_parts.at[slot ^ by], out_arrived.at[by - 1], sems, line[by - 1])

    in_swap = GroupExchange(me, in_done, in_total, piece_sems)
    gate_swap = GroupExchange(me, gate_parts, gate_total, gate_sems)
    own = [
        pltpu.make_async_copy(in_parts.at[slot], in_kept, own_sems.at[0]),
        pltpu.make_async_copy(out_parts.at[slot], out_kept, own_sems.at[1]),
    ]
    for by in range(1, slow):
        in_line(by).start()
    for by in range(1, slow):
        out_line(by).start()
    own[0].start()
    own[1].start()
    for array in (0, 1):
        for part in (0, 1):
            move_start(*move(array, part))
    gate_swap.start()
    own[0].wait()
    value = in_kept[...].astype(jnp.float32)
    for by in range(1, slow):
        in_line(by).wait_recv()
        value = value + in_arrived[by - 1].astype(jnp.float32)
    in_done[...] = value.astype(jnp.bfloat16)
    in_swap.start()
    own[1].wait()
    value = out_kept[...].astype(jnp.float32)
    for by in range(1, slow):
        out_line(by).wait_recv()
        value = value + out_arrived[by - 1].astype(jnp.float32)
    out_done[...] = value.astype(jnp.bfloat16)
    to_home = (me, out_done, out_total, home, home_sems.at[0], home_sems.at[1])
    move_start(*to_home)
    pltpu.make_async_copy(out_done, out_total, home_sems.at[1]).wait()
    move_sent(*to_home)
    in_swap.finish()
    gate_swap.finish()
    for by in range(1, slow):
        in_line(by).wait_send()
        out_line(by).wait_send()
    for array in (0, 1):
        for part in (0, 1):
            pltpu.make_async_copy(
                (made_one, made_two)[array].at[part],
                (one, two)[array].at[part],
                move_recv.at[array, part],
            ).wait()
    for array in (0, 1):
        for part in (0, 1):
            move_sent(*move(array, part))


def last_sums(in_parts, out_parts, made, gate_parts, shards, splits, identity):
    low = jnp.bfloat16
    slow = shards // 2
    any_space = pl.BlockSpec(memory_space=pl.ANY)
    dma = pltpu.SemaphoreType.DMA
    return pl.pallas_call(
        functools.partial(last_kernel, shards, splits),
        out_shape=(
            jax.ShapeDtypeStruct(in_parts.shape[1:], low),
            jax.ShapeDtypeStruct(out_parts.shape[1:], low),
            jax.ShapeDtypeStruct(made[0].shape, low),
            jax.ShapeDtypeStruct(made[1].shape, low),
            jax.ShapeDtypeStruct(gate_parts.shape, low),
        ),
        in_specs=[any_space] * 5,
        out_specs=(any_space,) * 5,
        scratch_shapes=[
            pltpu.VMEM(in_parts.shape[1:], low),
            pltpu.VMEM((slow - 1,) + in_parts.shape[1:], low),
            pltpu.VMEM(in_parts.shape[1:], low),
            pltpu.VMEM(out_parts.shape[1:], low),
            pltpu.VMEM((slow - 1,) + out_parts.shape[1:], low),
            pltpu.VMEM(out_parts.shape[1:], low),
            dma((2, 2)),
            dma((2, 2)),
            dma((2,)),
            dma((2, slow - 1)),
            dma((2, slow - 1)),
            dma((2, 8)),
            dma((2,)),
            dma((2, 8)),
        ],
        compiler_params=pltpu.CompilerParams(
            collective_id=identity, has_side_effects=True, vmem_limit_bytes=24 << 20
        ),
        cost_estimate=pl.CostEstimate(flops=0, bytes_accessed=150 << 20, transcendentals=0),
    )(in_parts, out_parts, *made, gate_parts)


class GroupScatter:
    def __init__(self, me, parts, buffers, sems, steps):
        self.parts = parts
        self.core_in, self.kept, self.sent, self.came, self.held = buffers[:5]
        self.sent_last, self.came_last = buffers[5:]
        self.core_sems, self.kept_sems, self.one_sems, self.last_sems = sems
        self.core, self.across, self.beside = member(me, 2), member(me, 4), member(me, 1)
        self.size = parts.shape[3] // steps
        self.steps = steps

    def window(self, k):
        return slice(k * self.size, (k + 1) * self.size)

    def to_core(self, k, j):
        return remote(
            self.parts.at[:, 2 * j + 1, :, self.window(k)],
            self.core_in.at[:, j, :, self.window(k)],
            (self.core_sems.at[0, k, j], self.core_sems.at[1, k, j]),
            self.core,
        )

    def keep(self, k, j):
        return pltpu.make_async_copy(
            self.parts.at[:, 2 * j, :, self.window(k)],
            self.kept.at[:, j, :, self.window(k)],
            self.kept_sems.at[k, j],
        )

    def first(self, k, half):
        return remote(
            self.sent.at[half, :, self.window(k)],
            self.came.at[half, :, self.window(k)],
            (self.one_sems.at[0, k, half], self.one_sems.at[1, k, half]),
            (self.beside, self.across)[half],
        )

    def second(self, k, half):
        return remote(
            self.sent_last.at[half, self.window(k)],
            self.came_last.at[half, self.window(k)],
            (self.last_sems.at[0, k, half], self.last_sems.at[1, k, half]),
            (self.across, self.beside)[half],
        )

    def start(self):
        for k in range(self.steps):
            for j in (0, 1):
                self.to_core(k, j).start()
                self.keep(k, j).start()

    def send_first(self, k):
        wide = jnp.float32
        rows = self.window(k)
        for j in (0, 1):
            self.keep(k, j).wait()
            self.to_core(k, j).wait_recv()
        for half in (0, 1):
            for other in (0, 1):
                at = (1, other) if half == 0 else (other, 1)
                both = self.kept[at[0], at[1], half, rows].astype(wide)
                both = both + self.core_in[at[0], at[1], half, rows].astype(wide)
                self.sent[half, other, rows] = both.astype(jnp.bfloat16)
            self.first(k, half).start()
        for half in (0, 1):
            for other in (0, 1):
                at = (0, other) if half == 0 else (other, 0)
                both = self.kept[at[0], at[1], half, rows].astype(wide)
                self.held[half, other, rows] = both + self.core_in[at[0], at[1], half, rows].astype(
                    wide
                )

    def send_second(self, k):
        wide = jnp.float32
        rows = self.window(k)
        for half in (0, 1):
            self.first(k, half).wait_recv()
            both = self.held[half, 1, rows] + self.came[half, 1, rows].astype(wide)
            self.sent_last[half, rows] = both.astype(jnp.bfloat16)
            self.second(k, half).start()
            self.held[half, 0, rows] = self.held[half, 0, rows] + self.came[half, 0, rows].astype(
                wide
            )

    def total(self, k, half):
        self.second(k, half).wait_recv()
        rows = self.window(k)
        return self.held[half, 0, rows] + self.came_last[half, rows].astype(jnp.float32)

    def finish(self):
        for k in range(self.steps):
            for j in (0, 1):
                self.to_core(k, j).wait_send()
            for half in (0, 1):
                self.first(k, half).wait_send()
                self.second(k, half).wait_send()


def scatter_scratch(rows, width, steps):
    low, wide = jnp.bfloat16, jnp.float32
    dma = pltpu.SemaphoreType.DMA
    return [
        pltpu.VMEM((2, 2, 2, rows, width), low),
        pltpu.VMEM((2, 2, 2, rows, width), low),
        pltpu.VMEM((2, 2, rows, width), low),
        pltpu.VMEM((2, 2, rows, width), low),
        pltpu.VMEM((2, 2, rows, width), wide),
        pltpu.VMEM((2, rows, width), low),
        pltpu.VMEM((2, rows, width), low),
        dma((2, steps, 2)),
        dma((steps, 2)),
        dma((2, steps, 2)),
        dma((2, steps, 2)),
    ]


def reordered(rows, slow, back):
    each = rows.shape[1] // (4 * slow)
    if back:
        starts = [s * 4 + dp for dp in range(4) for s in range(slow)]
    else:
        starts = [dp * slow + s for s in range(slow) for dp in range(4)]
    return jnp.concatenate([rows[:, i * each : (i + 1) * each] for i in starts], 1)


def turn_kernel(slow, steps, backward, parts, gain, *refs):
    if backward:
        residual, cot, result, gain_grad, rows = refs[:5]
        scratch = refs[5:]
    else:
        tokens, result, rows = refs[:3]
        scratch = refs[3:]
    own, own_sems, group_sems = scratch[:3]
    me = (lax.axis_index("dp"), lax.axis_index("ctx"))
    greet(me, [member(me, by) for by in (1, 2, 4)], [])
    scatter = GroupScatter(me, parts, scratch[3:10], scratch[10:], steps)
    gathers = [GroupGather(me, rows, group_sems.at[k], own, scatter.window(k)) for k in range(steps)]
    scatter.start()
    for k in range(steps):
        scatter.send_first(k)
    for k in range(steps):
        scatter.send_second(k)
    for k in range(steps):
        span = scatter.window(k)
        for half in (0, 1):
            total = scatter.total(k, half)
            if backward:
                values = residual[half, span]
                factor = lax.rsqrt(jnp.mean(values * values, -1, keepdims=True) + norm_eps)
                normed = values * factor
                total = reordered(total, slow, True)
                part = jnp.sum(total * normed, 0, keepdims=True)
                if k == 0 and half == 0:
                    gain_grad[...] = part
                else:
                    gain_grad[...] += part
                back = total * gain[...]
                back = factor * (back - normed * jnp.mean(back * normed, -1, keepdims=True))
                back = cot[half, span].astype(jnp.float32) + back
                result[half, span] = back
                own[half, span] = back.astype(jnp.bfloat16)
            else:
                values = tokens[half, span].astype(jnp.float32) + total
                factor = lax.rsqrt(jnp.mean(values * values, -1, keepdims=True) + norm_eps)
                result[half, span] = values
                own[half, span] = reordered(values * factor * gain[...], slow, False).astype(
                    jnp.bfloat16
                )
        gathers[k].start()
        keep = pltpu.make_async_copy(own.at[:, span], rows.at[0, 0, :, span], own_sems.at[k])
        keep.start()
    for k in range(steps):
        gathers[k].pass_on()
    for k in range(steps):
        gathers[k].finish()
        span = scatter.window(k)
        pltpu.make_async_copy(own.at[:, span], rows.at[0, 0, :, span], own_sems.at[k]).wait()
    scatter.finish()


def turn(parts, gain, rows_in, slow, backward, identity):
    low, wide = jnp.bfloat16, jnp.float32
    dma = pltpu.SemaphoreType.DMA
    rows, width = parts.shape[3:]
    steps = 2
    any_space = pl.BlockSpec(memory_space=pl.ANY)
    vmem = pl.BlockSpec(memory_space=pltpu.VMEM)
    shapes = [jax.ShapeDtypeStruct((2, rows, width), wide)]
    if backward:
        shapes.append(jax.ShapeDtypeStruct((1, width), wide))
    return pl.pallas_call(
        functools.partial(turn_kernel, slow, steps, backward),
        out_shape=tuple(shapes) + (jax.ShapeDtypeStruct((2, 4, 2, rows, width), low),),
        in_specs=[any_space, vmem] + [vmem] * len(rows_in),
        out_specs=tuple([vmem] * len(shapes) + [any_space]),
        scratch_shapes=[pltpu.VMEM((2, rows, width), low), dma((steps,)), dma((steps, 2, 10))]
        + scatter_scratch(rows, width, steps),
        compiler_params=pltpu.CompilerParams(
            collective_id=identity, has_side_effects=True, vmem_limit_bytes=48 << 20
        ),
        cost_estimate=pl.CostEstimate(flops=0, bytes_accessed=250 << 20, transcendentals=0),
    )(parts, gain, *rows_in)


def swap_kernel(count, *refs):
    me = (lax.axis_index("dp"), lax.axis_index("ctx"))
    greet(me, [member(me, by) for by in range(1, 8)], [])
    swaps = [
        GroupExchange(me, refs[i], refs[count + i], refs[2 * count + i]) for i in range(count)
    ]
    for swap in swaps:
        swap.start()
    for swap in swaps:
        swap.finish()


def swap_group(arrays, identity):
    any_space = pl.BlockSpec(memory_space=pl.ANY)
    return pl.pallas_call(
        functools.partial(swap_kernel, len(arrays)),
        out_shape=tuple(jax.ShapeDtypeStruct(a.shape, a.dtype) for a in arrays),
        in_specs=[any_space] * len(arrays),
        out_specs=(any_space,) * len(arrays),
        scratch_shapes=[pltpu.SemaphoreType.DMA((2, 8)) for _ in arrays],
        compiler_params=pltpu.CompilerParams(
            collective_id=identity, has_side_effects=True, vmem_limit_bytes=4 << 20
        ),
        cost_estimate=pl.CostEstimate(flops=0, bytes_accessed=60 << 20, transcendentals=0),
    )(*arrays)


def position_tables(length):
    cosine, sine_table = rotary_tables(jnp.arange(length, dtype=jnp.int32), HEAD)
    sign = jnp.where(jnp.arange(HEAD) < HEAD // 2, -1.0, 1.0)
    return jnp.tile(cosine, (1, 2)), jnp.tile(sine_table * sign, (1, 2))


def attend(order, qkv, tables, q_heads, kv_heads):
    seqs, length, cols = qkv.shape
    whole = pl.BlockSpec(memory_space=pltpu.VMEM)
    return pl.pallas_call(
        functools.partial(attend_kernel, q_heads, kv_heads, 256),
        out_shape=(
            jax.ShapeDtypeStruct((seqs, length, q_heads * HEAD), jnp.bfloat16),
            jax.ShapeDtypeStruct((seqs, q_heads, length), jnp.float32),
            jax.ShapeDtypeStruct((seqs, length, cols), jnp.bfloat16),
        ),
        in_specs=[pl.BlockSpec(memory_space=pltpu.SMEM), whole, whole, whole],
        out_specs=(whole, whole, whole),
        scratch_shapes=[pltpu.VMEM((length, q_heads * HEAD), jnp.bfloat16)],
        compiler_params=pltpu.CompilerParams(vmem_limit_bytes=40 << 20),
        cost_estimate=pl.CostEstimate(
            flops=2 * seqs * length * length * q_heads * HEAD,
            bytes_accessed=8 * seqs * length * cols,
            transcendentals=seqs * length * length * q_heads // 2,
        ),
    )(order, qkv, *tables)


def attend_back(order, kept, back, lse, tables, q_heads, kv_heads):
    seqs, length, cols = kept.shape
    group = q_heads // kv_heads
    whole = pl.BlockSpec(memory_space=pltpu.VMEM)
    return pl.pallas_call(
        functools.partial(attend_back_kernel, q_heads, kv_heads, 256),
        out_shape=jax.ShapeDtypeStruct((seqs, length, cols), jnp.bfloat16),
        in_specs=[pl.BlockSpec(memory_space=pltpu.SMEM)] + [whole] * 5,
        out_specs=whole,
        scratch_shapes=[
            pltpu.VMEM((length, q_heads * HEAD), jnp.bfloat16),
            pltpu.VMEM((length, cols), jnp.float32),
            pltpu.VMEM((group, length), jnp.float32),
            pltpu.VMEM((group * HEAD, length), jnp.float32),
        ],
        compiler_params=pltpu.CompilerParams(vmem_limit_bytes=40 << 20),
        cost_estimate=pl.CostEstimate(
            flops=7 * seqs * length * length * q_heads * HEAD,
            bytes_accessed=6 * seqs * length * cols,
            transcendentals=seqs * length * length * q_heads // 2,
        ),
    )(order, kept, back, lse, *tables)


def local(
    tokens,
    cotangent,
    block_order,
    attention_in,
    attention_out,
    gate_up,
    down_matrix,
    gains,
    mean_attention_in,
    mean_attention_out,
    mean_gate_up,
    mean_down,
    mean_gains,
    square_attention_in,
    square_attention_out,
    square_gate_up,
    square_down,
    square_gains,
):
    seq_count, shard_rows, width = tokens.shape
    shards = lax.axis_size("ctx")
    slow = shards // 2
    mine = lax.axis_index("dp")
    beside = lax.axis_index("ctx") % 2
    low = jnp.bfloat16
    owned = attention_in.shape[0]
    hidden_units = gate_up.shape[1] // 2
    part_hidden = hidden_units // 8
    units = down_matrix.shape[0]
    part_q = HEADS * HEAD // 8
    part_k = KV_HEADS * HEAD // 8
    part_cols = part_q + 2 * part_k
    count = seq_count * shard_rows
    together = 8 * count
    spread = shards // (4 * seq_count)
    splits = max(1, slow // 8)
    seqs = 2 // spread if spread < 2 else 1
    length = shards * shard_rows
    q_heads = HEADS // 8 // splits
    kv_heads = KV_HEADS // 8

    in_low = attention_in.astype(low)
    gains_row = jnp.pad(gains.astype(low).reshape(1, -1), ((0, 15), (0, part_cols - 2 * owned)))
    pieces = jnp.stack(
        [
            jnp.concatenate(
                [
                    jnp.concatenate(
                        [
                            in_low[:, i * part_q : (i + 1) * part_q],
                            in_low[:, 8 * part_q + i * part_k :][:, :part_k],
                            in_low[:, 8 * (part_q + part_k) + i * part_k :][:, :part_k],
                        ],
                        1,
                    ),
                    gains_row,
                ]
            )
            for i in range(8)
        ]
    )
    gate_low = gate_up.astype(low)
    gate_pieces = jnp.stack(
        [
            jnp.concatenate(
                [
                    gate_low[:, side * hidden_units + (dp * shards + 2 * s + half) * units :][
                        :, :units
                    ]
                    for side in range(2)
                    for s in range(slow)
                ],
                1,
            )
            for dp in range(4)
            for half in range(2)
        ]
    )
    gate_rows, pieces = swap_group([gate_pieces, pieces], 1)
    tokens_all, cot_own, in_all, out_all = first_exchange(
        tokens,
        cotangent,
        pieces.reshape(4, 2, owned + 16, part_cols),
        attention_out.astype(low),
        shards,
        spread,
        2,
    )
    w_in = in_all[:, :, :, :owned].reshape(width, part_cols)
    w_out = lax.dynamic_slice_in_dim(out_all.reshape(-1, width), beside * part_q, part_q, 0)
    gains_all = in_all[:, :, :, owned, : 2 * owned].reshape(-1, 2, owned)
    gains_all = gains_all.astype(jnp.float32).swapaxes(0, 1).reshape(2, width)
    gain_one, gain_two = gains_all[0], gains_all[1]
    x_low = tokens_all[0, 0].reshape(count, width)
    cot_own = cot_own.reshape(count, width)
    back_all = gather_group(cot_own).reshape(together, width)
    w_gate = gather_line(gate_rows.reshape(8 * owned, 2 * part_hidden))
    w_down = gather_line((down_matrix + 0.0 * w_gate[0, 0].astype(jnp.float32)).astype(low))

    normed_all, _ = norm_parts(tokens_all.reshape(together, width).astype(jnp.float32))
    input_one = (normed_all * gain_one).astype(low)
    qkv = dot_nn(input_one, w_in)
    orders = block_order.reshape(2 * splits if spread > 1 else 1, 4, -1)
    slot_order = jnp.concatenate(
        [
            orders[(2 * s + (beside ^ i)) if spread > 1 else 0, part_owner(mine ^ j)]
            for s in range(splits)
            for i in range(2 // seqs)
            for j in range(4)
        ]
    )
    tables = position_tables(length)
    groups = [
        [2 * (s * splits + g) + half for g in range(splits)]
        for s in range(slow // splits)
        for half in (0, 1)
    ]

    def split_heads(values, widths, copies):
        parts = []
        start = 0
        for each, repeat in zip(widths, copies):
            kinds = splits // repeat
            piece = values[:, start : start + kinds * each].reshape(-1, kinds, each)
            parts.append(jnp.repeat(piece.swapaxes(0, 1), repeat, axis=0))
            start += kinds * each
        sent = jnp.concatenate(parts, 2)
        got = lax.all_to_all(sent, "ctx", 0, 0, axis_index_groups=groups, tiled=True)
        return got.reshape(length, -1)

    def join_heads(values):
        sent = values.reshape(splits, together, -1)
        return lax.all_to_all(sent, "ctx", 0, 0, axis_index_groups=groups, tiled=True)

    q_width, k_width = q_heads * HEAD, kv_heads * HEAD
    if splits > 1:
        qkv = split_heads(qkv, (q_width, k_width, k_width), (1, splits, splits))
    qkv = qkv.reshape(seqs, length, -1)
    attended, lse, kept = attend(slot_order, qkv, tables, q_heads, kv_heads)
    if splits > 1:
        attended = join_heads(attended).swapaxes(0, 1)
    attended = attended.reshape(together, part_q)

    def grouped(values):
        return scatter_group(values.reshape(2, 4, count, width))

    flat_rows = x_low.astype(jnp.float32)
    normed_one, factor_one = norm_parts(flat_rows)

    def parts(values):
        return values.astype(low).reshape((2, 4) + tokens.shape)

    residual_rows, input_two = turn(
        parts(dot_nn(attended, w_out)), gain_two[None], [tokens_all[0, 0]], slow, False, 3
    )
    residual = residual_rows.reshape(count, width)
    input_two = input_two.reshape(together, width)
    gate_both = dot_nn(input_two, w_gate)
    gate_part = gate_both[:, :part_hidden]
    up_part = gate_both[:, part_hidden:]
    sigmoid_gate = jax.nn.sigmoid(gate_part)
    active = gate_part * sigmoid_gate
    hidden = (active * up_part).astype(low)
    output_rows = residual + grouped(dot_nn(hidden, w_down))
    output_rows = output_rows.astype(low).reshape(seq_count, shard_rows, width)
    back_hidden = dot_nt(back_all, w_down)
    back_gate = back_hidden * up_part * sigmoid_gate * (1.0 + gate_part * (1.0 - sigmoid_gate))
    back_upper = back_hidden * active
    back_gate_up = jnp.concatenate([back_gate, back_upper], 1).astype(low)
    gate_low = sum_line(dot_tn(input_two, back_gate_up).astype(low))
    grad_down = dot_tn(hidden, back_all) + 0.0 * gate_low[0, 0].astype(jnp.float32)
    down_sum = sum_line(grad_down.astype(low)).astype(jnp.float32)
    back_rows, grad_gain_two, back_residual_all = turn(
        parts(dot_nt(back_gate_up, w_gate)),
        gain_two[None],
        [residual_rows, cot_own.reshape(tokens.shape)],
        slow,
        True,
        4,
    )
    back_residual = back_rows.reshape(count, width)
    back_residual_all = back_residual_all.reshape(together, width)
    grad_out = dot_tn(attended, back_residual_all).astype(low)
    back_attended = dot_nt(back_residual_all, w_out).astype(low)
    if splits > 1:
        back_attended = split_heads(back_attended, (q_width,), (1,))
    back_projected = attend_back(
        slot_order, kept, back_attended.reshape(seqs, length, -1), lse, tables, q_heads, kv_heads
    )
    if splits > 1:
        back_projected = join_heads(back_projected).astype(jnp.float32)
        back_projected = jnp.concatenate(
            [
                back_projected[..., :q_width].swapaxes(0, 1).reshape(together, part_q),
                back_projected[..., q_width:].sum(0),
            ],
            1,
        ).astype(low)
    back_projected = back_projected.reshape(together, part_cols)
    back_input_one = grouped(dot_nt(back_projected, w_in))
    grad_gain_one = jnp.sum(back_input_one * normed_one, 0)
    tokens_grad = back_residual + norm_back(back_input_one * gain_one, normed_one, factor_one)
    tokens_grad = tokens_grad.astype(low).reshape(seq_count, shard_rows, width)
    grad_gains = jnp.stack([grad_gain_one, grad_gain_two[0]]).reshape(2, 4, slow, 2, owned)
    gains_rows = grad_gains.transpose(2, 1, 3, 0, 4).reshape(slow, 8, 1, 2 * owned).astype(low)
    gains_rows = jnp.pad(gains_rows, ((0, 0), (0, 0), (0, 15), (0, part_cols - 2 * owned)))
    grad_in = dot_tn(input_one, back_projected).astype(low)
    grad_in = grad_in.reshape(4, slow, 2 * owned, part_cols).swapaxes(0, 1)
    grad_in = grad_in.reshape(slow, 8, owned, part_cols)
    in_sum, out_sum, block_out, tokens_grad, gate_sum = last_sums(
        jnp.concatenate([grad_in, gains_rows], 2),
        grad_out.reshape(slow, owned, width),
        [output_rows, tokens_grad],
        gate_low.reshape(8, owned, 2 * part_hidden),
        shards,
        spread,
        5,
    )
    gate_sum = jnp.concatenate(
        [
            gate_sum[2 * dp + half, :, (side * slow + s) * units :][:, :units]
            for side in range(2)
            for dp in range(4)
            for s in range(slow)
            for half in range(2)
        ],
        1,
    ).astype(jnp.float32)
    tokens_grad = tokens_grad.astype(jnp.float32)
    out_sum = out_sum.astype(jnp.float32)
    gains_sum = in_sum[:, owned, : 2 * owned].reshape(8, 2, owned).astype(jnp.float32).sum(0)
    cuts = ((0, part_q), (part_q, part_q + part_k), (part_q + part_k, part_cols))
    in_sum = jnp.concatenate(
        [in_sum[i, :owned, first:last] for first, last in cuts for i in range(8)], 1
    ).astype(jnp.float32)
    new_in = adam_update(
        attention_in,
        in_sum,
        mean_attention_in,
        square_attention_in,
        input_boost * D ** (-0.5),
        weight_decay,
    )
    new_out = adam_update(
        attention_out,
        out_sum,
        mean_attention_out,
        square_attention_out,
        (HEADS * HEAD // 32) ** (-0.5),
        weight_decay,
    )
    new_gate = adam_update(
        gate_up, gate_sum, mean_gate_up, square_gate_up, D ** (-0.5), weight_decay
    )
    new_down = adam_update(
        down_matrix, down_sum, mean_down, square_down, FF ** (-0.5), weight_decay
    )
    new_gain = adam_update(gains, gains_sum, mean_gains, square_gains, gain_rate, 0.0)
    return (
        block_out,
        tokens_grad,
        new_in[0],
        new_in[1],
        new_in[2],
        new_out[0],
        new_out[1],
        new_out[2],
        new_gate[0],
        new_gate[1],
        new_gate[2],
        new_down[0],
        new_down[1],
        new_down[2],
        new_gain[0],
        new_gain[1],
        new_gain[2],
    )


def solution(mesh):
    in_specs = (
        P("dp", "ctx", None),
        P("dp", "ctx", None),
        P(),
        P(("dp", "ctx"), None),
        P(("dp", "ctx"), None),
        P(("dp", "ctx"), None),
        P(("dp", "ctx"), None),
        P(None, ("dp", "ctx")),
        P(("dp", "ctx"), None),
        P(("dp", "ctx"), None),
        P(("dp", "ctx"), None),
        P(("dp", "ctx"), None),
        P(None, ("dp", "ctx")),
        P(("dp", "ctx"), None),
        P(("dp", "ctx"), None),
        P(("dp", "ctx"), None),
        P(("dp", "ctx"), None),
        P(None, ("dp", "ctx")),
    )
    out_specs = (
        P("dp", "ctx", None),
        P("dp", "ctx", None),
        P(("dp", "ctx"), None),
        P(("dp", "ctx"), None),
        P(("dp", "ctx"), None),
        P(("dp", "ctx"), None),
        P(("dp", "ctx"), None),
        P(("dp", "ctx"), None),
        P(("dp", "ctx"), None),
        P(("dp", "ctx"), None),
        P(("dp", "ctx"), None),
        P(("dp", "ctx"), None),
        P(("dp", "ctx"), None),
        P(("dp", "ctx"), None),
        P(None, ("dp", "ctx")),
        P(None, ("dp", "ctx")),
        P(None, ("dp", "ctx")),
    )
    return jax.shard_map(local, mesh=mesh, in_specs=in_specs, out_specs=out_specs, check_vma=False)
```

```python
import functools

import jax
import jax.numpy as jnp
from jax import lax
from jax.experimental import pallas as pl
from jax.experimental.pallas import tpu as pltpu
from jax.sharding import PartitionSpec as P

D = 2048
HEADS = 32
KV_HEADS = 8
HEAD = 64
FF = 8192
STEP = 5


norm_eps = 1e-05
rope_base = 500000.0
beta_one = 0.9
beta_two = 0.95
gain_rate = 1.25
input_boost = 2.5
weight_decay = 0.1
adam_eps = 1e-08
masked_score = -1e30


def rotary_tables(positions, head_width):
    half_width = head_width // 2
    frequency = rope_base ** (-(jnp.arange(half_width, dtype=jnp.float32) * 2.0 / head_width))
    angles = positions.astype(jnp.float32)[:, None] * frequency[None, :]
    angles = jnp.concatenate([angles, angles], 1)
    return (jnp.cos(angles), jnp.sin(angles))


def norm_parts(values):
    factor = lax.rsqrt(jnp.mean(values * values, -1, keepdims=True) + norm_eps)
    return (values * factor, factor)


def norm_back(back_normed, normed, factor):
    return factor * (back_normed - normed * jnp.mean(back_normed * normed, -1, keepdims=True))


def adam_update(weight, gradient, first_moment, second_moment, step_rate, decay_rate):
    first_new = beta_one * first_moment + (1.0 - beta_one) * gradient
    second_new = beta_two * second_moment + (1.0 - beta_two) * gradient * gradient
    update = (
        first_new
        / (1.0 - beta_one**STEP)
        / (jnp.sqrt(second_new / (1.0 - beta_two**STEP)) + adam_eps)
    )
    return (first_new, second_new, weight - step_rate * (update + decay_rate * weight))


def line_groups(shards):
    return [[2 * s + half for s in range(shards // 2)] for half in (0, 1)]


def gather_line(rows):
    return lax.all_gather(
        rows, "ctx", axis=0, tiled=True, axis_index_groups=line_groups(lax.axis_size("ctx"))
    )


def sum_line(gradient):
    return lax.psum_scatter(
        gradient,
        "ctx",
        scatter_dimension=0,
        tiled=True,
        axis_index_groups=line_groups(lax.axis_size("ctx")),
    )


def dot_nn(a, b):
    return lax.dot_general(a, b, (((1,), (0,)), ((), ())), preferred_element_type=jnp.float32)


def dot_nt(a, b):
    return lax.dot_general(a, b, (((1,), (1,)), ((), ())), preferred_element_type=jnp.float32)


def dot_tn(a, b):
    return lax.dot_general(a, b, (((0,), (0,)), ((), ())), preferred_element_type=jnp.float32)


def causal_keep(tile):
    keys = lax.broadcasted_iota(jnp.int32, (tile, tile), 0)
    queries = lax.broadcasted_iota(jnp.int32, (tile, tile), 1)
    return keys <= queries


def turn_group(values, cos, sin, forward):
    lanes = lax.broadcasted_iota(jnp.int32, values.shape, 1)
    other = jnp.where(
        lanes % HEAD < HEAD // 2,
        pltpu.roll(values, 2 * HEAD - HEAD // 2, 1),
        pltpu.roll(values, HEAD // 2, 1),
    )
    if forward:
        return values * cos + other * sin
    return values * cos - other * sin


def turn_columns(values, start, turned_cols, cos, sin, forward):
    if start >= turned_cols:
        return values
    turned = turn_group(values, cos, sin, forward)
    if start + 2 * HEAD <= turned_cols:
        return turned
    lanes = lax.broadcasted_iota(jnp.int32, values.shape, 1)
    return jnp.where(lanes < turned_cols - start, turned, values)


def attend_kernel(
    q_heads,
    kv_heads,
    tile,
    order_ref,
    all_qkv_ref,
    cos_ref,
    sin_ref,
    all_out_ref,
    all_lse_ref,
    all_kept_ref,
    made,
):
    for sequence in range(all_qkv_ref.shape[0]):
        attend_sequence(
            q_heads,
            kv_heads,
            tile,
            order_ref,
            all_qkv_ref.at[sequence],
            cos_ref,
            sin_ref,
            all_out_ref.at[sequence],
            all_lse_ref.at[sequence],
            all_kept_ref.at[sequence],
            made,
        )


def attend_sequence(
    q_heads, kv_heads, tile, order_ref, qkv_ref, cos_ref, sin_ref, out_ref, lse_ref, kept_ref, made
):
    length, cols = qkv_ref.shape
    blocks = order_ref.shape[0]
    rows = length // blocks
    group = q_heads // kv_heads
    q_cols, k_cols = q_heads * HEAD, kv_heads * HEAD
    scale = HEAD ** (-0.5)

    def take_block(i, _):
        start = pl.multiple_of(order_ref[i] * rows, rows)
        source = pl.multiple_of(i * rows, rows)
        cos = cos_ref[pl.ds(start, rows), :]
        sin = sin_ref[pl.ds(start, rows), :]
        for c in range(0, cols, 2 * HEAD):
            values = qkv_ref[pl.ds(source, rows), c : c + 2 * HEAD]
            values = turn_columns(values, c, q_cols + k_cols, cos, sin, True)
            kept_ref[pl.ds(start, rows), c : c + 2 * HEAD] = values.astype(jnp.bfloat16)
        return 0

    lax.fori_loop(0, blocks, take_block, 0)
    keep = causal_keep(tile)
    for kv in range(kv_heads):
        k_at = q_cols + kv * HEAD
        v_at = q_cols + k_cols + kv * HEAD

        def query_step(i, _):
            q_start = pl.multiple_of(i * tile, tile)
            queries = [
                kept_ref[
                    pl.ds(q_start, tile), (kv * group + g) * HEAD : (kv * group + g + 1) * HEAD
                ]
                for g in range(group)
            ]

            def key_tile(j, carry, masked):
                k_start = pl.multiple_of(j * tile, tile)
                keys = kept_ref[pl.ds(k_start, tile), k_at : k_at + HEAD]
                values = kept_ref[pl.ds(k_start, tile), v_at : v_at + HEAD]
                result = []
                for g in range(group):
                    peak, total, weighted = carry[g]
                    scores = dot_nt(keys, queries[g]) * scale
                    if masked:
                        scores = jnp.where(keep, scores, masked_score)
                    new_peak = jnp.maximum(peak, jnp.max(scores, 0, keepdims=True))
                    weights = jnp.exp(scores - new_peak)
                    shrink = jnp.exp(peak - new_peak)
                    total = total * shrink + jnp.sum(weights, 0, keepdims=True)
                    weighted = weighted * shrink + dot_tn(values, weights.astype(jnp.bfloat16))
                    result.append((new_peak, total, weighted))
                return tuple(result)

            start = tuple(
                (
                    jnp.full((1, tile), masked_score, jnp.float32),
                    jnp.zeros((1, tile), jnp.float32),
                    jnp.zeros((HEAD, tile), jnp.float32),
                )
                for _ in range(group)
            )
            carry = lax.fori_loop(0, i, lambda j, c: key_tile(j, c, False), start)
            carry = key_tile(i, carry, True)
            for g in range(group):
                head = kv * group + g
                peak, total, weighted = carry[g]
                lse_ref[head : head + 1, pl.ds(q_start, tile)] = peak + jnp.log(total)
                made[pl.ds(q_start, tile), head * HEAD : (head + 1) * HEAD] = (
                    (weighted / total).T.astype(jnp.bfloat16)
                )
            return 0

        lax.fori_loop(0, length // tile, query_step, 0)

    def give_block(i, _):
        start = pl.multiple_of(order_ref[i] * rows, rows)
        target = pl.multiple_of(i * rows, rows)
        out_ref[pl.ds(target, rows), :] = made[pl.ds(start, rows), :]
        return 0

    lax.fori_loop(0, blocks, give_block, 0)


def attend_back_kernel(
    q_heads,
    kv_heads,
    tile,
    order_ref,
    all_kept_ref,
    all_back_ref,
    all_lse_ref,
    cos_ref,
    sin_ref,
    all_out_ref,
    *scratch,
):
    for sequence in range(all_kept_ref.shape[0]):
        attend_back_sequence(
            q_heads,
            kv_heads,
            tile,
            order_ref,
            all_kept_ref.at[sequence],
            all_back_ref.at[sequence],
            all_lse_ref.at[sequence],
            cos_ref,
            sin_ref,
            all_out_ref.at[sequence],
            *scratch,
        )


def attend_back_sequence(
    q_heads,
    kv_heads,
    tile,
    order_ref,
    kept_ref,
    back_ref,
    lse_ref,
    cos_ref,
    sin_ref,
    out_ref,
    back_sorted,
    grad,
    delta_ref,
    dq_ref,
):
    length, cols = kept_ref.shape
    blocks = order_ref.shape[0]
    rows = length // blocks
    group = q_heads // kv_heads
    q_cols, k_cols = q_heads * HEAD, kv_heads * HEAD
    scale = HEAD ** (-0.5)
    tiles = length // tile

    def take_block(i, _):
        start = pl.multiple_of(order_ref[i] * rows, rows)
        source = pl.multiple_of(i * rows, rows)
        back_sorted[pl.ds(start, rows), :] = back_ref[pl.ds(source, rows), :]
        return 0

    lax.fori_loop(0, blocks, take_block, 0)
    keep = causal_keep(tile)
    for kv in range(kv_heads):
        k_at = q_cols + kv * HEAD
        v_at = q_cols + k_cols + kv * HEAD

        def load(i, g):
            start = pl.multiple_of(i * tile, tile)
            head = kv * group + g
            at = slice(head * HEAD, (head + 1) * HEAD)
            return (
                kept_ref[pl.ds(start, tile), at],
                back_sorted[pl.ds(start, tile), at],
                lse_ref[head : head + 1, pl.ds(start, tile)],
            )

        def load_kv(j):
            start = pl.multiple_of(j * tile, tile)
            return (
                kept_ref[pl.ds(start, tile), k_at : k_at + HEAD],
                kept_ref[pl.ds(start, tile), v_at : v_at + HEAD],
            )

        def tile_terms(keys, values, query, back, lse, masked):
            weights = jnp.exp(dot_nt(keys, query) * scale - lse)
            if masked:
                weights = jnp.where(keep, weights, 0.0)
            return weights, dot_nt(values, back)

        def delta_step(i, _):
            rows_i = [load(i, g) for g in range(group)]

            def one(j, carry, masked):
                keys, values = load_kv(j)
                result = []
                for g in range(group):
                    weights, back_weights = tile_terms(keys, values, *rows_i[g], masked)
                    result.append(carry[g] + jnp.sum(weights * back_weights, 0, keepdims=True))
                return tuple(result)

            carry = tuple(jnp.zeros((1, tile), jnp.float32) for _ in range(group))
            carry = lax.fori_loop(0, i, lambda j, c: one(j, c, False), carry)
            carry = one(i, carry, True)
            for g in range(group):
                delta_ref[g : g + 1, pl.ds(pl.multiple_of(i * tile, tile), tile)] = carry[g]
            return 0

        lax.fori_loop(0, tiles, delta_step, 0)
        dq_ref[...] = jnp.zeros_like(dq_ref)

        def key_step(j, _):
            keys, values = load_kv(j)

            def one(i, carry, masked):
                back_key, back_value = carry
                start = pl.multiple_of(i * tile, tile)
                for g in range(group):
                    query, back, lse = load(i, g)
                    weights, back_weights = tile_terms(keys, values, query, back, lse, masked)
                    delta = delta_ref[g : g + 1, pl.ds(start, tile)]
                    back_scores = (weights * (back_weights - delta)).astype(jnp.bfloat16)
                    back_key = back_key + dot_nn(back_scores, query)
                    back_value = back_value + dot_nn(weights.astype(jnp.bfloat16), back)
                    dq_ref[g * HEAD : (g + 1) * HEAD, pl.ds(start, tile)] += dot_tn(
                        keys, back_scores
                    )
                return back_key, back_value

            zero = jnp.zeros((tile, HEAD), jnp.float32)
            carry = one(j, (zero, zero), True)
            carry = lax.fori_loop(j + 1, tiles, lambda i, c: one(i, c, False), carry)
            start = pl.multiple_of(j * tile, tile)
            grad[pl.ds(start, tile), k_at : k_at + HEAD] = carry[0] * scale
            grad[pl.ds(start, tile), v_at : v_at + HEAD] = carry[1]
            return 0

        lax.fori_loop(0, tiles, key_step, 0)
        for g in range(group):
            head = kv * group + g
            grad[:, head * HEAD : (head + 1) * HEAD] = (
                dq_ref[g * HEAD : (g + 1) * HEAD, :] * scale
            ).T

    def give_block(i, _):
        start = pl.multiple_of(order_ref[i] * rows, rows)
        target = pl.multiple_of(i * rows, rows)
        cos = cos_ref[pl.ds(start, rows), :]
        sin = sin_ref[pl.ds(start, rows), :]
        for c in range(0, cols, 2 * HEAD):
            values = grad[pl.ds(start, rows), c : c + 2 * HEAD]
            values = turn_columns(values, c, q_cols + k_cols, cos, sin, False)
            out_ref[pl.ds(target, rows), c : c + 2 * HEAD] = values.astype(jnp.bfloat16)
        return 0

    lax.fori_loop(0, blocks, give_block, 0)


MESH = pl.DeviceIdType.MESH


def part_owner(part):
    return part % 2 * 2 + part // 2


def sequence_target(group, place, second, splits):
    part = place // 2
    target = (part_owner(part % 4), (2 * group + second) * splits + part // 4)
    return target, place % 2


def token_target(group, place, half, splits):
    sequence = place // splits
    part = part_owner(group) + 4 * (place % splits)
    return (sequence // 2, 2 * part + half), sequence % 2


def remote(source, target, sems, device):
    return pltpu.make_async_remote_copy(
        src_ref=source,
        dst_ref=target,
        send_sem=sems[0],
        recv_sem=sems[1],
        device_id=device,
        device_id_type=MESH,
    )


def same(one, other):
    return jnp.logical_and(one[0] == other[0], one[1] == other[1])


def greet(me, peers, movers):
    barrier = pltpu.get_barrier_semaphore()
    for peer in peers:
        pl.semaphore_signal(barrier, inc=1, device_id=peer, device_id_type=MESH)
    expected = len(peers)
    for source, target in movers:

        @pl.when(jnp.logical_not(same(source, me)))
        def _():
            pl.semaphore_signal(barrier, inc=1, device_id=source, device_id_type=MESH)

        expected = expected + jnp.where(same(target, me), 0, 1)
    pl.semaphore_wait(barrier, expected)


def move_start(me, source, target, target_device, send, receive):
    here = same(target_device, me)

    @pl.when(here)
    def _():
        pltpu.make_async_copy(source, target, receive).start()

    @pl.when(jnp.logical_not(here))
    def _():
        remote(source, target, (send, receive), target_device).start()


def move_sent(me, source, target, target_device, send, receive):
    @pl.when(jnp.logical_not(same(target_device, me)))
    def _():
        remote(source, target, (send, receive), target_device).wait_send()


def member(me, by):
    return (me[0] ^ (by // 2), me[1] ^ (by % 2))


def group_index(device):
    return 2 * device[0] + device[1] % 2


class GroupExchange:
    def __init__(self, me, pieces, got, sems):
        self.me, self.pieces, self.got, self.sems = me, pieces, got, sems

    def hop(self, by):
        peer = member(self.me, by)
        sems = (self.sems.at[0, by - 1], self.sems.at[1, by - 1])
        return remote(
            self.pieces.at[group_index(peer)], self.got.at[group_index(self.me)], sems, peer
        )

    def own(self):
        mine = group_index(self.me)
        return pltpu.make_async_copy(self.pieces.at[mine], self.got.at[mine], self.sems.at[0, 7])

    def start(self):
        for by in range(1, 8):
            self.hop(by).start()
        self.own().start()

    def finish(self):
        self.own().wait()
        for by in range(1, 8):
            self.hop(by).wait()


class GroupGather:
    def __init__(self, me, rows, sems, own, window):
        self.rows, self.sems, self.own, self.window = rows, sems, own, window
        self.core, self.across, self.beside = member(me, 2), member(me, 4), member(me, 1)

    def hop(self, index):
        across, beside, core = self.across, self.beside, self.core
        source, i, j, half, device = (
            (None, 0, 2, 0, across),
            (None, 1, 0, 1, beside),
            (None, 1, 0, 0, beside),
            (None, 0, 2, 1, across),
            ((0, 2), 1, 2, 0, beside),
            ((1, 0), 1, 2, 1, across),
            (None, 0, 1, slice(0, 2), core),
            ((0, 2), 0, 3, slice(0, 2), core),
            ((1, 0), 1, 1, slice(0, 2), core),
            ((1, 2), 1, 3, slice(0, 2), core),
        )[index]
        if source is None:
            source = self.own.at[half, self.window]
        else:
            source = self.rows.at[source[0], source[1], half, self.window]
        target = self.rows.at[i, j, half, self.window]
        return remote(source, target, (self.sems.at[0, index], self.sems.at[1, index]), device)

    def start(self):
        for index in (0, 1, 2, 3, 6):
            self.hop(index).start()

    def pass_on(self):
        self.hop(0).wait_recv()
        self.hop(4).start()
        self.hop(1).wait_recv()
        self.hop(5).start()
        self.hop(3).wait_recv()
        self.hop(7).start()
        self.hop(2).wait_recv()
        self.hop(8).start()

    def finish(self):
        self.hop(4).wait_recv()
        self.hop(5).wait_recv()
        self.hop(9).start()
        for index in (6, 7, 8, 9):
            self.hop(index).wait_recv()
        for index in range(10):
            self.hop(index).wait_send()


class Moves:
    def __init__(self, me, splits, source, target, sems, back):
        self.me, self.splits, self.source, self.target = me, splits, source, target
        self.sems, self.back = sems, back

    def one(self, i):
        find = token_target if self.back else sequence_target
        device, place = find(self.me[0], self.me[1], i, self.splits)
        return (
            self.me,
            self.source.at[i],
            self.target.at[place],
            device,
            self.sems.at[0, i],
            self.sems.at[1, place],
        )

    def start(self):
        for i in (0, 1):
            move_start(*self.one(i))

    def wait_recv(self):
        for i in (0, 1):
            pltpu.make_async_copy(self.source.at[0], self.target.at[i], self.sems.at[1, i]).wait()

    def finish(self):
        for i in (0, 1):
            move_sent(*self.one(i))


def movers_of(me, splits, back):
    into = [sequence_target(me[0], me[1], i, splits)[0] for i in (0, 1)]
    home = [token_target(me[0], me[1], i, splits)[0] for i in (0, 1)]
    return list(zip(into, home)) if back else list(zip(home, into))


def first_kernel(shards, splits, tokens, pieces, out_own, gate_pieces, *refs):
    rows, in_all, out_all, gate_rows, held = refs[:5]
    move_sems, group_sems, piece_sems, gate_sems, own_sem, in_sems, out_sems = refs[5:]
    me = (lax.axis_index("dp"), lax.axis_index("ctx"))
    group, place = me
    slow = shards // 2
    slot = place // 2
    line = [(group, place ^ (2 * by)) for by in range(1, slow)]
    wanted, block = place // slow, place % slow
    takers = [(group, 2 * (slot ^ by) + wanted) for by in range(slow)]
    givers = [(group, place % 2 * slow + block_by) for block_by in range(slow)]
    movers = movers_of(me, splits, False) + list(zip(givers, takers))
    greet(me, [member(me, by) for by in range(1, 8)] + line, movers)
    swap = GroupExchange(me, pieces, held, piece_sems)
    gate_swap = GroupExchange(me, gate_pieces, gate_rows, gate_sems)
    move = Moves(me, splits, tokens, rows.at[0, 0], move_sems, False)

    def in_line(by):
        sems = (in_sems.at[0, by - 1], in_sems.at[1, by - 1])
        return remote(held, in_all.at[slot], sems, line[by - 1])

    def out_send(by):
        return (
            me,
            out_own,
            out_all.at[block],
            takers[by],
            out_sems.at[0, by],
            out_sems.at[1, block],
        )

    own = pltpu.make_async_copy(held, in_all.at[slot], own_sem)
    swap.start()
    move.start()
    swap.finish()
    for by in range(1, slow):
        in_line(by).start()
    own.start()
    move.wait_recv()
    spread = GroupGather(me, rows, group_sems, rows.at[0, 0], slice(0, tokens.shape[1]))
    spread.start()
    for by in range(slow):
        move_start(*out_send(by))
    spread.pass_on()
    gate_swap.start()
    spread.finish()
    own.wait()
    for by in range(1, slow):
        in_line(by).wait()
    for by in range(slow):
        pltpu.make_async_copy(out_own, out_all.at[by], out_sems.at[1, by]).wait()
    for by in range(slow):
        move_sent(*out_send(by))
    gate_swap.finish()
    move.finish()


def first_exchange(tokens, pieces, out_own, gate_pieces, shards, splits, identity):
    low = jnp.bfloat16
    slow = shards // 2
    any_space = pl.BlockSpec(memory_space=pl.ANY)
    dma = pltpu.SemaphoreType.DMA
    made = pl.pallas_call(
        functools.partial(first_kernel, shards, splits),
        out_shape=(
            jax.ShapeDtypeStruct((2, 4) + tokens.shape, low),
            jax.ShapeDtypeStruct((slow,) + pieces.shape, low),
            jax.ShapeDtypeStruct((slow,) + out_own.shape, low),
            jax.ShapeDtypeStruct(gate_pieces.shape, low),
            jax.ShapeDtypeStruct(pieces.shape, low),
        ),
        in_specs=[any_space] * 4,
        out_specs=(any_space,) * 5,
        scratch_shapes=[
            dma((2, 2)),
            dma((2, 10)),
            dma((2, 8)),
            dma((2, 8)),
            dma,
            dma((2, slow - 1)),
            dma((2, slow)),
        ],
        compiler_params=pltpu.CompilerParams(
            collective_id=identity, has_side_effects=True, vmem_limit_bytes=8 << 20
        ),
        cost_estimate=pl.CostEstimate(flops=0, bytes_accessed=200 << 20, transcendentals=0),
    )(tokens, pieces, out_own, gate_pieces)
    return made[:4]


def spread_kernel(splits, tokens, rows, move_sems, group_sems):
    me = (lax.axis_index("dp"), lax.axis_index("ctx"))
    greet(me, [member(me, by) for by in (1, 2, 4)], movers_of(me, splits, False))
    move = Moves(me, splits, tokens, rows.at[0, 0], move_sems, False)
    spread = GroupGather(me, rows, group_sems, rows.at[0, 0], slice(0, tokens.shape[1]))
    move.start()
    move.wait_recv()
    spread.start()
    spread.pass_on()
    spread.finish()
    move.finish()


def spread_tokens(tokens, shards, splits, identity):
    any_space = pl.BlockSpec(memory_space=pl.ANY)
    dma = pltpu.SemaphoreType.DMA
    return pl.pallas_call(
        functools.partial(spread_kernel, splits),
        out_shape=(jax.ShapeDtypeStruct((2, 4) + tokens.shape, tokens.dtype),),
        in_specs=[any_space],
        out_specs=(any_space,),
        scratch_shapes=[dma((2, 2)), dma((2, 10))],
        compiler_params=pltpu.CompilerParams(
            collective_id=identity, has_side_effects=True, vmem_limit_bytes=4 << 20
        ),
        cost_estimate=pl.CostEstimate(flops=0, bytes_accessed=100 << 20, transcendentals=0),
    )(tokens)


class GroupScatter:
    def __init__(self, me, parts, buffers, sems, steps):
        self.parts = parts
        self.core_in, self.kept, self.sent, self.came, self.held = buffers[:5]
        self.sent_last, self.came_last = buffers[5:]
        self.core_sems, self.kept_sems, self.one_sems, self.last_sems = sems
        self.core, self.across, self.beside = member(me, 2), member(me, 4), member(me, 1)
        self.size = parts.shape[3] // steps
        self.steps = steps

    def window(self, k):
        return slice(k * self.size, (k + 1) * self.size)

    def to_core(self, k, j):
        return remote(
            self.parts.at[:, 2 * j + 1, :, self.window(k)],
            self.core_in.at[:, j, :, self.window(k)],
            (self.core_sems.at[0, k, j], self.core_sems.at[1, k, j]),
            self.core,
        )

    def keep(self, k, j):
        return pltpu.make_async_copy(
            self.parts.at[:, 2 * j, :, self.window(k)],
            self.kept.at[:, j, :, self.window(k)],
            self.kept_sems.at[k, j],
        )

    def first(self, k, half):
        return remote(
            self.sent.at[half, :, self.window(k)],
            self.came.at[half, :, self.window(k)],
            (self.one_sems.at[0, k, half], self.one_sems.at[1, k, half]),
            (self.beside, self.across)[half],
        )

    def second(self, k, half):
        return remote(
            self.sent_last.at[half, self.window(k)],
            self.came_last.at[half, self.window(k)],
            (self.last_sems.at[0, k, half], self.last_sems.at[1, k, half]),
            (self.across, self.beside)[half],
        )

    def start(self):
        for k in range(self.steps):
            for j in (0, 1):
                self.to_core(k, j).start()
                self.keep(k, j).start()

    def send_first(self, k):
        wide = jnp.float32
        rows = self.window(k)
        for j in (0, 1):
            self.keep(k, j).wait()
            self.to_core(k, j).wait_recv()
        for half in (0, 1):
            for other in (0, 1):
                at = (1, other) if half == 0 else (other, 1)
                both = self.kept[at[0], at[1], half, rows].astype(wide)
                both = both + self.core_in[at[0], at[1], half, rows].astype(wide)
                self.sent[half, other, rows] = both.astype(jnp.bfloat16)
            self.first(k, half).start()
        for half in (0, 1):
            for other in (0, 1):
                at = (0, other) if half == 0 else (other, 0)
                both = self.kept[at[0], at[1], half, rows].astype(wide)
                self.held[half, other, rows] = both + self.core_in[at[0], at[1], half, rows].astype(
                    wide
                )

    def send_second(self, k):
        wide = jnp.float32
        rows = self.window(k)
        for half in (0, 1):
            self.first(k, half).wait_recv()
            both = self.held[half, 1, rows] + self.came[half, 1, rows].astype(wide)
            self.sent_last[half, rows] = both.astype(jnp.bfloat16)
            self.second(k, half).start()
            self.held[half, 0, rows] = self.held[half, 0, rows] + self.came[half, 0, rows].astype(
                wide
            )

    def total(self, k, half):
        self.second(k, half).wait_recv()
        rows = self.window(k)
        return self.held[half, 0, rows] + self.came_last[half, rows].astype(jnp.float32)

    def finish(self):
        for k in range(self.steps):
            for j in (0, 1):
                self.to_core(k, j).wait_send()
            for half in (0, 1):
                self.first(k, half).wait_send()
                self.second(k, half).wait_send()


def scatter_scratch(rows, width, steps):
    low, wide = jnp.bfloat16, jnp.float32
    dma = pltpu.SemaphoreType.DMA
    return [
        pltpu.VMEM((2, 2, 2, rows, width), low),
        pltpu.VMEM((2, 2, 2, rows, width), low),
        pltpu.VMEM((2, 2, rows, width), low),
        pltpu.VMEM((2, 2, rows, width), low),
        pltpu.VMEM((2, 2, rows, width), wide),
        pltpu.VMEM((2, rows, width), low),
        pltpu.VMEM((2, rows, width), low),
        dma((2, steps, 2)),
        dma((steps, 2)),
        dma((2, steps, 2)),
        dma((2, steps, 2)),
    ]


def reordered(rows, slow, back):
    each = rows.shape[1] // (4 * slow)
    if back:
        starts = [s * 4 + dp for dp in range(4) for s in range(slow)]
    else:
        starts = [dp * slow + s for s in range(slow) for dp in range(4)]
    return jnp.concatenate([rows[:, i * each : (i + 1) * each] for i in starts], 1)


def turn_kernel(slow, steps, backward, parts, gain, *refs):
    if backward:
        residual, cot, result, gain_grad, rows = refs[:5]
        scratch = refs[5:]
    else:
        tokens, result, rows = refs[:3]
        scratch = refs[3:]
    own, own_sems, group_sems = scratch[:3]
    me = (lax.axis_index("dp"), lax.axis_index("ctx"))
    greet(me, [member(me, by) for by in (1, 2, 4)], [])
    scatter = GroupScatter(me, parts, scratch[3:10], scratch[10:], steps)
    gathers = [GroupGather(me, rows, group_sems.at[k], own, scatter.window(k)) for k in range(steps)]
    scatter.start()
    for k in range(steps):
        scatter.send_first(k)
    for k in range(steps):
        scatter.send_second(k)
    for k in range(steps):
        span = scatter.window(k)
        for half in (0, 1):
            total = scatter.total(k, half)
            if backward:
                values = residual[half, span]
                factor = lax.rsqrt(jnp.mean(values * values, -1, keepdims=True) + norm_eps)
                normed = values * factor
                total = reordered(total, slow, True)
                part = jnp.sum(total * normed, 0, keepdims=True)
                if k == 0 and half == 0:
                    gain_grad[...] = part
                else:
                    gain_grad[...] += part
                back = total * gain[...]
                back = factor * (back - normed * jnp.mean(back * normed, -1, keepdims=True))
                back = cot[half, span].astype(jnp.float32) + back
                result[half, span] = back
                own[half, span] = back.astype(jnp.bfloat16)
            else:
                values = tokens[half, span].astype(jnp.float32) + total
                factor = lax.rsqrt(jnp.mean(values * values, -1, keepdims=True) + norm_eps)
                result[half, span] = values
                own[half, span] = reordered(values * factor * gain[...], slow, False).astype(
                    jnp.bfloat16
                )
        gathers[k].start()
        keep = pltpu.make_async_copy(own.at[:, span], rows.at[0, 0, :, span], own_sems.at[k])
        keep.start()
    for k in range(steps):
        gathers[k].pass_on()
    for k in range(steps):
        gathers[k].finish()
        span = scatter.window(k)
        pltpu.make_async_copy(own.at[:, span], rows.at[0, 0, :, span], own_sems.at[k]).wait()
    scatter.finish()


def turn(parts, gain, rows_in, slow, backward, identity):
    low, wide = jnp.bfloat16, jnp.float32
    dma = pltpu.SemaphoreType.DMA
    rows, width = parts.shape[3:]
    steps = 2
    any_space = pl.BlockSpec(memory_space=pl.ANY)
    vmem = pl.BlockSpec(memory_space=pltpu.VMEM)
    shapes = [jax.ShapeDtypeStruct((2, rows, width), wide)]
    if backward:
        shapes.append(jax.ShapeDtypeStruct((1, width), wide))
    return pl.pallas_call(
        functools.partial(turn_kernel, slow, steps, backward),
        out_shape=tuple(shapes) + (jax.ShapeDtypeStruct((2, 4, 2, rows, width), low),),
        in_specs=[any_space, vmem] + [vmem] * len(rows_in),
        out_specs=tuple([vmem] * len(shapes) + [any_space]),
        scratch_shapes=[pltpu.VMEM((2, rows, width), low), dma((steps,)), dma((steps, 2, 10))]
        + scatter_scratch(rows, width, steps),
        compiler_params=pltpu.CompilerParams(
            collective_id=identity, has_side_effects=True, vmem_limit_bytes=48 << 20
        ),
        cost_estimate=pl.CostEstimate(flops=0, bytes_accessed=250 << 20, transcendentals=0),
    )(parts, gain, *rows_in)


class LineSum:
    def __init__(self, me, slow, parts, buffers, sems):
        self.parts = parts
        self.kept, self.arrived = buffers
        self.sems, self.own_sem = sems
        self.slot = me[1] // 2
        self.slow = slow
        self.line = [(me[0], me[1] ^ (2 * by)) for by in range(1, slow)]

    def hop(self, by):
        sems = (self.sems.at[0, by - 1], self.sems.at[1, by - 1])
        return remote(
            self.parts.at[self.slot ^ by], self.arrived.at[by - 1], sems, self.line[by - 1]
        )

    def own(self):
        return pltpu.make_async_copy(self.parts.at[self.slot], self.kept, self.own_sem)

    def start(self):
        for by in range(1, self.slow):
            self.hop(by).start()
        self.own().start()

    def total(self):
        self.own().wait()
        value = self.kept[...].astype(jnp.float32)
        for by in range(1, self.slow):
            self.hop(by).wait_recv()
            value = value + self.arrived[by - 1].astype(jnp.float32)
        return value

    def finish(self):
        for by in range(1, self.slow):
            self.hop(by).wait_send()


def line_scratch(shape, kind, slow):
    dma = pltpu.SemaphoreType.DMA
    return [
        pltpu.VMEM(shape, kind),
        pltpu.VMEM((slow - 1,) + shape, kind),
        dma((2, slow - 1)),
        dma,
    ]


def last_kernel(shards, splits, steps, in_parts, out_parts, gate_parts, in_back, out_rows, *refs):
    gain, gain_two_grad, tokens, back_rows, residual = refs[:5]
    in_total, out_total, gate_total, gains_total, block_out, tokens_grad = refs[5:11]
    scratch = list(refs[11:])

    def take(count):
        taken = scratch[:count]
        del scratch[:count]
        return taken

    me = (lax.axis_index("dp"), lax.axis_index("ctx"))
    group, place = me
    slow = shards // 2
    slot, half = place // 2, place % 2
    owned = in_parts.shape[2]
    home = (group, half * slow + slot)
    movers = movers_of(me, splits, True)
    movers.append(((group, place % slow * 2 + place // slow), home))
    line = [(group, place ^ (2 * by)) for by in range(1, slow)]
    greet(me, [member(me, by) for by in range(1, 8)] + line, movers)
    one = take(11)
    two = take(11)
    back_sum = GroupScatter(me, in_back, one[:7], one[7:], steps)
    out_sum = GroupScatter(me, out_rows, two[:7], two[7:], steps)
    line_in = take(4)
    line_out = take(4)
    line_gains = take(4)
    in_done, out_done, gains_own, gains_done, made_one, made_two, gain_grad = take(7)
    in_sems, gate_sems, gains_sems, one_sems, two_sems, home_sems = take(6)
    in_line = LineSum(me, slow, in_parts, line_in[:2], line_in[2:])
    out_line = LineSum(me, slow, out_parts, line_out[:2], line_out[2:])
    gains_line = LineSum(me, slow, gains_own, line_gains[:2], line_gains[2:])
    in_swap = GroupExchange(me, in_done, in_total, in_sems)
    gate_swap = GroupExchange(me, gate_parts, gate_total, gate_sems)
    gains_swap = GroupExchange(me, gains_done, gains_total, gains_sems)
    move_grad = Moves(me, splits, made_one, tokens_grad, one_sems, True)
    move_out = Moves(me, splits, made_two, block_out, two_sems, True)
    back_sum.start()
    out_sum.start()
    in_line.start()
    out_line.start()
    for k in range(steps):
        back_sum.send_first(k)
    for k in range(steps):
        out_sum.send_first(k)
    for k in range(steps):
        back_sum.send_second(k)
    gate_swap.start()
    for k in range(steps):
        span = back_sum.window(k)
        for part in (0, 1):
            total = back_sum.total(k, part)
            values = tokens[part, span].astype(jnp.float32)
            normed, factor = norm_parts(values)
            grad = jnp.sum(total * normed, 0, keepdims=True)
            if k == 0 and part == 0:
                gain_grad[...] = grad
            else:
                gain_grad[...] += grad
            value = back_rows[part, span] + norm_back(total * gain[...], normed, factor)
            made_one[part, span] = value.astype(jnp.bfloat16)
    move_grad.start()
    gains_own[...] = jnp.zeros_like(gains_own)
    for dp in range(4):
        for s in range(slow):
            for side in range(2):
                at = ((dp * slow + s) * 2 + side) * owned
                index = 2 * dp + side
                gains_own[s, index, 0:1, 0:owned] = gain_grad[:, at : at + owned]
                gains_own[s, index, 0:1, owned : 2 * owned] = gain_two_grad[:, at : at + owned]
    gains_line.start()
    for k in range(steps):
        out_sum.send_second(k)
    in_done[...] = in_line.total().astype(jnp.bfloat16)
    in_swap.start()
    for k in range(steps):
        span = out_sum.window(k)
        for part in (0, 1):
            value = residual[part, span] + out_sum.total(k, part)
            made_two[part, span] = value.astype(jnp.bfloat16)
    move_out.start()
    gains_done[...] = gains_line.total()
    gains_swap.start()
    out_done[...] = out_line.total().astype(jnp.bfloat16)
    to_home = (me, out_done, out_total, home, home_sems.at[0], home_sems.at[1])
    move_start(*to_home)
    pltpu.make_async_copy(out_done, out_total, home_sems.at[1]).wait()
    move_sent(*to_home)
    for swap in (in_swap, gate_swap, gains_swap):
        swap.finish()
    for move in (move_grad, move_out):
        move.wait_recv()
        move.finish()
    for part in (in_line, out_line, gains_line, back_sum, out_sum):
        part.finish()


def last_sums(in_parts, out_parts, gate_parts, in_back, out_rows, others, shards, splits, identity):
    low, wide = jnp.bfloat16, jnp.float32
    slow = shards // 2
    steps = 2
    any_space = pl.BlockSpec(memory_space=pl.ANY)
    vmem = pl.BlockSpec(memory_space=pltpu.VMEM)
    dma = pltpu.SemaphoreType.DMA
    rows, width = in_back.shape[3:]
    gains_shape = (8, 8, 128)
    moved = jax.ShapeDtypeStruct((2, rows, width), low)
    return pl.pallas_call(
        functools.partial(last_kernel, shards, splits, steps),
        out_shape=(
            jax.ShapeDtypeStruct(in_parts.shape[1:], low),
            jax.ShapeDtypeStruct(out_parts.shape[1:], low),
            jax.ShapeDtypeStruct(gate_parts.shape, low),
            jax.ShapeDtypeStruct(gains_shape, wide),
            moved,
            moved,
        ),
        in_specs=[any_space] * 5 + [vmem] * 5,
        out_specs=(any_space,) * 6,
        scratch_shapes=scatter_scratch(rows, width, steps)
        + scatter_scratch(rows, width, steps)
        + line_scratch(in_parts.shape[1:], low, slow)
        + line_scratch(out_parts.shape[1:], low, slow)
        + line_scratch(gains_shape, wide, slow)
        + [
            pltpu.VMEM(in_parts.shape[1:], low),
            pltpu.VMEM(out_parts.shape[1:], low),
            pltpu.VMEM((slow,) + gains_shape, wide),
            pltpu.VMEM(gains_shape, wide),
            pltpu.VMEM(moved.shape, low),
            pltpu.VMEM(moved.shape, low),
            pltpu.VMEM((1, width), wide),
            dma((2, 8)),
            dma((2, 8)),
            dma((2, 8)),
            dma((2, 2)),
            dma((2, 2)),
            dma((2,)),
        ],
        compiler_params=pltpu.CompilerParams(
            collective_id=identity, has_side_effects=True, vmem_limit_bytes=56 << 20
        ),
        cost_estimate=pl.CostEstimate(flops=0, bytes_accessed=300 << 20, transcendentals=0),
    )(in_parts, out_parts, gate_parts, in_back, out_rows, *others)


def position_tables(length):
    cosine, sine_table = rotary_tables(jnp.arange(length, dtype=jnp.int32), HEAD)
    sign = jnp.where(jnp.arange(HEAD) < HEAD // 2, -1.0, 1.0)
    return jnp.tile(cosine, (1, 2)), jnp.tile(sine_table * sign, (1, 2))


def attend(order, qkv, tables, q_heads, kv_heads):
    seqs, length, cols = qkv.shape
    whole = pl.BlockSpec(memory_space=pltpu.VMEM)
    return pl.pallas_call(
        functools.partial(attend_kernel, q_heads, kv_heads, 256),
        out_shape=(
            jax.ShapeDtypeStruct((seqs, length, q_heads * HEAD), jnp.bfloat16),
            jax.ShapeDtypeStruct((seqs, q_heads, length), jnp.float32),
            jax.ShapeDtypeStruct((seqs, length, cols), jnp.bfloat16),
        ),
        in_specs=[pl.BlockSpec(memory_space=pltpu.SMEM), whole, whole, whole],
        out_specs=(whole, whole, whole),
        scratch_shapes=[pltpu.VMEM((length, q_heads * HEAD), jnp.bfloat16)],
        compiler_params=pltpu.CompilerParams(vmem_limit_bytes=40 << 20),
        cost_estimate=pl.CostEstimate(
            flops=2 * seqs * length * length * q_heads * HEAD,
            bytes_accessed=8 * seqs * length * cols,
            transcendentals=seqs * length * length * q_heads // 2,
        ),
    )(order, qkv, *tables)


def attend_back(order, kept, back, lse, tables, q_heads, kv_heads):
    seqs, length, cols = kept.shape
    group = q_heads // kv_heads
    whole = pl.BlockSpec(memory_space=pltpu.VMEM)
    return pl.pallas_call(
        functools.partial(attend_back_kernel, q_heads, kv_heads, 256),
        out_shape=jax.ShapeDtypeStruct((seqs, length, cols), jnp.bfloat16),
        in_specs=[pl.BlockSpec(memory_space=pltpu.SMEM)] + [whole] * 5,
        out_specs=whole,
        scratch_shapes=[
            pltpu.VMEM((length, q_heads * HEAD), jnp.bfloat16),
            pltpu.VMEM((length, cols), jnp.float32),
            pltpu.VMEM((group, length), jnp.float32),
            pltpu.VMEM((group * HEAD, length), jnp.float32),
        ],
        compiler_params=pltpu.CompilerParams(vmem_limit_bytes=40 << 20),
        cost_estimate=pl.CostEstimate(
            flops=7 * seqs * length * length * q_heads * HEAD,
            bytes_accessed=6 * seqs * length * cols,
            transcendentals=seqs * length * length * q_heads // 2,
        ),
    )(order, kept, back, lse, *tables)


def local(
    tokens,
    cotangent,
    block_order,
    attention_in,
    attention_out,
    gate_up,
    down_matrix,
    gains,
    mean_attention_in,
    mean_attention_out,
    mean_gate_up,
    mean_down,
    mean_gains,
    square_attention_in,
    square_attention_out,
    square_gate_up,
    square_down,
    square_gains,
):
    seq_count, shard_rows, width = tokens.shape
    shards = lax.axis_size("ctx")
    slow = shards // 2
    mine = lax.axis_index("dp")
    beside = lax.axis_index("ctx") % 2
    low = jnp.bfloat16
    owned = attention_in.shape[0]
    hidden_units = gate_up.shape[1] // 2
    part_hidden = hidden_units // 8
    units = down_matrix.shape[0]
    part_q = HEADS * HEAD // 8
    part_k = KV_HEADS * HEAD // 8
    part_cols = part_q + 2 * part_k
    count = seq_count * shard_rows
    together = 8 * count
    spread = shards // (4 * seq_count)
    splits = max(1, slow // 8)
    seqs = 2 // spread if spread < 2 else 1
    length = shards * shard_rows
    q_heads = HEADS // 8 // splits
    kv_heads = KV_HEADS // 8

    in_low = attention_in.astype(low)
    gains_row = jnp.pad(gains.astype(low).reshape(1, -1), ((0, 15), (0, part_cols - 2 * owned)))
    pieces = jnp.stack(
        [
            jnp.concatenate(
                [
                    jnp.concatenate(
                        [
                            in_low[:, i * part_q : (i + 1) * part_q],
                            in_low[:, 8 * part_q + i * part_k :][:, :part_k],
                            in_low[:, 8 * (part_q + part_k) + i * part_k :][:, :part_k],
                        ],
                        1,
                    ),
                    gains_row,
                ]
            )
            for i in range(8)
        ]
    )
    gate_low = gate_up.astype(low)
    gate_pieces = jnp.stack(
        [
            jnp.concatenate(
                [
                    gate_low[:, side * hidden_units + (dp * shards + 2 * s + half) * units :][
                        :, :units
                    ]
                    for side in range(2)
                    for s in range(slow)
                ],
                1,
            )
            for dp in range(4)
            for half in range(2)
        ]
    )
    tokens_all, in_all, w_out, gate_rows = first_exchange(
        tokens, pieces, attention_out.astype(low), gate_pieces, shards, spread, 1
    )
    in_all = in_all.reshape(slow, 4, 2, owned + 16, part_cols).swapaxes(0, 1)
    w_in = in_all[:, :, :, :owned].reshape(width, part_cols)
    w_out = w_out.reshape(part_q, width)
    gains_all = in_all[:, :, :, owned, : 2 * owned].reshape(-1, 2, owned)
    gains_all = gains_all.astype(jnp.float32).swapaxes(0, 1).reshape(2, width)
    gain_one, gain_two = gains_all[0], gains_all[1]
    w_gate = gather_line(gate_rows.reshape(8 * owned, 2 * part_hidden))
    w_down = gather_line((down_matrix + 0.0 * w_gate[0, 0].astype(jnp.float32)).astype(low))

    normed_all, _ = norm_parts(tokens_all.reshape(together, width).astype(jnp.float32))
    input_one = (normed_all * gain_one).astype(low)
    qkv = dot_nn(input_one, w_in)
    orders = block_order.reshape(2 * splits if spread > 1 else 1, 4, -1)
    slot_order = jnp.concatenate(
        [
            orders[(2 * s + (beside ^ i)) if spread > 1 else 0, part_owner(mine ^ j)]
            for s in range(splits)
            for i in range(2 // seqs)
            for j in range(4)
        ]
    )
    tables = position_tables(length)
    groups = [
        [2 * (s * splits + g) + half for g in range(splits)]
        for s in range(slow // splits)
        for half in (0, 1)
    ]

    def split_heads(values, widths, copies):
        parts = []
        start = 0
        for each, repeat in zip(widths, copies):
            kinds = splits // repeat
            piece = values[:, start : start + kinds * each].reshape(-1, kinds, each)
            parts.append(jnp.repeat(piece.swapaxes(0, 1), repeat, axis=0))
            start += kinds * each
        sent = jnp.concatenate(parts, 2)
        got = lax.all_to_all(sent, "ctx", 0, 0, axis_index_groups=groups, tiled=True)
        return got.reshape(length, -1)

    def join_heads(values):
        sent = values.reshape(splits, together, -1)
        return lax.all_to_all(sent, "ctx", 0, 0, axis_index_groups=groups, tiled=True)

    q_width, k_width = q_heads * HEAD, kv_heads * HEAD
    if splits > 1:
        qkv = split_heads(qkv, (q_width, k_width, k_width), (1, splits, splits))
    qkv = qkv.reshape(seqs, length, -1)
    attended, lse, kept = attend(slot_order, qkv, tables, q_heads, kv_heads)
    if splits > 1:
        attended = join_heads(attended).swapaxes(0, 1)
    attended = attended.reshape(together, part_q)

    def parts(values):
        return values.astype(low).reshape((2, 4) + tokens.shape)

    residual_rows, input_two = turn(
        parts(dot_nn(attended, w_out)), gain_two[None], [tokens_all[0, 0]], slow, False, 3
    )
    input_two = input_two.reshape(together, width)
    gate_both = dot_nn(input_two, w_gate)
    gate_part = gate_both[:, :part_hidden]
    up_part = gate_both[:, part_hidden:]
    sigmoid_gate = jax.nn.sigmoid(gate_part)
    active = gate_part * sigmoid_gate
    hidden = (active * up_part).astype(low)
    (back_all,) = spread_tokens(cotangent + 0.0 * hidden[0, 0], shards, spread, 2)
    cot_rows = back_all[0, 0]
    back_all = back_all.reshape(together, width)
    grad_down = dot_tn(hidden, back_all) + 0.0 * w_down[0, 0].astype(jnp.float32)
    down_sum = sum_line(grad_down.astype(low)).astype(jnp.float32)
    back_hidden = dot_nt(back_all, w_down)
    back_gate = back_hidden * up_part * sigmoid_gate * (1.0 + gate_part * (1.0 - sigmoid_gate))
    back_upper = back_hidden * active
    back_gate_up = jnp.concatenate([back_gate, back_upper], 1).astype(low)
    gate_low = sum_line(dot_tn(input_two, back_gate_up).astype(low))
    back_rows, grad_gain_two, back_residual_all = turn(
        parts(dot_nt(back_gate_up, w_gate)),
        gain_two[None],
        [residual_rows, cot_rows],
        slow,
        True,
        4,
    )
    back_residual_all = back_residual_all.reshape(together, width)
    grad_out = dot_tn(attended, back_residual_all).astype(low)
    back_attended = dot_nt(back_residual_all, w_out).astype(low)
    if splits > 1:
        back_attended = split_heads(back_attended, (q_width,), (1,))
    back_projected = attend_back(
        slot_order, kept, back_attended.reshape(seqs, length, -1), lse, tables, q_heads, kv_heads
    )
    if splits > 1:
        back_projected = join_heads(back_projected).astype(jnp.float32)
        back_projected = jnp.concatenate(
            [
                back_projected[..., :q_width].swapaxes(0, 1).reshape(together, part_q),
                back_projected[..., q_width:].sum(0),
            ],
            1,
        ).astype(low)
    back_projected = back_projected.reshape(together, part_cols)
    grad_in = dot_tn(input_one, back_projected).astype(low)
    grad_in = grad_in.reshape(4, slow, 2 * owned, part_cols).swapaxes(0, 1)
    in_sum, out_sum, gate_sum, gains_sum, block_out, tokens_grad = last_sums(
        grad_in.reshape(slow, 8, owned, part_cols),
        grad_out.reshape(slow, owned, width),
        gate_low.reshape(8, owned, 2 * part_hidden),
        parts(dot_nt(back_projected, w_in)),
        parts(dot_nn(hidden, w_down)),
        [gain_one[None], grad_gain_two, tokens_all[0, 0], back_rows, residual_rows],
        shards,
        spread,
        5,
    )
    tokens_grad = tokens_grad.astype(jnp.float32)
    out_sum = out_sum.astype(jnp.float32)
    gains_sum = gains_sum[:, 0, : 2 * owned].reshape(8, 2, owned).sum(0)
    gate_sum = jnp.concatenate(
        [
            gate_sum[2 * dp + half, :, (side * slow + s) * units :][:, :units]
            for side in range(2)
            for dp in range(4)
            for s in range(slow)
            for half in range(2)
        ],
        1,
    ).astype(jnp.float32)
    cuts = ((0, part_q), (part_q, part_q + part_k), (part_q + part_k, part_cols))
    in_sum = jnp.concatenate(
        [in_sum[i, :, first:last] for first, last in cuts for i in range(8)], 1
    ).astype(jnp.float32)
    new_in = adam_update(
        attention_in,
        in_sum,
        mean_attention_in,
        square_attention_in,
        input_boost * D ** (-0.5),
        weight_decay,
    )
    new_out = adam_update(
        attention_out,
        out_sum,
        mean_attention_out,
        square_attention_out,
        (HEADS * HEAD // 32) ** (-0.5),
        weight_decay,
    )
    new_gate = adam_update(
        gate_up, gate_sum, mean_gate_up, square_gate_up, D ** (-0.5), weight_decay
    )
    new_down = adam_update(
        down_matrix, down_sum, mean_down, square_down, FF ** (-0.5), weight_decay
    )
    new_gain = adam_update(gains, gains_sum, mean_gains, square_gains, gain_rate, 0.0)
    return (
        block_out,
        tokens_grad,
        new_in[0],
        new_in[1],
        new_in[2],
        new_out[0],
        new_out[1],
        new_out[2],
        new_gate[0],
        new_gate[1],
        new_gate[2],
        new_down[0],
        new_down[1],
        new_down[2],
        new_gain[0],
        new_gain[1],
        new_gain[2],
    )


def solution(mesh):
    in_specs = (
        P("dp", "ctx", None),
        P("dp", "ctx", None),
        P(),
        P(("dp", "ctx"), None),
        P(("dp", "ctx"), None),
        P(("dp", "ctx"), None),
        P(("dp", "ctx"), None),
        P(None, ("dp", "ctx")),
        P(("dp", "ctx"), None),
        P(("dp", "ctx"), None),
        P(("dp", "ctx"), None),
        P(("dp", "ctx"), None),
        P(None, ("dp", "ctx")),
        P(("dp", "ctx"), None),
        P(("dp", "ctx"), None),
        P(("dp", "ctx"), None),
        P(("dp", "ctx"), None),
        P(None, ("dp", "ctx")),
    )
    out_specs = (
        P("dp", "ctx", None),
        P("dp", "ctx", None),
        P(("dp", "ctx"), None),
        P(("dp", "ctx"), None),
        P(("dp", "ctx"), None),
        P(("dp", "ctx"), None),
        P(("dp", "ctx"), None),
        P(("dp", "ctx"), None),
        P(("dp", "ctx"), None),
        P(("dp", "ctx"), None),
        P(("dp", "ctx"), None),
        P(("dp", "ctx"), None),
        P(("dp", "ctx"), None),
        P(("dp", "ctx"), None),
        P(None, ("dp", "ctx")),
        P(None, ("dp", "ctx")),
        P(None, ("dp", "ctx")),
    )
    return jax.shard_map(local, mesh=mesh, in_specs=in_specs, out_specs=out_specs, check_vma=False)
```

```python
import functools

import jax
import jax.numpy as jnp
import numpy as np
from jax import lax
from jax.experimental import pallas as pl
from jax.experimental.pallas import tpu as pltpu
from jax.sharding import PartitionSpec as P

D = 2048
HEADS = 32
KV_HEADS = 8
HEAD = 64
FF = 8192
STEP = 5


norm_eps = 1e-05
rope_base = 500000.0
beta_one = 0.9
beta_two = 0.95
gain_rate = 1.25
input_boost = 2.5
weight_decay = 0.1
adam_eps = 1e-08
masked_score = -1e30


def norm_parts(values):
    factor = lax.rsqrt(jnp.mean(values * values, -1, keepdims=True) + norm_eps)
    return (values * factor, factor)


def norm_back(back_normed, normed, factor):
    return factor * (back_normed - normed * jnp.mean(back_normed * normed, -1, keepdims=True))


def adam_update(weight, gradient, first_moment, second_moment, step_rate, decay_rate):
    first_new = beta_one * first_moment + (1.0 - beta_one) * gradient
    second_new = beta_two * second_moment + (1.0 - beta_two) * gradient * gradient
    update = (
        first_new
        / (1.0 - beta_one**STEP)
        / (jnp.sqrt(second_new / (1.0 - beta_two**STEP)) + adam_eps)
    )
    return (first_new, second_new, weight - step_rate * (update + decay_rate * weight))


def line_groups(shards):
    return [[2 * s + half for s in range(shards // 2)] for half in (0, 1)]


def gather_line(rows):
    return lax.all_gather(
        rows, "ctx", axis=0, tiled=True, axis_index_groups=line_groups(lax.axis_size("ctx"))
    )


def sum_line(gradient):
    return lax.psum_scatter(
        gradient,
        "ctx",
        scatter_dimension=0,
        tiled=True,
        axis_index_groups=line_groups(lax.axis_size("ctx")),
    )


def dot_nn(a, b):
    return lax.dot_general(a, b, (((1,), (0,)), ((), ())), preferred_element_type=jnp.float32)


def dot_nt(a, b):
    return lax.dot_general(a, b, (((1,), (1,)), ((), ())), preferred_element_type=jnp.float32)


def dot_tn(a, b):
    return lax.dot_general(a, b, (((0,), (0,)), ((), ())), preferred_element_type=jnp.float32)


def causal_keep(tile):
    keys = lax.broadcasted_iota(jnp.int32, (tile, tile), 0)
    queries = lax.broadcasted_iota(jnp.int32, (tile, tile), 1)
    return keys <= queries


def turn_group(values, cos, sin, forward):
    lanes = lax.broadcasted_iota(jnp.int32, values.shape, 1)
    other = jnp.where(
        lanes % HEAD < HEAD // 2,
        pltpu.roll(values, 2 * HEAD - HEAD // 2, 1),
        pltpu.roll(values, HEAD // 2, 1),
    )
    if forward:
        return values * cos + other * sin
    return values * cos - other * sin


def turn_columns(values, start, turned_cols, cos, sin, forward):
    if start >= turned_cols:
        return values
    turned = turn_group(values, cos, sin, forward)
    if start + 2 * HEAD <= turned_cols:
        return turned
    lanes = lax.broadcasted_iota(jnp.int32, values.shape, 1)
    return jnp.where(lanes < turned_cols - start, turned, values)


def attend_kernel(
    q_heads,
    kv_heads,
    tile,
    order_ref,
    where_ref,
    all_qkv_ref,
    cos_ref,
    sin_ref,
    cot,
    all_out_ref,
    all_lse_ref,
    all_kept_ref,
    cot_rows,
    made,
    group_sems,
    own_sem,
):
    me = (lax.axis_index("dp"), lax.axis_index("ctx"))
    greet(me, [member(me, by) for by in (1, 2, 4)], [])
    spread = GroupGather(me, cot_rows, group_sems, cot, slice(0, cot.shape[1]))
    own = pltpu.make_async_copy(cot, cot_rows.at[0, 0], own_sem)
    spread.start()
    own.start()
    count = all_qkv_ref.shape[0]
    for sequence in range(count):
        attend_sequence(
            q_heads,
            kv_heads,
            tile,
            order_ref,
            where_ref,
            all_qkv_ref.at[sequence],
            cos_ref,
            sin_ref,
            all_out_ref.at[sequence],
            all_lse_ref.at[sequence],
            all_kept_ref.at[sequence],
            made,
        )
        if sequence == 0:
            spread.pass_on()
    spread.finish()
    own.wait()


def attend_sequence(
    q_heads,
    kv_heads,
    tile,
    order_ref,
    where_ref,
    qkv_ref,
    cos_ref,
    sin_ref,
    out_ref,
    lse_ref,
    kept_ref,
    made,
):
    blocks, rows, cols = qkv_ref.shape
    length = blocks * rows
    group = q_heads // kv_heads
    q_cols, k_cols = q_heads * HEAD, kv_heads * HEAD
    scale = HEAD ** (-0.5)

    def take_block(i, _):
        start = pl.multiple_of(i * rows, rows)
        cos = cos_ref[i]
        sin = sin_ref[i]
        for c in range(0, cols, 2 * HEAD):
            values = qkv_ref[where_ref[i], :, c : c + 2 * HEAD]
            values = turn_columns(values, c, q_cols + k_cols, cos, sin, True)
            kept_ref[pl.ds(start, rows), c : c + 2 * HEAD] = values.astype(jnp.bfloat16)
        return 0

    lax.fori_loop(0, blocks, take_block, 0)
    keep = causal_keep(tile)
    for kv in range(kv_heads):
        k_at = q_cols + kv * HEAD
        v_at = q_cols + k_cols + kv * HEAD

        def query_step(i, _):
            q_start = pl.multiple_of(i * tile, tile)
            queries = [
                kept_ref[
                    pl.ds(q_start, tile), (kv * group + g) * HEAD : (kv * group + g + 1) * HEAD
                ]
                for g in range(group)
            ]

            def key_tile(j, carry, masked):
                k_start = pl.multiple_of(j * tile, tile)
                keys = kept_ref[pl.ds(k_start, tile), k_at : k_at + HEAD]
                values = kept_ref[pl.ds(k_start, tile), v_at : v_at + HEAD]
                result = []
                for g in range(group):
                    peak, total, weighted = carry[g]
                    scores = dot_nt(keys, queries[g]) * scale
                    if masked:
                        scores = jnp.where(keep, scores, masked_score)
                    new_peak = jnp.maximum(peak, jnp.max(scores, 0, keepdims=True))
                    weights = jnp.exp(scores - new_peak)
                    shrink = jnp.exp(peak - new_peak)
                    total = total * shrink + jnp.sum(weights, 0, keepdims=True)
                    weighted = weighted * shrink + dot_tn(values, weights.astype(jnp.bfloat16))
                    result.append((new_peak, total, weighted))
                return tuple(result)

            start = tuple(
                (
                    jnp.full((1, tile), masked_score, jnp.float32),
                    jnp.zeros((1, tile), jnp.float32),
                    jnp.zeros((HEAD, tile), jnp.float32),
                )
                for _ in range(group)
            )
            carry = lax.fori_loop(0, i, lambda j, c: key_tile(j, c, False), start)
            carry = key_tile(i, carry, True)
            for g in range(group):
                head = kv * group + g
                peak, total, weighted = carry[g]
                lse_ref[head : head + 1, pl.ds(q_start, tile)] = peak + jnp.log(total)
                made[pl.ds(i * (tile // rows), tile // rows), :, head * HEAD : (head + 1) * HEAD] = (
                    (weighted / total).T.astype(jnp.bfloat16).reshape(-1, rows, HEAD)
                )
            return 0

        lax.fori_loop(0, length // tile, query_step, 0)

    def give_block(i, _):
        out_ref[i] = made[order_ref[i]]
        return 0

    lax.fori_loop(0, blocks, give_block, 0)


def attend_back_kernel(
    q_heads,
    kv_heads,
    tile,
    splits,
    steps,
    order_ref,
    where_ref,
    all_kept_ref,
    all_back_ref,
    all_lse_ref,
    cos_ref,
    sin_ref,
    out_rows,
    residual,
    all_out_ref,
    block_out,
    *scratch,
):
    me = (lax.axis_index("dp"), lax.axis_index("ctx"))
    greet(me, [member(me, by) for by in (1, 2, 4)], movers_of(me, splits, True))
    work, scratch = scratch[:4], scratch[4:]
    made, move_sems = scratch[:2]
    scatter = GroupScatter(me, out_rows, scratch[2:9], scratch[9:], steps)
    move = Moves(me, splits, made, block_out, move_sems, True)

    def one():
        for k in range(steps):
            scatter.send_first(k)

    def two():
        for k in range(steps):
            scatter.send_second(k)

    def three():
        for k in range(steps):
            span = scatter.window(k)
            for part in (0, 1):
                value = residual[part, span] + scatter.total(k, part)
                made[part, span] = value.astype(jnp.bfloat16)
        move.start()

    tasks = [one, two, three]

    def pause():
        if tasks:
            tasks.pop(0)()

    scatter.start()
    for sequence in range(all_kept_ref.shape[0]):
        attend_back_sequence(
            q_heads,
            kv_heads,
            tile,
            pause,
            order_ref,
            where_ref,
            all_kept_ref.at[sequence],
            all_back_ref.at[sequence],
            all_lse_ref.at[sequence],
            cos_ref,
            sin_ref,
            all_out_ref.at[sequence],
            *work,
        )
        pause()
    while tasks:
        pause()
    move.wait_recv()
    move.finish()
    scatter.finish()


def attend_back_sequence(
    q_heads,
    kv_heads,
    tile,
    pause,
    order_ref,
    where_ref,
    kept_ref,
    back_ref,
    lse_ref,
    cos_ref,
    sin_ref,
    out_ref,
    back_sorted,
    grad,
    delta_ref,
    dq_ref,
):
    length, cols = kept_ref.shape
    blocks, rows = back_ref.shape[:2]
    group = q_heads // kv_heads
    q_cols, k_cols = q_heads * HEAD, kv_heads * HEAD
    scale = HEAD ** (-0.5)
    tiles = length // tile

    def take_block(i, _):
        start = pl.multiple_of(i * rows, rows)
        back_sorted[pl.ds(start, rows), :] = back_ref[where_ref[i]]
        return 0

    lax.fori_loop(0, blocks, take_block, 0)
    keep = causal_keep(tile)
    for kv in range(kv_heads):
        k_at = q_cols + kv * HEAD
        v_at = q_cols + k_cols + kv * HEAD

        def load(i, g):
            start = pl.multiple_of(i * tile, tile)
            head = kv * group + g
            at = slice(head * HEAD, (head + 1) * HEAD)
            return (
                kept_ref[pl.ds(start, tile), at],
                back_sorted[pl.ds(start, tile), at],
                lse_ref[head : head + 1, pl.ds(start, tile)],
            )

        def load_kv(j):
            start = pl.multiple_of(j * tile, tile)
            return (
                kept_ref[pl.ds(start, tile), k_at : k_at + HEAD],
                kept_ref[pl.ds(start, tile), v_at : v_at + HEAD],
            )

        def tile_terms(keys, values, query, back, lse, masked):
            weights = jnp.exp(dot_nt(keys, query) * scale - lse)
            if masked:
                weights = jnp.where(keep, weights, 0.0)
            return weights, dot_nt(values, back)

        def delta_step(i, _):
            rows_i = [load(i, g) for g in range(group)]

            def one(j, carry, masked):
                keys, values = load_kv(j)
                result = []
                for g in range(group):
                    weights, back_weights = tile_terms(keys, values, *rows_i[g], masked)
                    result.append(carry[g] + jnp.sum(weights * back_weights, 0, keepdims=True))
                return tuple(result)

            carry = tuple(jnp.zeros((1, tile), jnp.float32) for _ in range(group))
            carry = lax.fori_loop(0, i, lambda j, c: one(j, c, False), carry)
            carry = one(i, carry, True)
            for g in range(group):
                delta_ref[g : g + 1, pl.ds(pl.multiple_of(i * tile, tile), tile)] = carry[g]
            return 0

        lax.fori_loop(0, tiles, delta_step, 0)
        if kv == 0:
            pause()
        dq_ref[...] = jnp.zeros_like(dq_ref)

        def key_step(j, _):
            keys, values = load_kv(j)

            def one(i, carry, masked):
                back_key, back_value = carry
                start = pl.multiple_of(i * tile, tile)
                for g in range(group):
                    query, back, lse = load(i, g)
                    weights, back_weights = tile_terms(keys, values, query, back, lse, masked)
                    delta = delta_ref[g : g + 1, pl.ds(start, tile)]
                    back_scores = (weights * (back_weights - delta)).astype(jnp.bfloat16)
                    back_key = back_key + dot_nn(back_scores, query)
                    back_value = back_value + dot_nn(weights.astype(jnp.bfloat16), back)
                    dq_ref[g * HEAD : (g + 1) * HEAD, pl.ds(start, tile)] += dot_tn(
                        keys, back_scores
                    )
                return back_key, back_value

            zero = jnp.zeros((tile, HEAD), jnp.float32)
            carry = one(j, (zero, zero), True)
            carry = lax.fori_loop(j + 1, tiles, lambda i, c: one(i, c, False), carry)
            span = pl.ds(j * (tile // rows), tile // rows)
            grad[span, :, k_at : k_at + HEAD] = (carry[0] * scale).reshape(-1, rows, HEAD)
            grad[span, :, v_at : v_at + HEAD] = carry[1].reshape(-1, rows, HEAD)
            return 0

        lax.fori_loop(0, tiles, key_step, 0)
        for g in range(group):
            head = kv * group + g
            turned = (dq_ref[g * HEAD : (g + 1) * HEAD, :] * scale).T
            grad[:, :, head * HEAD : (head + 1) * HEAD] = turned.reshape(-1, rows, HEAD)

    def give_block(i, _):
        cos = cos_ref[order_ref[i]]
        sin = sin_ref[order_ref[i]]
        for c in range(0, cols, 2 * HEAD):
            values = grad[order_ref[i], :, c : c + 2 * HEAD]
            values = turn_columns(values, c, q_cols + k_cols, cos, sin, False)
            out_ref[i, :, c : c + 2 * HEAD] = values.astype(jnp.bfloat16)
        return 0

    lax.fori_loop(0, blocks, give_block, 0)


MESH = pl.DeviceIdType.MESH


def part_owner(part):
    return part % 2 * 2 + part // 2


def sequence_target(group, place, second, splits):
    part = place // 2
    target = (part_owner(part % 4), (2 * group + second) * splits + part // 4)
    return target, place % 2


def token_target(group, place, half, splits):
    sequence = place // splits
    part = part_owner(group) + 4 * (place % splits)
    return (sequence // 2, 2 * part + half), sequence % 2


def remote(source, target, sems, device):
    return pltpu.make_async_remote_copy(
        src_ref=source,
        dst_ref=target,
        send_sem=sems[0],
        recv_sem=sems[1],
        device_id=device,
        device_id_type=MESH,
    )


def same(one, other):
    return jnp.logical_and(one[0] == other[0], one[1] == other[1])


def greet(me, peers, movers):
    barrier = pltpu.get_barrier_semaphore()
    for peer in peers:
        pl.semaphore_signal(barrier, inc=1, device_id=peer, device_id_type=MESH)
    expected = len(peers)
    for source, target in movers:

        @pl.when(jnp.logical_not(same(source, me)))
        def _():
            pl.semaphore_signal(barrier, inc=1, device_id=source, device_id_type=MESH)

        expected = expected + jnp.where(same(target, me), 0, 1)
    pl.semaphore_wait(barrier, expected)


def move_start(me, source, target, target_device, send, receive):
    here = same(target_device, me)

    @pl.when(here)
    def _():
        pltpu.make_async_copy(source, target, receive).start()

    @pl.when(jnp.logical_not(here))
    def _():
        remote(source, target, (send, receive), target_device).start()


def move_sent(me, source, target, target_device, send, receive):
    @pl.when(jnp.logical_not(same(target_device, me)))
    def _():
        remote(source, target, (send, receive), target_device).wait_send()


def member(me, by):
    return (me[0] ^ (by // 2), me[1] ^ (by % 2))


def group_index(device):
    return 2 * device[0] + device[1] % 2


class GroupExchange:
    def __init__(self, me, pieces, got, sems):
        self.me, self.pieces, self.got, self.sems = me, pieces, got, sems

    def hop(self, by):
        peer = member(self.me, by)
        sems = (self.sems.at[0, by - 1], self.sems.at[1, by - 1])
        return remote(
            self.pieces.at[group_index(peer)], self.got.at[group_index(self.me)], sems, peer
        )

    def own(self):
        mine = group_index(self.me)
        return pltpu.make_async_copy(self.pieces.at[mine], self.got.at[mine], self.sems.at[0, 7])

    def start(self):
        for by in range(1, 8):
            self.hop(by).start()
        self.own().start()

    def finish(self):
        self.own().wait()
        for by in range(1, 8):
            self.hop(by).wait()


class GroupGather:
    def __init__(self, me, rows, sems, own, window):
        self.rows, self.sems, self.own, self.window = rows, sems, own, window
        self.core, self.across, self.beside = member(me, 2), member(me, 4), member(me, 1)

    def hop(self, index):
        across, beside, core = self.across, self.beside, self.core
        source, i, j, half, device = (
            (None, 0, 2, 0, across),
            (None, 1, 0, 1, beside),
            (None, 1, 0, 0, beside),
            (None, 0, 2, 1, across),
            ((0, 2), 1, 2, 0, beside),
            ((1, 0), 1, 2, 1, across),
            (None, 0, 1, slice(0, 2), core),
            ((0, 2), 0, 3, slice(0, 2), core),
            ((1, 0), 1, 1, slice(0, 2), core),
            ((1, 2), 1, 3, slice(0, 2), core),
        )[index]
        if source is None:
            source = self.own.at[half, self.window]
        else:
            source = self.rows.at[source[0], source[1], half, self.window]
        target = self.rows.at[i, j, half, self.window]
        return remote(source, target, (self.sems.at[0, index], self.sems.at[1, index]), device)

    def start(self):
        for index in (0, 1, 2, 3, 6):
            self.hop(index).start()

    def pass_on(self):
        self.hop(0).wait_recv()
        self.hop(4).start()
        self.hop(1).wait_recv()
        self.hop(5).start()
        self.hop(3).wait_recv()
        self.hop(7).start()
        self.hop(2).wait_recv()
        self.hop(8).start()

    def finish(self):
        self.hop(4).wait_recv()
        self.hop(5).wait_recv()
        self.hop(9).start()
        for index in (6, 7, 8, 9):
            self.hop(index).wait_recv()
        for index in range(10):
            self.hop(index).wait_send()


class Moves:
    def __init__(self, me, splits, source, target, sems, back):
        self.me, self.splits, self.source, self.target = me, splits, source, target
        self.sems, self.back = sems, back

    def one(self, i):
        find = token_target if self.back else sequence_target
        device, place = find(self.me[0], self.me[1], i, self.splits)
        return (
            self.me,
            self.source.at[i],
            self.target.at[place],
            device,
            self.sems.at[0, i],
            self.sems.at[1, place],
        )

    def start(self):
        for i in (0, 1):
            move_start(*self.one(i))

    def wait_recv(self):
        for i in (0, 1):
            pltpu.make_async_copy(self.source.at[0], self.target.at[i], self.sems.at[1, i]).wait()

    def finish(self):
        for i in (0, 1):
            move_sent(*self.one(i))


def movers_of(me, splits, back):
    into = [sequence_target(me[0], me[1], i, splits)[0] for i in (0, 1)]
    home = [token_target(me[0], me[1], i, splits)[0] for i in (0, 1)]
    return list(zip(into, home)) if back else list(zip(home, into))


def first_kernel(shards, splits, tokens, cot, pieces, out_own, gate_pieces, *refs):
    rows, cot_rows, in_all, out_all, gate_rows, held = refs[:6]
    move_sems, cot_sems, group_sems, piece_sems, gate_sems, own_sem, in_sems, out_sems = refs[6:]
    me = (lax.axis_index("dp"), lax.axis_index("ctx"))
    group, place = me
    slow = shards // 2
    slot = place // 2
    line = [(group, place ^ (2 * by)) for by in range(1, slow)]
    wanted, block = place // slow, place % slow
    takers = [(group, 2 * (slot ^ by) + wanted) for by in range(slow)]
    givers = [(group, place % 2 * slow + block_by) for block_by in range(slow)]
    movers = movers_of(me, splits, False) + list(zip(givers, takers))
    greet(me, [member(me, by) for by in range(1, 8)] + line, movers)
    swap = GroupExchange(me, pieces, held, piece_sems)
    gate_swap = GroupExchange(me, gate_pieces, gate_rows, gate_sems)
    move = Moves(me, splits, tokens, rows.at[0, 0], move_sems, False)
    cot_move = Moves(me, splits, cot, cot_rows, cot_sems, False)

    def in_line(by):
        sems = (in_sems.at[0, by - 1], in_sems.at[1, by - 1])
        return remote(held, in_all.at[slot], sems, line[by - 1])

    def out_send(by):
        return (
            me,
            out_own,
            out_all.at[block],
            takers[by],
            out_sems.at[0, by],
            out_sems.at[1, block],
        )

    own = pltpu.make_async_copy(held, in_all.at[slot], own_sem)
    swap.start()
    move.start()
    gate_swap.start()
    swap.finish()
    for by in range(1, slow):
        in_line(by).start()
    own.start()
    move.wait_recv()
    spread = GroupGather(me, rows, group_sems, rows.at[0, 0], slice(0, tokens.shape[1]))
    spread.start()
    for by in range(slow):
        move_start(*out_send(by))
    for by in range(1, slow):
        in_line(by).wait()
    cot_move.start()
    spread.pass_on()
    spread.finish()
    own.wait()
    for by in range(slow):
        pltpu.make_async_copy(out_own, out_all.at[by], out_sems.at[1, by]).wait()
    for by in range(slow):
        move_sent(*out_send(by))
    gate_swap.finish()
    cot_move.wait_recv()
    move.finish()
    cot_move.finish()


def first_exchange(tokens, cot, pieces, out_own, gate_pieces, shards, splits, identity):
    low = jnp.bfloat16
    slow = shards // 2
    any_space = pl.BlockSpec(memory_space=pl.ANY)
    dma = pltpu.SemaphoreType.DMA
    made = pl.pallas_call(
        functools.partial(first_kernel, shards, splits),
        out_shape=(
            jax.ShapeDtypeStruct((2, 4) + tokens.shape, low),
            jax.ShapeDtypeStruct(cot.shape, low),
            jax.ShapeDtypeStruct((slow,) + pieces.shape, low),
            jax.ShapeDtypeStruct((slow,) + out_own.shape, low),
            jax.ShapeDtypeStruct(gate_pieces.shape, low),
            jax.ShapeDtypeStruct(pieces.shape, low),
        ),
        in_specs=[any_space] * 5,
        out_specs=(any_space,) * 6,
        scratch_shapes=[
            dma((2, 2)),
            dma((2, 2)),
            dma((2, 10)),
            dma((2, 8)),
            dma((2, 8)),
            dma,
            dma((2, slow - 1)),
            dma((2, slow)),
        ],
        compiler_params=pltpu.CompilerParams(
            collective_id=identity, has_side_effects=True, vmem_limit_bytes=8 << 20
        ),
        cost_estimate=pl.CostEstimate(flops=0, bytes_accessed=200 << 20, transcendentals=0),
    )(tokens, cot, pieces, out_own, gate_pieces)
    return made[:5]


class GroupScatter:
    def __init__(self, me, parts, buffers, sems, steps):
        self.parts = parts
        self.core_in, self.kept, self.sent, self.came, self.held = buffers[:5]
        self.sent_last, self.came_last = buffers[5:]
        self.core_sems, self.kept_sems, self.one_sems, self.last_sems = sems
        self.core, self.across, self.beside = member(me, 2), member(me, 4), member(me, 1)
        self.size = parts.shape[3] // steps
        self.steps = steps

    def window(self, k):
        return slice(k * self.size, (k + 1) * self.size)

    def to_core(self, k, j):
        return remote(
            self.parts.at[:, 2 * j + 1, :, self.window(k)],
            self.core_in.at[:, j, :, self.window(k)],
            (self.core_sems.at[0, k, j], self.core_sems.at[1, k, j]),
            self.core,
        )

    def keep(self, k, j):
        return pltpu.make_async_copy(
            self.parts.at[:, 2 * j, :, self.window(k)],
            self.kept.at[:, j, :, self.window(k)],
            self.kept_sems.at[k, j],
        )

    def first(self, k, half):
        return remote(
            self.sent.at[half, :, self.window(k)],
            self.came.at[half, :, self.window(k)],
            (self.one_sems.at[0, k, half], self.one_sems.at[1, k, half]),
            (self.beside, self.across)[half],
        )

    def second(self, k, half):
        return remote(
            self.sent_last.at[half, self.window(k)],
            self.came_last.at[half, self.window(k)],
            (self.last_sems.at[0, k, half], self.last_sems.at[1, k, half]),
            (self.across, self.beside)[half],
        )

    def start(self):
        for k in range(self.steps):
            for j in (0, 1):
                self.to_core(k, j).start()
                self.keep(k, j).start()

    def send_first(self, k):
        wide = jnp.float32
        rows = self.window(k)
        for j in (0, 1):
            self.keep(k, j).wait()
            self.to_core(k, j).wait_recv()
        for half in (0, 1):
            for other in (0, 1):
                at = (1, other) if half == 0 else (other, 1)
                both = self.kept[at[0], at[1], half, rows].astype(wide)
                both = both + self.core_in[at[0], at[1], half, rows].astype(wide)
                self.sent[half, other, rows] = both.astype(jnp.bfloat16)
            self.first(k, half).start()
        for half in (0, 1):
            for other in (0, 1):
                at = (0, other) if half == 0 else (other, 0)
                both = self.kept[at[0], at[1], half, rows].astype(wide)
                self.held[half, other, rows] = both + self.core_in[at[0], at[1], half, rows].astype(
                    wide
                )

    def send_second(self, k):
        wide = jnp.float32
        rows = self.window(k)
        for half in (0, 1):
            self.first(k, half).wait_recv()
            both = self.held[half, 1, rows] + self.came[half, 1, rows].astype(wide)
            self.sent_last[half, rows] = both.astype(jnp.bfloat16)
            self.second(k, half).start()
            self.held[half, 0, rows] = self.held[half, 0, rows] + self.came[half, 0, rows].astype(
                wide
            )

    def total(self, k, half):
        self.second(k, half).wait_recv()
        rows = self.window(k)
        return self.held[half, 0, rows] + self.came_last[half, rows].astype(jnp.float32)

    def finish(self):
        for k in range(self.steps):
            for j in (0, 1):
                self.to_core(k, j).wait_send()
            for half in (0, 1):
                self.first(k, half).wait_send()
                self.second(k, half).wait_send()


def scatter_scratch(rows, width, steps):
    low, wide = jnp.bfloat16, jnp.float32
    dma = pltpu.SemaphoreType.DMA
    return [
        pltpu.VMEM((2, 2, 2, rows, width), low),
        pltpu.VMEM((2, 2, 2, rows, width), low),
        pltpu.VMEM((2, 2, rows, width), low),
        pltpu.VMEM((2, 2, rows, width), low),
        pltpu.VMEM((2, 2, rows, width), wide),
        pltpu.VMEM((2, rows, width), low),
        pltpu.VMEM((2, rows, width), low),
        dma((2, steps, 2)),
        dma((steps, 2)),
        dma((2, steps, 2)),
        dma((2, steps, 2)),
    ]


def reordered(rows, slow, back):
    each = rows.shape[1] // (4 * slow)
    if back:
        starts = [s * 4 + dp for dp in range(4) for s in range(slow)]
    else:
        starts = [dp * slow + s for s in range(slow) for dp in range(4)]
    return jnp.concatenate([rows[:, i * each : (i + 1) * each] for i in starts], 1)


def turn_kernel(slow, steps, backward, parts, gain, *refs):
    if backward:
        residual, cot, result, gain_grad, rows = refs[:5]
        scratch = refs[5:]
    else:
        tokens, result, rows = refs[:3]
        scratch = refs[3:]
    own, own_sems, group_sems = scratch[:3]
    me = (lax.axis_index("dp"), lax.axis_index("ctx"))
    greet(me, [member(me, by) for by in (1, 2, 4)], [])
    scatter = GroupScatter(me, parts, scratch[3:10], scratch[10:], steps)
    gathers = [GroupGather(me, rows, group_sems.at[k], own, scatter.window(k)) for k in range(steps)]
    scatter.start()
    for k in range(steps):
        scatter.send_first(k)
    for k in range(steps):
        scatter.send_second(k)
    for k in range(steps):
        span = scatter.window(k)
        for half in (0, 1):
            total = scatter.total(k, half)
            if backward:
                values = residual[half, span]
                factor = lax.rsqrt(jnp.mean(values * values, -1, keepdims=True) + norm_eps)
                normed = values * factor
                total = reordered(total, slow, True)
                part = jnp.sum(total * normed, 0, keepdims=True)
                if k == 0 and half == 0:
                    gain_grad[...] = part
                else:
                    gain_grad[...] += part
                back = total * gain[...]
                back = factor * (back - normed * jnp.mean(back * normed, -1, keepdims=True))
                back = cot[half, span].astype(jnp.float32) + back
                result[half, span] = back
                own[half, span] = back.astype(jnp.bfloat16)
            else:
                values = tokens[half, span].astype(jnp.float32) + total
                factor = lax.rsqrt(jnp.mean(values * values, -1, keepdims=True) + norm_eps)
                result[half, span] = values
                own[half, span] = reordered(values * factor * gain[...], slow, False).astype(
                    jnp.bfloat16
                )
        gathers[k].start()
        keep = pltpu.make_async_copy(own.at[:, span], rows.at[0, 0, :, span], own_sems.at[k])
        keep.start()
    for k in range(steps):
        gathers[k].pass_on()
    for k in range(steps):
        gathers[k].finish()
        span = scatter.window(k)
        pltpu.make_async_copy(own.at[:, span], rows.at[0, 0, :, span], own_sems.at[k]).wait()
    scatter.finish()


def turn(parts, gain, rows_in, slow, backward, identity):
    low, wide = jnp.bfloat16, jnp.float32
    dma = pltpu.SemaphoreType.DMA
    rows, width = parts.shape[3:]
    steps = 2
    any_space = pl.BlockSpec(memory_space=pl.ANY)
    vmem = pl.BlockSpec(memory_space=pltpu.VMEM)
    shapes = [jax.ShapeDtypeStruct((2, rows, width), wide)]
    if backward:
        shapes.append(jax.ShapeDtypeStruct((1, width), wide))
    return pl.pallas_call(
        functools.partial(turn_kernel, slow, steps, backward),
        out_shape=tuple(shapes) + (jax.ShapeDtypeStruct((2, 4, 2, rows, width), low),),
        in_specs=[any_space, vmem] + [vmem] * len(rows_in),
        out_specs=tuple([vmem] * len(shapes) + [any_space]),
        scratch_shapes=[pltpu.VMEM((2, rows, width), low), dma((steps,)), dma((steps, 2, 10))]
        + scatter_scratch(rows, width, steps),
        compiler_params=pltpu.CompilerParams(
            collective_id=identity, has_side_effects=True, vmem_limit_bytes=48 << 20
        ),
        cost_estimate=pl.CostEstimate(flops=0, bytes_accessed=250 << 20, transcendentals=0),
    )(parts, gain, *rows_in)


class LineSum:
    def __init__(self, me, slow, parts, buffers, sems):
        self.parts = parts
        self.kept, self.arrived = buffers
        self.sems, self.own_sem = sems
        self.slot = me[1] // 2
        self.slow = slow
        self.line = [(me[0], me[1] ^ (2 * by)) for by in range(1, slow)]

    def hop(self, by):
        sems = (self.sems.at[0, by - 1], self.sems.at[1, by - 1])
        return remote(
            self.parts.at[self.slot ^ by], self.arrived.at[by - 1], sems, self.line[by - 1]
        )

    def own(self):
        return pltpu.make_async_copy(self.parts.at[self.slot], self.kept, self.own_sem)

    def start(self):
        for by in range(1, self.slow):
            self.hop(by).start()
        self.own().start()

    def total(self):
        self.own().wait()
        value = self.kept[...].astype(jnp.float32)
        for by in range(1, self.slow):
            self.hop(by).wait_recv()
            value = value + self.arrived[by - 1].astype(jnp.float32)
        return value

    def finish(self):
        for by in range(1, self.slow):
            self.hop(by).wait_send()


def line_scratch(shape, kind, slow):
    dma = pltpu.SemaphoreType.DMA
    return [
        pltpu.VMEM(shape, kind),
        pltpu.VMEM((slow - 1,) + shape, kind),
        dma((2, slow - 1)),
        dma,
    ]


def last_kernel(shards, splits, steps, in_parts, out_parts, gate_parts, in_back, *refs):
    gain, gain_two_grad, tokens, back_rows = refs[:4]
    in_total, out_total, gate_total, gains_total, tokens_grad = refs[4:9]
    scratch = list(refs[9:])

    def take(count):
        taken = scratch[:count]
        del scratch[:count]
        return taken

    me = (lax.axis_index("dp"), lax.axis_index("ctx"))
    group, place = me
    slow = shards // 2
    slot, half = place // 2, place % 2
    owned = in_parts.shape[2]
    home = (group, half * slow + slot)
    movers = movers_of(me, splits, True)
    movers.append(((group, place % slow * 2 + place // slow), home))
    line = [(group, place ^ (2 * by)) for by in range(1, slow)]
    greet(me, [member(me, by) for by in range(1, 8)] + line, movers)
    one = take(11)
    back_sum = GroupScatter(me, in_back, one[:7], one[7:], steps)
    line_in = take(4)
    line_out = take(4)
    line_gains = take(4)
    in_done, out_done, gains_own, gains_done, made_one, gain_grad = take(6)
    in_sems, gate_sems, gains_sems, one_sems, home_sems = take(5)
    in_line = LineSum(me, slow, in_parts, line_in[:2], line_in[2:])
    out_line = LineSum(me, slow, out_parts, line_out[:2], line_out[2:])
    gains_line = LineSum(me, slow, gains_own, line_gains[:2], line_gains[2:])
    in_swap = GroupExchange(me, in_done, in_total, in_sems)
    gate_swap = GroupExchange(me, gate_parts, gate_total, gate_sems)
    gains_swap = GroupExchange(me, gains_done, gains_total, gains_sems)
    move_grad = Moves(me, splits, made_one, tokens_grad, one_sems, True)
    back_sum.start()
    in_line.start()
    out_line.start()
    for k in range(steps):
        back_sum.send_first(k)
    for k in range(steps):
        back_sum.send_second(k)
    gate_swap.start()
    for k in range(steps):
        span = back_sum.window(k)
        for part in (0, 1):
            total = back_sum.total(k, part)
            values = tokens[part, span].astype(jnp.float32)
            normed, factor = norm_parts(values)
            grad = jnp.sum(total * normed, 0, keepdims=True)
            if k == 0 and part == 0:
                gain_grad[...] = grad
            else:
                gain_grad[...] += grad
            value = back_rows[part, span] + norm_back(total * gain[...], normed, factor)
            made_one[part, span] = value.astype(jnp.bfloat16)
    move_grad.start()
    gains_own[...] = jnp.zeros_like(gains_own)
    for dp in range(4):
        for s in range(slow):
            for side in range(2):
                at = ((dp * slow + s) * 2 + side) * owned
                index = 2 * dp + side
                gains_own[s, index, 0:1, 0:owned] = gain_grad[:, at : at + owned]
                gains_own[s, index, 0:1, owned : 2 * owned] = gain_two_grad[:, at : at + owned]
    gains_line.start()
    in_done[...] = in_line.total().astype(jnp.bfloat16)
    in_swap.start()
    gains_done[...] = gains_line.total()
    gains_swap.start()
    out_done[...] = out_line.total().astype(jnp.bfloat16)
    to_home = (me, out_done, out_total, home, home_sems.at[0], home_sems.at[1])
    move_start(*to_home)
    pltpu.make_async_copy(out_done, out_total, home_sems.at[1]).wait()
    move_sent(*to_home)
    for swap in (in_swap, gate_swap, gains_swap):
        swap.finish()
    move_grad.wait_recv()
    move_grad.finish()
    for part in (in_line, out_line, gains_line, back_sum):
        part.finish()


def last_sums(in_parts, out_parts, gate_parts, in_back, others, shards, splits, identity):
    low, wide = jnp.bfloat16, jnp.float32
    slow = shards // 2
    steps = 2
    any_space = pl.BlockSpec(memory_space=pl.ANY)
    vmem = pl.BlockSpec(memory_space=pltpu.VMEM)
    dma = pltpu.SemaphoreType.DMA
    rows, width = in_back.shape[3:]
    gains_shape = (8, 8, 128)
    moved = jax.ShapeDtypeStruct((2, rows, width), low)
    return pl.pallas_call(
        functools.partial(last_kernel, shards, splits, steps),
        out_shape=(
            jax.ShapeDtypeStruct(in_parts.shape[1:], low),
            jax.ShapeDtypeStruct(out_parts.shape[1:], low),
            jax.ShapeDtypeStruct(gate_parts.shape, low),
            jax.ShapeDtypeStruct(gains_shape, wide),
            moved,
        ),
        in_specs=[any_space] * 4 + [vmem] * 4,
        out_specs=(any_space,) * 5,
        scratch_shapes=scatter_scratch(rows, width, steps)
        + line_scratch(in_parts.shape[1:], low, slow)
        + line_scratch(out_parts.shape[1:], low, slow)
        + line_scratch(gains_shape, wide, slow)
        + [
            pltpu.VMEM(in_parts.shape[1:], low),
            pltpu.VMEM(out_parts.shape[1:], low),
            pltpu.VMEM((slow,) + gains_shape, wide),
            pltpu.VMEM(gains_shape, wide),
            pltpu.VMEM(moved.shape, low),
            pltpu.VMEM((1, width), wide),
            dma((2, 8)),
            dma((2, 8)),
            dma((2, 8)),
            dma((2, 2)),
            dma((2,)),
        ],
        compiler_params=pltpu.CompilerParams(
            collective_id=identity, has_side_effects=True, vmem_limit_bytes=56 << 20
        ),
        cost_estimate=pl.CostEstimate(flops=0, bytes_accessed=300 << 20, transcendentals=0),
    )(in_parts, out_parts, gate_parts, in_back, *others)


def position_tables(blocks, rows):
    frequency = rope_base ** (-(np.arange(HEAD // 2) * 2.0 / HEAD))
    angles = np.arange(blocks * rows).reshape(blocks, rows, 1) * frequency
    cos, sin = np.cos(angles), np.sin(angles)
    cosine = np.concatenate([cos, cos, cos, cos], 2)
    sines = np.concatenate([-sin, sin, -sin, sin], 2)
    return jnp.asarray(cosine, jnp.float32), jnp.asarray(sines, jnp.float32)


def attend(order, where, qkv, tables, cot, q_heads, kv_heads, identity):
    seqs, length, cols = qkv.shape
    blocks = order.shape[0]
    rows = length // blocks
    whole = pl.BlockSpec(memory_space=pltpu.VMEM)
    small = pl.BlockSpec(memory_space=pltpu.SMEM)
    any_space = pl.BlockSpec(memory_space=pl.ANY)
    return pl.pallas_call(
        functools.partial(attend_kernel, q_heads, kv_heads, 256),
        out_shape=(
            jax.ShapeDtypeStruct((seqs, blocks, rows, q_heads * HEAD), jnp.bfloat16),
            jax.ShapeDtypeStruct((seqs, q_heads, length), jnp.float32),
            jax.ShapeDtypeStruct((seqs, length, cols), jnp.bfloat16),
            jax.ShapeDtypeStruct((2, 4) + cot.shape, cot.dtype),
        ),
        in_specs=[small, small, whole, whole, whole, any_space],
        out_specs=(whole, whole, whole, any_space),
        scratch_shapes=[
            pltpu.VMEM((blocks, rows, q_heads * HEAD), jnp.bfloat16),
            pltpu.SemaphoreType.DMA((2, 10)),
            pltpu.SemaphoreType.DMA,
        ],
        compiler_params=pltpu.CompilerParams(
            collective_id=identity, has_side_effects=True, vmem_limit_bytes=40 << 20
        ),
        cost_estimate=pl.CostEstimate(
            flops=2 * seqs * length * length * q_heads * HEAD,
            bytes_accessed=100 << 20,
            transcendentals=seqs * length * length * q_heads // 2,
        ),
    )(order, where, qkv.reshape(seqs, blocks, rows, cols), *tables, cot)


def attend_back(
    order, where, kept, back, lse, tables, out_rows, residual, q_heads, kv_heads, splits, identity
):
    seqs, length, cols = kept.shape
    blocks = order.shape[0]
    block = length // blocks
    group = q_heads // kv_heads
    rows, width = out_rows.shape[3:]
    steps = 2
    whole = pl.BlockSpec(memory_space=pltpu.VMEM)
    small = pl.BlockSpec(memory_space=pltpu.SMEM)
    any_space = pl.BlockSpec(memory_space=pl.ANY)
    return pl.pallas_call(
        functools.partial(attend_back_kernel, q_heads, kv_heads, 256, splits, steps),
        out_shape=(
            jax.ShapeDtypeStruct((seqs, blocks, block, cols), jnp.bfloat16),
            jax.ShapeDtypeStruct((2, rows, width), jnp.bfloat16),
        ),
        in_specs=[small, small] + [whole] * 5 + [any_space, whole],
        out_specs=(whole, any_space),
        scratch_shapes=[
            pltpu.VMEM((length, q_heads * HEAD), jnp.bfloat16),
            pltpu.VMEM((blocks, block, cols), jnp.float32),
            pltpu.VMEM((group, length), jnp.float32),
            pltpu.VMEM((group * HEAD, length), jnp.float32),
            pltpu.VMEM((2, rows, width), jnp.bfloat16),
            pltpu.SemaphoreType.DMA((2, 2)),
        ]
        + scatter_scratch(rows, width, steps),
        compiler_params=pltpu.CompilerParams(
            collective_id=identity, has_side_effects=True, vmem_limit_bytes=56 << 20
        ),
        cost_estimate=pl.CostEstimate(
            flops=7 * seqs * length * length * q_heads * HEAD,
            bytes_accessed=100 << 20,
            transcendentals=seqs * length * length * q_heads // 2,
        ),
    )(
        order,
        where,
        kept,
        back.reshape(seqs, blocks, block, -1),
        lse,
        *tables,
        out_rows,
        residual,
    )


def gate_update_kernel(slow, step_rate, grad, weight, first, second, new_first, new_second, new):
    units = grad.shape[2] // slow
    pieces = [grad[half, :, s * units : (s + 1) * units] for s in range(slow) for half in (0, 1)]
    gradient = jnp.concatenate(pieces, 1).astype(jnp.float32)
    new_first[...], new_second[...], new[...] = adam_update(
        weight[...], gradient, first[...], second[...], step_rate, weight_decay
    )


def gate_update(grad, weight, first, second, slow, step_rate):
    rows, width = weight.shape
    block = pl.BlockSpec((rows, width // 8), lambda side, dp: (0, 4 * side + dp))
    piece = pl.BlockSpec((2, rows, width // 16), lambda side, dp: (dp, 0, side))
    return pl.pallas_call(
        functools.partial(gate_update_kernel, slow, step_rate),
        grid=(2, 4),
        out_shape=(jax.ShapeDtypeStruct(weight.shape, jnp.float32),) * 3,
        in_specs=[piece, block, block, block],
        out_specs=(block,) * 3,
        compiler_params=pltpu.CompilerParams(vmem_limit_bytes=32 << 20),
    )(grad, weight, first, second)


def local(
    tokens,
    cotangent,
    block_order,
    attention_in,
    attention_out,
    gate_up,
    down_matrix,
    gains,
    mean_attention_in,
    mean_attention_out,
    mean_gate_up,
    mean_down,
    mean_gains,
    square_attention_in,
    square_attention_out,
    square_gate_up,
    square_down,
    square_gains,
):
    seq_count, shard_rows, width = tokens.shape
    shards = lax.axis_size("ctx")
    slow = shards // 2
    mine = lax.axis_index("dp")
    beside = lax.axis_index("ctx") % 2
    low = jnp.bfloat16
    owned = attention_in.shape[0]
    hidden_units = gate_up.shape[1] // 2
    part_hidden = hidden_units // 8
    units = down_matrix.shape[0]
    part_q = HEADS * HEAD // 8
    part_k = KV_HEADS * HEAD // 8
    part_cols = part_q + 2 * part_k
    count = seq_count * shard_rows
    together = 8 * count
    spread = shards // (4 * seq_count)
    splits = max(1, slow // 8)
    seqs = 2 // spread if spread < 2 else 1
    length = shards * shard_rows
    q_heads = HEADS // 8 // splits
    kv_heads = KV_HEADS // 8

    in_low = attention_in.astype(low)
    gains_row = jnp.pad(gains.astype(low).reshape(1, -1), ((0, 15), (0, part_cols - 2 * owned)))
    pieces = jnp.stack(
        [
            jnp.concatenate(
                [
                    jnp.concatenate(
                        [
                            in_low[:, i * part_q : (i + 1) * part_q],
                            in_low[:, 8 * part_q + i * part_k :][:, :part_k],
                            in_low[:, 8 * (part_q + part_k) + i * part_k :][:, :part_k],
                        ],
                        1,
                    ),
                    gains_row,
                ]
            )
            for i in range(8)
        ]
    )
    gate_low = gate_up.astype(low)
    gate_pieces = jnp.stack(
        [
            jnp.concatenate(
                [
                    gate_low[:, side * hidden_units + (dp * shards + 2 * s + half) * units :][
                        :, :units
                    ]
                    for side in range(2)
                    for s in range(slow)
                ],
                1,
            )
            for dp in range(4)
            for half in range(2)
        ]
    )
    tokens_all, cot_own, in_all, w_out, gate_rows = first_exchange(
        tokens, cotangent, pieces, attention_out.astype(low), gate_pieces, shards, spread, 1
    )
    in_all = in_all.reshape(slow, 4, 2, owned + 16, part_cols).swapaxes(0, 1)
    w_in = in_all[:, :, :, :owned].reshape(width, part_cols)
    w_out = w_out.reshape(part_q, width)
    gains_all = in_all[:, :, :, owned, : 2 * owned].reshape(-1, 2, owned)
    gains_all = gains_all.astype(jnp.float32).swapaxes(0, 1).reshape(2, width)
    gain_one, gain_two = gains_all[0], gains_all[1]
    w_gate = gather_line(gate_rows.reshape(8 * owned, 2 * part_hidden))

    normed_all, _ = norm_parts(tokens_all.reshape(together, width).astype(jnp.float32))
    input_one = (normed_all * gain_one).astype(low)
    qkv = dot_nn(input_one, w_in)
    orders = block_order.reshape(2 * splits if spread > 1 else 1, 4, -1)
    slot_order = jnp.concatenate(
        [
            orders[(2 * s + (beside ^ i)) if spread > 1 else 0, part_owner(mine ^ j)]
            for s in range(splits)
            for i in range(2 // seqs)
            for j in range(4)
        ]
    )
    tables = position_tables(slot_order.shape[0], length // slot_order.shape[0])
    groups = [
        [2 * (s * splits + g) + half for g in range(splits)]
        for s in range(slow // splits)
        for half in (0, 1)
    ]

    def split_heads(values, widths, copies):
        parts = []
        start = 0
        for each, repeat in zip(widths, copies):
            kinds = splits // repeat
            piece = values[:, start : start + kinds * each].reshape(-1, kinds, each)
            parts.append(jnp.repeat(piece.swapaxes(0, 1), repeat, axis=0))
            start += kinds * each
        sent = jnp.concatenate(parts, 2)
        got = lax.all_to_all(sent, "ctx", 0, 0, axis_index_groups=groups, tiled=True)
        return got.reshape(length, -1)

    def join_heads(values):
        sent = values.reshape(splits, together, -1)
        return lax.all_to_all(sent, "ctx", 0, 0, axis_index_groups=groups, tiled=True)

    q_width, k_width = q_heads * HEAD, kv_heads * HEAD
    if splits > 1:
        qkv = split_heads(qkv, (q_width, k_width, k_width), (1, splits, splits))
    qkv = qkv.reshape(seqs, length, -1)
    blocks = slot_order.shape[0]
    slot_where = jnp.sum(
        jnp.where(
            slot_order[None, :] == jnp.arange(blocks, dtype=jnp.int32)[:, None],
            jnp.arange(blocks, dtype=jnp.int32)[None, :],
            0,
        ),
        1,
    )
    attended, lse, kept, back_all = attend(
        slot_order, slot_where, qkv, tables, cot_own, q_heads, kv_heads, 2
    )
    cot_rows = cot_own
    back_all = back_all.reshape(together, width)
    if splits > 1:
        attended = join_heads(attended.reshape(length, q_width)).swapaxes(0, 1)
    attended = attended.reshape(together, part_q)

    def parts(values):
        return values.astype(low).reshape((2, 4) + tokens.shape)

    residual_rows, input_two = turn(
        parts(dot_nn(attended, w_out)), gain_two[None], [tokens_all[0, 0]], slow, False, 3
    )
    input_two = input_two.reshape(together, width)
    w_down = gather_line((down_matrix + 0.0 * residual_rows[0, 0, 0]).astype(low))
    gate_both = dot_nn(input_two, w_gate)
    gate_part = gate_both[:, :part_hidden]
    up_part = gate_both[:, part_hidden:]
    sigmoid_gate = jax.nn.sigmoid(gate_part)
    active = gate_part * sigmoid_gate
    hidden = (active * up_part).astype(low)
    grad_down = dot_tn(hidden, back_all) + 0.0 * w_down[0, 0].astype(jnp.float32)
    down_sum = sum_line(grad_down.astype(low)).astype(jnp.float32)
    back_hidden = dot_nt(back_all, w_down)
    back_gate = back_hidden * up_part * sigmoid_gate * (1.0 + gate_part * (1.0 - sigmoid_gate))
    back_upper = back_hidden * active
    back_gate_up = jnp.concatenate([back_gate, back_upper], 1).astype(low)
    gate_low = sum_line(dot_tn(input_two, back_gate_up).astype(low))
    back_rows, grad_gain_two, back_residual_all = turn(
        parts(dot_nt(back_gate_up, w_gate)),
        gain_two[None],
        [residual_rows, cot_rows],
        slow,
        True,
        4,
    )
    back_residual_all = back_residual_all.reshape(together, width)
    grad_out = dot_tn(attended, back_residual_all).astype(low)
    back_attended = dot_nt(back_residual_all, w_out).astype(low)
    if splits > 1:
        back_attended = split_heads(back_attended, (q_width,), (1,))
    back_projected, block_out = attend_back(
        slot_order,
        slot_where,
        kept,
        back_attended.reshape(seqs, length, -1),
        lse,
        tables,
        parts(dot_nn(hidden, w_down)),
        residual_rows,
        q_heads,
        kv_heads,
        spread,
        6,
    )
    if splits > 1:
        back_projected = join_heads(back_projected.reshape(length, -1)).astype(jnp.float32)
        back_projected = jnp.concatenate(
            [
                back_projected[..., :q_width].swapaxes(0, 1).reshape(together, part_q),
                back_projected[..., q_width:].sum(0),
            ],
            1,
        ).astype(low)
    back_projected = back_projected.reshape(together, part_cols)
    grad_in = dot_tn(input_one, back_projected).astype(low)
    grad_in = grad_in.reshape(4, slow, 2 * owned, part_cols).swapaxes(0, 1)
    in_sum, out_sum, gate_sum, gains_sum, tokens_grad = last_sums(
        grad_in.reshape(slow, 8, owned, part_cols),
        grad_out.reshape(slow, owned, width),
        gate_low.reshape(8, owned, 2 * part_hidden),
        parts(dot_nt(back_projected, w_in)),
        [gain_one[None], grad_gain_two, tokens_all[0, 0], back_rows],
        shards,
        spread,
        5,
    )
    tokens_grad = tokens_grad.astype(jnp.float32)
    out_sum = out_sum.astype(jnp.float32)
    gains_sum = gains_sum[:, 0, : 2 * owned].reshape(8, 2, owned).sum(0)
    cuts = ((0, part_q), (part_q, part_q + part_k), (part_q + part_k, part_cols))
    in_sum = jnp.concatenate(
        [in_sum[i, :, first:last] for first, last in cuts for i in range(8)], 1
    ).astype(jnp.float32)
    new_in = adam_update(
        attention_in,
        in_sum,
        mean_attention_in,
        square_attention_in,
        input_boost * D ** (-0.5),
        weight_decay,
    )
    new_out = adam_update(
        attention_out,
        out_sum,
        mean_attention_out,
        square_attention_out,
        (HEADS * HEAD // 32) ** (-0.5),
        weight_decay,
    )
    new_gate = gate_update(
        gate_sum, gate_up, mean_gate_up, square_gate_up, slow, D ** (-0.5)
    )
    new_down = adam_update(
        down_matrix, down_sum, mean_down, square_down, FF ** (-0.5), weight_decay
    )
    new_gain = adam_update(gains, gains_sum, mean_gains, square_gains, gain_rate, 0.0)
    return (
        block_out,
        tokens_grad,
        new_in[0],
        new_in[1],
        new_in[2],
        new_out[0],
        new_out[1],
        new_out[2],
        new_gate[0],
        new_gate[1],
        new_gate[2],
        new_down[0],
        new_down[1],
        new_down[2],
        new_gain[0],
        new_gain[1],
        new_gain[2],
    )


def solution(mesh):
    in_specs = (
        P("dp", "ctx", None),
        P("dp", "ctx", None),
        P(),
        P(("dp", "ctx"), None),
        P(("dp", "ctx"), None),
        P(("dp", "ctx"), None),
        P(("dp", "ctx"), None),
        P(None, ("dp", "ctx")),
        P(("dp", "ctx"), None),
        P(("dp", "ctx"), None),
        P(("dp", "ctx"), None),
        P(("dp", "ctx"), None),
        P(None, ("dp", "ctx")),
        P(("dp", "ctx"), None),
        P(("dp", "ctx"), None),
        P(("dp", "ctx"), None),
        P(("dp", "ctx"), None),
        P(None, ("dp", "ctx")),
    )
    out_specs = (
        P("dp", "ctx", None),
        P("dp", "ctx", None),
        P(("dp", "ctx"), None),
        P(("dp", "ctx"), None),
        P(("dp", "ctx"), None),
        P(("dp", "ctx"), None),
        P(("dp", "ctx"), None),
        P(("dp", "ctx"), None),
        P(("dp", "ctx"), None),
        P(("dp", "ctx"), None),
        P(("dp", "ctx"), None),
        P(("dp", "ctx"), None),
        P(("dp", "ctx"), None),
        P(("dp", "ctx"), None),
        P(None, ("dp", "ctx")),
        P(None, ("dp", "ctx")),
        P(None, ("dp", "ctx")),
    )
    return jax.shard_map(local, mesh=mesh, in_specs=in_specs, out_specs=out_specs, check_vma=False)
```

```python
import functools

import jax
import jax.numpy as jnp
import numpy as np
from jax import lax
from jax.experimental import pallas as pl
from jax.experimental.pallas import tpu as pltpu
from jax.sharding import PartitionSpec as P

D = 2048
HEADS = 32
KV_HEADS = 8
HEAD = 64
FF = 8192
STEP = 5


norm_eps = 1e-05
rope_base = 500000.0
beta_one = 0.9
beta_two = 0.95
gain_rate = 1.25
input_boost = 2.5
weight_decay = 0.1
adam_eps = 1e-08
masked_score = -1e30


def norm_parts(values):
    factor = lax.rsqrt(jnp.mean(values * values, -1, keepdims=True) + norm_eps)
    return (values * factor, factor)


def norm_back(back_normed, normed, factor):
    return factor * (back_normed - normed * jnp.mean(back_normed * normed, -1, keepdims=True))


def adam_update(weight, gradient, first_moment, second_moment, step_rate, decay_rate):
    first_new = beta_one * first_moment + (1.0 - beta_one) * gradient
    second_new = beta_two * second_moment + (1.0 - beta_two) * gradient * gradient
    update = (
        first_new
        / (1.0 - beta_one**STEP)
        / (jnp.sqrt(second_new / (1.0 - beta_two**STEP)) + adam_eps)
    )
    return (first_new, second_new, weight - step_rate * (update + decay_rate * weight))


def line_groups(shards):
    return [[2 * s + half for s in range(shards // 2)] for half in (0, 1)]


def gather_line(rows):
    return lax.all_gather(
        rows, "ctx", axis=0, tiled=True, axis_index_groups=line_groups(lax.axis_size("ctx"))
    )


def sum_line(gradient):
    return lax.psum_scatter(
        gradient,
        "ctx",
        scatter_dimension=0,
        tiled=True,
        axis_index_groups=line_groups(lax.axis_size("ctx")),
    )


def dot_nn(a, b):
    return lax.dot_general(a, b, (((1,), (0,)), ((), ())), preferred_element_type=jnp.float32)


def dot_nt(a, b):
    return lax.dot_general(a, b, (((1,), (1,)), ((), ())), preferred_element_type=jnp.float32)


def dot_tn(a, b):
    return lax.dot_general(a, b, (((0,), (0,)), ((), ())), preferred_element_type=jnp.float32)


def causal_keep(tile):
    keys = lax.broadcasted_iota(jnp.int32, (tile, tile), 0)
    queries = lax.broadcasted_iota(jnp.int32, (tile, tile), 1)
    return keys <= queries


def turn_group(values, cos, sin, forward):
    lanes = lax.broadcasted_iota(jnp.int32, values.shape, 1)
    other = jnp.where(
        lanes % HEAD < HEAD // 2,
        pltpu.roll(values, 2 * HEAD - HEAD // 2, 1),
        pltpu.roll(values, HEAD // 2, 1),
    )
    if forward:
        return values * cos + other * sin
    return values * cos - other * sin


def turn_columns(values, start, turned_cols, cos, sin, forward):
    if start >= turned_cols:
        return values
    turned = turn_group(values, cos, sin, forward)
    if start + 2 * HEAD <= turned_cols:
        return turned
    lanes = lax.broadcasted_iota(jnp.int32, values.shape, 1)
    return jnp.where(lanes < turned_cols - start, turned, values)


def attend_kernel(
    q_heads,
    kv_heads,
    tile,
    order_ref,
    where_ref,
    all_qkv_ref,
    cos_ref,
    sin_ref,
    cot,
    all_out_ref,
    all_lse_ref,
    all_kept_ref,
    cot_rows,
    made,
    group_sems,
    own_sem,
):
    me = (lax.axis_index("dp"), lax.axis_index("ctx"))
    greet(me, [member(me, by) for by in (1, 2, 4)], [])
    spread = GroupGather(me, cot_rows, group_sems, cot, slice(0, cot.shape[1]))
    own = pltpu.make_async_copy(cot, cot_rows.at[0, 0], own_sem)
    spread.start()
    own.start()
    count = all_qkv_ref.shape[0]
    for sequence in range(count):
        attend_sequence(
            q_heads,
            kv_heads,
            tile,
            order_ref,
            where_ref,
            all_qkv_ref.at[sequence],
            cos_ref,
            sin_ref,
            all_out_ref.at[sequence],
            all_lse_ref.at[sequence],
            all_kept_ref.at[sequence],
            made,
        )
        if sequence == 0:
            spread.pass_on()
    spread.finish()
    own.wait()


def attend_sequence(
    q_heads,
    kv_heads,
    tile,
    order_ref,
    where_ref,
    qkv_ref,
    cos_ref,
    sin_ref,
    out_ref,
    lse_ref,
    kept_ref,
    made,
):
    blocks, rows, cols = qkv_ref.shape
    length = blocks * rows
    group = q_heads // kv_heads
    q_cols, k_cols = q_heads * HEAD, kv_heads * HEAD
    scale = HEAD ** (-0.5)

    def take_block(i, _):
        start = pl.multiple_of(i * rows, rows)
        cos = cos_ref[i]
        sin = sin_ref[i]
        for c in range(0, cols, 2 * HEAD):
            values = qkv_ref[where_ref[i], :, c : c + 2 * HEAD]
            values = turn_columns(values, c, q_cols + k_cols, cos, sin, True)
            kept_ref[pl.ds(start, rows), c : c + 2 * HEAD] = values.astype(jnp.bfloat16)
        return 0

    lax.fori_loop(0, blocks, take_block, 0)
    keep = causal_keep(tile)
    for kv in range(kv_heads):
        k_at = q_cols + kv * HEAD
        v_at = q_cols + k_cols + kv * HEAD

        def query_step(i, _):
            q_start = pl.multiple_of(i * tile, tile)
            queries = [
                kept_ref[
                    pl.ds(q_start, tile), (kv * group + g) * HEAD : (kv * group + g + 1) * HEAD
                ]
                for g in range(group)
            ]

            def key_tile(j, carry, masked):
                k_start = pl.multiple_of(j * tile, tile)
                keys = kept_ref[pl.ds(k_start, tile), k_at : k_at + HEAD]
                values = kept_ref[pl.ds(k_start, tile), v_at : v_at + HEAD]
                result = []
                for g in range(group):
                    peak, total, weighted = carry[g]
                    scores = dot_nt(keys, queries[g]) * scale
                    if masked:
                        scores = jnp.where(keep, scores, masked_score)
                    new_peak = jnp.maximum(peak, jnp.max(scores, 0, keepdims=True))
                    weights = jnp.exp(scores - new_peak)
                    shrink = jnp.exp(peak - new_peak)
                    total = total * shrink + jnp.sum(weights, 0, keepdims=True)
                    weighted = weighted * shrink + dot_tn(values, weights.astype(jnp.bfloat16))
                    result.append((new_peak, total, weighted))
                return tuple(result)

            start = tuple(
                (
                    jnp.full((1, tile), masked_score, jnp.float32),
                    jnp.zeros((1, tile), jnp.float32),
                    jnp.zeros((HEAD, tile), jnp.float32),
                )
                for _ in range(group)
            )
            carry = lax.fori_loop(0, i, lambda j, c: key_tile(j, c, False), start)
            carry = key_tile(i, carry, True)
            for g in range(group):
                head = kv * group + g
                peak, total, weighted = carry[g]
                lse_ref[head : head + 1, pl.ds(q_start, tile)] = peak + jnp.log(total)
                made[pl.ds(i * (tile // rows), tile // rows), :, head * HEAD : (head + 1) * HEAD] = (
                    (weighted / total).T.astype(jnp.bfloat16).reshape(-1, rows, HEAD)
                )
            return 0

        lax.fori_loop(0, length // tile, query_step, 0)

    def give_block(i, _):
        out_ref[i] = made[order_ref[i]]
        return 0

    lax.fori_loop(0, blocks, give_block, 0)


def attend_back_kernel(
    q_heads,
    kv_heads,
    tile,
    splits,
    steps,
    order_ref,
    where_ref,
    all_kept_ref,
    all_back_ref,
    all_lse_ref,
    cos_ref,
    sin_ref,
    out_rows,
    residual,
    all_out_ref,
    block_out,
    *scratch,
):
    me = (lax.axis_index("dp"), lax.axis_index("ctx"))
    greet(me, [member(me, by) for by in (1, 2, 4)], movers_of(me, splits, True))
    work, scratch = scratch[:4], scratch[4:]
    made, move_sems = scratch[:2]
    scatter = GroupScatter(me, out_rows, scratch[2:9], scratch[9:], steps)
    move = Moves(me, splits, made, block_out, move_sems, True)

    def one():
        for k in range(steps):
            scatter.send_first(k)

    def two():
        for k in range(steps):
            scatter.send_second(k)

    def three():
        for k in range(steps):
            span = scatter.window(k)
            for part in (0, 1):
                value = residual[part, span] + scatter.total(k, part)
                made[part, span] = value.astype(jnp.bfloat16)
        move.start()

    tasks = [one, two, three]

    def pause():
        if tasks:
            tasks.pop(0)()

    scatter.start()
    for sequence in range(all_kept_ref.shape[0]):
        attend_back_sequence(
            q_heads,
            kv_heads,
            tile,
            pause,
            order_ref,
            where_ref,
            all_kept_ref.at[sequence],
            all_back_ref.at[sequence],
            all_lse_ref.at[sequence],
            cos_ref,
            sin_ref,
            all_out_ref.at[sequence],
            *work,
        )
        pause()
    while tasks:
        pause()
    move.wait_recv()
    move.finish()
    scatter.finish()


def attend_back_sequence(
    q_heads,
    kv_heads,
    tile,
    pause,
    order_ref,
    where_ref,
    kept_ref,
    back_ref,
    lse_ref,
    cos_ref,
    sin_ref,
    out_ref,
    back_sorted,
    grad,
    delta_ref,
    dq_ref,
):
    length, cols = kept_ref.shape
    blocks, rows = back_ref.shape[:2]
    group = q_heads // kv_heads
    q_cols, k_cols = q_heads * HEAD, kv_heads * HEAD
    scale = HEAD ** (-0.5)
    tiles = length // tile

    def take_block(i, _):
        start = pl.multiple_of(i * rows, rows)
        back_sorted[pl.ds(start, rows), :] = back_ref[where_ref[i]]
        return 0

    lax.fori_loop(0, blocks, take_block, 0)
    keep = causal_keep(tile)
    for kv in range(kv_heads):
        k_at = q_cols + kv * HEAD
        v_at = q_cols + k_cols + kv * HEAD

        def load(i, g):
            start = pl.multiple_of(i * tile, tile)
            head = kv * group + g
            at = slice(head * HEAD, (head + 1) * HEAD)
            return (
                kept_ref[pl.ds(start, tile), at],
                back_sorted[pl.ds(start, tile), at],
                lse_ref[head : head + 1, pl.ds(start, tile)],
            )

        def load_kv(j):
            start = pl.multiple_of(j * tile, tile)
            return (
                kept_ref[pl.ds(start, tile), k_at : k_at + HEAD],
                kept_ref[pl.ds(start, tile), v_at : v_at + HEAD],
            )

        def tile_terms(keys, values, query, back, lse, masked):
            weights = jnp.exp(dot_nt(keys, query) * scale - lse)
            if masked:
                weights = jnp.where(keep, weights, 0.0)
            return weights, dot_nt(values, back)

        def delta_step(i, _):
            rows_i = [load(i, g) for g in range(group)]

            def one(j, carry, masked):
                keys, values = load_kv(j)
                result = []
                for g in range(group):
                    weights, back_weights = tile_terms(keys, values, *rows_i[g], masked)
                    result.append(carry[g] + jnp.sum(weights * back_weights, 0, keepdims=True))
                return tuple(result)

            carry = tuple(jnp.zeros((1, tile), jnp.float32) for _ in range(group))
            carry = lax.fori_loop(0, i, lambda j, c: one(j, c, False), carry)
            carry = one(i, carry, True)
            for g in range(group):
                delta_ref[g : g + 1, pl.ds(pl.multiple_of(i * tile, tile), tile)] = carry[g]
            return 0

        lax.fori_loop(0, tiles, delta_step, 0)
        if kv == 0:
            pause()
        dq_ref[...] = jnp.zeros_like(dq_ref)

        def key_step(j, _):
            keys, values = load_kv(j)

            def one(i, carry, masked):
                back_key, back_value = carry
                start = pl.multiple_of(i * tile, tile)
                for g in range(group):
                    query, back, lse = load(i, g)
                    weights, back_weights = tile_terms(keys, values, query, back, lse, masked)
                    delta = delta_ref[g : g + 1, pl.ds(start, tile)]
                    back_scores = (weights * (back_weights - delta)).astype(jnp.bfloat16)
                    back_key = back_key + dot_nn(back_scores, query)
                    back_value = back_value + dot_nn(weights.astype(jnp.bfloat16), back)
                    dq_ref[g * HEAD : (g + 1) * HEAD, pl.ds(start, tile)] += dot_tn(
                        keys, back_scores
                    )
                return back_key, back_value

            zero = jnp.zeros((tile, HEAD), jnp.float32)
            carry = one(j, (zero, zero), True)
            carry = lax.fori_loop(j + 1, tiles, lambda i, c: one(i, c, False), carry)
            span = pl.ds(j * (tile // rows), tile // rows)
            grad[span, :, k_at : k_at + HEAD] = (carry[0] * scale).reshape(-1, rows, HEAD)
            grad[span, :, v_at : v_at + HEAD] = carry[1].reshape(-1, rows, HEAD)
            return 0

        lax.fori_loop(0, tiles, key_step, 0)
        for g in range(group):
            head = kv * group + g
            turned = (dq_ref[g * HEAD : (g + 1) * HEAD, :] * scale).T
            grad[:, :, head * HEAD : (head + 1) * HEAD] = turned.reshape(-1, rows, HEAD)

    def give_block(i, _):
        cos = cos_ref[order_ref[i]]
        sin = sin_ref[order_ref[i]]
        for c in range(0, cols, 2 * HEAD):
            values = grad[order_ref[i], :, c : c + 2 * HEAD]
            values = turn_columns(values, c, q_cols + k_cols, cos, sin, False)
            out_ref[i, :, c : c + 2 * HEAD] = values.astype(jnp.bfloat16)
        return 0

    lax.fori_loop(0, blocks, give_block, 0)


MESH = pl.DeviceIdType.MESH


def part_owner(part):
    return part % 2 * 2 + part // 2


def sequence_target(group, place, second, splits):
    part = place // 2
    target = (part_owner(part % 4), (2 * group + second) * splits + part // 4)
    return target, place % 2


def token_target(group, place, half, splits):
    sequence = place // splits
    part = part_owner(group) + 4 * (place % splits)
    return (sequence // 2, 2 * part + half), sequence % 2


def remote(source, target, sems, device):
    return pltpu.make_async_remote_copy(
        src_ref=source,
        dst_ref=target,
        send_sem=sems[0],
        recv_sem=sems[1],
        device_id=device,
        device_id_type=MESH,
    )


def same(one, other):
    return jnp.logical_and(one[0] == other[0], one[1] == other[1])


def greet(me, peers, movers):
    barrier = pltpu.get_barrier_semaphore()
    for peer in peers:
        pl.semaphore_signal(barrier, inc=1, device_id=peer, device_id_type=MESH)
    expected = len(peers)
    for source, target in movers:

        @pl.when(jnp.logical_not(same(source, me)))
        def _():
            pl.semaphore_signal(barrier, inc=1, device_id=source, device_id_type=MESH)

        expected = expected + jnp.where(same(target, me), 0, 1)
    pl.semaphore_wait(barrier, expected)


def move_start(me, source, target, target_device, send, receive):
    here = same(target_device, me)

    @pl.when(here)
    def _():
        pltpu.make_async_copy(source, target, receive).start()

    @pl.when(jnp.logical_not(here))
    def _():
        remote(source, target, (send, receive), target_device).start()


def move_sent(me, source, target, target_device, send, receive):
    @pl.when(jnp.logical_not(same(target_device, me)))
    def _():
        remote(source, target, (send, receive), target_device).wait_send()


def member(me, by):
    return (me[0] ^ (by // 2), me[1] ^ (by % 2))


def group_index(device):
    return 2 * device[0] + device[1] % 2


class GroupExchange:
    def __init__(self, me, pieces, got, sems):
        self.me, self.pieces, self.got, self.sems = me, pieces, got, sems

    def hop(self, by):
        peer = member(self.me, by)
        sems = (self.sems.at[0, by - 1], self.sems.at[1, by - 1])
        return remote(
            self.pieces.at[group_index(peer)], self.got.at[group_index(self.me)], sems, peer
        )

    def own(self):
        mine = group_index(self.me)
        return pltpu.make_async_copy(self.pieces.at[mine], self.got.at[mine], self.sems.at[0, 7])

    def start(self):
        for by in range(1, 8):
            self.hop(by).start()
        self.own().start()

    def finish(self):
        self.own().wait()
        for by in range(1, 8):
            self.hop(by).wait()


class GroupGather:
    def __init__(self, me, rows, sems, own, window):
        self.rows, self.sems, self.own, self.window = rows, sems, own, window
        self.core, self.across, self.beside = member(me, 2), member(me, 4), member(me, 1)

    def hop(self, index):
        across, beside, core = self.across, self.beside, self.core
        source, i, j, half, device = (
            (None, 0, 2, 0, across),
            (None, 1, 0, 1, beside),
            (None, 1, 0, 0, beside),
            (None, 0, 2, 1, across),
            ((0, 2), 1, 2, 0, beside),
            ((1, 0), 1, 2, 1, across),
            (None, 0, 1, slice(0, 2), core),
            ((0, 2), 0, 3, slice(0, 2), core),
            ((1, 0), 1, 1, slice(0, 2), core),
            ((1, 2), 1, 3, slice(0, 2), core),
        )[index]
        if source is None:
            source = self.own.at[half, self.window]
        else:
            source = self.rows.at[source[0], source[1], half, self.window]
        target = self.rows.at[i, j, half, self.window]
        return remote(source, target, (self.sems.at[0, index], self.sems.at[1, index]), device)

    def start(self):
        for index in (0, 1, 2, 3, 6):
            self.hop(index).start()

    def pass_on(self):
        self.hop(0).wait_recv()
        self.hop(4).start()
        self.hop(1).wait_recv()
        self.hop(5).start()
        self.hop(3).wait_recv()
        self.hop(7).start()
        self.hop(2).wait_recv()
        self.hop(8).start()

    def finish(self):
        self.hop(4).wait_recv()
        self.hop(5).wait_recv()
        self.hop(9).start()
        for index in (6, 7, 8, 9):
            self.hop(index).wait_recv()
        for index in range(10):
            self.hop(index).wait_send()


class Moves:
    def __init__(self, me, splits, source, target, sems, back):
        self.me, self.splits, self.source, self.target = me, splits, source, target
        self.sems, self.back = sems, back

    def one(self, i):
        find = token_target if self.back else sequence_target
        device, place = find(self.me[0], self.me[1], i, self.splits)
        return (
            self.me,
            self.source.at[i],
            self.target.at[place],
            device,
            self.sems.at[0, i],
            self.sems.at[1, place],
        )

    def start(self):
        for i in (0, 1):
            move_start(*self.one(i))

    def wait_recv(self):
        for i in (0, 1):
            pltpu.make_async_copy(self.source.at[0], self.target.at[i], self.sems.at[1, i]).wait()

    def finish(self):
        for i in (0, 1):
            move_sent(*self.one(i))


def movers_of(me, splits, back):
    into = [sequence_target(me[0], me[1], i, splits)[0] for i in (0, 1)]
    home = [token_target(me[0], me[1], i, splits)[0] for i in (0, 1)]
    return list(zip(into, home)) if back else list(zip(home, into))


def first_kernel(shards, splits, tokens, cot, pieces, out_own, gate_pieces, *refs):
    rows, cot_rows, in_all, out_all, gate_rows, held = refs[:6]
    move_sems, cot_sems, group_sems, piece_sems, gate_sems, own_sem, in_sems, out_sems = refs[6:]
    me = (lax.axis_index("dp"), lax.axis_index("ctx"))
    group, place = me
    slow = shards // 2
    slot = place // 2
    line = [(group, place ^ (2 * by)) for by in range(1, slow)]
    wanted, block = place // slow, place % slow
    takers = [(group, 2 * (slot ^ by) + wanted) for by in range(slow)]
    givers = [(group, place % 2 * slow + block_by) for block_by in range(slow)]
    movers = movers_of(me, splits, False) + list(zip(givers, takers))
    greet(me, [member(me, by) for by in range(1, 8)] + line, movers)
    swap = GroupExchange(me, pieces, held, piece_sems)
    gate_swap = GroupExchange(me, gate_pieces, gate_rows, gate_sems)
    move = Moves(me, splits, tokens, rows.at[0, 0], move_sems, False)
    cot_move = Moves(me, splits, cot, cot_rows, cot_sems, False)

    def in_line(by):
        sems = (in_sems.at[0, by - 1], in_sems.at[1, by - 1])
        return remote(held, in_all.at[slot], sems, line[by - 1])

    def out_send(by):
        return (
            me,
            out_own,
            out_all.at[block],
            takers[by],
            out_sems.at[0, by],
            out_sems.at[1, block],
        )

    own = pltpu.make_async_copy(held, in_all.at[slot], own_sem)
    swap.start()
    move.start()
    swap.finish()
    for by in range(1, slow):
        in_line(by).start()
    own.start()
    gate_swap.start()
    move.wait_recv()
    spread = GroupGather(me, rows, group_sems, rows.at[0, 0], slice(0, tokens.shape[1]))
    spread.start()
    for by in range(slow):
        move_start(*out_send(by))
    for by in range(1, slow):
        in_line(by).wait()
    cot_move.start()
    spread.pass_on()
    spread.finish()
    own.wait()
    for by in range(slow):
        pltpu.make_async_copy(out_own, out_all.at[by], out_sems.at[1, by]).wait()
    for by in range(slow):
        move_sent(*out_send(by))
    gate_swap.finish()
    cot_move.wait_recv()
    move.finish()
    cot_move.finish()


def first_exchange(tokens, cot, pieces, out_own, gate_pieces, shards, splits, identity):
    low = jnp.bfloat16
    slow = shards // 2
    any_space = pl.BlockSpec(memory_space=pl.ANY)
    dma = pltpu.SemaphoreType.DMA
    made = pl.pallas_call(
        functools.partial(first_kernel, shards, splits),
        out_shape=(
            jax.ShapeDtypeStruct((2, 4) + tokens.shape, low),
            jax.ShapeDtypeStruct(cot.shape, low),
            jax.ShapeDtypeStruct((slow,) + pieces.shape, low),
            jax.ShapeDtypeStruct((slow,) + out_own.shape, low),
            jax.ShapeDtypeStruct(gate_pieces.shape, low),
            jax.ShapeDtypeStruct(pieces.shape, low),
        ),
        in_specs=[any_space] * 5,
        out_specs=(any_space,) * 6,
        scratch_shapes=[
            dma((2, 2)),
            dma((2, 2)),
            dma((2, 10)),
            dma((2, 8)),
            dma((2, 8)),
            dma,
            dma((2, slow - 1)),
            dma((2, slow)),
        ],
        compiler_params=pltpu.CompilerParams(
            collective_id=identity, has_side_effects=True, vmem_limit_bytes=8 << 20
        ),
        cost_estimate=pl.CostEstimate(flops=0, bytes_accessed=200 << 20, transcendentals=0),
    )(tokens, cot, pieces, out_own, gate_pieces)
    return made[:5]


class GroupScatter:
    def __init__(self, me, parts, buffers, sems, steps):
        self.parts = parts
        self.core_in, self.kept, self.sent, self.came, self.held = buffers[:5]
        self.sent_last, self.came_last = buffers[5:]
        self.core_sems, self.kept_sems, self.one_sems, self.last_sems = sems
        self.core, self.across, self.beside = member(me, 2), member(me, 4), member(me, 1)
        self.size = parts.shape[3] // steps
        self.steps = steps

    def window(self, k):
        return slice(k * self.size, (k + 1) * self.size)

    def to_core(self, k, j):
        return remote(
            self.parts.at[:, 2 * j + 1, :, self.window(k)],
            self.core_in.at[:, j, :, self.window(k)],
            (self.core_sems.at[0, k, j], self.core_sems.at[1, k, j]),
            self.core,
        )

    def keep(self, k, j):
        return pltpu.make_async_copy(
            self.parts.at[:, 2 * j, :, self.window(k)],
            self.kept.at[:, j, :, self.window(k)],
            self.kept_sems.at[k, j],
        )

    def first(self, k, half):
        return remote(
            self.sent.at[half, :, self.window(k)],
            self.came.at[half, :, self.window(k)],
            (self.one_sems.at[0, k, half], self.one_sems.at[1, k, half]),
            (self.beside, self.across)[half],
        )

    def second(self, k, half):
        return remote(
            self.sent_last.at[half, self.window(k)],
            self.came_last.at[half, self.window(k)],
            (self.last_sems.at[0, k, half], self.last_sems.at[1, k, half]),
            (self.across, self.beside)[half],
        )

    def start(self):
        for k in range(self.steps):
            for j in (0, 1):
                self.to_core(k, j).start()
                self.keep(k, j).start()

    def send_first(self, k):
        wide = jnp.float32
        rows = self.window(k)
        for j in (0, 1):
            self.keep(k, j).wait()
            self.to_core(k, j).wait_recv()
        for half in (0, 1):
            for other in (0, 1):
                at = (1, other) if half == 0 else (other, 1)
                both = self.kept[at[0], at[1], half, rows].astype(wide)
                both = both + self.core_in[at[0], at[1], half, rows].astype(wide)
                self.sent[half, other, rows] = both.astype(jnp.bfloat16)
            self.first(k, half).start()
        for half in (0, 1):
            for other in (0, 1):
                at = (0, other) if half == 0 else (other, 0)
                both = self.kept[at[0], at[1], half, rows].astype(wide)
                self.held[half, other, rows] = both + self.core_in[at[0], at[1], half, rows].astype(
                    wide
                )

    def send_second(self, k):
        wide = jnp.float32
        rows = self.window(k)
        for half in (0, 1):
            self.first(k, half).wait_recv()
            both = self.held[half, 1, rows] + self.came[half, 1, rows].astype(wide)
            self.sent_last[half, rows] = both.astype(jnp.bfloat16)
            self.second(k, half).start()
            self.held[half, 0, rows] = self.held[half, 0, rows] + self.came[half, 0, rows].astype(
                wide
            )

    def total(self, k, half):
        self.second(k, half).wait_recv()
        rows = self.window(k)
        return self.held[half, 0, rows] + self.came_last[half, rows].astype(jnp.float32)

    def finish(self):
        for k in range(self.steps):
            for j in (0, 1):
                self.to_core(k, j).wait_send()
            for half in (0, 1):
                self.first(k, half).wait_send()
                self.second(k, half).wait_send()


def scatter_scratch(rows, width, steps):
    low, wide = jnp.bfloat16, jnp.float32
    dma = pltpu.SemaphoreType.DMA
    return [
        pltpu.VMEM((2, 2, 2, rows, width), low),
        pltpu.VMEM((2, 2, 2, rows, width), low),
        pltpu.VMEM((2, 2, rows, width), low),
        pltpu.VMEM((2, 2, rows, width), low),
        pltpu.VMEM((2, 2, rows, width), wide),
        pltpu.VMEM((2, rows, width), low),
        pltpu.VMEM((2, rows, width), low),
        dma((2, steps, 2)),
        dma((steps, 2)),
        dma((2, steps, 2)),
        dma((2, steps, 2)),
    ]


def reordered(rows, slow, back):
    each = rows.shape[1] // (4 * slow)
    if back:
        starts = [s * 4 + dp for dp in range(4) for s in range(slow)]
    else:
        starts = [dp * slow + s for s in range(slow) for dp in range(4)]
    return jnp.concatenate([rows[:, i * each : (i + 1) * each] for i in starts], 1)


def turn_kernel(slow, steps, backward, parts, gain, *refs):
    if backward:
        residual, cot, result, gain_grad, rows = refs[:5]
        scratch = refs[5:]
    else:
        tokens, result, rows = refs[:3]
        scratch = refs[3:]
    own, own_sems, group_sems = scratch[:3]
    me = (lax.axis_index("dp"), lax.axis_index("ctx"))
    greet(me, [member(me, by) for by in (1, 2, 4)], [])
    scatter = GroupScatter(me, parts, scratch[3:10], scratch[10:], steps)
    gathers = [GroupGather(me, rows, group_sems.at[k], own, scatter.window(k)) for k in range(steps)]
    scatter.start()
    for k in range(steps):
        scatter.send_first(k)
    for k in range(steps):
        scatter.send_second(k)
    for k in range(steps):
        span = scatter.window(k)
        for half in (0, 1):
            total = scatter.total(k, half)
            if backward:
                values = residual[half, span]
                factor = lax.rsqrt(jnp.mean(values * values, -1, keepdims=True) + norm_eps)
                normed = values * factor
                total = reordered(total, slow, True)
                part = jnp.sum(total * normed, 0, keepdims=True)
                if k == 0 and half == 0:
                    gain_grad[...] = part
                else:
                    gain_grad[...] += part
                back = total * gain[...]
                back = factor * (back - normed * jnp.mean(back * normed, -1, keepdims=True))
                back = cot[half, span].astype(jnp.float32) + back
                result[half, span] = back
                own[half, span] = back.astype(jnp.bfloat16)
            else:
                values = tokens[half, span].astype(jnp.float32) + total
                factor = lax.rsqrt(jnp.mean(values * values, -1, keepdims=True) + norm_eps)
                result[half, span] = values
                own[half, span] = reordered(values * factor * gain[...], slow, False).astype(
                    jnp.bfloat16
                )
        gathers[k].start()
        keep = pltpu.make_async_copy(own.at[:, span], rows.at[0, 0, :, span], own_sems.at[k])
        keep.start()
    for k in range(steps):
        gathers[k].pass_on()
    for k in range(steps):
        gathers[k].finish()
        span = scatter.window(k)
        pltpu.make_async_copy(own.at[:, span], rows.at[0, 0, :, span], own_sems.at[k]).wait()
    scatter.finish()


def turn(parts, gain, rows_in, slow, backward, identity):
    low, wide = jnp.bfloat16, jnp.float32
    dma = pltpu.SemaphoreType.DMA
    rows, width = parts.shape[3:]
    steps = 2
    any_space = pl.BlockSpec(memory_space=pl.ANY)
    vmem = pl.BlockSpec(memory_space=pltpu.VMEM)
    shapes = [jax.ShapeDtypeStruct((2, rows, width), wide)]
    if backward:
        shapes.append(jax.ShapeDtypeStruct((1, width), wide))
    return pl.pallas_call(
        functools.partial(turn_kernel, slow, steps, backward),
        out_shape=tuple(shapes) + (jax.ShapeDtypeStruct((2, 4, 2, rows, width), low),),
        in_specs=[any_space, vmem] + [vmem] * len(rows_in),
        out_specs=tuple([vmem] * len(shapes) + [any_space]),
        scratch_shapes=[pltpu.VMEM((2, rows, width), low), dma((steps,)), dma((steps, 2, 10))]
        + scatter_scratch(rows, width, steps),
        compiler_params=pltpu.CompilerParams(
            collective_id=identity, has_side_effects=True, vmem_limit_bytes=48 << 20
        ),
        cost_estimate=pl.CostEstimate(flops=0, bytes_accessed=250 << 20, transcendentals=0),
    )(parts, gain, *rows_in)


class LineSum:
    def __init__(self, me, slow, parts, buffers, sems):
        self.parts = parts
        self.kept, self.arrived = buffers
        self.sems, self.own_sem = sems
        self.slot = me[1] // 2
        self.slow = slow
        self.line = [(me[0], me[1] ^ (2 * by)) for by in range(1, slow)]

    def hop(self, by):
        sems = (self.sems.at[0, by - 1], self.sems.at[1, by - 1])
        return remote(
            self.parts.at[self.slot ^ by], self.arrived.at[by - 1], sems, self.line[by - 1]
        )

    def own(self):
        return pltpu.make_async_copy(self.parts.at[self.slot], self.kept, self.own_sem)

    def start(self):
        for by in range(1, self.slow):
            self.hop(by).start()
        self.own().start()

    def total(self):
        self.own().wait()
        value = self.kept[...].astype(jnp.float32)
        for by in range(1, self.slow):
            self.hop(by).wait_recv()
            value = value + self.arrived[by - 1].astype(jnp.float32)
        return value

    def finish(self):
        for by in range(1, self.slow):
            self.hop(by).wait_send()


def line_scratch(shape, kind, slow):
    dma = pltpu.SemaphoreType.DMA
    return [
        pltpu.VMEM(shape, kind),
        pltpu.VMEM((slow - 1,) + shape, kind),
        dma((2, slow - 1)),
        dma,
    ]


def last_kernel(shards, splits, steps, in_parts, out_parts, gate_parts, in_back, *refs):
    gain, gain_two_grad, tokens, back_rows = refs[:4]
    in_total, out_total, gate_total, gains_total, tokens_grad = refs[4:9]
    scratch = list(refs[9:])

    def take(count):
        taken = scratch[:count]
        del scratch[:count]
        return taken

    me = (lax.axis_index("dp"), lax.axis_index("ctx"))
    group, place = me
    slow = shards // 2
    slot, half = place // 2, place % 2
    owned = in_parts.shape[2]
    home = (group, half * slow + slot)
    movers = movers_of(me, splits, True)
    movers.append(((group, place % slow * 2 + place // slow), home))
    line = [(group, place ^ (2 * by)) for by in range(1, slow)]
    greet(me, [member(me, by) for by in range(1, 8)] + line, movers)
    one = take(11)
    back_sum = GroupScatter(me, in_back, one[:7], one[7:], steps)
    line_in = take(4)
    line_out = take(4)
    line_gains = take(4)
    in_done, out_done, gains_own, gains_done, made_one, gain_grad = take(6)
    in_sems, gate_sems, gains_sems, one_sems, home_sems = take(5)
    in_line = LineSum(me, slow, in_parts, line_in[:2], line_in[2:])
    out_line = LineSum(me, slow, out_parts, line_out[:2], line_out[2:])
    gains_line = LineSum(me, slow, gains_own, line_gains[:2], line_gains[2:])
    in_swap = GroupExchange(me, in_done, in_total, in_sems)
    gate_swap = GroupExchange(me, gate_parts, gate_total, gate_sems)
    gains_swap = GroupExchange(me, gains_done, gains_total, gains_sems)
    move_grad = Moves(me, splits, made_one, tokens_grad, one_sems, True)
    back_sum.start()
    in_line.start()
    out_line.start()
    for k in range(steps):
        back_sum.send_first(k)
    for k in range(steps):
        back_sum.send_second(k)
    for k in range(steps):
        span = back_sum.window(k)
        for part in (0, 1):
            total = back_sum.total(k, part)
            values = tokens[part, span].astype(jnp.float32)
            normed, factor = norm_parts(values)
            grad = jnp.sum(total * normed, 0, keepdims=True)
            if k == 0 and part == 0:
                gain_grad[...] = grad
            else:
                gain_grad[...] += grad
            value = back_rows[part, span] + norm_back(total * gain[...], normed, factor)
            made_one[part, span] = value.astype(jnp.bfloat16)
    move_grad.start()
    gate_swap.start()
    gains_own[...] = jnp.zeros_like(gains_own)
    for dp in range(4):
        for s in range(slow):
            for side in range(2):
                at = ((dp * slow + s) * 2 + side) * owned
                index = 2 * dp + side
                gains_own[s, index, 0:1, 0:owned] = gain_grad[:, at : at + owned]
                gains_own[s, index, 0:1, owned : 2 * owned] = gain_two_grad[:, at : at + owned]
    gains_line.start()
    in_done[...] = in_line.total().astype(jnp.bfloat16)
    in_swap.start()
    gains_done[...] = gains_line.total()
    gains_swap.start()
    out_done[...] = out_line.total().astype(jnp.bfloat16)
    to_home = (me, out_done, out_total, home, home_sems.at[0], home_sems.at[1])
    move_start(*to_home)
    pltpu.make_async_copy(out_done, out_total, home_sems.at[1]).wait()
    move_sent(*to_home)
    for swap in (in_swap, gate_swap, gains_swap):
        swap.finish()
    move_grad.wait_recv()
    move_grad.finish()
    for part in (in_line, out_line, gains_line, back_sum):
        part.finish()


def last_sums(in_parts, out_parts, gate_parts, in_back, others, shards, splits, identity):
    low, wide = jnp.bfloat16, jnp.float32
    slow = shards // 2
    steps = 2
    any_space = pl.BlockSpec(memory_space=pl.ANY)
    vmem = pl.BlockSpec(memory_space=pltpu.VMEM)
    dma = pltpu.SemaphoreType.DMA
    rows, width = in_back.shape[3:]
    gains_shape = (8, 8, 128)
    moved = jax.ShapeDtypeStruct((2, rows, width), low)
    return pl.pallas_call(
        functools.partial(last_kernel, shards, splits, steps),
        out_shape=(
            jax.ShapeDtypeStruct(in_parts.shape[1:], low),
            jax.ShapeDtypeStruct(out_parts.shape[1:], low),
            jax.ShapeDtypeStruct(gate_parts.shape, low),
            jax.ShapeDtypeStruct(gains_shape, wide),
            moved,
        ),
        in_specs=[any_space] * 4 + [vmem] * 4,
        out_specs=(any_space,) * 5,
        scratch_shapes=scatter_scratch(rows, width, steps)
        + line_scratch(in_parts.shape[1:], low, slow)
        + line_scratch(out_parts.shape[1:], low, slow)
        + line_scratch(gains_shape, wide, slow)
        + [
            pltpu.VMEM(in_parts.shape[1:], low),
            pltpu.VMEM(out_parts.shape[1:], low),
            pltpu.VMEM((slow,) + gains_shape, wide),
            pltpu.VMEM(gains_shape, wide),
            pltpu.VMEM(moved.shape, low),
            pltpu.VMEM((1, width), wide),
            dma((2, 8)),
            dma((2, 8)),
            dma((2, 8)),
            dma((2, 2)),
            dma((2,)),
        ],
        compiler_params=pltpu.CompilerParams(
            collective_id=identity, has_side_effects=True, vmem_limit_bytes=56 << 20
        ),
        cost_estimate=pl.CostEstimate(flops=0, bytes_accessed=300 << 20, transcendentals=0),
    )(in_parts, out_parts, gate_parts, in_back, *others)


def position_tables(blocks, rows):
    frequency = rope_base ** (-(np.arange(HEAD // 2) * 2.0 / HEAD))
    angles = np.arange(blocks * rows).reshape(blocks, rows, 1) * frequency
    cos, sin = np.cos(angles), np.sin(angles)
    cosine = np.concatenate([cos, cos, cos, cos], 2)
    sines = np.concatenate([-sin, sin, -sin, sin], 2)
    return jnp.asarray(cosine, jnp.float32), jnp.asarray(sines, jnp.float32)


def attend(order, where, qkv, tables, cot, q_heads, kv_heads, identity):
    seqs, length, cols = qkv.shape
    blocks = order.shape[0]
    rows = length // blocks
    whole = pl.BlockSpec(memory_space=pltpu.VMEM)
    small = pl.BlockSpec(memory_space=pltpu.SMEM)
    any_space = pl.BlockSpec(memory_space=pl.ANY)
    return pl.pallas_call(
        functools.partial(attend_kernel, q_heads, kv_heads, 256),
        out_shape=(
            jax.ShapeDtypeStruct((seqs, blocks, rows, q_heads * HEAD), jnp.bfloat16),
            jax.ShapeDtypeStruct((seqs, q_heads, length), jnp.float32),
            jax.ShapeDtypeStruct((seqs, length, cols), jnp.bfloat16),
            jax.ShapeDtypeStruct((2, 4) + cot.shape, cot.dtype),
        ),
        in_specs=[small, small, whole, whole, whole, any_space],
        out_specs=(whole, whole, whole, any_space),
        scratch_shapes=[
            pltpu.VMEM((blocks, rows, q_heads * HEAD), jnp.bfloat16),
            pltpu.SemaphoreType.DMA((2, 10)),
            pltpu.SemaphoreType.DMA,
        ],
        compiler_params=pltpu.CompilerParams(
            collective_id=identity, has_side_effects=True, vmem_limit_bytes=40 << 20
        ),
        cost_estimate=pl.CostEstimate(
            flops=2 * seqs * length * length * q_heads * HEAD,
            bytes_accessed=100 << 20,
            transcendentals=seqs * length * length * q_heads // 2,
        ),
    )(order, where, qkv.reshape(seqs, blocks, rows, cols), *tables, cot)


def attend_back(
    order, where, kept, back, lse, tables, out_rows, residual, q_heads, kv_heads, splits, identity
):
    seqs, length, cols = kept.shape
    blocks = order.shape[0]
    block = length // blocks
    group = q_heads // kv_heads
    rows, width = out_rows.shape[3:]
    steps = 2
    whole = pl.BlockSpec(memory_space=pltpu.VMEM)
    small = pl.BlockSpec(memory_space=pltpu.SMEM)
    any_space = pl.BlockSpec(memory_space=pl.ANY)
    return pl.pallas_call(
        functools.partial(attend_back_kernel, q_heads, kv_heads, 256, splits, steps),
        out_shape=(
            jax.ShapeDtypeStruct((seqs, blocks, block, cols), jnp.bfloat16),
            jax.ShapeDtypeStruct((2, rows, width), jnp.bfloat16),
        ),
        in_specs=[small, small] + [whole] * 5 + [any_space, whole],
        out_specs=(whole, any_space),
        scratch_shapes=[
            pltpu.VMEM((length, q_heads * HEAD), jnp.bfloat16),
            pltpu.VMEM((blocks, block, cols), jnp.float32),
            pltpu.VMEM((group, length), jnp.float32),
            pltpu.VMEM((group * HEAD, length), jnp.float32),
            pltpu.VMEM((2, rows, width), jnp.bfloat16),
            pltpu.SemaphoreType.DMA((2, 2)),
        ]
        + scatter_scratch(rows, width, steps),
        compiler_params=pltpu.CompilerParams(
            collective_id=identity, has_side_effects=True, vmem_limit_bytes=56 << 20
        ),
        cost_estimate=pl.CostEstimate(
            flops=7 * seqs * length * length * q_heads * HEAD,
            bytes_accessed=100 << 20,
            transcendentals=seqs * length * length * q_heads // 2,
        ),
    )(
        order,
        where,
        kept,
        back.reshape(seqs, blocks, block, -1),
        lse,
        *tables,
        out_rows,
        residual,
    )


def gate_update_kernel(slow, step_rate, grad, weight, first, second, new_first, new_second, new):
    units = grad.shape[2] // slow
    pieces = [grad[half, :, s * units : (s + 1) * units] for s in range(slow) for half in (0, 1)]
    gradient = jnp.concatenate(pieces, 1).astype(jnp.float32)
    new_first[...], new_second[...], new[...] = adam_update(
        weight[...], gradient, first[...], second[...], step_rate, weight_decay
    )


def gate_update(grad, weight, first, second, slow, step_rate):
    rows, width = weight.shape
    block = pl.BlockSpec((rows, width // 8), lambda side, dp: (0, 4 * side + dp))
    piece = pl.BlockSpec((2, rows, width // 16), lambda side, dp: (dp, 0, side))
    return pl.pallas_call(
        functools.partial(gate_update_kernel, slow, step_rate),
        grid=(2, 4),
        out_shape=(jax.ShapeDtypeStruct(weight.shape, jnp.float32),) * 3,
        in_specs=[piece, block, block, block],
        out_specs=(block,) * 3,
        compiler_params=pltpu.CompilerParams(vmem_limit_bytes=32 << 20),
    )(grad, weight, first, second)


def local(
    tokens,
    cotangent,
    block_order,
    attention_in,
    attention_out,
    gate_up,
    down_matrix,
    gains,
    mean_attention_in,
    mean_attention_out,
    mean_gate_up,
    mean_down,
    mean_gains,
    square_attention_in,
    square_attention_out,
    square_gate_up,
    square_down,
    square_gains,
):
    seq_count, shard_rows, width = tokens.shape
    shards = lax.axis_size("ctx")
    slow = shards // 2
    mine = lax.axis_index("dp")
    beside = lax.axis_index("ctx") % 2
    low = jnp.bfloat16
    owned = attention_in.shape[0]
    hidden_units = gate_up.shape[1] // 2
    part_hidden = hidden_units // 8
    units = down_matrix.shape[0]
    part_q = HEADS * HEAD // 8
    part_k = KV_HEADS * HEAD // 8
    part_cols = part_q + 2 * part_k
    count = seq_count * shard_rows
    together = 8 * count
    spread = shards // (4 * seq_count)
    splits = max(1, slow // 8)
    seqs = 2 // spread if spread < 2 else 1
    length = shards * shard_rows
    q_heads = HEADS // 8 // splits
    kv_heads = KV_HEADS // 8

    in_low = attention_in.astype(low)
    gains_row = jnp.pad(gains.astype(low).reshape(1, -1), ((0, 15), (0, part_cols - 2 * owned)))
    pieces = jnp.stack(
        [
            jnp.concatenate(
                [
                    jnp.concatenate(
                        [
                            in_low[:, i * part_q : (i + 1) * part_q],
                            in_low[:, 8 * part_q + i * part_k :][:, :part_k],
                            in_low[:, 8 * (part_q + part_k) + i * part_k :][:, :part_k],
                        ],
                        1,
                    ),
                    gains_row,
                ]
            )
            for i in range(8)
        ]
    )
    gate_low = gate_up.astype(low)
    gate_pieces = jnp.stack(
        [
            jnp.concatenate(
                [
                    gate_low[:, side * hidden_units + (dp * shards + 2 * s + half) * units :][
                        :, :units
                    ]
                    for side in range(2)
                    for s in range(slow)
                ],
                1,
            )
            for dp in range(4)
            for half in range(2)
        ]
    )
    tokens_all, cot_own, in_all, w_out, gate_rows = first_exchange(
        tokens, cotangent, pieces, attention_out.astype(low), gate_pieces, shards, spread, 1
    )
    in_all = in_all.reshape(slow, 4, 2, owned + 16, part_cols).swapaxes(0, 1)
    w_in = in_all[:, :, :, :owned].reshape(width, part_cols)
    w_out = w_out.reshape(part_q, width)
    gains_all = in_all[:, :, :, owned, : 2 * owned].reshape(-1, 2, owned)
    gains_all = gains_all.astype(jnp.float32).swapaxes(0, 1).reshape(2, width)
    gain_one, gain_two = gains_all[0], gains_all[1]
    w_gate = gather_line(gate_rows.reshape(8 * owned, 2 * part_hidden))
    w_down = gather_line(down_matrix.astype(low))

    normed_all, _ = norm_parts(tokens_all.reshape(together, width).astype(jnp.float32))
    input_one = (normed_all * gain_one).astype(low)
    qkv = dot_nn(input_one, w_in)
    orders = block_order.reshape(2 * splits if spread > 1 else 1, 4, -1)
    slot_order = jnp.concatenate(
        [
            orders[(2 * s + (beside ^ i)) if spread > 1 else 0, part_owner(mine ^ j)]
            for s in range(splits)
            for i in range(2 // seqs)
            for j in range(4)
        ]
    )
    tables = position_tables(slot_order.shape[0], length // slot_order.shape[0])
    groups = [
        [2 * (s * splits + g) + half for g in range(splits)]
        for s in range(slow // splits)
        for half in (0, 1)
    ]

    def split_heads(values, widths, copies):
        parts = []
        start = 0
        for each, repeat in zip(widths, copies):
            kinds = splits // repeat
            piece = values[:, start : start + kinds * each].reshape(-1, kinds, each)
            parts.append(jnp.repeat(piece.swapaxes(0, 1), repeat, axis=0))
            start += kinds * each
        sent = jnp.concatenate(parts, 2)
        got = lax.all_to_all(sent, "ctx", 0, 0, axis_index_groups=groups, tiled=True)
        return got.reshape(length, -1)

    def join_heads(values):
        sent = values.reshape(splits, together, -1)
        return lax.all_to_all(sent, "ctx", 0, 0, axis_index_groups=groups, tiled=True)

    q_width, k_width = q_heads * HEAD, kv_heads * HEAD
    if splits > 1:
        qkv = split_heads(qkv, (q_width, k_width, k_width), (1, splits, splits))
    qkv = qkv.reshape(seqs, length, -1)
    blocks = slot_order.shape[0]
    slot_where = jnp.sum(
        jnp.where(
            slot_order[None, :] == jnp.arange(blocks, dtype=jnp.int32)[:, None],
            jnp.arange(blocks, dtype=jnp.int32)[None, :],
            0,
        ),
        1,
    )
    attended, lse, kept, back_all = attend(
        slot_order, slot_where, qkv, tables, cot_own, q_heads, kv_heads, 2
    )
    cot_rows = cot_own
    back_all = back_all.reshape(together, width)
    if splits > 1:
        attended = join_heads(attended.reshape(length, q_width)).swapaxes(0, 1)
    attended = attended.reshape(together, part_q)

    def parts(values):
        return values.astype(low).reshape((2, 4) + tokens.shape)

    residual_rows, input_two = turn(
        parts(dot_nn(attended, w_out)), gain_two[None], [tokens_all[0, 0]], slow, False, 3
    )
    input_two = input_two.reshape(together, width)
    gate_both = dot_nn(input_two, w_gate)
    gate_part = gate_both[:, :part_hidden]
    up_part = gate_both[:, part_hidden:]
    sigmoid_gate = jax.nn.sigmoid(gate_part)
    active = gate_part * sigmoid_gate
    hidden = (active * up_part).astype(low)
    grad_down = lax.optimization_barrier(dot_tn(hidden, back_all).astype(low))
    down_sum = sum_line(grad_down + 0.0 * w_down[0, 0]).astype(jnp.float32)
    back_hidden = dot_nt(back_all, w_down)
    back_gate = back_hidden * up_part * sigmoid_gate * (1.0 + gate_part * (1.0 - sigmoid_gate))
    back_upper = back_hidden * active
    back_gate_up = jnp.concatenate([back_gate, back_upper], 1).astype(low)
    gate_low = sum_line(dot_tn(input_two, back_gate_up).astype(low))
    back_rows, grad_gain_two, back_residual_all = turn(
        parts(dot_nt(back_gate_up, w_gate)),
        gain_two[None],
        [residual_rows, cot_rows],
        slow,
        True,
        4,
    )
    back_residual_all = back_residual_all.reshape(together, width)
    grad_out = dot_tn(attended, back_residual_all).astype(low)
    back_attended = dot_nt(back_residual_all, w_out).astype(low)
    if splits > 1:
        back_attended = split_heads(back_attended, (q_width,), (1,))
    back_projected, block_out = attend_back(
        slot_order,
        slot_where,
        kept,
        back_attended.reshape(seqs, length, -1),
        lse,
        tables,
        parts(dot_nn(hidden, w_down)),
        residual_rows,
        q_heads,
        kv_heads,
        spread,
        6,
    )
    if splits > 1:
        back_projected = join_heads(back_projected.reshape(length, -1)).astype(jnp.float32)
        back_projected = jnp.concatenate(
            [
                back_projected[..., :q_width].swapaxes(0, 1).reshape(together, part_q),
                back_projected[..., q_width:].sum(0),
            ],
            1,
        ).astype(low)
    back_projected = back_projected.reshape(together, part_cols)
    grad_in = dot_tn(input_one, back_projected).astype(low)
    grad_in = grad_in.reshape(4, slow, 2 * owned, part_cols).swapaxes(0, 1)
    in_sum, out_sum, gate_sum, gains_sum, tokens_grad = last_sums(
        grad_in.reshape(slow, 8, owned, part_cols),
        grad_out.reshape(slow, owned, width),
        gate_low.reshape(8, owned, 2 * part_hidden),
        parts(dot_nt(back_projected, w_in)),
        [gain_one[None], grad_gain_two, tokens_all[0, 0], back_rows],
        shards,
        spread,
        5,
    )
    tokens_grad = tokens_grad.astype(jnp.float32)
    out_sum = out_sum.astype(jnp.float32)
    gains_sum = gains_sum[:, 0, : 2 * owned].reshape(8, 2, owned).sum(0)
    cuts = ((0, part_q), (part_q, part_q + part_k), (part_q + part_k, part_cols))
    in_sum = jnp.concatenate(
        [in_sum[i, :, first:last] for first, last in cuts for i in range(8)], 1
    ).astype(jnp.float32)
    new_in = adam_update(
        attention_in,
        in_sum,
        mean_attention_in,
        square_attention_in,
        input_boost * D ** (-0.5),
        weight_decay,
    )
    new_out = adam_update(
        attention_out,
        out_sum,
        mean_attention_out,
        square_attention_out,
        (HEADS * HEAD // 32) ** (-0.5),
        weight_decay,
    )
    new_gate = gate_update(
        gate_sum, gate_up, mean_gate_up, square_gate_up, slow, D ** (-0.5)
    )
    new_down = adam_update(
        down_matrix, down_sum, mean_down, square_down, FF ** (-0.5), weight_decay
    )
    new_gain = adam_update(gains, gains_sum, mean_gains, square_gains, gain_rate, 0.0)
    return (
        block_out,
        tokens_grad,
        new_in[0],
        new_in[1],
        new_in[2],
        new_out[0],
        new_out[1],
        new_out[2],
        new_gate[0],
        new_gate[1],
        new_gate[2],
        new_down[0],
        new_down[1],
        new_down[2],
        new_gain[0],
        new_gain[1],
        new_gain[2],
    )


def solution(mesh):
    in_specs = (
        P("dp", "ctx", None),
        P("dp", "ctx", None),
        P(),
        P(("dp", "ctx"), None),
        P(("dp", "ctx"), None),
        P(("dp", "ctx"), None),
        P(("dp", "ctx"), None),
        P(None, ("dp", "ctx")),
        P(("dp", "ctx"), None),
        P(("dp", "ctx"), None),
        P(("dp", "ctx"), None),
        P(("dp", "ctx"), None),
        P(None, ("dp", "ctx")),
        P(("dp", "ctx"), None),
        P(("dp", "ctx"), None),
        P(("dp", "ctx"), None),
        P(("dp", "ctx"), None),
        P(None, ("dp", "ctx")),
    )
    out_specs = (
        P("dp", "ctx", None),
        P("dp", "ctx", None),
        P(("dp", "ctx"), None),
        P(("dp", "ctx"), None),
        P(("dp", "ctx"), None),
        P(("dp", "ctx"), None),
        P(("dp", "ctx"), None),
        P(("dp", "ctx"), None),
        P(("dp", "ctx"), None),
        P(("dp", "ctx"), None),
        P(("dp", "ctx"), None),
        P(("dp", "ctx"), None),
        P(("dp", "ctx"), None),
        P(("dp", "ctx"), None),
        P(None, ("dp", "ctx")),
        P(None, ("dp", "ctx")),
        P(None, ("dp", "ctx")),
    )
    return jax.shard_map(local, mesh=mesh, in_specs=in_specs, out_specs=out_specs, check_vma=False)
```

```python
import functools

import jax
import jax.numpy as jnp
import numpy as np
from jax import lax
from jax.experimental import pallas as pl
from jax.experimental.pallas import tpu as pltpu
from jax.sharding import PartitionSpec as P

D = 2048
HEADS = 32
KV_HEADS = 8
HEAD = 64
FF = 8192
STEP = 5


norm_eps = 1e-05
rope_base = 500000.0
beta_one = 0.9
beta_two = 0.95
gain_rate = 1.25
input_boost = 2.5
weight_decay = 0.1
adam_eps = 1e-08
masked_score = -1e30


def norm_parts(values):
    factor = lax.rsqrt(jnp.mean(values * values, -1, keepdims=True) + norm_eps)
    return (values * factor, factor)


def norm_back(back_normed, normed, factor):
    return factor * (back_normed - normed * jnp.mean(back_normed * normed, -1, keepdims=True))


def adam_update(weight, gradient, first_moment, second_moment, step_rate, decay_rate):
    first_new = beta_one * first_moment + (1.0 - beta_one) * gradient
    second_new = beta_two * second_moment + (1.0 - beta_two) * gradient * gradient
    update = (
        first_new
        / (1.0 - beta_one**STEP)
        / (jnp.sqrt(second_new / (1.0 - beta_two**STEP)) + adam_eps)
    )
    return (first_new, second_new, weight - step_rate * (update + decay_rate * weight))


def line_groups(shards):
    return [[2 * s + half for s in range(shards // 2)] for half in (0, 1)]


def gather_line(rows):
    return lax.all_gather(
        rows, "ctx", axis=0, tiled=True, axis_index_groups=line_groups(lax.axis_size("ctx"))
    )


def sum_line(gradient):
    return lax.psum_scatter(
        gradient,
        "ctx",
        scatter_dimension=0,
        tiled=True,
        axis_index_groups=line_groups(lax.axis_size("ctx")),
    )


def dot_nn(a, b):
    return lax.dot_general(a, b, (((1,), (0,)), ((), ())), preferred_element_type=jnp.float32)


def dot_nt(a, b):
    return lax.dot_general(a, b, (((1,), (1,)), ((), ())), preferred_element_type=jnp.float32)


def dot_tn(a, b):
    return lax.dot_general(a, b, (((0,), (0,)), ((), ())), preferred_element_type=jnp.float32)


def causal_keep(tile):
    keys = lax.broadcasted_iota(jnp.int32, (tile, tile), 0)
    queries = lax.broadcasted_iota(jnp.int32, (tile, tile), 1)
    return keys <= queries


def turn_group(values, cos, sin, forward):
    lanes = lax.broadcasted_iota(jnp.int32, values.shape, 1)
    other = jnp.where(
        lanes % HEAD < HEAD // 2,
        pltpu.roll(values, 2 * HEAD - HEAD // 2, 1),
        pltpu.roll(values, HEAD // 2, 1),
    )
    if forward:
        return values * cos + other * sin
    return values * cos - other * sin


def turn_columns(values, start, turned_cols, cos, sin, forward):
    if start >= turned_cols:
        return values
    turned = turn_group(values, cos, sin, forward)
    if start + 2 * HEAD <= turned_cols:
        return turned
    lanes = lax.broadcasted_iota(jnp.int32, values.shape, 1)
    return jnp.where(lanes < turned_cols - start, turned, values)


def attend_kernel(
    q_heads,
    kv_heads,
    tile,
    order_ref,
    where_ref,
    all_qkv_ref,
    cos_ref,
    sin_ref,
    cot,
    all_out_ref,
    all_lse_ref,
    all_kept_ref,
    cot_rows,
    made,
    group_sems,
    own_sem,
):
    me = (lax.axis_index("dp"), lax.axis_index("ctx"))
    greet(me, [member(me, by) for by in (1, 2, 4)], [])
    spread = GroupGather(me, cot_rows, group_sems, cot, slice(0, cot.shape[1]))
    own = pltpu.make_async_copy(cot, cot_rows.at[0, 0], own_sem)
    spread.start()
    own.start()
    count = all_qkv_ref.shape[0]
    for sequence in range(count):
        attend_sequence(
            q_heads,
            kv_heads,
            tile,
            order_ref,
            where_ref,
            all_qkv_ref.at[sequence],
            cos_ref,
            sin_ref,
            all_out_ref.at[sequence],
            all_lse_ref.at[sequence],
            all_kept_ref.at[sequence],
            made,
            spread.pass_on if sequence == count - 1 else None,
        )
    spread.finish()
    own.wait()


def attend_sequence(
    q_heads,
    kv_heads,
    tile,
    order_ref,
    where_ref,
    qkv_ref,
    cos_ref,
    sin_ref,
    out_ref,
    lse_ref,
    kept_ref,
    made,
    pause,
):
    blocks, rows, cols = qkv_ref.shape
    length = blocks * rows
    group = q_heads // kv_heads
    q_cols, k_cols = q_heads * HEAD, kv_heads * HEAD
    scale = HEAD ** (-0.5)

    def take_block(i, _):
        start = pl.multiple_of(i * rows, rows)
        cos = cos_ref[i]
        sin = sin_ref[i]
        for c in range(0, cols, 2 * HEAD):
            values = qkv_ref[where_ref[i], :, c : c + 2 * HEAD]
            values = turn_columns(values, c, q_cols + k_cols, cos, sin, True)
            kept_ref[pl.ds(start, rows), c : c + 2 * HEAD] = values.astype(jnp.bfloat16)
        return 0

    lax.fori_loop(0, blocks, take_block, 0)
    keep = causal_keep(tile)
    for kv in range(kv_heads):
        k_at = q_cols + kv * HEAD
        v_at = q_cols + k_cols + kv * HEAD

        def query_step(i, _):
            q_start = pl.multiple_of(i * tile, tile)
            queries = [
                kept_ref[
                    pl.ds(q_start, tile), (kv * group + g) * HEAD : (kv * group + g + 1) * HEAD
                ]
                for g in range(group)
            ]

            def key_tile(j, carry, masked):
                k_start = pl.multiple_of(j * tile, tile)
                keys = kept_ref[pl.ds(k_start, tile), k_at : k_at + HEAD]
                values = kept_ref[pl.ds(k_start, tile), v_at : v_at + HEAD]
                result = []
                for g in range(group):
                    peak, total, weighted = carry[g]
                    scores = dot_nt(keys, queries[g]) * scale
                    if masked:
                        scores = jnp.where(keep, scores, masked_score)
                    new_peak = jnp.maximum(peak, jnp.max(scores, 0, keepdims=True))
                    weights = jnp.exp(scores - new_peak)
                    shrink = jnp.exp(peak - new_peak)
                    total = total * shrink + jnp.sum(weights, 0, keepdims=True)
                    weighted = weighted * shrink + dot_tn(values, weights.astype(jnp.bfloat16))
                    result.append((new_peak, total, weighted))
                return tuple(result)

            start = tuple(
                (
                    jnp.full((1, tile), masked_score, jnp.float32),
                    jnp.zeros((1, tile), jnp.float32),
                    jnp.zeros((HEAD, tile), jnp.float32),
                )
                for _ in range(group)
            )
            carry = lax.fori_loop(0, i, lambda j, c: key_tile(j, c, False), start)
            carry = key_tile(i, carry, True)
            for g in range(group):
                head = kv * group + g
                peak, total, weighted = carry[g]
                lse_ref[head : head + 1, pl.ds(q_start, tile)] = peak + jnp.log(total)
                made[pl.ds(i * (tile // rows), tile // rows), :, head * HEAD : (head + 1) * HEAD] = (
                    (weighted / total).T.astype(jnp.bfloat16).reshape(-1, rows, HEAD)
                )
            return 0

        middle = length // tile // 2
        lax.fori_loop(0, middle, query_step, 0)
        if kv == 0 and pause is not None:
            pause()
        lax.fori_loop(middle, length // tile, query_step, 0)

    def give_block(i, _):
        out_ref[i] = made[order_ref[i]]
        return 0

    lax.fori_loop(0, blocks, give_block, 0)


def attend_back_kernel(
    q_heads,
    kv_heads,
    tile,
    splits,
    steps,
    order_ref,
    where_ref,
    all_kept_ref,
    all_back_ref,
    all_lse_ref,
    cos_ref,
    sin_ref,
    out_rows,
    residual,
    all_out_ref,
    block_out,
    *scratch,
):
    me = (lax.axis_index("dp"), lax.axis_index("ctx"))
    greet(me, [member(me, by) for by in (1, 2, 4)], movers_of(me, splits, True))
    work, scratch = scratch[:4], scratch[4:]
    made, move_sems = scratch[:2]
    scatter = GroupScatter(me, out_rows, scratch[2:9], scratch[9:], steps)
    move = Moves(me, splits, made, block_out, move_sems, True)

    def one():
        for k in range(steps):
            scatter.send_first(k)

    def two():
        for k in range(steps):
            scatter.send_second(k)

    def three():
        for k in range(steps):
            span = scatter.window(k)
            for part in (0, 1):
                value = residual[part, span] + scatter.total(k, part)
                made[part, span] = value.astype(jnp.bfloat16)
        move.start()

    tasks = [one, two, three]

    def pause():
        if tasks:
            tasks.pop(0)()

    scatter.start()
    for sequence in range(all_kept_ref.shape[0]):
        attend_back_sequence(
            q_heads,
            kv_heads,
            tile,
            pause,
            order_ref,
            where_ref,
            all_kept_ref.at[sequence],
            all_back_ref.at[sequence],
            all_lse_ref.at[sequence],
            cos_ref,
            sin_ref,
            all_out_ref.at[sequence],
            *work,
        )
    while tasks:
        pause()
    move.wait_recv()
    move.finish()
    scatter.finish()


def attend_back_sequence(
    q_heads,
    kv_heads,
    tile,
    pause,
    order_ref,
    where_ref,
    kept_ref,
    back_ref,
    lse_ref,
    cos_ref,
    sin_ref,
    out_ref,
    back_sorted,
    grad,
    delta_ref,
    dq_ref,
):
    length, cols = kept_ref.shape
    blocks, rows = back_ref.shape[:2]
    group = q_heads // kv_heads
    q_cols, k_cols = q_heads * HEAD, kv_heads * HEAD
    scale = HEAD ** (-0.5)
    tiles = length // tile

    def take_block(i, _):
        start = pl.multiple_of(i * rows, rows)
        back_sorted[pl.ds(start, rows), :] = back_ref[where_ref[i]]
        return 0

    lax.fori_loop(0, blocks, take_block, 0)
    keep = causal_keep(tile)
    for kv in range(kv_heads):
        k_at = q_cols + kv * HEAD
        v_at = q_cols + k_cols + kv * HEAD

        def load(i, g):
            start = pl.multiple_of(i * tile, tile)
            head = kv * group + g
            at = slice(head * HEAD, (head + 1) * HEAD)
            return (
                kept_ref[pl.ds(start, tile), at],
                back_sorted[pl.ds(start, tile), at],
                lse_ref[head : head + 1, pl.ds(start, tile)],
            )

        def load_kv(j):
            start = pl.multiple_of(j * tile, tile)
            return (
                kept_ref[pl.ds(start, tile), k_at : k_at + HEAD],
                kept_ref[pl.ds(start, tile), v_at : v_at + HEAD],
            )

        def tile_terms(keys, values, query, back, lse, masked):
            weights = jnp.exp(dot_nt(keys, query) * scale - lse)
            if masked:
                weights = jnp.where(keep, weights, 0.0)
            return weights, dot_nt(values, back)

        def delta_step(i, _):
            rows_i = [load(i, g) for g in range(group)]

            def one(j, carry, masked):
                keys, values = load_kv(j)
                result = []
                for g in range(group):
                    weights, back_weights = tile_terms(keys, values, *rows_i[g], masked)
                    result.append(carry[g] + jnp.sum(weights * back_weights, 0, keepdims=True))
                return tuple(result)

            carry = tuple(jnp.zeros((1, tile), jnp.float32) for _ in range(group))
            carry = lax.fori_loop(0, i, lambda j, c: one(j, c, False), carry)
            carry = one(i, carry, True)
            for g in range(group):
                delta_ref[g : g + 1, pl.ds(pl.multiple_of(i * tile, tile), tile)] = carry[g]
            return 0

        lax.fori_loop(0, tiles, delta_step, 0)
        if kv == 0:
            pause()
        dq_ref[...] = jnp.zeros_like(dq_ref)

        def key_step(j, _):
            keys, values = load_kv(j)

            def one(i, carry, masked):
                back_key, back_value = carry
                start = pl.multiple_of(i * tile, tile)
                for g in range(group):
                    query, back, lse = load(i, g)
                    weights, back_weights = tile_terms(keys, values, query, back, lse, masked)
                    delta = delta_ref[g : g + 1, pl.ds(start, tile)]
                    back_scores = (weights * (back_weights - delta)).astype(jnp.bfloat16)
                    back_key = back_key + dot_nn(back_scores, query)
                    back_value = back_value + dot_nn(weights.astype(jnp.bfloat16), back)
                    dq_ref[g * HEAD : (g + 1) * HEAD, pl.ds(start, tile)] += dot_tn(
                        keys, back_scores
                    )
                return back_key, back_value

            zero = jnp.zeros((tile, HEAD), jnp.float32)
            carry = one(j, (zero, zero), True)
            carry = lax.fori_loop(j + 1, tiles, lambda i, c: one(i, c, False), carry)
            span = pl.ds(j * (tile // rows), tile // rows)
            grad[span, :, k_at : k_at + HEAD] = (carry[0] * scale).reshape(-1, rows, HEAD)
            grad[span, :, v_at : v_at + HEAD] = carry[1].reshape(-1, rows, HEAD)
            return 0

        lax.fori_loop(0, tiles, key_step, 0)
        for g in range(group):
            head = kv * group + g
            turned = (dq_ref[g * HEAD : (g + 1) * HEAD, :] * scale).T
            grad[:, :, head * HEAD : (head + 1) * HEAD] = turned.reshape(-1, rows, HEAD)

    def give_block(i, _):
        cos = cos_ref[order_ref[i]]
        sin = sin_ref[order_ref[i]]
        for c in range(0, cols, 2 * HEAD):
            values = grad[order_ref[i], :, c : c + 2 * HEAD]
            values = turn_columns(values, c, q_cols + k_cols, cos, sin, False)
            out_ref[i, :, c : c + 2 * HEAD] = values.astype(jnp.bfloat16)
        return 0

    lax.fori_loop(0, blocks, give_block, 0)


MESH = pl.DeviceIdType.MESH


def part_owner(part):
    return part % 2 * 2 + part // 2


def sequence_target(group, place, second, splits):
    part = place // 2
    target = (part_owner(part % 4), (2 * group + second) * splits + part // 4)
    return target, place % 2


def token_target(group, place, half, splits):
    sequence = place // splits
    part = part_owner(group) + 4 * (place % splits)
    return (sequence // 2, 2 * part + half), sequence % 2


def remote(source, target, sems, device):
    return pltpu.make_async_remote_copy(
        src_ref=source,
        dst_ref=target,
        send_sem=sems[0],
        recv_sem=sems[1],
        device_id=device,
        device_id_type=MESH,
    )


def same(one, other):
    return jnp.logical_and(one[0] == other[0], one[1] == other[1])


def greet(me, peers, movers):
    barrier = pltpu.get_barrier_semaphore()
    for peer in peers:
        pl.semaphore_signal(barrier, inc=1, device_id=peer, device_id_type=MESH)
    expected = len(peers)
    for source, target in movers:

        @pl.when(jnp.logical_not(same(source, me)))
        def _():
            pl.semaphore_signal(barrier, inc=1, device_id=source, device_id_type=MESH)

        expected = expected + jnp.where(same(target, me), 0, 1)
    pl.semaphore_wait(barrier, expected)


def move_start(me, source, target, target_device, send, receive):
    here = same(target_device, me)

    @pl.when(here)
    def _():
        pltpu.make_async_copy(source, target, receive).start()

    @pl.when(jnp.logical_not(here))
    def _():
        remote(source, target, (send, receive), target_device).start()


def move_sent(me, source, target, target_device, send, receive):
    @pl.when(jnp.logical_not(same(target_device, me)))
    def _():
        remote(source, target, (send, receive), target_device).wait_send()


def member(me, by):
    return (me[0] ^ (by // 2), me[1] ^ (by % 2))


def group_index(device):
    return 2 * device[0] + device[1] % 2


class GroupExchange:
    def __init__(self, me, pieces, got, sems):
        self.me, self.pieces, self.got, self.sems = me, pieces, got, sems

    def hop(self, by):
        peer = member(self.me, by)
        sems = (self.sems.at[0, by - 1], self.sems.at[1, by - 1])
        return remote(
            self.pieces.at[group_index(peer)], self.got.at[group_index(self.me)], sems, peer
        )

    def own(self):
        mine = group_index(self.me)
        return pltpu.make_async_copy(self.pieces.at[mine], self.got.at[mine], self.sems.at[0, 7])

    def start(self):
        for by in range(1, 8):
            self.hop(by).start()
        self.own().start()

    def finish(self):
        self.own().wait()
        for by in range(1, 8):
            self.hop(by).wait()


class GroupGather:
    def __init__(self, me, rows, sems, own, window):
        self.rows, self.sems, self.own, self.window = rows, sems, own, window
        self.core, self.across, self.beside = member(me, 2), member(me, 4), member(me, 1)

    def hop(self, index):
        across, beside, core = self.across, self.beside, self.core
        source, i, j, half, device = (
            (None, 0, 2, 0, across),
            (None, 1, 0, 1, beside),
            (None, 1, 0, 0, beside),
            (None, 0, 2, 1, across),
            ((0, 2), 1, 2, 0, beside),
            ((1, 0), 1, 2, 1, across),
            (None, 0, 1, slice(0, 2), core),
            ((0, 2), 0, 3, slice(0, 2), core),
            ((1, 0), 1, 1, slice(0, 2), core),
            ((1, 2), 1, 3, slice(0, 2), core),
        )[index]
        if source is None:
            source = self.own.at[half, self.window]
        else:
            source = self.rows.at[source[0], source[1], half, self.window]
        target = self.rows.at[i, j, half, self.window]
        return remote(source, target, (self.sems.at[0, index], self.sems.at[1, index]), device)

    def start(self):
        for index in (0, 1, 2, 3, 6):
            self.hop(index).start()

    def pass_on(self):
        self.hop(0).wait_recv()
        self.hop(4).start()
        self.hop(1).wait_recv()
        self.hop(5).start()
        self.hop(3).wait_recv()
        self.hop(7).start()
        self.hop(2).wait_recv()
        self.hop(8).start()

    def finish(self):
        self.hop(4).wait_recv()
        self.hop(5).wait_recv()
        self.hop(9).start()
        for index in (6, 7, 8, 9):
            self.hop(index).wait_recv()
        for index in range(10):
            self.hop(index).wait_send()


class Moves:
    def __init__(self, me, splits, source, target, sems, back):
        self.me, self.splits, self.source, self.target = me, splits, source, target
        self.sems, self.back = sems, back

    def one(self, i):
        find = token_target if self.back else sequence_target
        device, place = find(self.me[0], self.me[1], i, self.splits)
        return (
            self.me,
            self.source.at[i],
            self.target.at[place],
            device,
            self.sems.at[0, i],
            self.sems.at[1, place],
        )

    def start(self):
        for i in (0, 1):
            move_start(*self.one(i))

    def wait_recv(self):
        for i in (0, 1):
            pltpu.make_async_copy(self.source.at[0], self.target.at[i], self.sems.at[1, i]).wait()

    def finish(self):
        for i in (0, 1):
            move_sent(*self.one(i))


def movers_of(me, splits, back):
    into = [sequence_target(me[0], me[1], i, splits)[0] for i in (0, 1)]
    home = [token_target(me[0], me[1], i, splits)[0] for i in (0, 1)]
    return list(zip(into, home)) if back else list(zip(home, into))


def first_kernel(shards, splits, tokens, cot, pieces, out_own, gate_pieces, *refs):
    rows, cot_rows, in_all, out_all, gate_rows, held = refs[:6]
    move_sems, cot_sems, group_sems, piece_sems, gate_sems, own_sem, in_sems, out_sems = refs[6:]
    me = (lax.axis_index("dp"), lax.axis_index("ctx"))
    group, place = me
    slow = shards // 2
    slot = place // 2
    line = [(group, place ^ (2 * by)) for by in range(1, slow)]
    wanted, block = place // slow, place % slow
    takers = [(group, 2 * (slot ^ by) + wanted) for by in range(slow)]
    givers = [(group, place % 2 * slow + block_by) for block_by in range(slow)]
    movers = movers_of(me, splits, False) + list(zip(givers, takers))
    greet(me, [member(me, by) for by in range(1, 8)] + line, movers)
    swap = GroupExchange(me, pieces, held, piece_sems)
    gate_swap = GroupExchange(me, gate_pieces, gate_rows, gate_sems)
    move = Moves(me, splits, tokens, rows.at[0, 0], move_sems, False)
    cot_move = Moves(me, splits, cot, cot_rows, cot_sems, False)

    def in_line(by):
        sems = (in_sems.at[0, by - 1], in_sems.at[1, by - 1])
        return remote(held, in_all.at[slot], sems, line[by - 1])

    def out_send(by):
        return (
            me,
            out_own,
            out_all.at[block],
            takers[by],
            out_sems.at[0, by],
            out_sems.at[1, block],
        )

    own = pltpu.make_async_copy(held, in_all.at[slot], own_sem)
    swap.start()
    move.start()
    swap.finish()
    for by in range(1, slow):
        in_line(by).start()
    own.start()
    gate_swap.start()
    move.wait_recv()
    spread = GroupGather(me, rows, group_sems, rows.at[0, 0], slice(0, tokens.shape[1]))
    spread.start()
    for by in range(slow):
        move_start(*out_send(by))
    for by in range(1, slow):
        in_line(by).wait()
    cot_move.start()
    spread.pass_on()
    spread.finish()
    own.wait()
    for by in range(slow):
        pltpu.make_async_copy(out_own, out_all.at[by], out_sems.at[1, by]).wait()
    for by in range(slow):
        move_sent(*out_send(by))
    gate_swap.finish()
    cot_move.wait_recv()
    move.finish()
    cot_move.finish()


def first_exchange(tokens, cot, pieces, out_own, gate_pieces, shards, splits, identity):
    low = jnp.bfloat16
    slow = shards // 2
    any_space = pl.BlockSpec(memory_space=pl.ANY)
    dma = pltpu.SemaphoreType.DMA
    made = pl.pallas_call(
        functools.partial(first_kernel, shards, splits),
        out_shape=(
            jax.ShapeDtypeStruct((2, 4) + tokens.shape, low),
            jax.ShapeDtypeStruct(cot.shape, low),
            jax.ShapeDtypeStruct((slow,) + pieces.shape, low),
            jax.ShapeDtypeStruct((slow,) + out_own.shape, low),
            jax.ShapeDtypeStruct(gate_pieces.shape, low),
            jax.ShapeDtypeStruct(pieces.shape, low),
        ),
        in_specs=[any_space] * 5,
        out_specs=(any_space,) * 6,
        scratch_shapes=[
            dma((2, 2)),
            dma((2, 2)),
            dma((2, 10)),
            dma((2, 8)),
            dma((2, 8)),
            dma,
            dma((2, slow - 1)),
            dma((2, slow)),
        ],
        compiler_params=pltpu.CompilerParams(
            collective_id=identity, has_side_effects=True, vmem_limit_bytes=8 << 20
        ),
        cost_estimate=pl.CostEstimate(flops=0, bytes_accessed=200 << 20, transcendentals=0),
    )(tokens, cot, pieces, out_own, gate_pieces)
    return made[:5]


class GroupScatter:
    def __init__(self, me, parts, buffers, sems, steps):
        self.parts = parts
        self.core_in, self.kept, self.sent, self.came, self.held = buffers[:5]
        self.sent_last, self.came_last = buffers[5:]
        self.core_sems, self.kept_sems, self.one_sems, self.last_sems = sems
        self.core, self.across, self.beside = member(me, 2), member(me, 4), member(me, 1)
        self.size = parts.shape[3] // steps
        self.steps = steps

    def window(self, k):
        return slice(k * self.size, (k + 1) * self.size)

    def to_core(self, k, j):
        return remote(
            self.parts.at[:, 2 * j + 1, :, self.window(k)],
            self.core_in.at[:, j, :, self.window(k)],
            (self.core_sems.at[0, k, j], self.core_sems.at[1, k, j]),
            self.core,
        )

    def keep(self, k, j):
        return pltpu.make_async_copy(
            self.parts.at[:, 2 * j, :, self.window(k)],
            self.kept.at[:, j, :, self.window(k)],
            self.kept_sems.at[k, j],
        )

    def first(self, k, half):
        return remote(
            self.sent.at[half, :, self.window(k)],
            self.came.at[half, :, self.window(k)],
            (self.one_sems.at[0, k, half], self.one_sems.at[1, k, half]),
            (self.beside, self.across)[half],
        )

    def second(self, k, half):
        return remote(
            self.sent_last.at[half, self.window(k)],
            self.came_last.at[half, self.window(k)],
            (self.last_sems.at[0, k, half], self.last_sems.at[1, k, half]),
            (self.across, self.beside)[half],
        )

    def start(self):
        for k in range(self.steps):
            for j in (0, 1):
                self.to_core(k, j).start()
                self.keep(k, j).start()

    def send_first(self, k):
        wide = jnp.float32
        rows = self.window(k)
        for j in (0, 1):
            self.keep(k, j).wait()
            self.to_core(k, j).wait_recv()
        for half in (0, 1):
            for other in (0, 1):
                at = (1, other) if half == 0 else (other, 1)
                both = self.kept[at[0], at[1], half, rows].astype(wide)
                both = both + self.core_in[at[0], at[1], half, rows].astype(wide)
                self.sent[half, other, rows] = both.astype(jnp.bfloat16)
            self.first(k, half).start()
        for half in (0, 1):
            for other in (0, 1):
                at = (0, other) if half == 0 else (other, 0)
                both = self.kept[at[0], at[1], half, rows].astype(wide)
                self.held[half, other, rows] = both + self.core_in[at[0], at[1], half, rows].astype(
                    wide
                )

    def send_second(self, k):
        wide = jnp.float32
        rows = self.window(k)
        for half in (0, 1):
            self.first(k, half).wait_recv()
            both = self.held[half, 1, rows] + self.came[half, 1, rows].astype(wide)
            self.sent_last[half, rows] = both.astype(jnp.bfloat16)
            self.second(k, half).start()
            self.held[half, 0, rows] = self.held[half, 0, rows] + self.came[half, 0, rows].astype(
                wide
            )

    def total(self, k, half):
        self.second(k, half).wait_recv()
        rows = self.window(k)
        return self.held[half, 0, rows] + self.came_last[half, rows].astype(jnp.float32)

    def finish(self):
        for k in range(self.steps):
            for j in (0, 1):
                self.to_core(k, j).wait_send()
            for half in (0, 1):
                self.first(k, half).wait_send()
                self.second(k, half).wait_send()


def scatter_scratch(rows, width, steps):
    low, wide = jnp.bfloat16, jnp.float32
    dma = pltpu.SemaphoreType.DMA
    return [
        pltpu.VMEM((2, 2, 2, rows, width), low),
        pltpu.VMEM((2, 2, 2, rows, width), low),
        pltpu.VMEM((2, 2, rows, width), low),
        pltpu.VMEM((2, 2, rows, width), low),
        pltpu.VMEM((2, 2, rows, width), wide),
        pltpu.VMEM((2, rows, width), low),
        pltpu.VMEM((2, rows, width), low),
        dma((2, steps, 2)),
        dma((steps, 2)),
        dma((2, steps, 2)),
        dma((2, steps, 2)),
    ]


def reordered(rows, slow, back):
    each = rows.shape[1] // (4 * slow)
    if back:
        starts = [s * 4 + dp for dp in range(4) for s in range(slow)]
    else:
        starts = [dp * slow + s for s in range(slow) for dp in range(4)]
    return jnp.concatenate([rows[:, i * each : (i + 1) * each] for i in starts], 1)


def turn_kernel(slow, steps, backward, parts, gain, *refs):
    if backward:
        residual, cot, result, gain_grad, rows = refs[:5]
        scratch = refs[5:]
    else:
        tokens, result, rows = refs[:3]
        scratch = refs[3:]
    own, own_sems, group_sems = scratch[:3]
    me = (lax.axis_index("dp"), lax.axis_index("ctx"))
    greet(me, [member(me, by) for by in (1, 2, 4)], [])
    scatter = GroupScatter(me, parts, scratch[3:10], scratch[10:], steps)
    gathers = [GroupGather(me, rows, group_sems.at[k], own, scatter.window(k)) for k in range(steps)]
    scatter.start()
    for k in range(steps):
        scatter.send_first(k)
    for k in range(steps):
        scatter.send_second(k)
    for k in range(steps):
        span = scatter.window(k)
        for half in (0, 1):
            total = scatter.total(k, half)
            if backward:
                values = residual[half, span]
                factor = lax.rsqrt(jnp.mean(values * values, -1, keepdims=True) + norm_eps)
                normed = values * factor
                total = reordered(total, slow, True)
                part = jnp.sum(total * normed, 0, keepdims=True)
                if k == 0 and half == 0:
                    gain_grad[...] = part
                else:
                    gain_grad[...] += part
                back = total * gain[...]
                back = factor * (back - normed * jnp.mean(back * normed, -1, keepdims=True))
                back = cot[half, span].astype(jnp.float32) + back
                result[half, span] = back
                own[half, span] = back.astype(jnp.bfloat16)
            else:
                values = tokens[half, span].astype(jnp.float32) + total
                factor = lax.rsqrt(jnp.mean(values * values, -1, keepdims=True) + norm_eps)
                result[half, span] = values
                own[half, span] = reordered(values * factor * gain[...], slow, False).astype(
                    jnp.bfloat16
                )
        gathers[k].start()
        keep = pltpu.make_async_copy(own.at[:, span], rows.at[0, 0, :, span], own_sems.at[k])
        keep.start()
    for k in range(steps):
        gathers[k].pass_on()
    for k in range(steps):
        gathers[k].finish()
        span = scatter.window(k)
        pltpu.make_async_copy(own.at[:, span], rows.at[0, 0, :, span], own_sems.at[k]).wait()
    scatter.finish()


def turn(parts, gain, rows_in, slow, backward, identity):
    low, wide = jnp.bfloat16, jnp.float32
    dma = pltpu.SemaphoreType.DMA
    rows, width = parts.shape[3:]
    steps = 2
    any_space = pl.BlockSpec(memory_space=pl.ANY)
    vmem = pl.BlockSpec(memory_space=pltpu.VMEM)
    shapes = [jax.ShapeDtypeStruct((2, rows, width), wide)]
    if backward:
        shapes.append(jax.ShapeDtypeStruct((1, width), wide))
    return pl.pallas_call(
        functools.partial(turn_kernel, slow, steps, backward),
        out_shape=tuple(shapes) + (jax.ShapeDtypeStruct((2, 4, 2, rows, width), low),),
        in_specs=[any_space, vmem] + [vmem] * len(rows_in),
        out_specs=tuple([vmem] * len(shapes) + [any_space]),
        scratch_shapes=[pltpu.VMEM((2, rows, width), low), dma((steps,)), dma((steps, 2, 10))]
        + scatter_scratch(rows, width, steps),
        compiler_params=pltpu.CompilerParams(
            collective_id=identity, has_side_effects=True, vmem_limit_bytes=48 << 20
        ),
        cost_estimate=pl.CostEstimate(flops=0, bytes_accessed=250 << 20, transcendentals=0),
    )(parts, gain, *rows_in)


class LineSum:
    def __init__(self, me, slow, parts, buffers, sems):
        self.parts = parts
        self.kept, self.arrived = buffers
        self.sems, self.own_sem = sems
        self.slot = me[1] // 2
        self.slow = slow
        self.line = [(me[0], me[1] ^ (2 * by)) for by in range(1, slow)]

    def hop(self, by):
        sems = (self.sems.at[0, by - 1], self.sems.at[1, by - 1])
        return remote(
            self.parts.at[self.slot ^ by], self.arrived.at[by - 1], sems, self.line[by - 1]
        )

    def own(self):
        return pltpu.make_async_copy(self.parts.at[self.slot], self.kept, self.own_sem)

    def start(self):
        for by in range(1, self.slow):
            self.hop(by).start()
        self.own().start()

    def total(self):
        self.own().wait()
        value = self.kept[...].astype(jnp.float32)
        for by in range(1, self.slow):
            self.hop(by).wait_recv()
            value = value + self.arrived[by - 1].astype(jnp.float32)
        return value

    def finish(self):
        for by in range(1, self.slow):
            self.hop(by).wait_send()


def line_scratch(shape, kind, slow):
    dma = pltpu.SemaphoreType.DMA
    return [
        pltpu.VMEM(shape, kind),
        pltpu.VMEM((slow - 1,) + shape, kind),
        dma((2, slow - 1)),
        dma,
    ]


def last_kernel(shards, splits, steps, in_parts, out_parts, gate_parts, in_back, *refs):
    gain, gain_two_grad, tokens, back_rows = refs[:4]
    in_total, out_total, gate_total, gains_total, tokens_grad = refs[4:9]
    scratch = list(refs[9:])

    def take(count):
        taken = scratch[:count]
        del scratch[:count]
        return taken

    me = (lax.axis_index("dp"), lax.axis_index("ctx"))
    group, place = me
    slow = shards // 2
    slot, half = place // 2, place % 2
    owned = in_parts.shape[2]
    home = (group, half * slow + slot)
    movers = movers_of(me, splits, True)
    movers.append(((group, place % slow * 2 + place // slow), home))
    line = [(group, place ^ (2 * by)) for by in range(1, slow)]
    greet(me, [member(me, by) for by in range(1, 8)] + line, movers)
    one = take(11)
    back_sum = GroupScatter(me, in_back, one[:7], one[7:], steps)
    line_in = take(4)
    line_out = take(4)
    line_gains = take(4)
    in_done, out_done, gains_own, gains_done, made_one, gain_grad = take(6)
    in_sems, gate_sems, gains_sems, one_sems, home_sems = take(5)
    in_line = LineSum(me, slow, in_parts, line_in[:2], line_in[2:])
    out_line = LineSum(me, slow, out_parts, line_out[:2], line_out[2:])
    gains_line = LineSum(me, slow, gains_own, line_gains[:2], line_gains[2:])
    in_swap = GroupExchange(me, in_done, in_total, in_sems)
    gate_swap = GroupExchange(me, gate_parts, gate_total, gate_sems)
    gains_swap = GroupExchange(me, gains_done, gains_total, gains_sems)
    move_grad = Moves(me, splits, made_one, tokens_grad, one_sems, True)
    back_sum.start()
    in_line.start()
    out_line.start()
    for k in range(steps):
        back_sum.send_first(k)
    for k in range(steps):
        back_sum.send_second(k)
    for k in range(steps):
        span = back_sum.window(k)
        for part in (0, 1):
            total = back_sum.total(k, part)
            values = tokens[part, span].astype(jnp.float32)
            normed, factor = norm_parts(values)
            grad = jnp.sum(total * normed, 0, keepdims=True)
            if k == 0 and part == 0:
                gain_grad[...] = grad
            else:
                gain_grad[...] += grad
            value = back_rows[part, span] + norm_back(total * gain[...], normed, factor)
            made_one[part, span] = value.astype(jnp.bfloat16)
    move_grad.start()
    gains_own[...] = jnp.zeros_like(gains_own)
    for dp in range(4):
        for s in range(slow):
            for side in range(2):
                at = ((dp * slow + s) * 2 + side) * owned
                index = 2 * dp + side
                gains_own[s, index, 0:1, 0:owned] = gain_grad[:, at : at + owned]
                gains_own[s, index, 0:1, owned : 2 * owned] = gain_two_grad[:, at : at + owned]
    gains_line.start()
    gate_swap.start()
    in_done[...] = in_line.total().astype(jnp.bfloat16)
    in_swap.start()
    gains_done[...] = gains_line.total()
    gains_swap.start()
    out_done[...] = out_line.total().astype(jnp.bfloat16)
    to_home = (me, out_done, out_total, home, home_sems.at[0], home_sems.at[1])
    move_start(*to_home)
    pltpu.make_async_copy(out_done, out_total, home_sems.at[1]).wait()
    move_sent(*to_home)
    for swap in (in_swap, gate_swap, gains_swap):
        swap.finish()
    move_grad.wait_recv()
    move_grad.finish()
    for part in (in_line, out_line, gains_line, back_sum):
        part.finish()


def last_sums(in_parts, out_parts, gate_parts, in_back, others, shards, splits, identity):
    low, wide = jnp.bfloat16, jnp.float32
    slow = shards // 2
    steps = 2
    any_space = pl.BlockSpec(memory_space=pl.ANY)
    vmem = pl.BlockSpec(memory_space=pltpu.VMEM)
    dma = pltpu.SemaphoreType.DMA
    rows, width = in_back.shape[3:]
    gains_shape = (8, 8, 128)
    moved = jax.ShapeDtypeStruct((2, rows, width), low)
    return pl.pallas_call(
        functools.partial(last_kernel, shards, splits, steps),
        out_shape=(
            jax.ShapeDtypeStruct(in_parts.shape[1:], low),
            jax.ShapeDtypeStruct(out_parts.shape[1:], low),
            jax.ShapeDtypeStruct(gate_parts.shape, low),
            jax.ShapeDtypeStruct(gains_shape, wide),
            moved,
        ),
        in_specs=[any_space] * 4 + [vmem] * 4,
        out_specs=(any_space,) * 5,
        scratch_shapes=scatter_scratch(rows, width, steps)
        + line_scratch(in_parts.shape[1:], low, slow)
        + line_scratch(out_parts.shape[1:], low, slow)
        + line_scratch(gains_shape, wide, slow)
        + [
            pltpu.VMEM(in_parts.shape[1:], low),
            pltpu.VMEM(out_parts.shape[1:], low),
            pltpu.VMEM((slow,) + gains_shape, wide),
            pltpu.VMEM(gains_shape, wide),
            pltpu.VMEM(moved.shape, low),
            pltpu.VMEM((1, width), wide),
            dma((2, 8)),
            dma((2, 8)),
            dma((2, 8)),
            dma((2, 2)),
            dma((2,)),
        ],
        compiler_params=pltpu.CompilerParams(
            collective_id=identity, has_side_effects=True, vmem_limit_bytes=56 << 20
        ),
        cost_estimate=pl.CostEstimate(flops=0, bytes_accessed=300 << 20, transcendentals=0),
    )(in_parts, out_parts, gate_parts, in_back, *others)


def position_tables(blocks, rows):
    frequency = rope_base ** (-(np.arange(HEAD // 2) * 2.0 / HEAD))
    angles = np.arange(blocks * rows).reshape(blocks, rows, 1) * frequency
    cos, sin = np.cos(angles), np.sin(angles)
    cosine = np.concatenate([cos, cos, cos, cos], 2)
    sines = np.concatenate([-sin, sin, -sin, sin], 2)
    return jnp.asarray(cosine, jnp.float32), jnp.asarray(sines, jnp.float32)


def attend(order, where, qkv, tables, cot, q_heads, kv_heads, identity):
    seqs, length, cols = qkv.shape
    blocks = order.shape[0]
    rows = length // blocks
    whole = pl.BlockSpec(memory_space=pltpu.VMEM)
    small = pl.BlockSpec(memory_space=pltpu.SMEM)
    any_space = pl.BlockSpec(memory_space=pl.ANY)
    return pl.pallas_call(
        functools.partial(attend_kernel, q_heads, kv_heads, 256),
        out_shape=(
            jax.ShapeDtypeStruct((seqs, blocks, rows, q_heads * HEAD), jnp.bfloat16),
            jax.ShapeDtypeStruct((seqs, q_heads, length), jnp.float32),
            jax.ShapeDtypeStruct((seqs, length, cols), jnp.bfloat16),
            jax.ShapeDtypeStruct((2, 4) + cot.shape, cot.dtype),
        ),
        in_specs=[small, small, whole, whole, whole, any_space],
        out_specs=(whole, whole, whole, any_space),
        scratch_shapes=[
            pltpu.VMEM((blocks, rows, q_heads * HEAD), jnp.bfloat16),
            pltpu.SemaphoreType.DMA((2, 10)),
            pltpu.SemaphoreType.DMA,
        ],
        compiler_params=pltpu.CompilerParams(
            collective_id=identity, has_side_effects=True, vmem_limit_bytes=40 << 20
        ),
        cost_estimate=pl.CostEstimate(
            flops=2 * seqs * length * length * q_heads * HEAD,
            bytes_accessed=100 << 20,
            transcendentals=seqs * length * length * q_heads // 2,
        ),
    )(order, where, qkv.reshape(seqs, blocks, rows, cols), *tables, cot)


def attend_back(
    order, where, kept, back, lse, tables, out_rows, residual, q_heads, kv_heads, splits, identity
):
    seqs, length, cols = kept.shape
    blocks = order.shape[0]
    block = length // blocks
    group = q_heads // kv_heads
    rows, width = out_rows.shape[3:]
    steps = 2
    whole = pl.BlockSpec(memory_space=pltpu.VMEM)
    small = pl.BlockSpec(memory_space=pltpu.SMEM)
    any_space = pl.BlockSpec(memory_space=pl.ANY)
    return pl.pallas_call(
        functools.partial(attend_back_kernel, q_heads, kv_heads, 256, splits, steps),
        out_shape=(
            jax.ShapeDtypeStruct((seqs, blocks, block, cols), jnp.bfloat16),
            jax.ShapeDtypeStruct((2, rows, width), jnp.bfloat16),
        ),
        in_specs=[small, small] + [whole] * 5 + [any_space, whole],
        out_specs=(whole, any_space),
        scratch_shapes=[
            pltpu.VMEM((length, q_heads * HEAD), jnp.bfloat16),
            pltpu.VMEM((blocks, block, cols), jnp.float32),
            pltpu.VMEM((group, length), jnp.float32),
            pltpu.VMEM((group * HEAD, length), jnp.float32),
            pltpu.VMEM((2, rows, width), jnp.bfloat16),
            pltpu.SemaphoreType.DMA((2, 2)),
        ]
        + scatter_scratch(rows, width, steps),
        compiler_params=pltpu.CompilerParams(
            collective_id=identity, has_side_effects=True, vmem_limit_bytes=56 << 20
        ),
        cost_estimate=pl.CostEstimate(
            flops=7 * seqs * length * length * q_heads * HEAD,
            bytes_accessed=100 << 20,
            transcendentals=seqs * length * length * q_heads // 2,
        ),
    )(
        order,
        where,
        kept,
        back.reshape(seqs, blocks, block, -1),
        lse,
        *tables,
        out_rows,
        residual,
    )


def gate_update_kernel(slow, step_rate, grad, weight, first, second, new_first, new_second, new):
    units = grad.shape[2] // slow
    pieces = [grad[half, :, s * units : (s + 1) * units] for s in range(slow) for half in (0, 1)]
    gradient = jnp.concatenate(pieces, 1).astype(jnp.float32)
    new_first[...], new_second[...], new[...] = adam_update(
        weight[...], gradient, first[...], second[...], step_rate, weight_decay
    )


def gate_update(grad, weight, first, second, slow, step_rate):
    rows, width = weight.shape
    block = pl.BlockSpec((rows, width // 8), lambda side, dp: (0, 4 * side + dp))
    piece = pl.BlockSpec((2, rows, width // 16), lambda side, dp: (dp, 0, side))
    return pl.pallas_call(
        functools.partial(gate_update_kernel, slow, step_rate),
        grid=(2, 4),
        out_shape=(jax.ShapeDtypeStruct(weight.shape, jnp.float32),) * 3,
        in_specs=[piece, block, block, block],
        out_specs=(block,) * 3,
        compiler_params=pltpu.CompilerParams(vmem_limit_bytes=32 << 20),
    )(grad, weight, first, second)


def local(
    tokens,
    cotangent,
    block_order,
    attention_in,
    attention_out,
    gate_up,
    down_matrix,
    gains,
    mean_attention_in,
    mean_attention_out,
    mean_gate_up,
    mean_down,
    mean_gains,
    square_attention_in,
    square_attention_out,
    square_gate_up,
    square_down,
    square_gains,
):
    seq_count, shard_rows, width = tokens.shape
    shards = lax.axis_size("ctx")
    slow = shards // 2
    mine = lax.axis_index("dp")
    beside = lax.axis_index("ctx") % 2
    low = jnp.bfloat16
    owned = attention_in.shape[0]
    hidden_units = gate_up.shape[1] // 2
    part_hidden = hidden_units // 8
    units = down_matrix.shape[0]
    part_q = HEADS * HEAD // 8
    part_k = KV_HEADS * HEAD // 8
    part_cols = part_q + 2 * part_k
    count = seq_count * shard_rows
    together = 8 * count
    spread = shards // (4 * seq_count)
    splits = max(1, slow // 8)
    seqs = 2 // spread if spread < 2 else 1
    length = shards * shard_rows
    q_heads = HEADS // 8 // splits
    kv_heads = KV_HEADS // 8

    in_low = attention_in.astype(low)
    gains_row = jnp.pad(gains.astype(low).reshape(1, -1), ((0, 15), (0, part_cols - 2 * owned)))
    pieces = jnp.stack(
        [
            jnp.concatenate(
                [
                    jnp.concatenate(
                        [
                            in_low[:, i * part_q : (i + 1) * part_q],
                            in_low[:, 8 * part_q + i * part_k :][:, :part_k],
                            in_low[:, 8 * (part_q + part_k) + i * part_k :][:, :part_k],
                        ],
                        1,
                    ),
                    gains_row,
                ]
            )
            for i in range(8)
        ]
    )
    gate_low = gate_up.astype(low)
    gate_pieces = jnp.stack(
        [
            jnp.concatenate(
                [
                    gate_low[:, side * hidden_units + (dp * shards + 2 * s + half) * units :][
                        :, :units
                    ]
                    for side in range(2)
                    for s in range(slow)
                ],
                1,
            )
            for dp in range(4)
            for half in range(2)
        ]
    )
    tokens_all, cot_own, in_all, w_out, gate_rows = first_exchange(
        tokens, cotangent, pieces, attention_out.astype(low), gate_pieces, shards, spread, 1
    )
    in_all = in_all.reshape(slow, 4, 2, owned + 16, part_cols).swapaxes(0, 1)
    w_in = in_all[:, :, :, :owned].reshape(width, part_cols)
    w_out = w_out.reshape(part_q, width)
    gains_all = in_all[:, :, :, owned, : 2 * owned].reshape(-1, 2, owned)
    gains_all = gains_all.astype(jnp.float32).swapaxes(0, 1).reshape(2, width)
    gain_one, gain_two = gains_all[0], gains_all[1]
    w_gate = gather_line(gate_rows.reshape(8 * owned, 2 * part_hidden))

    normed_all, _ = norm_parts(tokens_all.reshape(together, width).astype(jnp.float32))
    input_one = (normed_all * gain_one).astype(low)
    qkv = dot_nn(input_one, w_in)
    orders = block_order.reshape(2 * splits if spread > 1 else 1, 4, -1)
    slot_order = jnp.concatenate(
        [
            orders[(2 * s + (beside ^ i)) if spread > 1 else 0, part_owner(mine ^ j)]
            for s in range(splits)
            for i in range(2 // seqs)
            for j in range(4)
        ]
    )
    tables = position_tables(slot_order.shape[0], length // slot_order.shape[0])
    groups = [
        [2 * (s * splits + g) + half for g in range(splits)]
        for s in range(slow // splits)
        for half in (0, 1)
    ]

    def split_heads(values, widths, copies):
        parts = []
        start = 0
        for each, repeat in zip(widths, copies):
            kinds = splits // repeat
            piece = values[:, start : start + kinds * each].reshape(-1, kinds, each)
            parts.append(jnp.repeat(piece.swapaxes(0, 1), repeat, axis=0))
            start += kinds * each
        sent = jnp.concatenate(parts, 2)
        got = lax.all_to_all(sent, "ctx", 0, 0, axis_index_groups=groups, tiled=True)
        return got.reshape(length, -1)

    def join_heads(values):
        sent = values.reshape(splits, together, -1)
        return lax.all_to_all(sent, "ctx", 0, 0, axis_index_groups=groups, tiled=True)

    q_width, k_width = q_heads * HEAD, kv_heads * HEAD
    if splits > 1:
        qkv = split_heads(qkv, (q_width, k_width, k_width), (1, splits, splits))
    qkv = qkv.reshape(seqs, length, -1)
    blocks = slot_order.shape[0]
    slot_where = jnp.sum(
        jnp.where(
            slot_order[None, :] == jnp.arange(blocks, dtype=jnp.int32)[:, None],
            jnp.arange(blocks, dtype=jnp.int32)[None, :],
            0,
        ),
        1,
    )
    attended, lse, kept, back_all = attend(
        slot_order, slot_where, qkv, tables, cot_own, q_heads, kv_heads, 2
    )
    cot_rows = cot_own
    back_all = back_all.reshape(together, width)
    if splits > 1:
        attended = join_heads(attended.reshape(length, q_width)).swapaxes(0, 1)
    attended = attended.reshape(together, part_q)

    def parts(values):
        return values.astype(low).reshape((2, 4) + tokens.shape)

    residual_rows, input_two = turn(
        parts(dot_nn(attended, w_out)), gain_two[None], [tokens_all[0, 0]], slow, False, 3
    )
    input_two = input_two.reshape(together, width)
    after = 0.0 * (residual_rows[0, 0, 0] + w_gate[0, 0].astype(jnp.float32))
    w_down = gather_line((down_matrix + after).astype(low))
    gate_both = dot_nn(input_two, w_gate)
    gate_part = gate_both[:, :part_hidden]
    up_part = gate_both[:, part_hidden:]
    sigmoid_gate = jax.nn.sigmoid(gate_part)
    active = gate_part * sigmoid_gate
    hidden = lax.optimization_barrier((active * up_part).astype(low))
    grad_down = lax.optimization_barrier(dot_tn(hidden, back_all).astype(low))
    down_sum = sum_line(grad_down + 0.0 * w_down[0, 0]).astype(jnp.float32)
    back_hidden = dot_nt(back_all, w_down)
    back_gate = back_hidden * up_part * sigmoid_gate * (1.0 + gate_part * (1.0 - sigmoid_gate))
    back_upper = back_hidden * active
    back_gate_up = jnp.concatenate([back_gate, back_upper], 1).astype(low)
    gate_low = sum_line(dot_tn(input_two, back_gate_up).astype(low))
    back_rows, grad_gain_two, back_residual_all = turn(
        parts(dot_nt(back_gate_up, w_gate)),
        gain_two[None],
        [residual_rows, cot_rows],
        slow,
        True,
        4,
    )
    back_residual_all = back_residual_all.reshape(together, width)
    grad_out = dot_tn(attended, back_residual_all).astype(low)
    back_attended = dot_nt(back_residual_all, w_out).astype(low)
    if splits > 1:
        back_attended = split_heads(back_attended, (q_width,), (1,))
    back_projected, block_out = attend_back(
        slot_order,
        slot_where,
        kept,
        back_attended.reshape(seqs, length, -1),
        lse,
        tables,
        parts(dot_nn(hidden, w_down)),
        residual_rows,
        q_heads,
        kv_heads,
        spread,
        6,
    )
    if splits > 1:
        back_projected = join_heads(back_projected.reshape(length, -1)).astype(jnp.float32)
        back_projected = jnp.concatenate(
            [
                back_projected[..., :q_width].swapaxes(0, 1).reshape(together, part_q),
                back_projected[..., q_width:].sum(0),
            ],
            1,
        ).astype(low)
    back_projected = back_projected.reshape(together, part_cols)
    grad_in = dot_tn(input_one, back_projected).astype(low)
    grad_in = grad_in.reshape(4, slow, 2 * owned, part_cols).swapaxes(0, 1)
    in_sum, out_sum, gate_sum, gains_sum, tokens_grad = last_sums(
        grad_in.reshape(slow, 8, owned, part_cols),
        grad_out.reshape(slow, owned, width),
        gate_low.reshape(8, owned, 2 * part_hidden),
        parts(dot_nt(back_projected, w_in)),
        [gain_one[None], grad_gain_two, tokens_all[0, 0], back_rows],
        shards,
        spread,
        5,
    )
    tokens_grad = tokens_grad.astype(jnp.float32)
    out_sum = out_sum.astype(jnp.float32)
    gains_sum = gains_sum[:, 0, : 2 * owned].reshape(8, 2, owned).sum(0)
    cuts = ((0, part_q), (part_q, part_q + part_k), (part_q + part_k, part_cols))
    in_sum = jnp.concatenate(
        [in_sum[i, :, first:last] for first, last in cuts for i in range(8)], 1
    ).astype(jnp.float32)
    new_in = adam_update(
        attention_in,
        in_sum,
        mean_attention_in,
        square_attention_in,
        input_boost * D ** (-0.5),
        weight_decay,
    )
    new_out = adam_update(
        attention_out,
        out_sum,
        mean_attention_out,
        square_attention_out,
        (HEADS * HEAD // 32) ** (-0.5),
        weight_decay,
    )
    new_gate = gate_update(
        gate_sum, gate_up, mean_gate_up, square_gate_up, slow, D ** (-0.5)
    )
    new_down = adam_update(
        down_matrix, down_sum, mean_down, square_down, FF ** (-0.5), weight_decay
    )
    new_gain = adam_update(gains, gains_sum, mean_gains, square_gains, gain_rate, 0.0)
    return (
        block_out,
        tokens_grad,
        new_in[0],
        new_in[1],
        new_in[2],
        new_out[0],
        new_out[1],
        new_out[2],
        new_gate[0],
        new_gate[1],
        new_gate[2],
        new_down[0],
        new_down[1],
        new_down[2],
        new_gain[0],
        new_gain[1],
        new_gain[2],
    )


def solution(mesh):
    in_specs = (
        P("dp", "ctx", None),
        P("dp", "ctx", None),
        P(),
        P(("dp", "ctx"), None),
        P(("dp", "ctx"), None),
        P(("dp", "ctx"), None),
        P(("dp", "ctx"), None),
        P(None, ("dp", "ctx")),
        P(("dp", "ctx"), None),
        P(("dp", "ctx"), None),
        P(("dp", "ctx"), None),
        P(("dp", "ctx"), None),
        P(None, ("dp", "ctx")),
        P(("dp", "ctx"), None),
        P(("dp", "ctx"), None),
        P(("dp", "ctx"), None),
        P(("dp", "ctx"), None),
        P(None, ("dp", "ctx")),
    )
    out_specs = (
        P("dp", "ctx", None),
        P("dp", "ctx", None),
        P(("dp", "ctx"), None),
        P(("dp", "ctx"), None),
        P(("dp", "ctx"), None),
        P(("dp", "ctx"), None),
        P(("dp", "ctx"), None),
        P(("dp", "ctx"), None),
        P(("dp", "ctx"), None),
        P(("dp", "ctx"), None),
        P(("dp", "ctx"), None),
        P(("dp", "ctx"), None),
        P(("dp", "ctx"), None),
        P(("dp", "ctx"), None),
        P(None, ("dp", "ctx")),
        P(None, ("dp", "ctx")),
        P(None, ("dp", "ctx")),
    )
    return jax.shard_map(local, mesh=mesh, in_specs=in_specs, out_specs=out_specs, check_vma=False)
```

```python
import functools

import jax
import jax.numpy as jnp
import numpy as np
from jax import lax
from jax.experimental import pallas as pl
from jax.experimental.pallas import tpu as pltpu
from jax.sharding import PartitionSpec as P

D = 2048
HEADS = 32
KV_HEADS = 8
HEAD = 64
FF = 8192
STEP = 5


norm_eps = 1e-05
rope_base = 500000.0
beta_one = 0.9
beta_two = 0.95
gain_rate = 1.25
input_boost = 2.5
weight_decay = 0.1
adam_eps = 1e-08
masked_score = -1e30


def norm_parts(values):
    factor = lax.rsqrt(jnp.mean(values * values, -1, keepdims=True) + norm_eps)
    return (values * factor, factor)


def norm_back(back_normed, normed, factor):
    return factor * (back_normed - normed * jnp.mean(back_normed * normed, -1, keepdims=True))


def adam_update(weight, gradient, first_moment, second_moment, step_rate, decay_rate):
    first_new = beta_one * first_moment + (1.0 - beta_one) * gradient
    second_new = beta_two * second_moment + (1.0 - beta_two) * gradient * gradient
    update = (
        first_new
        / (1.0 - beta_one**STEP)
        / (jnp.sqrt(second_new / (1.0 - beta_two**STEP)) + adam_eps)
    )
    return (first_new, second_new, weight - step_rate * (update + decay_rate * weight))


def line_groups(shards):
    return [[2 * s + half for s in range(shards // 2)] for half in (0, 1)]


def gather_line(rows):
    return lax.all_gather(
        rows, "ctx", axis=0, tiled=True, axis_index_groups=line_groups(lax.axis_size("ctx"))
    )


def sum_line(gradient):
    return lax.psum_scatter(
        gradient,
        "ctx",
        scatter_dimension=0,
        tiled=True,
        axis_index_groups=line_groups(lax.axis_size("ctx")),
    )


def dot_nn(a, b):
    return lax.dot_general(a, b, (((1,), (0,)), ((), ())), preferred_element_type=jnp.float32)


def dot_nt(a, b):
    return lax.dot_general(a, b, (((1,), (1,)), ((), ())), preferred_element_type=jnp.float32)


def dot_tn(a, b):
    return lax.dot_general(a, b, (((0,), (0,)), ((), ())), preferred_element_type=jnp.float32)


def causal_keep(tile):
    keys = lax.broadcasted_iota(jnp.int32, (tile, tile), 0)
    queries = lax.broadcasted_iota(jnp.int32, (tile, tile), 1)
    return keys <= queries


def turn_group(values, cos, sin, forward):
    lanes = lax.broadcasted_iota(jnp.int32, values.shape, 1)
    other = jnp.where(
        lanes % HEAD < HEAD // 2,
        pltpu.roll(values, 2 * HEAD - HEAD // 2, 1),
        pltpu.roll(values, HEAD // 2, 1),
    )
    if forward:
        return values * cos + other * sin
    return values * cos - other * sin


def turn_columns(values, start, turned_cols, cos, sin, forward):
    if start >= turned_cols:
        return values
    turned = turn_group(values, cos, sin, forward)
    if start + 2 * HEAD <= turned_cols:
        return turned
    lanes = lax.broadcasted_iota(jnp.int32, values.shape, 1)
    return jnp.where(lanes < turned_cols - start, turned, values)


def attend_kernel(
    q_heads,
    kv_heads,
    tile,
    order_ref,
    where_ref,
    all_qkv_ref,
    cos_ref,
    sin_ref,
    all_out_ref,
    all_lse_ref,
    all_kept_ref,
    made,
):
    for sequence in range(all_qkv_ref.shape[0]):
        attend_sequence(
            q_heads,
            kv_heads,
            tile,
            order_ref,
            where_ref,
            all_qkv_ref.at[sequence],
            cos_ref,
            sin_ref,
            all_out_ref.at[sequence],
            all_lse_ref.at[sequence],
            all_kept_ref.at[sequence],
            made,
        )


def attend_sequence(
    q_heads,
    kv_heads,
    tile,
    order_ref,
    where_ref,
    qkv_ref,
    cos_ref,
    sin_ref,
    out_ref,
    lse_ref,
    kept_ref,
    made,
):
    blocks, rows, cols = qkv_ref.shape
    length = blocks * rows
    group = q_heads // kv_heads
    q_cols, k_cols = q_heads * HEAD, kv_heads * HEAD
    scale = HEAD ** (-0.5)

    def take_block(i, _):
        start = pl.multiple_of(i * rows, rows)
        cos = cos_ref[i]
        sin = sin_ref[i]
        for c in range(0, cols, 2 * HEAD):
            values = qkv_ref[where_ref[i], :, c : c + 2 * HEAD]
            values = turn_columns(values, c, q_cols + k_cols, cos, sin, True)
            kept_ref[pl.ds(start, rows), c : c + 2 * HEAD] = values.astype(jnp.bfloat16)
        return 0

    lax.fori_loop(0, blocks, take_block, 0)
    keep = causal_keep(tile)
    for kv in range(kv_heads):
        k_at = q_cols + kv * HEAD
        v_at = q_cols + k_cols + kv * HEAD

        def query_step(i, _):
            q_start = pl.multiple_of(i * tile, tile)
            queries = [
                kept_ref[
                    pl.ds(q_start, tile), (kv * group + g) * HEAD : (kv * group + g + 1) * HEAD
                ]
                for g in range(group)
            ]

            def key_tile(j, carry, masked):
                k_start = pl.multiple_of(j * tile, tile)
                keys = kept_ref[pl.ds(k_start, tile), k_at : k_at + HEAD]
                values = kept_ref[pl.ds(k_start, tile), v_at : v_at + HEAD]
                result = []
                for g in range(group):
                    peak, total, weighted = carry[g]
                    scores = dot_nt(keys, queries[g]) * scale
                    if masked:
                        scores = jnp.where(keep, scores, masked_score)
                    new_peak = jnp.maximum(peak, jnp.max(scores, 0, keepdims=True))
                    weights = jnp.exp(scores - new_peak)
                    shrink = jnp.exp(peak - new_peak)
                    total = total * shrink + jnp.sum(weights, 0, keepdims=True)
                    weighted = weighted * shrink + dot_tn(values, weights.astype(jnp.bfloat16))
                    result.append((new_peak, total, weighted))
                return tuple(result)

            start = tuple(
                (
                    jnp.full((1, tile), masked_score, jnp.float32),
                    jnp.zeros((1, tile), jnp.float32),
                    jnp.zeros((HEAD, tile), jnp.float32),
                )
                for _ in range(group)
            )
            carry = lax.fori_loop(0, i, lambda j, c: key_tile(j, c, False), start)
            carry = key_tile(i, carry, True)
            for g in range(group):
                head = kv * group + g
                peak, total, weighted = carry[g]
                lse_ref[head : head + 1, pl.ds(q_start, tile)] = peak + jnp.log(total)
                made[pl.ds(i * (tile // rows), tile // rows), :, head * HEAD : (head + 1) * HEAD] = (
                    (weighted / total).T.astype(jnp.bfloat16).reshape(-1, rows, HEAD)
                )
            return 0

        lax.fori_loop(0, length // tile, query_step, 0)

    def give_block(i, _):
        out_ref[i] = made[order_ref[i]]
        return 0

    lax.fori_loop(0, blocks, give_block, 0)


def attend_back_kernel(
    q_heads,
    kv_heads,
    tile,
    splits,
    steps,
    order_ref,
    where_ref,
    all_kept_ref,
    all_back_ref,
    all_lse_ref,
    cos_ref,
    sin_ref,
    out_rows,
    residual,
    all_out_ref,
    block_out,
    *scratch,
):
    me = (lax.axis_index("dp"), lax.axis_index("ctx"))
    greet(me, [member(me, by) for by in (1, 2, 4)], movers_of(me, splits, True))
    work, scratch = scratch[:4], scratch[4:]
    made, move_sems = scratch[:2]
    scatter = GroupScatter(me, out_rows, scratch[2:9], scratch[9:], steps)
    move = Moves(me, splits, made, block_out, move_sems, True)

    def one():
        for k in range(steps):
            scatter.send_first(k)

    def two():
        for k in range(steps):
            scatter.send_second(k)

    def three():
        for k in range(steps):
            span = scatter.window(k)
            for part in (0, 1):
                value = residual[part, span] + scatter.total(k, part)
                made[part, span] = value.astype(jnp.bfloat16)
        move.start()

    tasks = [one, two, three]

    def pause():
        if tasks:
            tasks.pop(0)()

    scatter.start()
    for sequence in range(all_kept_ref.shape[0]):
        attend_back_sequence(
            q_heads,
            kv_heads,
            tile,
            pause,
            order_ref,
            where_ref,
            all_kept_ref.at[sequence],
            all_back_ref.at[sequence],
            all_lse_ref.at[sequence],
            cos_ref,
            sin_ref,
            all_out_ref.at[sequence],
            *work,
        )
    while tasks:
        pause()
    move.wait_recv()
    move.finish()
    scatter.finish()


def attend_back_sequence(
    q_heads,
    kv_heads,
    tile,
    pause,
    order_ref,
    where_ref,
    kept_ref,
    back_ref,
    lse_ref,
    cos_ref,
    sin_ref,
    out_ref,
    back_sorted,
    grad,
    delta_ref,
    dq_ref,
):
    length, cols = kept_ref.shape
    blocks, rows = back_ref.shape[:2]
    group = q_heads // kv_heads
    q_cols, k_cols = q_heads * HEAD, kv_heads * HEAD
    scale = HEAD ** (-0.5)
    tiles = length // tile

    def take_block(i, _):
        start = pl.multiple_of(i * rows, rows)
        back_sorted[pl.ds(start, rows), :] = back_ref[where_ref[i]]
        return 0

    lax.fori_loop(0, blocks, take_block, 0)
    keep = causal_keep(tile)
    for kv in range(kv_heads):
        k_at = q_cols + kv * HEAD
        v_at = q_cols + k_cols + kv * HEAD

        def load(i, g):
            start = pl.multiple_of(i * tile, tile)
            head = kv * group + g
            at = slice(head * HEAD, (head + 1) * HEAD)
            return (
                kept_ref[pl.ds(start, tile), at],
                back_sorted[pl.ds(start, tile), at],
                lse_ref[head : head + 1, pl.ds(start, tile)],
            )

        def load_kv(j):
            start = pl.multiple_of(j * tile, tile)
            return (
                kept_ref[pl.ds(start, tile), k_at : k_at + HEAD],
                kept_ref[pl.ds(start, tile), v_at : v_at + HEAD],
            )

        def tile_terms(keys, values, query, back, lse, masked):
            weights = jnp.exp(dot_nt(keys, query) * scale - lse)
            if masked:
                weights = jnp.where(keep, weights, 0.0)
            return weights, dot_nt(values, back)

        def delta_step(i, _):
            rows_i = [load(i, g) for g in range(group)]

            def one(j, carry, masked):
                keys, values = load_kv(j)
                result = []
                for g in range(group):
                    weights, back_weights = tile_terms(keys, values, *rows_i[g], masked)
                    result.append(carry[g] + jnp.sum(weights * back_weights, 0, keepdims=True))
                return tuple(result)

            carry = tuple(jnp.zeros((1, tile), jnp.float32) for _ in range(group))
            carry = lax.fori_loop(0, i, lambda j, c: one(j, c, False), carry)
            carry = one(i, carry, True)
            for g in range(group):
                delta_ref[g : g + 1, pl.ds(pl.multiple_of(i * tile, tile), tile)] = carry[g]
            return 0

        lax.fori_loop(0, tiles, delta_step, 0)
        if kv == 0:
            pause()
        dq_ref[...] = jnp.zeros_like(dq_ref)

        def key_step(j, _):
            keys, values = load_kv(j)

            def one(i, carry, masked):
                back_key, back_value = carry
                start = pl.multiple_of(i * tile, tile)
                for g in range(group):
                    query, back, lse = load(i, g)
                    weights, back_weights = tile_terms(keys, values, query, back, lse, masked)
                    delta = delta_ref[g : g + 1, pl.ds(start, tile)]
                    back_scores = (weights * (back_weights - delta)).astype(jnp.bfloat16)
                    back_key = back_key + dot_nn(back_scores, query)
                    back_value = back_value + dot_nn(weights.astype(jnp.bfloat16), back)
                    dq_ref[g * HEAD : (g + 1) * HEAD, pl.ds(start, tile)] += dot_tn(
                        keys, back_scores
                    )
                return back_key, back_value

            zero = jnp.zeros((tile, HEAD), jnp.float32)
            carry = one(j, (zero, zero), True)
            carry = lax.fori_loop(j + 1, tiles, lambda i, c: one(i, c, False), carry)
            span = pl.ds(j * (tile // rows), tile // rows)
            grad[span, :, k_at : k_at + HEAD] = (carry[0] * scale).reshape(-1, rows, HEAD)
            grad[span, :, v_at : v_at + HEAD] = carry[1].reshape(-1, rows, HEAD)
            return 0

        lax.fori_loop(0, tiles, key_step, 0)
        for g in range(group):
            head = kv * group + g
            turned = (dq_ref[g * HEAD : (g + 1) * HEAD, :] * scale).T
            grad[:, :, head * HEAD : (head + 1) * HEAD] = turned.reshape(-1, rows, HEAD)

    def give_block(i, _):
        cos = cos_ref[order_ref[i]]
        sin = sin_ref[order_ref[i]]
        for c in range(0, cols, 2 * HEAD):
            values = grad[order_ref[i], :, c : c + 2 * HEAD]
            values = turn_columns(values, c, q_cols + k_cols, cos, sin, False)
            out_ref[i, :, c : c + 2 * HEAD] = values.astype(jnp.bfloat16)
        return 0

    lax.fori_loop(0, blocks, give_block, 0)


MESH = pl.DeviceIdType.MESH


def part_owner(part):
    return part % 2 * 2 + part // 2


def sequence_target(group, place, second, splits):
    part = place // 2
    target = (part_owner(part % 4), (2 * group + second) * splits + part // 4)
    return target, place % 2


def token_target(group, place, half, splits):
    sequence = place // splits
    part = part_owner(group) + 4 * (place % splits)
    return (sequence // 2, 2 * part + half), sequence % 2


def remote(source, target, sems, device):
    return pltpu.make_async_remote_copy(
        src_ref=source,
        dst_ref=target,
        send_sem=sems[0],
        recv_sem=sems[1],
        device_id=device,
        device_id_type=MESH,
    )


def same(one, other):
    return jnp.logical_and(one[0] == other[0], one[1] == other[1])


def greet(me, peers, movers):
    barrier = pltpu.get_barrier_semaphore()
    for peer in peers:
        pl.semaphore_signal(barrier, inc=1, device_id=peer, device_id_type=MESH)
    expected = len(peers)
    for source, target in movers:

        @pl.when(jnp.logical_not(same(source, me)))
        def _():
            pl.semaphore_signal(barrier, inc=1, device_id=source, device_id_type=MESH)

        expected = expected + jnp.where(same(target, me), 0, 1)
    pl.semaphore_wait(barrier, expected)


def move_start(me, source, target, target_device, send, receive):
    here = same(target_device, me)

    @pl.when(here)
    def _():
        pltpu.make_async_copy(source, target, receive).start()

    @pl.when(jnp.logical_not(here))
    def _():
        remote(source, target, (send, receive), target_device).start()


def move_sent(me, source, target, target_device, send, receive):
    @pl.when(jnp.logical_not(same(target_device, me)))
    def _():
        remote(source, target, (send, receive), target_device).wait_send()


def member(me, by):
    return (me[0] ^ (by // 2), me[1] ^ (by % 2))


def group_index(device):
    return 2 * device[0] + device[1] % 2


class GroupExchange:
    def __init__(self, me, pieces, got, sems):
        self.me, self.pieces, self.got, self.sems = me, pieces, got, sems

    def hop(self, by):
        peer = member(self.me, by)
        sems = (self.sems.at[0, by - 1], self.sems.at[1, by - 1])
        return remote(
            self.pieces.at[group_index(peer)], self.got.at[group_index(self.me)], sems, peer
        )

    def own(self):
        mine = group_index(self.me)
        return pltpu.make_async_copy(self.pieces.at[mine], self.got.at[mine], self.sems.at[0, 7])

    def start(self):
        for by in range(1, 8):
            self.hop(by).start()
        self.own().start()

    def finish(self):
        self.own().wait()
        for by in range(1, 8):
            self.hop(by).wait()


class GroupGather:
    def __init__(self, me, rows, sems, own, window):
        self.rows, self.sems, self.own, self.window = rows, sems, own, window
        self.core, self.across, self.beside = member(me, 2), member(me, 4), member(me, 1)

    def hop(self, index):
        across, beside, core = self.across, self.beside, self.core
        source, i, j, half, device = (
            (None, 0, 2, 0, across),
            (None, 1, 0, 1, beside),
            (None, 1, 0, 0, beside),
            (None, 0, 2, 1, across),
            ((0, 2), 1, 2, 0, beside),
            ((1, 0), 1, 2, 1, across),
            (None, 0, 1, slice(0, 2), core),
            ((0, 2), 0, 3, slice(0, 2), core),
            ((1, 0), 1, 1, slice(0, 2), core),
            ((1, 2), 1, 3, slice(0, 2), core),
        )[index]
        if source is None:
            source = self.own.at[half, self.window]
        else:
            source = self.rows.at[source[0], source[1], half, self.window]
        target = self.rows.at[i, j, half, self.window]
        return remote(source, target, (self.sems.at[0, index], self.sems.at[1, index]), device)

    def start(self):
        for index in (0, 1, 2, 3, 6):
            self.hop(index).start()

    def pass_on(self):
        self.hop(0).wait_recv()
        self.hop(4).start()
        self.hop(1).wait_recv()
        self.hop(5).start()
        self.hop(3).wait_recv()
        self.hop(7).start()
        self.hop(2).wait_recv()
        self.hop(8).start()

    def finish(self):
        self.hop(4).wait_recv()
        self.hop(5).wait_recv()
        self.hop(9).start()
        for index in (6, 7, 8, 9):
            self.hop(index).wait_recv()
        for index in range(10):
            self.hop(index).wait_send()


class Moves:
    def __init__(self, me, splits, source, target, sems, back):
        self.me, self.splits, self.source, self.target = me, splits, source, target
        self.sems, self.back = sems, back

    def one(self, i):
        find = token_target if self.back else sequence_target
        device, place = find(self.me[0], self.me[1], i, self.splits)
        return (
            self.me,
            self.source.at[i],
            self.target.at[place],
            device,
            self.sems.at[0, i],
            self.sems.at[1, place],
        )

    def start(self):
        for i in (0, 1):
            move_start(*self.one(i))

    def wait_recv(self):
        for i in (0, 1):
            pltpu.make_async_copy(self.source.at[0], self.target.at[i], self.sems.at[1, i]).wait()

    def finish(self):
        for i in (0, 1):
            move_sent(*self.one(i))


def movers_of(me, splits, back):
    into = [sequence_target(me[0], me[1], i, splits)[0] for i in (0, 1)]
    home = [token_target(me[0], me[1], i, splits)[0] for i in (0, 1)]
    return list(zip(into, home)) if back else list(zip(home, into))


def first_kernel(shards, splits, tokens, pieces, out_own, gate_pieces, *refs):
    rows, in_all, out_all, gate_rows, held = refs[:5]
    move_sems, group_sems, piece_sems, gate_sems, own_sem, in_sems, out_sems = refs[5:]
    me = (lax.axis_index("dp"), lax.axis_index("ctx"))
    group, place = me
    slow = shards // 2
    slot = place // 2
    line = [(group, place ^ (2 * by)) for by in range(1, slow)]
    wanted, block = place // slow, place % slow
    takers = [(group, 2 * (slot ^ by) + wanted) for by in range(slow)]
    givers = [(group, place % 2 * slow + block_by) for block_by in range(slow)]
    movers = movers_of(me, splits, False) + list(zip(givers, takers))
    greet(me, [member(me, by) for by in range(1, 8)] + line, movers)
    swap = GroupExchange(me, pieces, held, piece_sems)
    gate_swap = GroupExchange(me, gate_pieces, gate_rows, gate_sems)
    move = Moves(me, splits, tokens, rows.at[0, 0], move_sems, False)

    def in_line(by):
        sems = (in_sems.at[0, by - 1], in_sems.at[1, by - 1])
        return remote(held, in_all.at[slot], sems, line[by - 1])

    def out_send(by):
        return (
            me,
            out_own,
            out_all.at[block],
            takers[by],
            out_sems.at[0, by],
            out_sems.at[1, block],
        )

    own = pltpu.make_async_copy(held, in_all.at[slot], own_sem)
    move.start()
    swap.start()
    gate_swap.start()
    swap.finish()
    move.wait_recv()
    spread = GroupGather(me, rows, group_sems, rows.at[0, 0], slice(0, tokens.shape[1]))
    spread.start()
    for by in range(1, slow):
        in_line(by).start()
    own.start()
    for by in range(slow):
        move_start(*out_send(by))
    spread.pass_on()
    for by in range(1, slow):
        in_line(by).wait()
    spread.finish()
    own.wait()
    for by in range(slow):
        pltpu.make_async_copy(out_own, out_all.at[by], out_sems.at[1, by]).wait()
    for by in range(slow):
        move_sent(*out_send(by))
    gate_swap.finish()
    move.finish()


def first_exchange(tokens, pieces, out_own, gate_pieces, shards, splits, identity):
    low = jnp.bfloat16
    slow = shards // 2
    any_space = pl.BlockSpec(memory_space=pl.ANY)
    dma = pltpu.SemaphoreType.DMA
    made = pl.pallas_call(
        functools.partial(first_kernel, shards, splits),
        out_shape=(
            jax.ShapeDtypeStruct((2, 4) + tokens.shape, low),
            jax.ShapeDtypeStruct((slow,) + pieces.shape, low),
            jax.ShapeDtypeStruct((slow,) + out_own.shape, low),
            jax.ShapeDtypeStruct(gate_pieces.shape, low),
            jax.ShapeDtypeStruct(pieces.shape, low),
        ),
        in_specs=[any_space] * 4,
        out_specs=(any_space,) * 5,
        scratch_shapes=[
            dma((2, 2)),
            dma((2, 10)),
            dma((2, 8)),
            dma((2, 8)),
            dma,
            dma((2, slow - 1)),
            dma((2, slow)),
        ],
        compiler_params=pltpu.CompilerParams(
            collective_id=identity, has_side_effects=True, vmem_limit_bytes=8 << 20
        ),
        cost_estimate=pl.CostEstimate(flops=0, bytes_accessed=200 << 20, transcendentals=0),
    )(tokens, pieces, out_own, gate_pieces)
    return made[:4]


class GroupScatter:
    def __init__(self, me, parts, buffers, sems, steps):
        self.parts = parts
        self.core_in, self.kept, self.sent, self.came, self.held = buffers[:5]
        self.sent_last, self.came_last = buffers[5:]
        self.core_sems, self.kept_sems, self.one_sems, self.last_sems = sems
        self.core, self.across, self.beside = member(me, 2), member(me, 4), member(me, 1)
        self.size = parts.shape[3] // steps
        self.steps = steps

    def window(self, k):
        return slice(k * self.size, (k + 1) * self.size)

    def to_core(self, k, j):
        return remote(
            self.parts.at[:, 2 * j + 1, :, self.window(k)],
            self.core_in.at[:, j, :, self.window(k)],
            (self.core_sems.at[0, k, j], self.core_sems.at[1, k, j]),
            self.core,
        )

    def keep(self, k, j):
        return pltpu.make_async_copy(
            self.parts.at[:, 2 * j, :, self.window(k)],
            self.kept.at[:, j, :, self.window(k)],
            self.kept_sems.at[k, j],
        )

    def first(self, k, half):
        return remote(
            self.sent.at[half, :, self.window(k)],
            self.came.at[half, :, self.window(k)],
            (self.one_sems.at[0, k, half], self.one_sems.at[1, k, half]),
            (self.beside, self.across)[half],
        )

    def second(self, k, half):
        return remote(
            self.sent_last.at[half, self.window(k)],
            self.came_last.at[half, self.window(k)],
            (self.last_sems.at[0, k, half], self.last_sems.at[1, k, half]),
            (self.across, self.beside)[half],
        )

    def start(self):
        for k in range(self.steps):
            for j in (0, 1):
                self.to_core(k, j).start()
                self.keep(k, j).start()

    def send_first(self, k):
        wide = jnp.float32
        rows = self.window(k)
        for j in (0, 1):
            self.keep(k, j).wait()
            self.to_core(k, j).wait_recv()
        for half in (0, 1):
            for other in (0, 1):
                at = (1, other) if half == 0 else (other, 1)
                both = self.kept[at[0], at[1], half, rows].astype(wide)
                both = both + self.core_in[at[0], at[1], half, rows].astype(wide)
                self.sent[half, other, rows] = both.astype(jnp.bfloat16)
            self.first(k, half).start()
        for half in (0, 1):
            for other in (0, 1):
                at = (0, other) if half == 0 else (other, 0)
                both = self.kept[at[0], at[1], half, rows].astype(wide)
                self.held[half, other, rows] = both + self.core_in[at[0], at[1], half, rows].astype(
                    wide
                )

    def send_second(self, k):
        wide = jnp.float32
        rows = self.window(k)
        for half in (0, 1):
            self.first(k, half).wait_recv()
            both = self.held[half, 1, rows] + self.came[half, 1, rows].astype(wide)
            self.sent_last[half, rows] = both.astype(jnp.bfloat16)
            self.second(k, half).start()
            self.held[half, 0, rows] = self.held[half, 0, rows] + self.came[half, 0, rows].astype(
                wide
            )

    def total(self, k, half):
        self.second(k, half).wait_recv()
        rows = self.window(k)
        return self.held[half, 0, rows] + self.came_last[half, rows].astype(jnp.float32)

    def finish(self):
        for k in range(self.steps):
            for j in (0, 1):
                self.to_core(k, j).wait_send()
            for half in (0, 1):
                self.first(k, half).wait_send()
                self.second(k, half).wait_send()


def scatter_scratch(rows, width, steps):
    low, wide = jnp.bfloat16, jnp.float32
    dma = pltpu.SemaphoreType.DMA
    return [
        pltpu.VMEM((2, 2, 2, rows, width), low),
        pltpu.VMEM((2, 2, 2, rows, width), low),
        pltpu.VMEM((2, 2, rows, width), low),
        pltpu.VMEM((2, 2, rows, width), low),
        pltpu.VMEM((2, 2, rows, width), wide),
        pltpu.VMEM((2, rows, width), low),
        pltpu.VMEM((2, rows, width), low),
        dma((2, steps, 2)),
        dma((steps, 2)),
        dma((2, steps, 2)),
        dma((2, steps, 2)),
    ]


def reordered(rows, slow, back):
    each = rows.shape[1] // (4 * slow)
    if back:
        starts = [s * 4 + dp for dp in range(4) for s in range(slow)]
    else:
        starts = [dp * slow + s for s in range(slow) for dp in range(4)]
    return jnp.concatenate([rows[:, i * each : (i + 1) * each] for i in starts], 1)


def turn_kernel(slow, splits, steps, backward, parts, gain, *refs):
    if backward:
        residual, cot, result, gain_grad, rows = refs[:5]
        scratch = refs[5:]
    else:
        tokens, cot, result, cot_rows, rows = refs[:5]
        scratch = refs[5:]
    own, own_sems, group_sems, move_sems = scratch[:4]
    scratch = scratch[1:]
    me = (lax.axis_index("dp"), lax.axis_index("ctx"))
    movers = [] if backward else movers_of(me, splits, False)
    greet(me, [member(me, by) for by in (1, 2, 4)], movers)
    scatter = GroupScatter(me, parts, scratch[3:10], scratch[10:], steps)
    gathers = [GroupGather(me, rows, group_sems.at[k], own, scatter.window(k)) for k in range(steps)]
    scatter.start()
    if not backward:
        move = Moves(me, splits, cot, cot_rows, move_sems, False)
        move.start()
    for k in range(steps):
        scatter.send_first(k)
    for k in range(steps):
        scatter.send_second(k)
    for k in range(steps):
        span = scatter.window(k)
        for half in (0, 1):
            total = scatter.total(k, half)
            if backward:
                values = residual[half, span]
                factor = lax.rsqrt(jnp.mean(values * values, -1, keepdims=True) + norm_eps)
                normed = values * factor
                total = reordered(total, slow, True)
                part = jnp.sum(total * normed, 0, keepdims=True)
                if k == 0 and half == 0:
                    gain_grad[...] = part
                else:
                    gain_grad[...] += part
                back = total * gain[...]
                back = factor * (back - normed * jnp.mean(back * normed, -1, keepdims=True))
                back = cot[half, span].astype(jnp.float32) + back
                result[half, span] = back
                own[half, span] = back.astype(jnp.bfloat16)
            else:
                values = tokens[half, span].astype(jnp.float32) + total
                factor = lax.rsqrt(jnp.mean(values * values, -1, keepdims=True) + norm_eps)
                result[half, span] = values
                own[half, span] = reordered(values * factor * gain[...], slow, False).astype(
                    jnp.bfloat16
                )
        gathers[k].start()
        keep = pltpu.make_async_copy(own.at[:, span], rows.at[0, 0, :, span], own_sems.at[k])
        keep.start()
    for k in range(steps):
        gathers[k].pass_on()
    for k in range(steps):
        gathers[k].finish()
        span = scatter.window(k)
        pltpu.make_async_copy(own.at[:, span], rows.at[0, 0, :, span], own_sems.at[k]).wait()
    scatter.finish()
    if not backward:
        move.wait_recv()
        move.finish()


def turn(parts, gain, rows_in, slow, splits, backward, identity):
    low, wide = jnp.bfloat16, jnp.float32
    dma = pltpu.SemaphoreType.DMA
    rows, width = parts.shape[3:]
    steps = 2
    any_space = pl.BlockSpec(memory_space=pl.ANY)
    vmem = pl.BlockSpec(memory_space=pltpu.VMEM)
    shapes = [jax.ShapeDtypeStruct((2, rows, width), wide)]
    spaces = [vmem] * 2
    if backward:
        shapes.append(jax.ShapeDtypeStruct((1, width), wide))
    else:
        shapes.append(jax.ShapeDtypeStruct((2, rows, width), low))
        spaces = [vmem, any_space]
    return pl.pallas_call(
        functools.partial(turn_kernel, slow, splits, steps, backward),
        out_shape=tuple(shapes) + (jax.ShapeDtypeStruct((2, 4, 2, rows, width), low),),
        in_specs=[any_space, vmem] + spaces,
        out_specs=tuple(spaces + [any_space]),
        scratch_shapes=[
            pltpu.VMEM((2, rows, width), low),
            dma((steps,)),
            dma((steps, 2, 10)),
            dma((2, 2)),
        ]
        + scatter_scratch(rows, width, steps),
        compiler_params=pltpu.CompilerParams(
            collective_id=identity, has_side_effects=True, vmem_limit_bytes=48 << 20
        ),
        cost_estimate=pl.CostEstimate(flops=0, bytes_accessed=250 << 20, transcendentals=0),
    )(parts, gain, *rows_in)


def spread_kernel(own, rows, group_sems, own_sem):
    me = (lax.axis_index("dp"), lax.axis_index("ctx"))
    greet(me, [member(me, by) for by in (1, 2, 4)], [])
    gather = GroupGather(me, rows, group_sems, own, slice(0, own.shape[1]))
    keep = pltpu.make_async_copy(own, rows.at[0, 0], own_sem)
    gather.start()
    keep.start()
    gather.pass_on()
    gather.finish()
    keep.wait()


def spread_group(own, identity):
    any_space = pl.BlockSpec(memory_space=pl.ANY)
    dma = pltpu.SemaphoreType.DMA
    return pl.pallas_call(
        spread_kernel,
        out_shape=jax.ShapeDtypeStruct((2, 4) + own.shape, own.dtype),
        in_specs=[any_space],
        out_specs=any_space,
        scratch_shapes=[dma((2, 10)), dma],
        compiler_params=pltpu.CompilerParams(
            collective_id=identity, has_side_effects=True, vmem_limit_bytes=4 << 20
        ),
        cost_estimate=pl.CostEstimate(flops=0, bytes_accessed=100 << 20, transcendentals=0),
    )(own)


class LineSum:
    def __init__(self, me, slow, parts, buffers, sems):
        self.parts = parts
        self.kept, self.arrived = buffers
        self.sems, self.own_sem = sems
        self.slot = me[1] // 2
        self.slow = slow
        self.line = [(me[0], me[1] ^ (2 * by)) for by in range(1, slow)]

    def hop(self, by):
        sems = (self.sems.at[0, by - 1], self.sems.at[1, by - 1])
        return remote(
            self.parts.at[self.slot ^ by], self.arrived.at[by - 1], sems, self.line[by - 1]
        )

    def own(self):
        return pltpu.make_async_copy(self.parts.at[self.slot], self.kept, self.own_sem)

    def start(self):
        for by in range(1, self.slow):
            self.hop(by).start()
        self.own().start()

    def total(self):
        self.own().wait()
        value = self.kept[...].astype(jnp.float32)
        for by in range(1, self.slow):
            self.hop(by).wait_recv()
            value = value + self.arrived[by - 1].astype(jnp.float32)
        return value

    def finish(self):
        for by in range(1, self.slow):
            self.hop(by).wait_send()


def line_scratch(shape, kind, slow):
    dma = pltpu.SemaphoreType.DMA
    return [
        pltpu.VMEM(shape, kind),
        pltpu.VMEM((slow - 1,) + shape, kind),
        dma((2, slow - 1)),
        dma,
    ]


def last_kernel(shards, splits, steps, in_parts, out_parts, gate_parts, in_back, *refs):
    gain, gain_two_grad, tokens, back_rows = refs[:4]
    in_total, out_total, gate_total, gains_total, tokens_grad = refs[4:9]
    scratch = list(refs[9:])

    def take(count):
        taken = scratch[:count]
        del scratch[:count]
        return taken

    me = (lax.axis_index("dp"), lax.axis_index("ctx"))
    group, place = me
    slow = shards // 2
    slot, half = place // 2, place % 2
    owned = in_parts.shape[2]
    home = (group, half * slow + slot)
    movers = movers_of(me, splits, True)
    movers.append(((group, place % slow * 2 + place // slow), home))
    line = [(group, place ^ (2 * by)) for by in range(1, slow)]
    greet(me, [member(me, by) for by in range(1, 8)] + line, movers)
    one = take(11)
    back_sum = GroupScatter(me, in_back, one[:7], one[7:], steps)
    line_in = take(4)
    line_out = take(4)
    line_gains = take(4)
    in_done, out_done, gains_own, gains_done, made_one, gain_grad = take(6)
    in_sems, gate_sems, gains_sems, one_sems, home_sems = take(5)
    in_line = LineSum(me, slow, in_parts, line_in[:2], line_in[2:])
    out_line = LineSum(me, slow, out_parts, line_out[:2], line_out[2:])
    gains_line = LineSum(me, slow, gains_own, line_gains[:2], line_gains[2:])
    in_swap = GroupExchange(me, in_done, in_total, in_sems)
    gate_swap = GroupExchange(me, gate_parts, gate_total, gate_sems)
    gains_swap = GroupExchange(me, gains_done, gains_total, gains_sems)
    move_grad = Moves(me, splits, made_one, tokens_grad, one_sems, True)
    back_sum.start()
    in_line.start()
    out_line.start()
    for k in range(steps):
        back_sum.send_first(k)
    for k in range(steps):
        back_sum.send_second(k)
    for k in range(steps):
        span = back_sum.window(k)
        for part in (0, 1):
            total = back_sum.total(k, part)
            values = tokens[part, span].astype(jnp.float32)
            normed, factor = norm_parts(values)
            grad = jnp.sum(total * normed, 0, keepdims=True)
            if k == 0 and part == 0:
                gain_grad[...] = grad
            else:
                gain_grad[...] += grad
            value = back_rows[part, span] + norm_back(total * gain[...], normed, factor)
            made_one[part, span] = value.astype(jnp.bfloat16)
    move_grad.start()
    gains_own[...] = jnp.zeros_like(gains_own)
    for dp in range(4):
        for s in range(slow):
            for side in range(2):
                at = ((dp * slow + s) * 2 + side) * owned
                index = 2 * dp + side
                gains_own[s, index, 0:1, 0:owned] = gain_grad[:, at : at + owned]
                gains_own[s, index, 0:1, owned : 2 * owned] = gain_two_grad[:, at : at + owned]
    gains_line.start()
    gate_swap.start()
    in_done[...] = in_line.total().astype(jnp.bfloat16)
    in_swap.start()
    gains_done[...] = gains_line.total()
    gains_swap.start()
    out_done[...] = out_line.total().astype(jnp.bfloat16)
    to_home = (me, out_done, out_total, home, home_sems.at[0], home_sems.at[1])
    move_start(*to_home)
    pltpu.make_async_copy(out_done, out_total, home_sems.at[1]).wait()
    move_sent(*to_home)
    for swap in (in_swap, gate_swap, gains_swap):
        swap.finish()
    move_grad.wait_recv()
    move_grad.finish()
    for part in (in_line, out_line, gains_line, back_sum):
        part.finish()


def last_sums(in_parts, out_parts, gate_parts, in_back, others, shards, splits, identity):
    low, wide = jnp.bfloat16, jnp.float32
    slow = shards // 2
    steps = 2
    any_space = pl.BlockSpec(memory_space=pl.ANY)
    vmem = pl.BlockSpec(memory_space=pltpu.VMEM)
    dma = pltpu.SemaphoreType.DMA
    rows, width = in_back.shape[3:]
    gains_shape = (8, 8, 128)
    moved = jax.ShapeDtypeStruct((2, rows, width), low)
    return pl.pallas_call(
        functools.partial(last_kernel, shards, splits, steps),
        out_shape=(
            jax.ShapeDtypeStruct(in_parts.shape[1:], low),
            jax.ShapeDtypeStruct(out_parts.shape[1:], low),
            jax.ShapeDtypeStruct(gate_parts.shape, low),
            jax.ShapeDtypeStruct(gains_shape, wide),
            moved,
        ),
        in_specs=[any_space] * 4 + [vmem] * 4,
        out_specs=(any_space,) * 5,
        scratch_shapes=scatter_scratch(rows, width, steps)
        + line_scratch(in_parts.shape[1:], low, slow)
        + line_scratch(out_parts.shape[1:], low, slow)
        + line_scratch(gains_shape, wide, slow)
        + [
            pltpu.VMEM(in_parts.shape[1:], low),
            pltpu.VMEM(out_parts.shape[1:], low),
            pltpu.VMEM((slow,) + gains_shape, wide),
            pltpu.VMEM(gains_shape, wide),
            pltpu.VMEM(moved.shape, low),
            pltpu.VMEM((1, width), wide),
            dma((2, 8)),
            dma((2, 8)),
            dma((2, 8)),
            dma((2, 2)),
            dma((2,)),
        ],
        compiler_params=pltpu.CompilerParams(
            collective_id=identity, has_side_effects=True, vmem_limit_bytes=56 << 20
        ),
        cost_estimate=pl.CostEstimate(flops=0, bytes_accessed=300 << 20, transcendentals=0),
    )(in_parts, out_parts, gate_parts, in_back, *others)


def position_tables(blocks, rows):
    frequency = rope_base ** (-(np.arange(HEAD // 2) * 2.0 / HEAD))
    angles = np.arange(blocks * rows).reshape(blocks, rows, 1) * frequency
    cos, sin = np.cos(angles), np.sin(angles)
    cosine = np.concatenate([cos, cos, cos, cos], 2)
    sines = np.concatenate([-sin, sin, -sin, sin], 2)
    return jnp.asarray(cosine, jnp.float32), jnp.asarray(sines, jnp.float32)


def attend(order, where, qkv, tables, q_heads, kv_heads):
    seqs, length, cols = qkv.shape
    blocks = order.shape[0]
    rows = length // blocks
    whole = pl.BlockSpec(memory_space=pltpu.VMEM)
    small = pl.BlockSpec(memory_space=pltpu.SMEM)
    return pl.pallas_call(
        functools.partial(attend_kernel, q_heads, kv_heads, 256),
        out_shape=(
            jax.ShapeDtypeStruct((seqs, blocks, rows, q_heads * HEAD), jnp.bfloat16),
            jax.ShapeDtypeStruct((seqs, q_heads, length), jnp.float32),
            jax.ShapeDtypeStruct((seqs, length, cols), jnp.bfloat16),
        ),
        in_specs=[small, small, whole, whole, whole],
        out_specs=(whole, whole, whole),
        scratch_shapes=[pltpu.VMEM((blocks, rows, q_heads * HEAD), jnp.bfloat16)],
        compiler_params=pltpu.CompilerParams(vmem_limit_bytes=40 << 20),
        cost_estimate=pl.CostEstimate(
            flops=2 * seqs * length * length * q_heads * HEAD,
            bytes_accessed=100 << 20,
            transcendentals=seqs * length * length * q_heads // 2,
        ),
    )(order, where, qkv.reshape(seqs, blocks, rows, cols), *tables)


def attend_back(
    order, where, kept, back, lse, tables, out_rows, residual, q_heads, kv_heads, splits, identity
):
    seqs, length, cols = kept.shape
    blocks = order.shape[0]
    block = length // blocks
    group = q_heads // kv_heads
    rows, width = out_rows.shape[3:]
    steps = 2
    whole = pl.BlockSpec(memory_space=pltpu.VMEM)
    small = pl.BlockSpec(memory_space=pltpu.SMEM)
    any_space = pl.BlockSpec(memory_space=pl.ANY)
    return pl.pallas_call(
        functools.partial(attend_back_kernel, q_heads, kv_heads, 256, splits, steps),
        out_shape=(
            jax.ShapeDtypeStruct((seqs, blocks, block, cols), jnp.bfloat16),
            jax.ShapeDtypeStruct((2, rows, width), jnp.bfloat16),
        ),
        in_specs=[small, small] + [whole] * 5 + [any_space, whole],
        out_specs=(whole, any_space),
        scratch_shapes=[
            pltpu.VMEM((length, q_heads * HEAD), jnp.bfloat16),
            pltpu.VMEM((blocks, block, cols), jnp.float32),
            pltpu.VMEM((group, length), jnp.float32),
            pltpu.VMEM((group * HEAD, length), jnp.float32),
            pltpu.VMEM((2, rows, width), jnp.bfloat16),
            pltpu.SemaphoreType.DMA((2, 2)),
        ]
        + scatter_scratch(rows, width, steps),
        compiler_params=pltpu.CompilerParams(
            collective_id=identity, has_side_effects=True, vmem_limit_bytes=56 << 20
        ),
        cost_estimate=pl.CostEstimate(
            flops=7 * seqs * length * length * q_heads * HEAD,
            bytes_accessed=100 << 20,
            transcendentals=seqs * length * length * q_heads // 2,
        ),
    )(
        order,
        where,
        kept,
        back.reshape(seqs, blocks, block, -1),
        lse,
        *tables,
        out_rows,
        residual,
    )


def gate_update_kernel(slow, step_rate, grad, weight, first, second, new_first, new_second, new):
    units = grad.shape[2] // slow
    pieces = [grad[half, :, s * units : (s + 1) * units] for s in range(slow) for half in (0, 1)]
    gradient = jnp.concatenate(pieces, 1).astype(jnp.float32)
    new_first[...], new_second[...], new[...] = adam_update(
        weight[...], gradient, first[...], second[...], step_rate, weight_decay
    )


def gate_update(grad, weight, first, second, slow, step_rate):
    rows, width = weight.shape
    block = pl.BlockSpec((rows, width // 8), lambda side, dp: (0, 4 * side + dp))
    piece = pl.BlockSpec((2, rows, width // 16), lambda side, dp: (dp, 0, side))
    return pl.pallas_call(
        functools.partial(gate_update_kernel, slow, step_rate),
        grid=(2, 4),
        out_shape=(jax.ShapeDtypeStruct(weight.shape, jnp.float32),) * 3,
        in_specs=[piece, block, block, block],
        out_specs=(block,) * 3,
        compiler_params=pltpu.CompilerParams(vmem_limit_bytes=32 << 20),
    )(grad, weight, first, second)


def local(
    tokens,
    cotangent,
    block_order,
    attention_in,
    attention_out,
    gate_up,
    down_matrix,
    gains,
    mean_attention_in,
    mean_attention_out,
    mean_gate_up,
    mean_down,
    mean_gains,
    square_attention_in,
    square_attention_out,
    square_gate_up,
    square_down,
    square_gains,
):
    seq_count, shard_rows, width = tokens.shape
    shards = lax.axis_size("ctx")
    slow = shards // 2
    mine = lax.axis_index("dp")
    beside = lax.axis_index("ctx") % 2
    low = jnp.bfloat16
    owned = attention_in.shape[0]
    hidden_units = gate_up.shape[1] // 2
    part_hidden = hidden_units // 8
    units = down_matrix.shape[0]
    part_q = HEADS * HEAD // 8
    part_k = KV_HEADS * HEAD // 8
    part_cols = part_q + 2 * part_k
    count = seq_count * shard_rows
    together = 8 * count
    spread = shards // (4 * seq_count)
    splits = max(1, slow // 8)
    seqs = 2 // spread if spread < 2 else 1
    length = shards * shard_rows
    q_heads = HEADS // 8 // splits
    kv_heads = KV_HEADS // 8

    in_low = attention_in.astype(low)
    gains_row = jnp.pad(gains.astype(low).reshape(1, -1), ((0, 15), (0, part_cols - 2 * owned)))
    pieces = jnp.stack(
        [
            jnp.concatenate(
                [
                    jnp.concatenate(
                        [
                            in_low[:, i * part_q : (i + 1) * part_q],
                            in_low[:, 8 * part_q + i * part_k :][:, :part_k],
                            in_low[:, 8 * (part_q + part_k) + i * part_k :][:, :part_k],
                        ],
                        1,
                    ),
                    gains_row,
                ]
            )
            for i in range(8)
        ]
    )
    gate_low = gate_up.astype(low)
    gate_pieces = jnp.stack(
        [
            jnp.concatenate(
                [
                    gate_low[:, side * hidden_units + (dp * shards + 2 * s + half) * units :][
                        :, :units
                    ]
                    for side in range(2)
                    for s in range(slow)
                ],
                1,
            )
            for dp in range(4)
            for half in range(2)
        ]
    )
    tokens_all, in_all, w_out, gate_rows = first_exchange(
        tokens, pieces, attention_out.astype(low), gate_pieces, shards, spread, 1
    )
    in_all = in_all.reshape(slow, 4, 2, owned + 16, part_cols).swapaxes(0, 1)
    w_in = in_all[:, :, :, :owned].reshape(width, part_cols)
    w_out = w_out.reshape(part_q, width)
    gains_all = in_all[:, :, :, owned, : 2 * owned].reshape(-1, 2, owned)
    gains_all = gains_all.astype(jnp.float32).swapaxes(0, 1).reshape(2, width)
    gain_one, gain_two = gains_all[0], gains_all[1]
    w_gate = gather_line(gate_rows.reshape(8 * owned, 2 * part_hidden))

    normed_all, _ = norm_parts(tokens_all.reshape(together, width).astype(jnp.float32))
    input_one = (normed_all * gain_one).astype(low)
    qkv = dot_nn(input_one, w_in)
    orders = block_order.reshape(2 * splits if spread > 1 else 1, 4, -1)
    slot_order = jnp.concatenate(
        [
            orders[(2 * s + (beside ^ i)) if spread > 1 else 0, part_owner(mine ^ j)]
            for s in range(splits)
            for i in range(2 // seqs)
            for j in range(4)
        ]
    )
    tables = position_tables(slot_order.shape[0], length // slot_order.shape[0])
    groups = [
        [2 * (s * splits + g) + half for g in range(splits)]
        for s in range(slow // splits)
        for half in (0, 1)
    ]

    def split_heads(values, widths, copies):
        parts = []
        start = 0
        for each, repeat in zip(widths, copies):
            kinds = splits // repeat
            piece = values[:, start : start + kinds * each].reshape(-1, kinds, each)
            parts.append(jnp.repeat(piece.swapaxes(0, 1), repeat, axis=0))
            start += kinds * each
        sent = jnp.concatenate(parts, 2)
        got = lax.all_to_all(sent, "ctx", 0, 0, axis_index_groups=groups, tiled=True)
        return got.reshape(length, -1)

    def join_heads(values):
        sent = values.reshape(splits, together, -1)
        return lax.all_to_all(sent, "ctx", 0, 0, axis_index_groups=groups, tiled=True)

    q_width, k_width = q_heads * HEAD, kv_heads * HEAD
    if splits > 1:
        qkv = split_heads(qkv, (q_width, k_width, k_width), (1, splits, splits))
    qkv = qkv.reshape(seqs, length, -1)
    blocks = slot_order.shape[0]
    slot_where = jnp.sum(
        jnp.where(
            slot_order[None, :] == jnp.arange(blocks, dtype=jnp.int32)[:, None],
            jnp.arange(blocks, dtype=jnp.int32)[None, :],
            0,
        ),
        1,
    )
    attended, lse, kept = attend(slot_order, slot_where, qkv, tables, q_heads, kv_heads)
    if splits > 1:
        attended = join_heads(attended.reshape(length, q_width)).swapaxes(0, 1)
    attended = attended.reshape(together, part_q)

    def parts(values):
        return values.astype(low).reshape((2, 4) + tokens.shape)

    residual_rows, cot_rows, input_two = turn(
        parts(dot_nn(attended, w_out)),
        gain_two[None],
        [tokens_all[0, 0], cotangent],
        slow,
        spread,
        False,
        3,
    )
    input_two = input_two.reshape(together, width)
    back_all = spread_group(cot_rows, 2).reshape(together, width)
    after = 0.0 * (residual_rows[0, 0, 0] + w_gate[0, 0].astype(jnp.float32))
    w_down = gather_line((down_matrix + after).astype(low))
    gate_both = dot_nn(input_two, w_gate)
    gate_part = gate_both[:, :part_hidden]
    up_part = gate_both[:, part_hidden:]
    sigmoid_gate = jax.nn.sigmoid(gate_part)
    active = gate_part * sigmoid_gate
    hidden = lax.optimization_barrier((active * up_part).astype(low))
    grad_down = lax.optimization_barrier(dot_tn(hidden, back_all).astype(low))
    down_sum = sum_line(grad_down + 0.0 * w_down[0, 0]).astype(jnp.float32)
    back_hidden = dot_nt(back_all, w_down + 0.0 * hidden[0, 0])
    back_gate = back_hidden * up_part * sigmoid_gate * (1.0 + gate_part * (1.0 - sigmoid_gate))
    back_upper = back_hidden * active
    back_gate_up = jnp.concatenate([back_gate, back_upper], 1).astype(low)
    gate_low = sum_line(dot_tn(input_two, back_gate_up).astype(low))
    back_rows, grad_gain_two, back_residual_all = turn(
        parts(dot_nt(back_gate_up, w_gate)),
        gain_two[None],
        [residual_rows, cot_rows],
        slow,
        spread,
        True,
        4,
    )
    back_residual_all = back_residual_all.reshape(together, width)
    grad_out = dot_tn(attended, back_residual_all).astype(low)
    back_attended = dot_nt(back_residual_all, w_out).astype(low)
    if splits > 1:
        back_attended = split_heads(back_attended, (q_width,), (1,))
    back_projected, block_out = attend_back(
        slot_order,
        slot_where,
        kept,
        back_attended.reshape(seqs, length, -1),
        lse,
        tables,
        parts(dot_nn(hidden, w_down)),
        residual_rows,
        q_heads,
        kv_heads,
        spread,
        6,
    )
    if splits > 1:
        back_projected = join_heads(back_projected.reshape(length, -1)).astype(jnp.float32)
        back_projected = jnp.concatenate(
            [
                back_projected[..., :q_width].swapaxes(0, 1).reshape(together, part_q),
                back_projected[..., q_width:].sum(0),
            ],
            1,
        ).astype(low)
    back_projected = back_projected.reshape(together, part_cols)
    grad_in = dot_tn(input_one, back_projected).astype(low)
    grad_in = grad_in.reshape(4, slow, 2 * owned, part_cols).swapaxes(0, 1)
    in_sum, out_sum, gate_sum, gains_sum, tokens_grad = last_sums(
        grad_in.reshape(slow, 8, owned, part_cols),
        grad_out.reshape(slow, owned, width),
        gate_low.reshape(8, owned, 2 * part_hidden),
        parts(dot_nt(back_projected, w_in)),
        [gain_one[None], grad_gain_two, tokens_all[0, 0], back_rows],
        shards,
        spread,
        5,
    )
    tokens_grad = tokens_grad.astype(jnp.float32)
    out_sum = out_sum.astype(jnp.float32)
    gains_sum = gains_sum[:, 0, : 2 * owned].reshape(8, 2, owned).sum(0)
    cuts = ((0, part_q), (part_q, part_q + part_k), (part_q + part_k, part_cols))
    in_sum = jnp.concatenate(
        [in_sum[i, :, first:last] for first, last in cuts for i in range(8)], 1
    ).astype(jnp.float32)
    new_in = adam_update(
        attention_in,
        in_sum,
        mean_attention_in,
        square_attention_in,
        input_boost * D ** (-0.5),
        weight_decay,
    )
    new_out = adam_update(
        attention_out,
        out_sum,
        mean_attention_out,
        square_attention_out,
        (HEADS * HEAD // 32) ** (-0.5),
        weight_decay,
    )
    new_gate = gate_update(
        gate_sum, gate_up, mean_gate_up, square_gate_up, slow, D ** (-0.5)
    )
    new_down = adam_update(
        down_matrix, down_sum, mean_down, square_down, FF ** (-0.5), weight_decay
    )
    new_gain = adam_update(gains, gains_sum, mean_gains, square_gains, gain_rate, 0.0)
    return (
        block_out,
        tokens_grad,
        new_in[0],
        new_in[1],
        new_in[2],
        new_out[0],
        new_out[1],
        new_out[2],
        new_gate[0],
        new_gate[1],
        new_gate[2],
        new_down[0],
        new_down[1],
        new_down[2],
        new_gain[0],
        new_gain[1],
        new_gain[2],
    )


def solution(mesh):
    in_specs = (
        P("dp", "ctx", None),
        P("dp", "ctx", None),
        P(),
        P(("dp", "ctx"), None),
        P(("dp", "ctx"), None),
        P(("dp", "ctx"), None),
        P(("dp", "ctx"), None),
        P(None, ("dp", "ctx")),
        P(("dp", "ctx"), None),
        P(("dp", "ctx"), None),
        P(("dp", "ctx"), None),
        P(("dp", "ctx"), None),
        P(None, ("dp", "ctx")),
        P(("dp", "ctx"), None),
        P(("dp", "ctx"), None),
        P(("dp", "ctx"), None),
        P(("dp", "ctx"), None),
        P(None, ("dp", "ctx")),
    )
    out_specs = (
        P("dp", "ctx", None),
        P("dp", "ctx", None),
        P(("dp", "ctx"), None),
        P(("dp", "ctx"), None),
        P(("dp", "ctx"), None),
        P(("dp", "ctx"), None),
        P(("dp", "ctx"), None),
        P(("dp", "ctx"), None),
        P(("dp", "ctx"), None),
        P(("dp", "ctx"), None),
        P(("dp", "ctx"), None),
        P(("dp", "ctx"), None),
        P(("dp", "ctx"), None),
        P(("dp", "ctx"), None),
        P(None, ("dp", "ctx")),
        P(None, ("dp", "ctx")),
        P(None, ("dp", "ctx")),
    )
    return jax.shard_map(local, mesh=mesh, in_specs=in_specs, out_specs=out_specs, check_vma=False)
```

```python
import functools

import jax
import jax.numpy as jnp
import numpy as np
from jax import lax
from jax.experimental import pallas as pl
from jax.experimental.pallas import tpu as pltpu
from jax.sharding import PartitionSpec as P

D = 2048
HEADS = 32
KV_HEADS = 8
HEAD = 64
FF = 8192
STEP = 5


norm_eps = 1e-05
rope_base = 500000.0
beta_one = 0.9
beta_two = 0.95
gain_rate = 1.25
input_boost = 2.5
weight_decay = 0.1
adam_eps = 1e-08
masked_score = -1e30


def norm_parts(values):
    factor = lax.rsqrt(jnp.mean(values * values, -1, keepdims=True) + norm_eps)
    return (values * factor, factor)


def norm_back(back_normed, normed, factor):
    return factor * (back_normed - normed * jnp.mean(back_normed * normed, -1, keepdims=True))


def adam_update(weight, gradient, first_moment, second_moment, step_rate, decay_rate):
    first_new = beta_one * first_moment + (1.0 - beta_one) * gradient
    second_new = beta_two * second_moment + (1.0 - beta_two) * gradient * gradient
    update = (
        first_new
        / (1.0 - beta_one**STEP)
        / (jnp.sqrt(second_new / (1.0 - beta_two**STEP)) + adam_eps)
    )
    return (first_new, second_new, weight - step_rate * (update + decay_rate * weight))


def line_groups(shards):
    return [[2 * s + half for s in range(shards // 2)] for half in (0, 1)]


def gather_line(rows):
    return lax.all_gather(
        rows, "ctx", axis=0, tiled=True, axis_index_groups=line_groups(lax.axis_size("ctx"))
    )


def sum_line(gradient):
    return lax.psum_scatter(
        gradient,
        "ctx",
        scatter_dimension=0,
        tiled=True,
        axis_index_groups=line_groups(lax.axis_size("ctx")),
    )


def dot_nn(a, b):
    return lax.dot_general(a, b, (((1,), (0,)), ((), ())), preferred_element_type=jnp.float32)


def dot_nt(a, b):
    return lax.dot_general(a, b, (((1,), (1,)), ((), ())), preferred_element_type=jnp.float32)


def dot_tn(a, b):
    return lax.dot_general(a, b, (((0,), (0,)), ((), ())), preferred_element_type=jnp.float32)


def causal_keep(tile):
    keys = lax.broadcasted_iota(jnp.int32, (tile, tile), 0)
    queries = lax.broadcasted_iota(jnp.int32, (tile, tile), 1)
    return keys <= queries


def turn_group(values, cos, sin, forward):
    lanes = lax.broadcasted_iota(jnp.int32, values.shape, 1)
    other = jnp.where(
        lanes % HEAD < HEAD // 2,
        pltpu.roll(values, 2 * HEAD - HEAD // 2, 1),
        pltpu.roll(values, HEAD // 2, 1),
    )
    if forward:
        return values * cos + other * sin
    return values * cos - other * sin


def turn_columns(values, start, turned_cols, cos, sin, forward):
    if start >= turned_cols:
        return values
    turned = turn_group(values, cos, sin, forward)
    if start + 2 * HEAD <= turned_cols:
        return turned
    lanes = lax.broadcasted_iota(jnp.int32, values.shape, 1)
    return jnp.where(lanes < turned_cols - start, turned, values)


def attend_kernel(
    q_heads,
    kv_heads,
    tile,
    order_ref,
    where_ref,
    all_qkv_ref,
    cos_ref,
    sin_ref,
    all_out_ref,
    all_lse_ref,
    all_kept_ref,
    made,
):
    for sequence in range(all_qkv_ref.shape[0]):
        attend_sequence(
            q_heads,
            kv_heads,
            tile,
            order_ref,
            where_ref,
            all_qkv_ref.at[sequence],
            cos_ref,
            sin_ref,
            all_out_ref.at[sequence],
            all_lse_ref.at[sequence],
            all_kept_ref.at[sequence],
            made,
        )


def attend_sequence(
    q_heads,
    kv_heads,
    tile,
    order_ref,
    where_ref,
    qkv_ref,
    cos_ref,
    sin_ref,
    out_ref,
    lse_ref,
    kept_ref,
    made,
):
    blocks, rows, cols = qkv_ref.shape
    length = blocks * rows
    group = q_heads // kv_heads
    q_cols, k_cols = q_heads * HEAD, kv_heads * HEAD
    scale = HEAD ** (-0.5)

    def take_block(i, _):
        start = pl.multiple_of(i * rows, rows)
        cos = cos_ref[i]
        sin = sin_ref[i]
        for c in range(0, cols, 2 * HEAD):
            values = qkv_ref[where_ref[i], :, c : c + 2 * HEAD]
            values = turn_columns(values, c, q_cols + k_cols, cos, sin, True)
            kept_ref[pl.ds(start, rows), c : c + 2 * HEAD] = values.astype(jnp.bfloat16)
        return 0

    lax.fori_loop(0, blocks, take_block, 0)
    keep = causal_keep(tile)
    for kv in range(kv_heads):
        k_at = q_cols + kv * HEAD
        v_at = q_cols + k_cols + kv * HEAD

        def query_step(i, _):
            q_start = pl.multiple_of(i * tile, tile)
            queries = [
                kept_ref[
                    pl.ds(q_start, tile), (kv * group + g) * HEAD : (kv * group + g + 1) * HEAD
                ]
                for g in range(group)
            ]

            def key_tile(j, carry, masked):
                k_start = pl.multiple_of(j * tile, tile)
                keys = kept_ref[pl.ds(k_start, tile), k_at : k_at + HEAD]
                values = kept_ref[pl.ds(k_start, tile), v_at : v_at + HEAD]
                result = []
                for g in range(group):
                    peak, total, weighted = carry[g]
                    scores = dot_nt(keys, queries[g]) * scale
                    if masked:
                        scores = jnp.where(keep, scores, masked_score)
                    new_peak = jnp.maximum(peak, jnp.max(scores, 0, keepdims=True))
                    weights = jnp.exp(scores - new_peak)
                    shrink = jnp.exp(peak - new_peak)
                    total = total * shrink + jnp.sum(weights, 0, keepdims=True)
                    weighted = weighted * shrink + dot_tn(values, weights.astype(jnp.bfloat16))
                    result.append((new_peak, total, weighted))
                return tuple(result)

            start = tuple(
                (
                    jnp.full((1, tile), masked_score, jnp.float32),
                    jnp.zeros((1, tile), jnp.float32),
                    jnp.zeros((HEAD, tile), jnp.float32),
                )
                for _ in range(group)
            )
            carry = lax.fori_loop(0, i, lambda j, c: key_tile(j, c, False), start)
            carry = key_tile(i, carry, True)
            for g in range(group):
                head = kv * group + g
                peak, total, weighted = carry[g]
                lse_ref[head : head + 1, pl.ds(q_start, tile)] = peak + jnp.log(total)
                made[pl.ds(i * (tile // rows), tile // rows), :, head * HEAD : (head + 1) * HEAD] = (
                    (weighted / total).T.astype(jnp.bfloat16).reshape(-1, rows, HEAD)
                )
            return 0

        lax.fori_loop(0, length // tile, query_step, 0)

    def give_block(i, _):
        out_ref[i] = made[order_ref[i]]
        return 0

    lax.fori_loop(0, blocks, give_block, 0)


def attend_back_kernel(
    q_heads,
    kv_heads,
    tile,
    steps,
    order_ref,
    where_ref,
    all_kept_ref,
    all_back_ref,
    all_lse_ref,
    cos_ref,
    sin_ref,
    out_rows,
    residual,
    all_out_ref,
    block_out,
    *scratch,
):
    me = (lax.axis_index("dp"), lax.axis_index("ctx"))
    greet(me, [member(me, by) for by in (1, 2, 4)], [])
    work, scratch = scratch[:4], scratch[4:]
    scatter = GroupScatter(me, out_rows, scratch[:7], scratch[7:], steps)

    def one():
        for k in range(steps):
            scatter.send_first(k)

    def two():
        for k in range(steps):
            scatter.send_second(k)

    def three():
        for k in range(steps):
            span = scatter.window(k)
            for part in (0, 1):
                value = residual[part, span] + scatter.total(k, part)
                block_out[part, span] = value.astype(jnp.bfloat16)

    tasks = [one, two, three]

    def pause():
        if tasks:
            tasks.pop(0)()

    scatter.start()
    for sequence in range(all_kept_ref.shape[0]):
        attend_back_sequence(
            q_heads,
            kv_heads,
            tile,
            pause,
            order_ref,
            where_ref,
            all_kept_ref.at[sequence],
            all_back_ref.at[sequence],
            all_lse_ref.at[sequence],
            cos_ref,
            sin_ref,
            all_out_ref.at[sequence],
            *work,
        )
    while tasks:
        pause()
    scatter.finish()


def attend_back_sequence(
    q_heads,
    kv_heads,
    tile,
    pause,
    order_ref,
    where_ref,
    kept_ref,
    back_ref,
    lse_ref,
    cos_ref,
    sin_ref,
    out_ref,
    back_sorted,
    grad,
    delta_ref,
    dq_ref,
):
    length, cols = kept_ref.shape
    blocks, rows = back_ref.shape[:2]
    group = q_heads // kv_heads
    q_cols, k_cols = q_heads * HEAD, kv_heads * HEAD
    scale = HEAD ** (-0.5)
    tiles = length // tile

    def take_block(i, _):
        start = pl.multiple_of(i * rows, rows)
        back_sorted[pl.ds(start, rows), :] = back_ref[where_ref[i]]
        return 0

    lax.fori_loop(0, blocks, take_block, 0)
    keep = causal_keep(tile)
    for kv in range(kv_heads):
        k_at = q_cols + kv * HEAD
        v_at = q_cols + k_cols + kv * HEAD

        def load(i, g):
            start = pl.multiple_of(i * tile, tile)
            head = kv * group + g
            at = slice(head * HEAD, (head + 1) * HEAD)
            return (
                kept_ref[pl.ds(start, tile), at],
                back_sorted[pl.ds(start, tile), at],
                lse_ref[head : head + 1, pl.ds(start, tile)],
            )

        def load_kv(j):
            start = pl.multiple_of(j * tile, tile)
            return (
                kept_ref[pl.ds(start, tile), k_at : k_at + HEAD],
                kept_ref[pl.ds(start, tile), v_at : v_at + HEAD],
            )

        def tile_terms(keys, values, query, back, lse, masked):
            weights = jnp.exp(dot_nt(keys, query) * scale - lse)
            if masked:
                weights = jnp.where(keep, weights, 0.0)
            return weights, dot_nt(values, back)

        def delta_step(i, _):
            rows_i = [load(i, g) for g in range(group)]

            def one(j, carry, masked):
                keys, values = load_kv(j)
                result = []
                for g in range(group):
                    weights, back_weights = tile_terms(keys, values, *rows_i[g], masked)
                    result.append(carry[g] + jnp.sum(weights * back_weights, 0, keepdims=True))
                return tuple(result)

            carry = tuple(jnp.zeros((1, tile), jnp.float32) for _ in range(group))
            carry = lax.fori_loop(0, i, lambda j, c: one(j, c, False), carry)
            carry = one(i, carry, True)
            for g in range(group):
                delta_ref[g : g + 1, pl.ds(pl.multiple_of(i * tile, tile), tile)] = carry[g]
            return 0

        lax.fori_loop(0, tiles, delta_step, 0)
        if kv == 0:
            pause()
        dq_ref[...] = jnp.zeros_like(dq_ref)

        def key_step(j, _):
            keys, values = load_kv(j)

            def one(i, carry, masked):
                back_key, back_value = carry
                start = pl.multiple_of(i * tile, tile)
                for g in range(group):
                    query, back, lse = load(i, g)
                    weights, back_weights = tile_terms(keys, values, query, back, lse, masked)
                    delta = delta_ref[g : g + 1, pl.ds(start, tile)]
                    back_scores = (weights * (back_weights - delta)).astype(jnp.bfloat16)
                    back_key = back_key + dot_nn(back_scores, query)
                    back_value = back_value + dot_nn(weights.astype(jnp.bfloat16), back)
                    dq_ref[g * HEAD : (g + 1) * HEAD, pl.ds(start, tile)] += dot_tn(
                        keys, back_scores
                    )
                return back_key, back_value

            zero = jnp.zeros((tile, HEAD), jnp.float32)
            carry = one(j, (zero, zero), True)
            carry = lax.fori_loop(j + 1, tiles, lambda i, c: one(i, c, False), carry)
            span = pl.ds(j * (tile // rows), tile // rows)
            grad[span, :, k_at : k_at + HEAD] = (carry[0] * scale).reshape(-1, rows, HEAD)
            grad[span, :, v_at : v_at + HEAD] = carry[1].reshape(-1, rows, HEAD)
            return 0

        lax.fori_loop(0, tiles, key_step, 0)
        for g in range(group):
            head = kv * group + g
            turned = (dq_ref[g * HEAD : (g + 1) * HEAD, :] * scale).T
            grad[:, :, head * HEAD : (head + 1) * HEAD] = turned.reshape(-1, rows, HEAD)

    def give_block(i, _):
        cos = cos_ref[order_ref[i]]
        sin = sin_ref[order_ref[i]]
        for c in range(0, cols, 2 * HEAD):
            values = grad[order_ref[i], :, c : c + 2 * HEAD]
            values = turn_columns(values, c, q_cols + k_cols, cos, sin, False)
            out_ref[i, :, c : c + 2 * HEAD] = values.astype(jnp.bfloat16)
        return 0

    lax.fori_loop(0, blocks, give_block, 0)


MESH = pl.DeviceIdType.MESH


def part_owner(part):
    return part % 2 * 2 + part // 2


def sequence_target(group, place, second, splits):
    part = place // 2
    target = (part_owner(part % 4), (2 * group + second) * splits + part // 4)
    return target, place % 2


def token_target(group, place, half, splits):
    sequence = place // splits
    part = part_owner(group) + 4 * (place % splits)
    return (sequence // 2, 2 * part + half), sequence % 2


def remote(source, target, sems, device):
    return pltpu.make_async_remote_copy(
        src_ref=source,
        dst_ref=target,
        send_sem=sems[0],
        recv_sem=sems[1],
        device_id=device,
        device_id_type=MESH,
    )


def same(one, other):
    return jnp.logical_and(one[0] == other[0], one[1] == other[1])


def greet(me, peers, movers):
    barrier = pltpu.get_barrier_semaphore()
    for peer in peers:
        pl.semaphore_signal(barrier, inc=1, device_id=peer, device_id_type=MESH)
    expected = len(peers)
    for source, target in movers:

        @pl.when(jnp.logical_not(same(source, me)))
        def _():
            pl.semaphore_signal(barrier, inc=1, device_id=source, device_id_type=MESH)

        expected = expected + jnp.where(same(target, me), 0, 1)
    pl.semaphore_wait(barrier, expected)


def move_start(me, source, target, target_device, send, receive):
    here = same(target_device, me)

    @pl.when(here)
    def _():
        pltpu.make_async_copy(source, target, receive).start()

    @pl.when(jnp.logical_not(here))
    def _():
        remote(source, target, (send, receive), target_device).start()


def move_sent(me, source, target, target_device, send, receive):
    @pl.when(jnp.logical_not(same(target_device, me)))
    def _():
        remote(source, target, (send, receive), target_device).wait_send()


def member(me, by):
    return (me[0] ^ (by // 2), me[1] ^ (by % 2))


def group_index(device):
    return 2 * device[0] + device[1] % 2


class GroupExchange:
    def __init__(self, me, pieces, got, sems):
        self.me, self.pieces, self.got, self.sems = me, pieces, got, sems

    def hop(self, by):
        peer = member(self.me, by)
        sems = (self.sems.at[0, by - 1], self.sems.at[1, by - 1])
        return remote(
            self.pieces.at[group_index(peer)], self.got.at[group_index(self.me)], sems, peer
        )

    def own(self):
        mine = group_index(self.me)
        return pltpu.make_async_copy(self.pieces.at[mine], self.got.at[mine], self.sems.at[0, 7])

    def start(self):
        for by in range(1, 8):
            self.hop(by).start()
        self.own().start()

    def finish(self):
        self.own().wait()
        for by in range(1, 8):
            self.hop(by).wait()


class GroupGather:
    def __init__(self, me, rows, sems, own, window):
        self.rows, self.sems, self.own, self.window = rows, sems, own, window
        self.core, self.across, self.beside = member(me, 2), member(me, 4), member(me, 1)

    def hop(self, index):
        across, beside, core = self.across, self.beside, self.core
        source, i, j, half, device = (
            (None, 0, 2, 0, across),
            (None, 1, 0, 1, beside),
            (None, 1, 0, 0, beside),
            (None, 0, 2, 1, across),
            ((0, 2), 1, 2, 0, beside),
            ((1, 0), 1, 2, 1, across),
            (None, 0, 1, slice(0, 2), core),
            ((0, 2), 0, 3, slice(0, 2), core),
            ((1, 0), 1, 1, slice(0, 2), core),
            ((1, 2), 1, 3, slice(0, 2), core),
        )[index]
        if source is None:
            source = self.own.at[half, self.window]
        else:
            source = self.rows.at[source[0], source[1], half, self.window]
        target = self.rows.at[i, j, half, self.window]
        return remote(source, target, (self.sems.at[0, index], self.sems.at[1, index]), device)

    def start(self):
        for index in (0, 1, 2, 3, 6):
            self.hop(index).start()

    def pass_on(self):
        self.hop(0).wait_recv()
        self.hop(4).start()
        self.hop(1).wait_recv()
        self.hop(5).start()
        self.hop(3).wait_recv()
        self.hop(7).start()
        self.hop(2).wait_recv()
        self.hop(8).start()

    def finish(self):
        self.hop(4).wait_recv()
        self.hop(5).wait_recv()
        self.hop(9).start()
        for index in (6, 7, 8, 9):
            self.hop(index).wait_recv()
        for index in range(10):
            self.hop(index).wait_send()


class Moves:
    def __init__(self, me, splits, source, target, sems, back):
        self.me, self.splits, self.source, self.target = me, splits, source, target
        self.sems, self.back = sems, back

    def one(self, i):
        find = token_target if self.back else sequence_target
        device, place = find(self.me[0], self.me[1], i, self.splits)
        return (
            self.me,
            self.source.at[i],
            self.target.at[place],
            device,
            self.sems.at[0, i],
            self.sems.at[1, place],
        )

    def start(self):
        for i in (0, 1):
            move_start(*self.one(i))

    def wait_recv(self):
        for i in (0, 1):
            pltpu.make_async_copy(self.source.at[0], self.target.at[i], self.sems.at[1, i]).wait()

    def finish(self):
        for i in (0, 1):
            move_sent(*self.one(i))


def movers_of(me, splits, back):
    into = [sequence_target(me[0], me[1], i, splits)[0] for i in (0, 1)]
    home = [token_target(me[0], me[1], i, splits)[0] for i in (0, 1)]
    return list(zip(into, home)) if back else list(zip(home, into))


def first_kernel(shards, splits, tokens, pieces, out_own, gate_pieces, *refs):
    rows, in_all, out_all, gate_rows, held = refs[:5]
    move_sems, group_sems, piece_sems, gate_sems, own_sem, in_sems, out_sems = refs[5:]
    me = (lax.axis_index("dp"), lax.axis_index("ctx"))
    group, place = me
    slow = shards // 2
    slot = place // 2
    line = [(group, place ^ (2 * by)) for by in range(1, slow)]
    wanted, block = place // slow, place % slow
    takers = [(group, 2 * (slot ^ by) + wanted) for by in range(slow)]
    givers = [(group, place % 2 * slow + block_by) for block_by in range(slow)]
    movers = movers_of(me, splits, False) + list(zip(givers, takers))
    greet(me, [member(me, by) for by in range(1, 8)] + line, movers)
    swap = GroupExchange(me, pieces, held, piece_sems)
    gate_swap = GroupExchange(me, gate_pieces, gate_rows, gate_sems)
    move = Moves(me, splits, tokens, rows.at[0, 0], move_sems, False)

    def in_line(by):
        sems = (in_sems.at[0, by - 1], in_sems.at[1, by - 1])
        return remote(held, in_all.at[slot], sems, line[by - 1])

    def out_send(by):
        return (
            me,
            out_own,
            out_all.at[block],
            takers[by],
            out_sems.at[0, by],
            out_sems.at[1, block],
        )

    own = pltpu.make_async_copy(held, in_all.at[slot], own_sem)
    move.start()
    swap.start()
    gate_swap.start()
    swap.finish()
    move.wait_recv()
    spread = GroupGather(me, rows, group_sems, rows.at[0, 0], slice(0, tokens.shape[1]))
    spread.start()
    for by in range(1, slow):
        in_line(by).start()
    own.start()
    for by in range(slow):
        move_start(*out_send(by))
    spread.pass_on()
    for by in range(1, slow):
        in_line(by).wait()
    spread.finish()
    own.wait()
    for by in range(slow):
        pltpu.make_async_copy(out_own, out_all.at[by], out_sems.at[1, by]).wait()
    for by in range(slow):
        move_sent(*out_send(by))
    gate_swap.finish()
    move.finish()


def first_exchange(tokens, pieces, out_own, gate_pieces, shards, splits, identity):
    low = jnp.bfloat16
    slow = shards // 2
    any_space = pl.BlockSpec(memory_space=pl.ANY)
    dma = pltpu.SemaphoreType.DMA
    made = pl.pallas_call(
        functools.partial(first_kernel, shards, splits),
        out_shape=(
            jax.ShapeDtypeStruct((2, 4) + tokens.shape, low),
            jax.ShapeDtypeStruct((slow,) + pieces.shape, low),
            jax.ShapeDtypeStruct((slow,) + out_own.shape, low),
            jax.ShapeDtypeStruct(gate_pieces.shape, low),
            jax.ShapeDtypeStruct(pieces.shape, low),
        ),
        in_specs=[any_space] * 4,
        out_specs=(any_space,) * 5,
        scratch_shapes=[
            dma((2, 2)),
            dma((2, 10)),
            dma((2, 8)),
            dma((2, 8)),
            dma,
            dma((2, slow - 1)),
            dma((2, slow)),
        ],
        compiler_params=pltpu.CompilerParams(
            collective_id=identity, has_side_effects=True, vmem_limit_bytes=8 << 20
        ),
        cost_estimate=pl.CostEstimate(flops=0, bytes_accessed=200 << 20, transcendentals=0),
    )(tokens, pieces, out_own, gate_pieces)
    return made[:4]


class GroupScatter:
    def __init__(self, me, parts, buffers, sems, steps):
        self.parts = parts
        self.core_in, self.kept, self.sent, self.came, self.held = buffers[:5]
        self.sent_last, self.came_last = buffers[5:]
        self.core_sems, self.kept_sems, self.one_sems, self.last_sems = sems
        self.core, self.across, self.beside = member(me, 2), member(me, 4), member(me, 1)
        self.size = parts.shape[3] // steps
        self.steps = steps

    def window(self, k):
        return slice(k * self.size, (k + 1) * self.size)

    def to_core(self, k, j):
        return remote(
            self.parts.at[:, 2 * j + 1, :, self.window(k)],
            self.core_in.at[:, j, :, self.window(k)],
            (self.core_sems.at[0, k, j], self.core_sems.at[1, k, j]),
            self.core,
        )

    def keep(self, k, j):
        return pltpu.make_async_copy(
            self.parts.at[:, 2 * j, :, self.window(k)],
            self.kept.at[:, j, :, self.window(k)],
            self.kept_sems.at[k, j],
        )

    def first(self, k, half):
        return remote(
            self.sent.at[half, :, self.window(k)],
            self.came.at[half, :, self.window(k)],
            (self.one_sems.at[0, k, half], self.one_sems.at[1, k, half]),
            (self.beside, self.across)[half],
        )

    def second(self, k, half):
        return remote(
            self.sent_last.at[half, self.window(k)],
            self.came_last.at[half, self.window(k)],
            (self.last_sems.at[0, k, half], self.last_sems.at[1, k, half]),
            (self.across, self.beside)[half],
        )

    def start(self):
        for k in range(self.steps):
            for j in (0, 1):
                self.to_core(k, j).start()
                self.keep(k, j).start()

    def send_first(self, k):
        wide = jnp.float32
        rows = self.window(k)
        for j in (0, 1):
            self.keep(k, j).wait()
            self.to_core(k, j).wait_recv()
        for half in (0, 1):
            for other in (0, 1):
                at = (1, other) if half == 0 else (other, 1)
                both = self.kept[at[0], at[1], half, rows].astype(wide)
                both = both + self.core_in[at[0], at[1], half, rows].astype(wide)
                self.sent[half, other, rows] = both.astype(jnp.bfloat16)
            self.first(k, half).start()
        for half in (0, 1):
            for other in (0, 1):
                at = (0, other) if half == 0 else (other, 0)
                both = self.kept[at[0], at[1], half, rows].astype(wide)
                self.held[half, other, rows] = both + self.core_in[at[0], at[1], half, rows].astype(
                    wide
                )

    def send_second(self, k):
        wide = jnp.float32
        rows = self.window(k)
        for half in (0, 1):
            self.first(k, half).wait_recv()
            both = self.held[half, 1, rows] + self.came[half, 1, rows].astype(wide)
            self.sent_last[half, rows] = both.astype(jnp.bfloat16)
            self.second(k, half).start()
            self.held[half, 0, rows] = self.held[half, 0, rows] + self.came[half, 0, rows].astype(
                wide
            )

    def total(self, k, half):
        self.second(k, half).wait_recv()
        rows = self.window(k)
        return self.held[half, 0, rows] + self.came_last[half, rows].astype(jnp.float32)

    def finish(self):
        for k in range(self.steps):
            for j in (0, 1):
                self.to_core(k, j).wait_send()
            for half in (0, 1):
                self.first(k, half).wait_send()
                self.second(k, half).wait_send()


def scatter_scratch(rows, width, steps):
    low, wide = jnp.bfloat16, jnp.float32
    dma = pltpu.SemaphoreType.DMA
    return [
        pltpu.VMEM((2, 2, 2, rows, width), low),
        pltpu.VMEM((2, 2, 2, rows, width), low),
        pltpu.VMEM((2, 2, rows, width), low),
        pltpu.VMEM((2, 2, rows, width), low),
        pltpu.VMEM((2, 2, rows, width), wide),
        pltpu.VMEM((2, rows, width), low),
        pltpu.VMEM((2, rows, width), low),
        dma((2, steps, 2)),
        dma((steps, 2)),
        dma((2, steps, 2)),
        dma((2, steps, 2)),
    ]


def reordered(rows, slow, back):
    each = rows.shape[1] // (4 * slow)
    if back:
        starts = [s * 4 + dp for dp in range(4) for s in range(slow)]
    else:
        starts = [dp * slow + s for s in range(slow) for dp in range(4)]
    return jnp.concatenate([rows[:, i * each : (i + 1) * each] for i in starts], 1)


def turn_kernel(slow, steps, backward, parts, gain, *refs):
    if backward:
        residual, cot, result, gain_grad, rows = refs[:5]
        scratch = refs[5:]
    else:
        tokens, result, rows = refs[:3]
        scratch = refs[3:]
    own, own_sems, group_sems = scratch[:3]
    me = (lax.axis_index("dp"), lax.axis_index("ctx"))
    greet(me, [member(me, by) for by in (1, 2, 4)], [])
    scatter = GroupScatter(me, parts, scratch[3:10], scratch[10:], steps)
    gathers = [GroupGather(me, rows, group_sems.at[k], own, scatter.window(k)) for k in range(steps)]
    scatter.start()
    for k in range(steps):
        scatter.send_first(k)
    for k in range(steps):
        scatter.send_second(k)
    for k in range(steps):
        span = scatter.window(k)
        for half in (0, 1):
            total = scatter.total(k, half)
            if backward:
                values = residual[half, span]
                factor = lax.rsqrt(jnp.mean(values * values, -1, keepdims=True) + norm_eps)
                normed = values * factor
                total = reordered(total, slow, True)
                part = jnp.sum(total * normed, 0, keepdims=True)
                if k == 0 and half == 0:
                    gain_grad[...] = part
                else:
                    gain_grad[...] += part
                back = total * gain[...]
                back = factor * (back - normed * jnp.mean(back * normed, -1, keepdims=True))
                back = cot[half, span].astype(jnp.float32) + back
                result[half, span] = back
                own[half, span] = back.astype(jnp.bfloat16)
            else:
                values = tokens[half, span].astype(jnp.float32) + total
                factor = lax.rsqrt(jnp.mean(values * values, -1, keepdims=True) + norm_eps)
                result[half, span] = values
                own[half, span] = reordered(values * factor * gain[...], slow, False).astype(
                    jnp.bfloat16
                )
        gathers[k].start()
        keep = pltpu.make_async_copy(own.at[:, span], rows.at[0, 0, :, span], own_sems.at[k])
        keep.start()
    for k in range(steps):
        gathers[k].pass_on()
    for k in range(steps):
        gathers[k].finish()
        span = scatter.window(k)
        pltpu.make_async_copy(own.at[:, span], rows.at[0, 0, :, span], own_sems.at[k]).wait()
    scatter.finish()


def turn(parts, gain, rows_in, slow, backward, identity):
    low, wide = jnp.bfloat16, jnp.float32
    dma = pltpu.SemaphoreType.DMA
    rows, width = parts.shape[3:]
    steps = 2
    any_space = pl.BlockSpec(memory_space=pl.ANY)
    vmem = pl.BlockSpec(memory_space=pltpu.VMEM)
    shapes = [jax.ShapeDtypeStruct((2, rows, width), wide)]
    if backward:
        shapes.append(jax.ShapeDtypeStruct((1, width), wide))
    return pl.pallas_call(
        functools.partial(turn_kernel, slow, steps, backward),
        out_shape=tuple(shapes) + (jax.ShapeDtypeStruct((2, 4, 2, rows, width), low),),
        in_specs=[any_space, vmem] + [vmem] * len(rows_in),
        out_specs=tuple([vmem] * len(shapes) + [any_space]),
        scratch_shapes=[
            pltpu.VMEM((2, rows, width), low),
            dma((steps,)),
            dma((steps, 2, 10)),
        ]
        + scatter_scratch(rows, width, steps),
        compiler_params=pltpu.CompilerParams(
            collective_id=identity, has_side_effects=True, vmem_limit_bytes=48 << 20
        ),
        cost_estimate=pl.CostEstimate(flops=0, bytes_accessed=250 << 20, transcendentals=0),
    )(parts, gain, *rows_in)


def spread_kernel(splits, tokens, rows, move_sems, group_sems):
    me = (lax.axis_index("dp"), lax.axis_index("ctx"))
    greet(me, [member(me, by) for by in (1, 2, 4)], movers_of(me, splits, False))
    move = Moves(me, splits, tokens, rows.at[0, 0], move_sems, False)
    spread = GroupGather(me, rows, group_sems, rows.at[0, 0], slice(0, tokens.shape[1]))
    move.start()
    move.wait_recv()
    spread.start()
    spread.pass_on()
    spread.finish()
    move.finish()


def spread_tokens(tokens, splits, identity):
    any_space = pl.BlockSpec(memory_space=pl.ANY)
    dma = pltpu.SemaphoreType.DMA
    return pl.pallas_call(
        functools.partial(spread_kernel, splits),
        out_shape=jax.ShapeDtypeStruct((2, 4) + tokens.shape, tokens.dtype),
        in_specs=[any_space],
        out_specs=any_space,
        scratch_shapes=[dma((2, 2)), dma((2, 10))],
        compiler_params=pltpu.CompilerParams(
            collective_id=identity, has_side_effects=True, vmem_limit_bytes=4 << 20
        ),
        cost_estimate=pl.CostEstimate(flops=0, bytes_accessed=100 << 20, transcendentals=0),
    )(tokens)


class LineSum:
    def __init__(self, me, slow, parts, buffers, sems):
        self.parts = parts
        self.kept, self.arrived = buffers
        self.sems, self.own_sem = sems
        self.slot = me[1] // 2
        self.slow = slow
        self.line = [(me[0], me[1] ^ (2 * by)) for by in range(1, slow)]

    def hop(self, by):
        sems = (self.sems.at[0, by - 1], self.sems.at[1, by - 1])
        return remote(
            self.parts.at[self.slot ^ by], self.arrived.at[by - 1], sems, self.line[by - 1]
        )

    def own(self):
        return pltpu.make_async_copy(self.parts.at[self.slot], self.kept, self.own_sem)

    def start(self):
        for by in range(1, self.slow):
            self.hop(by).start()
        self.own().start()

    def total(self):
        self.own().wait()
        value = self.kept[...].astype(jnp.float32)
        for by in range(1, self.slow):
            self.hop(by).wait_recv()
            value = value + self.arrived[by - 1].astype(jnp.float32)
        return value

    def finish(self):
        for by in range(1, self.slow):
            self.hop(by).wait_send()


def line_scratch(shape, kind, slow):
    dma = pltpu.SemaphoreType.DMA
    return [
        pltpu.VMEM(shape, kind),
        pltpu.VMEM((slow - 1,) + shape, kind),
        dma((2, slow - 1)),
        dma,
    ]


def last_kernel(shards, splits, steps, in_parts, out_parts, gate_parts, in_back, made_two, *refs):
    gain, gain_two_grad, tokens, back_rows = refs[:4]
    in_total, out_total, gate_total, gains_total, tokens_grad, block_out = refs[4:10]
    scratch = list(refs[10:])

    def take(count):
        taken = scratch[:count]
        del scratch[:count]
        return taken

    me = (lax.axis_index("dp"), lax.axis_index("ctx"))
    group, place = me
    slow = shards // 2
    slot, half = place // 2, place % 2
    owned = in_parts.shape[2]
    home = (group, half * slow + slot)
    movers = movers_of(me, splits, True)
    movers.append(((group, place % slow * 2 + place // slow), home))
    line = [(group, place ^ (2 * by)) for by in range(1, slow)]
    greet(me, [member(me, by) for by in range(1, 8)] + line, movers)
    one = take(11)
    back_sum = GroupScatter(me, in_back, one[:7], one[7:], steps)
    line_in = take(4)
    line_out = take(4)
    line_gains = take(4)
    in_done, out_done, gains_own, gains_done, made_one, gain_grad = take(6)
    in_sems, gate_sems, gains_sems, one_sems, two_sems, home_sems = take(6)
    in_line = LineSum(me, slow, in_parts, line_in[:2], line_in[2:])
    out_line = LineSum(me, slow, out_parts, line_out[:2], line_out[2:])
    gains_line = LineSum(me, slow, gains_own, line_gains[:2], line_gains[2:])
    in_swap = GroupExchange(me, in_done, in_total, in_sems)
    gate_swap = GroupExchange(me, gate_parts, gate_total, gate_sems)
    gains_swap = GroupExchange(me, gains_done, gains_total, gains_sems)
    move_grad = Moves(me, splits, made_one, tokens_grad, one_sems, True)
    move_out = Moves(me, splits, made_two, block_out, two_sems, True)
    back_sum.start()
    in_line.start()
    out_line.start()
    move_out.start()
    for k in range(steps):
        back_sum.send_first(k)
    for k in range(steps):
        back_sum.send_second(k)
    for k in range(steps):
        span = back_sum.window(k)
        for part in (0, 1):
            total = back_sum.total(k, part)
            values = tokens[part, span].astype(jnp.float32)
            normed, factor = norm_parts(values)
            grad = jnp.sum(total * normed, 0, keepdims=True)
            if k == 0 and part == 0:
                gain_grad[...] = grad
            else:
                gain_grad[...] += grad
            value = back_rows[part, span] + norm_back(total * gain[...], normed, factor)
            made_one[part, span] = value.astype(jnp.bfloat16)
    move_grad.start()
    gains_own[...] = jnp.zeros_like(gains_own)
    for dp in range(4):
        for s in range(slow):
            for side in range(2):
                at = ((dp * slow + s) * 2 + side) * owned
                index = 2 * dp + side
                gains_own[s, index, 0:1, 0:owned] = gain_grad[:, at : at + owned]
                gains_own[s, index, 0:1, owned : 2 * owned] = gain_two_grad[:, at : at + owned]
    gains_line.start()
    gate_swap.start()
    in_done[...] = in_line.total().astype(jnp.bfloat16)
    in_swap.start()
    gains_done[...] = gains_line.total()
    gains_swap.start()
    out_done[...] = out_line.total().astype(jnp.bfloat16)
    to_home = (me, out_done, out_total, home, home_sems.at[0], home_sems.at[1])
    move_start(*to_home)
    pltpu.make_async_copy(out_done, out_total, home_sems.at[1]).wait()
    move_sent(*to_home)
    for swap in (in_swap, gate_swap, gains_swap):
        swap.finish()
    for move in (move_out, move_grad):
        move.wait_recv()
        move.finish()
    for part in (in_line, out_line, gains_line, back_sum):
        part.finish()


def last_sums(
    in_parts, out_parts, gate_parts, in_back, out_rows, others, shards, splits, identity
):
    low, wide = jnp.bfloat16, jnp.float32
    slow = shards // 2
    steps = 2
    any_space = pl.BlockSpec(memory_space=pl.ANY)
    vmem = pl.BlockSpec(memory_space=pltpu.VMEM)
    dma = pltpu.SemaphoreType.DMA
    rows, width = in_back.shape[3:]
    gains_shape = (8, 8, 128)
    moved = jax.ShapeDtypeStruct((2, rows, width), low)
    return pl.pallas_call(
        functools.partial(last_kernel, shards, splits, steps),
        out_shape=(
            jax.ShapeDtypeStruct(in_parts.shape[1:], low),
            jax.ShapeDtypeStruct(out_parts.shape[1:], low),
            jax.ShapeDtypeStruct(gate_parts.shape, low),
            jax.ShapeDtypeStruct(gains_shape, wide),
            moved,
            moved,
        ),
        in_specs=[any_space] * 5 + [vmem] * 4,
        out_specs=(any_space,) * 6,
        scratch_shapes=scatter_scratch(rows, width, steps)
        + line_scratch(in_parts.shape[1:], low, slow)
        + line_scratch(out_parts.shape[1:], low, slow)
        + line_scratch(gains_shape, wide, slow)
        + [
            pltpu.VMEM(in_parts.shape[1:], low),
            pltpu.VMEM(out_parts.shape[1:], low),
            pltpu.VMEM((slow,) + gains_shape, wide),
            pltpu.VMEM(gains_shape, wide),
            pltpu.VMEM(moved.shape, low),
            pltpu.VMEM((1, width), wide),
            dma((2, 8)),
            dma((2, 8)),
            dma((2, 8)),
            dma((2, 2)),
            dma((2, 2)),
            dma((2,)),
        ],
        compiler_params=pltpu.CompilerParams(
            collective_id=identity, has_side_effects=True, vmem_limit_bytes=56 << 20
        ),
        cost_estimate=pl.CostEstimate(flops=0, bytes_accessed=300 << 20, transcendentals=0),
    )(in_parts, out_parts, gate_parts, in_back, out_rows, *others)


def position_tables(blocks, rows):
    frequency = rope_base ** (-(np.arange(HEAD // 2) * 2.0 / HEAD))
    angles = np.arange(blocks * rows).reshape(blocks, rows, 1) * frequency
    cos, sin = np.cos(angles), np.sin(angles)
    cosine = np.concatenate([cos, cos, cos, cos], 2)
    sines = np.concatenate([-sin, sin, -sin, sin], 2)
    return jnp.asarray(cosine, jnp.float32), jnp.asarray(sines, jnp.float32)


def attend(order, where, qkv, tables, q_heads, kv_heads):
    seqs, length, cols = qkv.shape
    blocks = order.shape[0]
    rows = length // blocks
    whole = pl.BlockSpec(memory_space=pltpu.VMEM)
    small = pl.BlockSpec(memory_space=pltpu.SMEM)
    return pl.pallas_call(
        functools.partial(attend_kernel, q_heads, kv_heads, 256),
        out_shape=(
            jax.ShapeDtypeStruct((seqs, blocks, rows, q_heads * HEAD), jnp.bfloat16),
            jax.ShapeDtypeStruct((seqs, q_heads, length), jnp.float32),
            jax.ShapeDtypeStruct((seqs, length, cols), jnp.bfloat16),
        ),
        in_specs=[small, small, whole, whole, whole],
        out_specs=(whole, whole, whole),
        scratch_shapes=[pltpu.VMEM((blocks, rows, q_heads * HEAD), jnp.bfloat16)],
        compiler_params=pltpu.CompilerParams(vmem_limit_bytes=40 << 20),
        cost_estimate=pl.CostEstimate(
            flops=2 * seqs * length * length * q_heads * HEAD,
            bytes_accessed=100 << 20,
            transcendentals=seqs * length * length * q_heads // 2,
        ),
    )(order, where, qkv.reshape(seqs, blocks, rows, cols), *tables)


def attend_back(
    order, where, kept, back, lse, tables, out_rows, residual, q_heads, kv_heads, identity
):
    seqs, length, cols = kept.shape
    blocks = order.shape[0]
    block = length // blocks
    group = q_heads // kv_heads
    rows, width = out_rows.shape[3:]
    steps = 2
    whole = pl.BlockSpec(memory_space=pltpu.VMEM)
    small = pl.BlockSpec(memory_space=pltpu.SMEM)
    any_space = pl.BlockSpec(memory_space=pl.ANY)
    return pl.pallas_call(
        functools.partial(attend_back_kernel, q_heads, kv_heads, 256, steps),
        out_shape=(
            jax.ShapeDtypeStruct((seqs, blocks, block, cols), jnp.bfloat16),
            jax.ShapeDtypeStruct((2, rows, width), jnp.bfloat16),
        ),
        in_specs=[small, small] + [whole] * 5 + [any_space, whole],
        out_specs=(whole, whole),
        scratch_shapes=[
            pltpu.VMEM((length, q_heads * HEAD), jnp.bfloat16),
            pltpu.VMEM((blocks, block, cols), jnp.float32),
            pltpu.VMEM((group, length), jnp.float32),
            pltpu.VMEM((group * HEAD, length), jnp.float32),
        ]
        + scatter_scratch(rows, width, steps),
        compiler_params=pltpu.CompilerParams(
            collective_id=identity, has_side_effects=True, vmem_limit_bytes=56 << 20
        ),
        cost_estimate=pl.CostEstimate(
            flops=7 * seqs * length * length * q_heads * HEAD,
            bytes_accessed=100 << 20,
            transcendentals=seqs * length * length * q_heads // 2,
        ),
    )(
        order,
        where,
        kept,
        back.reshape(seqs, blocks, block, -1),
        lse,
        *tables,
        out_rows,
        residual,
    )


def gate_update_kernel(slow, step_rate, grad, weight, first, second, new_first, new_second, new):
    units = grad.shape[2] // slow
    pieces = [grad[half, :, s * units : (s + 1) * units] for s in range(slow) for half in (0, 1)]
    gradient = jnp.concatenate(pieces, 1).astype(jnp.float32)
    new_first[...], new_second[...], new[...] = adam_update(
        weight[...], gradient, first[...], second[...], step_rate, weight_decay
    )


def gate_update(grad, weight, first, second, slow, step_rate):
    rows, width = weight.shape
    block = pl.BlockSpec((rows, width // 8), lambda side, dp: (0, 4 * side + dp))
    piece = pl.BlockSpec((2, rows, width // 16), lambda side, dp: (dp, 0, side))
    return pl.pallas_call(
        functools.partial(gate_update_kernel, slow, step_rate),
        grid=(2, 4),
        out_shape=(jax.ShapeDtypeStruct(weight.shape, jnp.float32),) * 3,
        in_specs=[piece, block, block, block],
        out_specs=(block,) * 3,
        compiler_params=pltpu.CompilerParams(vmem_limit_bytes=32 << 20),
    )(grad, weight, first, second)


def local(
    tokens,
    cotangent,
    block_order,
    attention_in,
    attention_out,
    gate_up,
    down_matrix,
    gains,
    mean_attention_in,
    mean_attention_out,
    mean_gate_up,
    mean_down,
    mean_gains,
    square_attention_in,
    square_attention_out,
    square_gate_up,
    square_down,
    square_gains,
):
    seq_count, shard_rows, width = tokens.shape
    shards = lax.axis_size("ctx")
    slow = shards // 2
    mine = lax.axis_index("dp")
    beside = lax.axis_index("ctx") % 2
    low = jnp.bfloat16
    owned = attention_in.shape[0]
    hidden_units = gate_up.shape[1] // 2
    part_hidden = hidden_units // 8
    units = down_matrix.shape[0]
    part_q = HEADS * HEAD // 8
    part_k = KV_HEADS * HEAD // 8
    part_cols = part_q + 2 * part_k
    count = seq_count * shard_rows
    together = 8 * count
    spread = shards // (4 * seq_count)
    splits = max(1, slow // 8)
    seqs = 2 // spread if spread < 2 else 1
    length = shards * shard_rows
    q_heads = HEADS // 8 // splits
    kv_heads = KV_HEADS // 8

    in_low = attention_in.astype(low)
    gains_row = jnp.pad(gains.astype(low).reshape(1, -1), ((0, 15), (0, part_cols - 2 * owned)))
    pieces = jnp.stack(
        [
            jnp.concatenate(
                [
                    jnp.concatenate(
                        [
                            in_low[:, i * part_q : (i + 1) * part_q],
                            in_low[:, 8 * part_q + i * part_k :][:, :part_k],
                            in_low[:, 8 * (part_q + part_k) + i * part_k :][:, :part_k],
                        ],
                        1,
                    ),
                    gains_row,
                ]
            )
            for i in range(8)
        ]
    )
    gate_low = gate_up.astype(low)
    gate_pieces = jnp.stack(
        [
            jnp.concatenate(
                [
                    gate_low[:, side * hidden_units + (dp * shards + 2 * s + half) * units :][
                        :, :units
                    ]
                    for side in range(2)
                    for s in range(slow)
                ],
                1,
            )
            for dp in range(4)
            for half in range(2)
        ]
    )
    tokens_all, in_all, w_out, gate_rows = first_exchange(
        tokens, pieces, attention_out.astype(low), gate_pieces, shards, spread, 1
    )
    in_all = in_all.reshape(slow, 4, 2, owned + 16, part_cols).swapaxes(0, 1)
    w_in = in_all[:, :, :, :owned].reshape(width, part_cols)
    w_out = w_out.reshape(part_q, width)
    gains_all = in_all[:, :, :, owned, : 2 * owned].reshape(-1, 2, owned)
    gains_all = gains_all.astype(jnp.float32).swapaxes(0, 1).reshape(2, width)
    gain_one, gain_two = gains_all[0], gains_all[1]
    w_gate = gather_line(gate_rows.reshape(8 * owned, 2 * part_hidden))

    normed_all, _ = norm_parts(tokens_all.reshape(together, width).astype(jnp.float32))
    input_one = (normed_all * gain_one).astype(low)
    qkv = dot_nn(input_one, w_in)
    orders = block_order.reshape(2 * splits if spread > 1 else 1, 4, -1)
    slot_order = jnp.concatenate(
        [
            orders[(2 * s + (beside ^ i)) if spread > 1 else 0, part_owner(mine ^ j)]
            for s in range(splits)
            for i in range(2 // seqs)
            for j in range(4)
        ]
    )
    tables = position_tables(slot_order.shape[0], length // slot_order.shape[0])
    groups = [
        [2 * (s * splits + g) + half for g in range(splits)]
        for s in range(slow // splits)
        for half in (0, 1)
    ]

    def split_heads(values, widths, copies):
        parts = []
        start = 0
        for each, repeat in zip(widths, copies):
            kinds = splits // repeat
            piece = values[:, start : start + kinds * each].reshape(-1, kinds, each)
            parts.append(jnp.repeat(piece.swapaxes(0, 1), repeat, axis=0))
            start += kinds * each
        sent = jnp.concatenate(parts, 2)
        got = lax.all_to_all(sent, "ctx", 0, 0, axis_index_groups=groups, tiled=True)
        return got.reshape(length, -1)

    def join_heads(values):
        sent = values.reshape(splits, together, -1)
        return lax.all_to_all(sent, "ctx", 0, 0, axis_index_groups=groups, tiled=True)

    q_width, k_width = q_heads * HEAD, kv_heads * HEAD
    if splits > 1:
        qkv = split_heads(qkv, (q_width, k_width, k_width), (1, splits, splits))
    qkv = qkv.reshape(seqs, length, -1)
    blocks = slot_order.shape[0]
    slot_where = jnp.sum(
        jnp.where(
            slot_order[None, :] == jnp.arange(blocks, dtype=jnp.int32)[:, None],
            jnp.arange(blocks, dtype=jnp.int32)[None, :],
            0,
        ),
        1,
    )
    attended, lse, kept = attend(slot_order, slot_where, qkv, tables, q_heads, kv_heads)
    if splits > 1:
        attended = join_heads(attended.reshape(length, q_width)).swapaxes(0, 1)
    attended = attended.reshape(together, part_q)

    def parts(values):
        return values.astype(low).reshape((2, 4) + tokens.shape)

    residual_rows, input_two = turn(
        parts(dot_nn(attended, w_out)), gain_two[None], [tokens_all[0, 0]], slow, False, 3
    )
    input_two = input_two.reshape(together, width)
    after = 0.0 * (residual_rows[0, 0, 0] + w_gate[0, 0].astype(jnp.float32))
    w_down = gather_line((down_matrix + after).astype(low))
    gate_both = dot_nn(input_two, w_gate)
    gate_part = gate_both[:, :part_hidden]
    up_part = gate_both[:, part_hidden:]
    sigmoid_gate = jax.nn.sigmoid(gate_part)
    active = gate_part * sigmoid_gate
    hidden = lax.optimization_barrier((active * up_part).astype(low))
    back_all = spread_tokens(cotangent + 0.0 * hidden[0, 0], spread, 2)
    cot_rows = back_all[0, 0]
    back_all = back_all.reshape(together, width)
    grad_down = lax.optimization_barrier(dot_tn(hidden, back_all).astype(low))
    down_sum = sum_line(grad_down + 0.0 * w_down[0, 0]).astype(jnp.float32)
    back_hidden = dot_nt(back_all, w_down + 0.0 * hidden[0, 0])
    back_gate = back_hidden * up_part * sigmoid_gate * (1.0 + gate_part * (1.0 - sigmoid_gate))
    back_upper = back_hidden * active
    back_gate_up = jnp.concatenate([back_gate, back_upper], 1).astype(low)
    gate_low = sum_line(dot_tn(input_two, back_gate_up).astype(low))
    back_rows, grad_gain_two, back_residual_all = turn(
        parts(dot_nt(back_gate_up, w_gate)),
        gain_two[None],
        [residual_rows, cot_rows],
        slow,
        True,
        4,
    )
    back_residual_all = back_residual_all.reshape(together, width)
    grad_out = dot_tn(attended, back_residual_all).astype(low)
    back_attended = dot_nt(back_residual_all, w_out).astype(low)
    if splits > 1:
        back_attended = split_heads(back_attended, (q_width,), (1,))
    back_projected, output_rows = attend_back(
        slot_order,
        slot_where,
        kept,
        back_attended.reshape(seqs, length, -1),
        lse,
        tables,
        parts(dot_nn(hidden, w_down)),
        residual_rows,
        q_heads,
        kv_heads,
        6,
    )
    if splits > 1:
        back_projected = join_heads(back_projected.reshape(length, -1)).astype(jnp.float32)
        back_projected = jnp.concatenate(
            [
                back_projected[..., :q_width].swapaxes(0, 1).reshape(together, part_q),
                back_projected[..., q_width:].sum(0),
            ],
            1,
        ).astype(low)
    back_projected = back_projected.reshape(together, part_cols)
    grad_in = dot_tn(input_one, back_projected).astype(low)
    grad_in = grad_in.reshape(4, slow, 2 * owned, part_cols).swapaxes(0, 1)
    in_sum, out_sum, gate_sum, gains_sum, tokens_grad, block_out = last_sums(
        grad_in.reshape(slow, 8, owned, part_cols),
        grad_out.reshape(slow, owned, width),
        gate_low.reshape(8, owned, 2 * part_hidden),
        parts(dot_nt(back_projected, w_in)),
        output_rows,
        [gain_one[None], grad_gain_two, tokens_all[0, 0], back_rows],
        shards,
        spread,
        5,
    )
    tokens_grad = tokens_grad.astype(jnp.float32)
    out_sum = out_sum.astype(jnp.float32)
    gains_sum = gains_sum[:, 0, : 2 * owned].reshape(8, 2, owned).sum(0)
    cuts = ((0, part_q), (part_q, part_q + part_k), (part_q + part_k, part_cols))
    in_sum = jnp.concatenate(
        [in_sum[i, :, first:last] for first, last in cuts for i in range(8)], 1
    ).astype(jnp.float32)
    new_in = adam_update(
        attention_in,
        in_sum,
        mean_attention_in,
        square_attention_in,
        input_boost * D ** (-0.5),
        weight_decay,
    )
    new_out = adam_update(
        attention_out,
        out_sum,
        mean_attention_out,
        square_attention_out,
        (HEADS * HEAD // 32) ** (-0.5),
        weight_decay,
    )
    new_gate = gate_update(
        gate_sum, gate_up, mean_gate_up, square_gate_up, slow, D ** (-0.5)
    )
    new_down = adam_update(
        down_matrix, down_sum, mean_down, square_down, FF ** (-0.5), weight_decay
    )
    new_gain = adam_update(gains, gains_sum, mean_gains, square_gains, gain_rate, 0.0)
    return (
        block_out,
        tokens_grad,
        new_in[0],
        new_in[1],
        new_in[2],
        new_out[0],
        new_out[1],
        new_out[2],
        new_gate[0],
        new_gate[1],
        new_gate[2],
        new_down[0],
        new_down[1],
        new_down[2],
        new_gain[0],
        new_gain[1],
        new_gain[2],
    )


def solution(mesh):
    in_specs = (
        P("dp", "ctx", None),
        P("dp", "ctx", None),
        P(),
        P(("dp", "ctx"), None),
        P(("dp", "ctx"), None),
        P(("dp", "ctx"), None),
        P(("dp", "ctx"), None),
        P(None, ("dp", "ctx")),
        P(("dp", "ctx"), None),
        P(("dp", "ctx"), None),
        P(("dp", "ctx"), None),
        P(("dp", "ctx"), None),
        P(None, ("dp", "ctx")),
        P(("dp", "ctx"), None),
        P(("dp", "ctx"), None),
        P(("dp", "ctx"), None),
        P(("dp", "ctx"), None),
        P(None, ("dp", "ctx")),
    )
    out_specs = (
        P("dp", "ctx", None),
        P("dp", "ctx", None),
        P(("dp", "ctx"), None),
        P(("dp", "ctx"), None),
        P(("dp", "ctx"), None),
        P(("dp", "ctx"), None),
        P(("dp", "ctx"), None),
        P(("dp", "ctx"), None),
        P(("dp", "ctx"), None),
        P(("dp", "ctx"), None),
        P(("dp", "ctx"), None),
        P(("dp", "ctx"), None),
        P(("dp", "ctx"), None),
        P(("dp", "ctx"), None),
        P(None, ("dp", "ctx")),
        P(None, ("dp", "ctx")),
        P(None, ("dp", "ctx")),
    )
    return jax.shard_map(local, mesh=mesh, in_specs=in_specs, out_specs=out_specs, check_vma=False)
```

```python
import functools

import jax
import jax.numpy as jnp
import numpy as np
from jax import lax
from jax.experimental import pallas as pl
from jax.experimental.pallas import tpu as pltpu
from jax.sharding import PartitionSpec as P

D = 2048
HEADS = 32
KV_HEADS = 8
HEAD = 64
FF = 8192
STEP = 5


norm_eps = 1e-05
rope_base = 500000.0
beta_one = 0.9
beta_two = 0.95
gain_rate = 1.25
input_boost = 2.5
weight_decay = 0.1
adam_eps = 1e-08
masked_score = -1e30


def norm_parts(values):
    factor = lax.rsqrt(jnp.mean(values * values, -1, keepdims=True) + norm_eps)
    return (values * factor, factor)


def norm_back(back_normed, normed, factor):
    return factor * (back_normed - normed * jnp.mean(back_normed * normed, -1, keepdims=True))


def adam_update(weight, gradient, first_moment, second_moment, step_rate, decay_rate):
    first_new = beta_one * first_moment + (1.0 - beta_one) * gradient
    second_new = beta_two * second_moment + (1.0 - beta_two) * gradient * gradient
    update = (
        first_new
        / (1.0 - beta_one**STEP)
        / (jnp.sqrt(second_new / (1.0 - beta_two**STEP)) + adam_eps)
    )
    return (first_new, second_new, weight - step_rate * (update + decay_rate * weight))


def line_groups(shards):
    return [[2 * s + half for s in range(shards // 2)] for half in (0, 1)]


def gather_line(rows):
    return lax.all_gather(
        rows, "ctx", axis=0, tiled=True, axis_index_groups=line_groups(lax.axis_size("ctx"))
    )


def sum_line(gradient):
    return lax.psum_scatter(
        gradient,
        "ctx",
        scatter_dimension=0,
        tiled=True,
        axis_index_groups=line_groups(lax.axis_size("ctx")),
    )


def dot_nn(a, b):
    return lax.dot_general(a, b, (((1,), (0,)), ((), ())), preferred_element_type=jnp.float32)


def dot_nt(a, b):
    return lax.dot_general(a, b, (((1,), (1,)), ((), ())), preferred_element_type=jnp.float32)


def dot_tn(a, b):
    return lax.dot_general(a, b, (((0,), (0,)), ((), ())), preferred_element_type=jnp.float32)


def causal_keep(tile):
    keys = lax.broadcasted_iota(jnp.int32, (tile, tile), 0)
    queries = lax.broadcasted_iota(jnp.int32, (tile, tile), 1)
    return keys <= queries


def turn_group(values, cos, sin, forward):
    lanes = lax.broadcasted_iota(jnp.int32, values.shape, 1)
    other = jnp.where(
        lanes % HEAD < HEAD // 2,
        pltpu.roll(values, 2 * HEAD - HEAD // 2, 1),
        pltpu.roll(values, HEAD // 2, 1),
    )
    if forward:
        return values * cos + other * sin
    return values * cos - other * sin


def turn_columns(values, start, turned_cols, cos, sin, forward):
    if start >= turned_cols:
        return values
    turned = turn_group(values, cos, sin, forward)
    if start + 2 * HEAD <= turned_cols:
        return turned
    lanes = lax.broadcasted_iota(jnp.int32, values.shape, 1)
    return jnp.where(lanes < turned_cols - start, turned, values)


def attend_kernel(
    q_heads,
    kv_heads,
    tile,
    order_ref,
    where_ref,
    all_qkv_ref,
    cos_ref,
    sin_ref,
    all_out_ref,
    all_lse_ref,
    all_kept_ref,
    made,
):
    for sequence in range(all_qkv_ref.shape[0]):
        attend_sequence(
            q_heads,
            kv_heads,
            tile,
            order_ref,
            where_ref,
            all_qkv_ref.at[sequence],
            cos_ref,
            sin_ref,
            all_out_ref.at[sequence],
            all_lse_ref.at[sequence],
            all_kept_ref.at[sequence],
            made,
        )


def attend_sequence(
    q_heads,
    kv_heads,
    tile,
    order_ref,
    where_ref,
    qkv_ref,
    cos_ref,
    sin_ref,
    out_ref,
    lse_ref,
    kept_ref,
    made,
):
    blocks, rows, cols = qkv_ref.shape
    length = blocks * rows
    group = q_heads // kv_heads
    q_cols, k_cols = q_heads * HEAD, kv_heads * HEAD
    scale = HEAD ** (-0.5)

    def take_block(i, _):
        start = pl.multiple_of(i * rows, rows)
        cos = cos_ref[i]
        sin = sin_ref[i]
        for c in range(0, cols, 2 * HEAD):
            values = qkv_ref[where_ref[i], :, c : c + 2 * HEAD]
            values = turn_columns(values, c, q_cols + k_cols, cos, sin, True)
            kept_ref[pl.ds(start, rows), c : c + 2 * HEAD] = values.astype(jnp.bfloat16)
        return 0

    lax.fori_loop(0, blocks, take_block, 0)
    keep = causal_keep(tile)
    for kv in range(kv_heads):
        k_at = q_cols + kv * HEAD
        v_at = q_cols + k_cols + kv * HEAD

        def query_step(i, _):
            q_start = pl.multiple_of(i * tile, tile)
            queries = [
                kept_ref[
                    pl.ds(q_start, tile), (kv * group + g) * HEAD : (kv * group + g + 1) * HEAD
                ]
                for g in range(group)
            ]

            def key_tile(j, carry, masked):
                k_start = pl.multiple_of(j * tile, tile)
                keys = kept_ref[pl.ds(k_start, tile), k_at : k_at + HEAD]
                values = kept_ref[pl.ds(k_start, tile), v_at : v_at + HEAD]
                result = []
                for g in range(group):
                    peak, total, weighted = carry[g]
                    scores = dot_nt(keys, queries[g]) * scale
                    if masked:
                        scores = jnp.where(keep, scores, masked_score)
                    new_peak = jnp.maximum(peak, jnp.max(scores, 0, keepdims=True))
                    weights = jnp.exp(scores - new_peak)
                    shrink = jnp.exp(peak - new_peak)
                    total = total * shrink + jnp.sum(weights, 0, keepdims=True)
                    weighted = weighted * shrink + dot_tn(values, weights.astype(jnp.bfloat16))
                    result.append((new_peak, total, weighted))
                return tuple(result)

            start = tuple(
                (
                    jnp.full((1, tile), masked_score, jnp.float32),
                    jnp.zeros((1, tile), jnp.float32),
                    jnp.zeros((HEAD, tile), jnp.float32),
                )
                for _ in range(group)
            )
            carry = lax.fori_loop(0, i, lambda j, c: key_tile(j, c, False), start)
            carry = key_tile(i, carry, True)
            for g in range(group):
                head = kv * group + g
                peak, total, weighted = carry[g]
                lse_ref[head : head + 1, pl.ds(q_start, tile)] = peak + jnp.log(total)
                made[pl.ds(i * (tile // rows), tile // rows), :, head * HEAD : (head + 1) * HEAD] = (
                    (weighted / total).T.astype(jnp.bfloat16).reshape(-1, rows, HEAD)
                )
            return 0

        lax.fori_loop(0, length // tile, query_step, 0)

    def give_block(i, _):
        out_ref[i] = made[order_ref[i]]
        return 0

    lax.fori_loop(0, blocks, give_block, 0)


def attend_back_kernel(
    q_heads,
    kv_heads,
    tile,
    steps,
    order_ref,
    where_ref,
    all_kept_ref,
    all_back_ref,
    all_lse_ref,
    cos_ref,
    sin_ref,
    out_rows,
    residual,
    out_parts,
    all_out_ref,
    block_out,
    out_sum,
    *scratch,
):
    me = (lax.axis_index("dp"), lax.axis_index("ctx"))
    slow = out_parts.shape[0]
    line = [(me[0], me[1] ^ (2 * by)) for by in range(1, slow)]
    greet(me, [member(me, by) for by in (1, 2, 4)] + line, [])
    work, line_out, scratch = scratch[:4], scratch[4:8], scratch[8:]
    scatter = GroupScatter(me, out_rows, scratch[:7], scratch[7:], steps)
    out_line = LineSum(me, slow, out_parts, line_out[:2], line_out[2:])

    def one():
        for k in range(steps):
            scatter.send_first(k)

    def two():
        for k in range(steps):
            scatter.send_second(k)

    def three():
        for k in range(steps):
            span = scatter.window(k)
            for part in (0, 1):
                value = residual[part, span] + scatter.total(k, part)
                block_out[part, span] = value.astype(jnp.bfloat16)

    tasks = [one, two, three]

    def pause():
        if tasks:
            tasks.pop(0)()

    scatter.start()
    out_line.start()
    for sequence in range(all_kept_ref.shape[0]):
        attend_back_sequence(
            q_heads,
            kv_heads,
            tile,
            pause,
            order_ref,
            where_ref,
            all_kept_ref.at[sequence],
            all_back_ref.at[sequence],
            all_lse_ref.at[sequence],
            cos_ref,
            sin_ref,
            all_out_ref.at[sequence],
            *work,
        )
    while tasks:
        pause()
    out_sum[...] = out_line.total().astype(jnp.bfloat16)
    out_line.finish()
    scatter.finish()


def attend_back_sequence(
    q_heads,
    kv_heads,
    tile,
    pause,
    order_ref,
    where_ref,
    kept_ref,
    back_ref,
    lse_ref,
    cos_ref,
    sin_ref,
    out_ref,
    back_sorted,
    grad,
    delta_ref,
    dq_ref,
):
    length, cols = kept_ref.shape
    blocks, rows = back_ref.shape[:2]
    group = q_heads // kv_heads
    q_cols, k_cols = q_heads * HEAD, kv_heads * HEAD
    scale = HEAD ** (-0.5)
    tiles = length // tile

    def take_block(i, _):
        start = pl.multiple_of(i * rows, rows)
        back_sorted[pl.ds(start, rows), :] = back_ref[where_ref[i]]
        return 0

    lax.fori_loop(0, blocks, take_block, 0)
    keep = causal_keep(tile)
    for kv in range(kv_heads):
        k_at = q_cols + kv * HEAD
        v_at = q_cols + k_cols + kv * HEAD

        def load(i, g):
            start = pl.multiple_of(i * tile, tile)
            head = kv * group + g
            at = slice(head * HEAD, (head + 1) * HEAD)
            return (
                kept_ref[pl.ds(start, tile), at],
                back_sorted[pl.ds(start, tile), at],
                lse_ref[head : head + 1, pl.ds(start, tile)],
            )

        def load_kv(j):
            start = pl.multiple_of(j * tile, tile)
            return (
                kept_ref[pl.ds(start, tile), k_at : k_at + HEAD],
                kept_ref[pl.ds(start, tile), v_at : v_at + HEAD],
            )

        def tile_terms(keys, values, query, back, lse, masked):
            weights = jnp.exp(dot_nt(keys, query) * scale - lse)
            if masked:
                weights = jnp.where(keep, weights, 0.0)
            return weights, dot_nt(values, back)

        def delta_step(i, _):
            rows_i = [load(i, g) for g in range(group)]

            def one(j, carry, masked):
                keys, values = load_kv(j)
                result = []
                for g in range(group):
                    weights, back_weights = tile_terms(keys, values, *rows_i[g], masked)
                    result.append(carry[g] + jnp.sum(weights * back_weights, 0, keepdims=True))
                return tuple(result)

            carry = tuple(jnp.zeros((1, tile), jnp.float32) for _ in range(group))
            carry = lax.fori_loop(0, i, lambda j, c: one(j, c, False), carry)
            carry = one(i, carry, True)
            for g in range(group):
                delta_ref[g : g + 1, pl.ds(pl.multiple_of(i * tile, tile), tile)] = carry[g]
            return 0

        lax.fori_loop(0, tiles, delta_step, 0)
        if kv == 0:
            pause()
        dq_ref[...] = jnp.zeros_like(dq_ref)

        def key_step(j, _):
            keys, values = load_kv(j)

            def one(i, carry, masked):
                back_key, back_value = carry
                start = pl.multiple_of(i * tile, tile)
                for g in range(group):
                    query, back, lse = load(i, g)
                    weights, back_weights = tile_terms(keys, values, query, back, lse, masked)
                    delta = delta_ref[g : g + 1, pl.ds(start, tile)]
                    back_scores = (weights * (back_weights - delta)).astype(jnp.bfloat16)
                    back_key = back_key + dot_nn(back_scores, query)
                    back_value = back_value + dot_nn(weights.astype(jnp.bfloat16), back)
                    dq_ref[g * HEAD : (g + 1) * HEAD, pl.ds(start, tile)] += dot_tn(
                        keys, back_scores
                    )
                return back_key, back_value

            zero = jnp.zeros((tile, HEAD), jnp.float32)
            carry = one(j, (zero, zero), True)
            carry = lax.fori_loop(j + 1, tiles, lambda i, c: one(i, c, False), carry)
            span = pl.ds(j * (tile // rows), tile // rows)
            grad[span, :, k_at : k_at + HEAD] = (carry[0] * scale).reshape(-1, rows, HEAD)
            grad[span, :, v_at : v_at + HEAD] = carry[1].reshape(-1, rows, HEAD)
            return 0

        lax.fori_loop(0, tiles, key_step, 0)
        for g in range(group):
            head = kv * group + g
            turned = (dq_ref[g * HEAD : (g + 1) * HEAD, :] * scale).T
            grad[:, :, head * HEAD : (head + 1) * HEAD] = turned.reshape(-1, rows, HEAD)

    def give_block(i, _):
        cos = cos_ref[order_ref[i]]
        sin = sin_ref[order_ref[i]]
        for c in range(0, cols, 2 * HEAD):
            values = grad[order_ref[i], :, c : c + 2 * HEAD]
            values = turn_columns(values, c, q_cols + k_cols, cos, sin, False)
            out_ref[i, :, c : c + 2 * HEAD] = values.astype(jnp.bfloat16)
        return 0

    lax.fori_loop(0, blocks, give_block, 0)


MESH = pl.DeviceIdType.MESH


def part_owner(part):
    return part % 2 * 2 + part // 2


def sequence_target(group, place, second, splits):
    part = place // 2
    target = (part_owner(part % 4), (2 * group + second) * splits + part // 4)
    return target, place % 2


def token_target(group, place, half, splits):
    sequence = place // splits
    part = part_owner(group) + 4 * (place % splits)
    return (sequence // 2, 2 * part + half), sequence % 2


def remote(source, target, sems, device):
    return pltpu.make_async_remote_copy(
        src_ref=source,
        dst_ref=target,
        send_sem=sems[0],
        recv_sem=sems[1],
        device_id=device,
        device_id_type=MESH,
    )


def same(one, other):
    return jnp.logical_and(one[0] == other[0], one[1] == other[1])


def greet(me, peers, movers):
    barrier = pltpu.get_barrier_semaphore()
    for peer in peers:
        pl.semaphore_signal(barrier, inc=1, device_id=peer, device_id_type=MESH)
    expected = len(peers)
    for source, target in movers:

        @pl.when(jnp.logical_not(same(source, me)))
        def _():
            pl.semaphore_signal(barrier, inc=1, device_id=source, device_id_type=MESH)

        expected = expected + jnp.where(same(target, me), 0, 1)
    pl.semaphore_wait(barrier, expected)


def move_start(me, source, target, target_device, send, receive):
    here = same(target_device, me)

    @pl.when(here)
    def _():
        pltpu.make_async_copy(source, target, receive).start()

    @pl.when(jnp.logical_not(here))
    def _():
        remote(source, target, (send, receive), target_device).start()


def move_sent(me, source, target, target_device, send, receive):
    @pl.when(jnp.logical_not(same(target_device, me)))
    def _():
        remote(source, target, (send, receive), target_device).wait_send()


def member(me, by):
    return (me[0] ^ (by // 2), me[1] ^ (by % 2))


def group_index(device):
    return 2 * device[0] + device[1] % 2


class GroupExchange:
    def __init__(self, me, pieces, got, sems):
        self.me, self.pieces, self.got, self.sems = me, pieces, got, sems

    def hop(self, by):
        peer = member(self.me, by)
        sems = (self.sems.at[0, by - 1], self.sems.at[1, by - 1])
        return remote(
            self.pieces.at[group_index(peer)], self.got.at[group_index(self.me)], sems, peer
        )

    def own(self):
        mine = group_index(self.me)
        return pltpu.make_async_copy(self.pieces.at[mine], self.got.at[mine], self.sems.at[0, 7])

    def start(self):
        for by in range(1, 8):
            self.hop(by).start()
        self.own().start()

    def finish(self):
        self.own().wait()
        for by in range(1, 8):
            self.hop(by).wait()


class GroupGather:
    def __init__(self, me, rows, sems, own, window):
        self.rows, self.sems, self.own, self.window = rows, sems, own, window
        self.core, self.across, self.beside = member(me, 2), member(me, 4), member(me, 1)

    def hop(self, index):
        across, beside, core = self.across, self.beside, self.core
        source, i, j, half, device = (
            (None, 0, 2, 0, across),
            (None, 1, 0, 1, beside),
            (None, 1, 0, 0, beside),
            (None, 0, 2, 1, across),
            ((0, 2), 1, 2, 0, beside),
            ((1, 0), 1, 2, 1, across),
            (None, 0, 1, slice(0, 2), core),
            ((0, 2), 0, 3, slice(0, 2), core),
            ((1, 0), 1, 1, slice(0, 2), core),
            ((1, 2), 1, 3, slice(0, 2), core),
        )[index]
        if source is None:
            source = self.own.at[half, self.window]
        else:
            source = self.rows.at[source[0], source[1], half, self.window]
        target = self.rows.at[i, j, half, self.window]
        return remote(source, target, (self.sems.at[0, index], self.sems.at[1, index]), device)

    def start(self):
        for index in (0, 1, 2, 3, 6):
            self.hop(index).start()

    def pass_on(self):
        self.hop(0).wait_recv()
        self.hop(4).start()
        self.hop(1).wait_recv()
        self.hop(5).start()
        self.hop(3).wait_recv()
        self.hop(7).start()
        self.hop(2).wait_recv()
        self.hop(8).start()

    def finish(self):
        self.hop(4).wait_recv()
        self.hop(5).wait_recv()
        self.hop(9).start()
        for index in (6, 7, 8, 9):
            self.hop(index).wait_recv()
        for index in range(10):
            self.hop(index).wait_send()


class Moves:
    def __init__(self, me, splits, source, target, sems, back):
        self.me, self.splits, self.source, self.target = me, splits, source, target
        self.sems, self.back = sems, back

    def one(self, i):
        find = token_target if self.back else sequence_target
        device, place = find(self.me[0], self.me[1], i, self.splits)
        return (
            self.me,
            self.source.at[i],
            self.target.at[place],
            device,
            self.sems.at[0, i],
            self.sems.at[1, place],
        )

    def start(self):
        for i in (0, 1):
            move_start(*self.one(i))

    def wait_recv(self):
        for i in (0, 1):
            pltpu.make_async_copy(self.source.at[0], self.target.at[i], self.sems.at[1, i]).wait()

    def finish(self):
        for i in (0, 1):
            move_sent(*self.one(i))


def movers_of(me, splits, back):
    into = [sequence_target(me[0], me[1], i, splits)[0] for i in (0, 1)]
    home = [token_target(me[0], me[1], i, splits)[0] for i in (0, 1)]
    return list(zip(into, home)) if back else list(zip(home, into))


def first_kernel(shards, splits, tokens, pieces, out_own, gate_pieces, *refs):
    rows, in_all, out_all, gate_rows, held = refs[:5]
    move_sems, group_sems, piece_sems, gate_sems, own_sem, in_sems, out_sems = refs[5:]
    me = (lax.axis_index("dp"), lax.axis_index("ctx"))
    group, place = me
    slow = shards // 2
    slot = place // 2
    line = [(group, place ^ (2 * by)) for by in range(1, slow)]
    wanted, block = place // slow, place % slow
    takers = [(group, 2 * (slot ^ by) + wanted) for by in range(slow)]
    givers = [(group, place % 2 * slow + block_by) for block_by in range(slow)]
    movers = movers_of(me, splits, False) + list(zip(givers, takers))
    greet(me, [member(me, by) for by in range(1, 8)] + line, movers)
    swap = GroupExchange(me, pieces, held, piece_sems)
    gate_swap = GroupExchange(me, gate_pieces, gate_rows, gate_sems)
    move = Moves(me, splits, tokens, rows.at[0, 0], move_sems, False)

    def in_line(by):
        sems = (in_sems.at[0, by - 1], in_sems.at[1, by - 1])
        return remote(held, in_all.at[slot], sems, line[by - 1])

    def out_send(by):
        return (
            me,
            out_own,
            out_all.at[block],
            takers[by],
            out_sems.at[0, by],
            out_sems.at[1, block],
        )

    own = pltpu.make_async_copy(held, in_all.at[slot], own_sem)
    move.start()
    swap.start()
    gate_swap.start()
    swap.finish()
    move.wait_recv()
    spread = GroupGather(me, rows, group_sems, rows.at[0, 0], slice(0, tokens.shape[1]))
    spread.start()
    for by in range(1, slow):
        in_line(by).start()
    own.start()
    for by in range(slow):
        move_start(*out_send(by))
    spread.pass_on()
    for by in range(1, slow):
        in_line(by).wait()
    spread.finish()
    own.wait()
    for by in range(slow):
        pltpu.make_async_copy(out_own, out_all.at[by], out_sems.at[1, by]).wait()
    for by in range(slow):
        move_sent(*out_send(by))
    gate_swap.finish()
    move.finish()


def first_exchange(tokens, pieces, out_own, gate_pieces, shards, splits, identity):
    low = jnp.bfloat16
    slow = shards // 2
    any_space = pl.BlockSpec(memory_space=pl.ANY)
    dma = pltpu.SemaphoreType.DMA
    made = pl.pallas_call(
        functools.partial(first_kernel, shards, splits),
        out_shape=(
            jax.ShapeDtypeStruct((2, 4) + tokens.shape, low),
            jax.ShapeDtypeStruct((slow,) + pieces.shape, low),
            jax.ShapeDtypeStruct((slow,) + out_own.shape, low),
            jax.ShapeDtypeStruct(gate_pieces.shape, low),
            jax.ShapeDtypeStruct(pieces.shape, low),
        ),
        in_specs=[any_space] * 4,
        out_specs=(any_space,) * 5,
        scratch_shapes=[
            dma((2, 2)),
            dma((2, 10)),
            dma((2, 8)),
            dma((2, 8)),
            dma,
            dma((2, slow - 1)),
            dma((2, slow)),
        ],
        compiler_params=pltpu.CompilerParams(
            collective_id=identity, has_side_effects=True, vmem_limit_bytes=8 << 20
        ),
        cost_estimate=pl.CostEstimate(flops=0, bytes_accessed=200 << 20, transcendentals=0),
    )(tokens, pieces, out_own, gate_pieces)
    return made[:4]


class GroupScatter:
    def __init__(self, me, parts, buffers, sems, steps):
        self.parts = parts
        self.core_in, self.kept, self.sent, self.came, self.held = buffers[:5]
        self.sent_last, self.came_last = buffers[5:]
        self.core_sems, self.kept_sems, self.one_sems, self.last_sems = sems
        self.core, self.across, self.beside = member(me, 2), member(me, 4), member(me, 1)
        self.size = parts.shape[3] // steps
        self.steps = steps

    def window(self, k):
        return slice(k * self.size, (k + 1) * self.size)

    def to_core(self, k, j):
        return remote(
            self.parts.at[:, 2 * j + 1, :, self.window(k)],
            self.core_in.at[:, j, :, self.window(k)],
            (self.core_sems.at[0, k, j], self.core_sems.at[1, k, j]),
            self.core,
        )

    def keep(self, k, j):
        return pltpu.make_async_copy(
            self.parts.at[:, 2 * j, :, self.window(k)],
            self.kept.at[:, j, :, self.window(k)],
            self.kept_sems.at[k, j],
        )

    def first(self, k, half):
        return remote(
            self.sent.at[half, :, self.window(k)],
            self.came.at[half, :, self.window(k)],
            (self.one_sems.at[0, k, half], self.one_sems.at[1, k, half]),
            (self.beside, self.across)[half],
        )

    def second(self, k, half):
        return remote(
            self.sent_last.at[half, self.window(k)],
            self.came_last.at[half, self.window(k)],
            (self.last_sems.at[0, k, half], self.last_sems.at[1, k, half]),
            (self.across, self.beside)[half],
        )

    def start(self):
        for k in range(self.steps):
            for j in (0, 1):
                self.to_core(k, j).start()
                self.keep(k, j).start()

    def send_first(self, k):
        wide = jnp.float32
        rows = self.window(k)
        for j in (0, 1):
            self.keep(k, j).wait()
            self.to_core(k, j).wait_recv()
        for half in (0, 1):
            for other in (0, 1):
                at = (1, other) if half == 0 else (other, 1)
                both = self.kept[at[0], at[1], half, rows].astype(wide)
                both = both + self.core_in[at[0], at[1], half, rows].astype(wide)
                self.sent[half, other, rows] = both.astype(jnp.bfloat16)
            self.first(k, half).start()
        for half in (0, 1):
            for other in (0, 1):
                at = (0, other) if half == 0 else (other, 0)
                both = self.kept[at[0], at[1], half, rows].astype(wide)
                self.held[half, other, rows] = both + self.core_in[at[0], at[1], half, rows].astype(
                    wide
                )

    def send_second(self, k):
        wide = jnp.float32
        rows = self.window(k)
        for half in (0, 1):
            self.first(k, half).wait_recv()
            both = self.held[half, 1, rows] + self.came[half, 1, rows].astype(wide)
            self.sent_last[half, rows] = both.astype(jnp.bfloat16)
            self.second(k, half).start()
            self.held[half, 0, rows] = self.held[half, 0, rows] + self.came[half, 0, rows].astype(
                wide
            )

    def total(self, k, half):
        self.second(k, half).wait_recv()
        rows = self.window(k)
        return self.held[half, 0, rows] + self.came_last[half, rows].astype(jnp.float32)

    def finish(self):
        for k in range(self.steps):
            for j in (0, 1):
                self.to_core(k, j).wait_send()
            for half in (0, 1):
                self.first(k, half).wait_send()
                self.second(k, half).wait_send()


def scatter_scratch(rows, width, steps):
    low, wide = jnp.bfloat16, jnp.float32
    dma = pltpu.SemaphoreType.DMA
    return [
        pltpu.VMEM((2, 2, 2, rows, width), low),
        pltpu.VMEM((2, 2, 2, rows, width), low),
        pltpu.VMEM((2, 2, rows, width), low),
        pltpu.VMEM((2, 2, rows, width), low),
        pltpu.VMEM((2, 2, rows, width), wide),
        pltpu.VMEM((2, rows, width), low),
        pltpu.VMEM((2, rows, width), low),
        dma((2, steps, 2)),
        dma((steps, 2)),
        dma((2, steps, 2)),
        dma((2, steps, 2)),
    ]


def reordered(rows, slow, back):
    each = rows.shape[1] // (4 * slow)
    if back:
        starts = [s * 4 + dp for dp in range(4) for s in range(slow)]
    else:
        starts = [dp * slow + s for s in range(slow) for dp in range(4)]
    return jnp.concatenate([rows[:, i * each : (i + 1) * each] for i in starts], 1)


def turn_kernel(slow, steps, backward, parts, gain, *refs):
    if backward:
        residual, cot, result, gain_grad, rows = refs[:5]
        scratch = refs[5:]
    else:
        tokens, result, rows = refs[:3]
        scratch = refs[3:]
    own, own_sems, group_sems = scratch[:3]
    me = (lax.axis_index("dp"), lax.axis_index("ctx"))
    greet(me, [member(me, by) for by in (1, 2, 4)], [])
    scatter = GroupScatter(me, parts, scratch[3:10], scratch[10:], steps)
    gathers = [GroupGather(me, rows, group_sems.at[k], own, scatter.window(k)) for k in range(steps)]
    scatter.start()
    for k in range(steps):
        scatter.send_first(k)
    for k in range(steps):
        scatter.send_second(k)
    for k in range(steps):
        span = scatter.window(k)
        for half in (0, 1):
            total = scatter.total(k, half)
            if backward:
                values = residual[half, span]
                factor = lax.rsqrt(jnp.mean(values * values, -1, keepdims=True) + norm_eps)
                normed = values * factor
                total = reordered(total, slow, True)
                part = jnp.sum(total * normed, 0, keepdims=True)
                if k == 0 and half == 0:
                    gain_grad[...] = part
                else:
                    gain_grad[...] += part
                back = total * gain[...]
                back = factor * (back - normed * jnp.mean(back * normed, -1, keepdims=True))
                back = cot[half, span].astype(jnp.float32) + back
                result[half, span] = back
                own[half, span] = back.astype(jnp.bfloat16)
            else:
                values = tokens[half, span].astype(jnp.float32) + total
                factor = lax.rsqrt(jnp.mean(values * values, -1, keepdims=True) + norm_eps)
                result[half, span] = values
                own[half, span] = reordered(values * factor * gain[...], slow, False).astype(
                    jnp.bfloat16
                )
        gathers[k].start()
        keep = pltpu.make_async_copy(own.at[:, span], rows.at[0, 0, :, span], own_sems.at[k])
        keep.start()
    for k in range(steps):
        gathers[k].pass_on()
    for k in range(steps):
        gathers[k].finish()
        span = scatter.window(k)
        pltpu.make_async_copy(own.at[:, span], rows.at[0, 0, :, span], own_sems.at[k]).wait()
    scatter.finish()


def turn(parts, gain, rows_in, slow, backward, identity):
    low, wide = jnp.bfloat16, jnp.float32
    dma = pltpu.SemaphoreType.DMA
    rows, width = parts.shape[3:]
    steps = 2
    any_space = pl.BlockSpec(memory_space=pl.ANY)
    vmem = pl.BlockSpec(memory_space=pltpu.VMEM)
    shapes = [jax.ShapeDtypeStruct((2, rows, width), wide)]
    if backward:
        shapes.append(jax.ShapeDtypeStruct((1, width), wide))
    return pl.pallas_call(
        functools.partial(turn_kernel, slow, steps, backward),
        out_shape=tuple(shapes) + (jax.ShapeDtypeStruct((2, 4, 2, rows, width), low),),
        in_specs=[any_space, vmem] + [vmem] * len(rows_in),
        out_specs=tuple([vmem] * len(shapes) + [any_space]),
        scratch_shapes=[
            pltpu.VMEM((2, rows, width), low),
            dma((steps,)),
            dma((steps, 2, 10)),
        ]
        + scatter_scratch(rows, width, steps),
        compiler_params=pltpu.CompilerParams(
            collective_id=identity, has_side_effects=True, vmem_limit_bytes=48 << 20
        ),
        cost_estimate=pl.CostEstimate(flops=0, bytes_accessed=250 << 20, transcendentals=0),
    )(parts, gain, *rows_in)


def move_kernel(splits, tokens, rows, move_sems):
    me = (lax.axis_index("dp"), lax.axis_index("ctx"))
    greet(me, [], movers_of(me, splits, False))
    move = Moves(me, splits, tokens, rows, move_sems, False)
    move.start()
    move.wait_recv()
    move.finish()


def move_tokens(tokens, splits, identity):
    any_space = pl.BlockSpec(memory_space=pl.ANY)
    return pl.pallas_call(
        functools.partial(move_kernel, splits),
        out_shape=jax.ShapeDtypeStruct(tokens.shape, tokens.dtype),
        in_specs=[any_space],
        out_specs=any_space,
        scratch_shapes=[pltpu.SemaphoreType.DMA((2, 2))],
        compiler_params=pltpu.CompilerParams(
            collective_id=identity, has_side_effects=True, vmem_limit_bytes=4 << 20
        ),
        cost_estimate=pl.CostEstimate(flops=0, bytes_accessed=40 << 20, transcendentals=0),
    )(tokens)


def spread_kernel(own, rows, group_sems, own_sem):
    me = (lax.axis_index("dp"), lax.axis_index("ctx"))
    greet(me, [member(me, by) for by in (1, 2, 4)], [])
    gather = GroupGather(me, rows, group_sems, own, slice(0, own.shape[1]))
    keep = pltpu.make_async_copy(own, rows.at[0, 0], own_sem)
    gather.start()
    keep.start()
    gather.pass_on()
    gather.finish()
    keep.wait()


def spread_group(own, identity):
    any_space = pl.BlockSpec(memory_space=pl.ANY)
    dma = pltpu.SemaphoreType.DMA
    return pl.pallas_call(
        spread_kernel,
        out_shape=jax.ShapeDtypeStruct((2, 4) + own.shape, own.dtype),
        in_specs=[any_space],
        out_specs=any_space,
        scratch_shapes=[dma((2, 10)), dma],
        compiler_params=pltpu.CompilerParams(
            collective_id=identity, has_side_effects=True, vmem_limit_bytes=4 << 20
        ),
        cost_estimate=pl.CostEstimate(flops=0, bytes_accessed=100 << 20, transcendentals=0),
    )(own)


class LineSum:
    def __init__(self, me, slow, parts, buffers, sems):
        self.parts = parts
        self.kept, self.arrived = buffers
        self.sems, self.own_sem = sems
        self.slot = me[1] // 2
        self.slow = slow
        self.line = [(me[0], me[1] ^ (2 * by)) for by in range(1, slow)]

    def hop(self, by):
        sems = (self.sems.at[0, by - 1], self.sems.at[1, by - 1])
        return remote(
            self.parts.at[self.slot ^ by], self.arrived.at[by - 1], sems, self.line[by - 1]
        )

    def own(self):
        return pltpu.make_async_copy(self.parts.at[self.slot], self.kept, self.own_sem)

    def start(self):
        for by in range(1, self.slow):
            self.hop(by).start()
        self.own().start()

    def total(self):
        self.own().wait()
        value = self.kept[...].astype(jnp.float32)
        for by in range(1, self.slow):
            self.hop(by).wait_recv()
            value = value + self.arrived[by - 1].astype(jnp.float32)
        return value

    def finish(self):
        for by in range(1, self.slow):
            self.hop(by).wait_send()


def line_scratch(shape, kind, slow):
    dma = pltpu.SemaphoreType.DMA
    return [
        pltpu.VMEM(shape, kind),
        pltpu.VMEM((slow - 1,) + shape, kind),
        dma((2, slow - 1)),
        dma,
    ]


def last_kernel(shards, splits, steps, in_parts, out_done, gate_parts, in_back, made_two, *refs):
    gain, gain_two_grad, tokens, back_rows = refs[:4]
    in_total, out_total, gate_total, gains_total, tokens_grad, block_out = refs[4:10]
    scratch = list(refs[10:])

    def take(count):
        taken = scratch[:count]
        del scratch[:count]
        return taken

    me = (lax.axis_index("dp"), lax.axis_index("ctx"))
    group, place = me
    slow = shards // 2
    slot, half = place // 2, place % 2
    owned = in_parts.shape[2]
    home = (group, half * slow + slot)
    movers = movers_of(me, splits, True)
    movers.append(((group, place % slow * 2 + place // slow), home))
    line = [(group, place ^ (2 * by)) for by in range(1, slow)]
    greet(me, [member(me, by) for by in range(1, 8)] + line, movers)
    one = take(11)
    back_sum = GroupScatter(me, in_back, one[:7], one[7:], steps)
    line_in = take(4)
    line_gains = take(4)
    in_done, gains_own, gains_done, made_one, gain_grad = take(5)
    in_sems, gate_sems, gains_sems, one_sems, two_sems, home_sems = take(6)
    in_line = LineSum(me, slow, in_parts, line_in[:2], line_in[2:])
    gains_line = LineSum(me, slow, gains_own, line_gains[:2], line_gains[2:])
    in_swap = GroupExchange(me, in_done, in_total, in_sems)
    gate_swap = GroupExchange(me, gate_parts, gate_total, gate_sems)
    gains_swap = GroupExchange(me, gains_done, gains_total, gains_sems)
    move_grad = Moves(me, splits, made_one, tokens_grad, one_sems, True)
    move_out = Moves(me, splits, made_two, block_out, two_sems, True)
    back_sum.start()
    to_home = (me, out_done, out_total, home, home_sems.at[0], home_sems.at[1])
    in_line.start()
    move_start(*to_home)
    move_out.start()
    for k in range(steps):
        back_sum.send_first(k)
    for k in range(steps):
        back_sum.send_second(k)
    for k in range(steps):
        span = back_sum.window(k)
        for part in (0, 1):
            total = back_sum.total(k, part)
            values = tokens[part, span].astype(jnp.float32)
            normed, factor = norm_parts(values)
            grad = jnp.sum(total * normed, 0, keepdims=True)
            if k == 0 and part == 0:
                gain_grad[...] = grad
            else:
                gain_grad[...] += grad
            value = back_rows[part, span] + norm_back(total * gain[...], normed, factor)
            made_one[part, span] = value.astype(jnp.bfloat16)
    move_grad.start()
    gains_own[...] = jnp.zeros_like(gains_own)
    for dp in range(4):
        for s in range(slow):
            for side in range(2):
                at = ((dp * slow + s) * 2 + side) * owned
                index = 2 * dp + side
                gains_own[s, index, 0:1, 0:owned] = gain_grad[:, at : at + owned]
                gains_own[s, index, 0:1, owned : 2 * owned] = gain_two_grad[:, at : at + owned]
    gains_line.start()
    gate_swap.start()
    in_done[...] = in_line.total().astype(jnp.bfloat16)
    in_swap.start()
    gains_done[...] = gains_line.total()
    gains_swap.start()
    pltpu.make_async_copy(out_done, out_total, home_sems.at[1]).wait()
    move_sent(*to_home)
    for swap in (in_swap, gate_swap, gains_swap):
        swap.finish()
    for move in (move_out, move_grad):
        move.wait_recv()
        move.finish()
    for part in (in_line, gains_line, back_sum):
        part.finish()


def last_sums(
    in_parts, out_done, gate_parts, in_back, out_rows, others, shards, splits, identity
):
    low, wide = jnp.bfloat16, jnp.float32
    slow = shards // 2
    steps = 2
    any_space = pl.BlockSpec(memory_space=pl.ANY)
    vmem = pl.BlockSpec(memory_space=pltpu.VMEM)
    dma = pltpu.SemaphoreType.DMA
    rows, width = in_back.shape[3:]
    gains_shape = (8, 8, 128)
    moved = jax.ShapeDtypeStruct((2, rows, width), low)
    return pl.pallas_call(
        functools.partial(last_kernel, shards, splits, steps),
        out_shape=(
            jax.ShapeDtypeStruct(in_parts.shape[1:], low),
            jax.ShapeDtypeStruct(out_done.shape, low),
            jax.ShapeDtypeStruct(gate_parts.shape, low),
            jax.ShapeDtypeStruct(gains_shape, wide),
            moved,
            moved,
        ),
        in_specs=[any_space] * 5 + [vmem] * 4,
        out_specs=(any_space,) * 6,
        scratch_shapes=scatter_scratch(rows, width, steps)
        + line_scratch(in_parts.shape[1:], low, slow)
        + line_scratch(gains_shape, wide, slow)
        + [
            pltpu.VMEM(in_parts.shape[1:], low),
            pltpu.VMEM((slow,) + gains_shape, wide),
            pltpu.VMEM(gains_shape, wide),
            pltpu.VMEM(moved.shape, low),
            pltpu.VMEM((1, width), wide),
            dma((2, 8)),
            dma((2, 8)),
            dma((2, 8)),
            dma((2, 2)),
            dma((2, 2)),
            dma((2,)),
        ],
        compiler_params=pltpu.CompilerParams(
            collective_id=identity, has_side_effects=True, vmem_limit_bytes=56 << 20
        ),
        cost_estimate=pl.CostEstimate(flops=0, bytes_accessed=300 << 20, transcendentals=0),
    )(in_parts, out_done, gate_parts, in_back, out_rows, *others)


def position_tables(blocks, rows):
    frequency = rope_base ** (-(np.arange(HEAD // 2) * 2.0 / HEAD))
    angles = np.arange(blocks * rows).reshape(blocks, rows, 1) * frequency
    cos, sin = np.cos(angles), np.sin(angles)
    cosine = np.concatenate([cos, cos, cos, cos], 2)
    sines = np.concatenate([-sin, sin, -sin, sin], 2)
    return jnp.asarray(cosine, jnp.float32), jnp.asarray(sines, jnp.float32)


def attend(order, where, qkv, tables, q_heads, kv_heads):
    seqs, length, cols = qkv.shape
    blocks = order.shape[0]
    rows = length // blocks
    whole = pl.BlockSpec(memory_space=pltpu.VMEM)
    small = pl.BlockSpec(memory_space=pltpu.SMEM)
    return pl.pallas_call(
        functools.partial(attend_kernel, q_heads, kv_heads, 256),
        out_shape=(
            jax.ShapeDtypeStruct((seqs, blocks, rows, q_heads * HEAD), jnp.bfloat16),
            jax.ShapeDtypeStruct((seqs, q_heads, length), jnp.float32),
            jax.ShapeDtypeStruct((seqs, length, cols), jnp.bfloat16),
        ),
        in_specs=[small, small, whole, whole, whole],
        out_specs=(whole, whole, whole),
        scratch_shapes=[pltpu.VMEM((blocks, rows, q_heads * HEAD), jnp.bfloat16)],
        compiler_params=pltpu.CompilerParams(vmem_limit_bytes=40 << 20),
        cost_estimate=pl.CostEstimate(
            flops=2 * seqs * length * length * q_heads * HEAD,
            bytes_accessed=100 << 20,
            transcendentals=seqs * length * length * q_heads // 2,
        ),
    )(order, where, qkv.reshape(seqs, blocks, rows, cols), *tables)


def attend_back(
    order, where, kept, back, lse, tables, out_rows, residual, out_parts, q_heads, kv_heads, identity
):
    seqs, length, cols = kept.shape
    blocks = order.shape[0]
    block = length // blocks
    group = q_heads // kv_heads
    rows, width = out_rows.shape[3:]
    steps = 2
    whole = pl.BlockSpec(memory_space=pltpu.VMEM)
    small = pl.BlockSpec(memory_space=pltpu.SMEM)
    any_space = pl.BlockSpec(memory_space=pl.ANY)
    return pl.pallas_call(
        functools.partial(attend_back_kernel, q_heads, kv_heads, 256, steps),
        out_shape=(
            jax.ShapeDtypeStruct((seqs, blocks, block, cols), jnp.bfloat16),
            jax.ShapeDtypeStruct((2, rows, width), jnp.bfloat16),
            jax.ShapeDtypeStruct(out_parts.shape[1:], jnp.bfloat16),
        ),
        in_specs=[small, small] + [whole] * 5 + [any_space, whole, any_space],
        out_specs=(whole, whole, whole),
        scratch_shapes=[
            pltpu.VMEM((length, q_heads * HEAD), jnp.bfloat16),
            pltpu.VMEM((blocks, block, cols), jnp.float32),
            pltpu.VMEM((group, length), jnp.float32),
            pltpu.VMEM((group * HEAD, length), jnp.float32),
        ]
        + line_scratch(out_parts.shape[1:], jnp.bfloat16, out_parts.shape[0])
        + scatter_scratch(rows, width, steps),
        compiler_params=pltpu.CompilerParams(
            collective_id=identity, has_side_effects=True, vmem_limit_bytes=56 << 20
        ),
        cost_estimate=pl.CostEstimate(
            flops=7 * seqs * length * length * q_heads * HEAD,
            bytes_accessed=100 << 20,
            transcendentals=seqs * length * length * q_heads // 2,
        ),
    )(
        order,
        where,
        kept,
        back.reshape(seqs, blocks, block, -1),
        lse,
        *tables,
        out_rows,
        residual,
        out_parts,
    )


def gate_update_kernel(slow, step_rate, grad, weight, first, second, new_first, new_second, new):
    units = grad.shape[2] // slow
    pieces = [grad[half, :, s * units : (s + 1) * units] for s in range(slow) for half in (0, 1)]
    gradient = jnp.concatenate(pieces, 1).astype(jnp.float32)
    new_first[...], new_second[...], new[...] = adam_update(
        weight[...], gradient, first[...], second[...], step_rate, weight_decay
    )


def gate_update(grad, weight, first, second, slow, step_rate):
    rows, width = weight.shape
    block = pl.BlockSpec((rows, width // 8), lambda side, dp: (0, 4 * side + dp))
    piece = pl.BlockSpec((2, rows, width // 16), lambda side, dp: (dp, 0, side))
    return pl.pallas_call(
        functools.partial(gate_update_kernel, slow, step_rate),
        grid=(2, 4),
        out_shape=(jax.ShapeDtypeStruct(weight.shape, jnp.float32),) * 3,
        in_specs=[piece, block, block, block],
        out_specs=(block,) * 3,
        compiler_params=pltpu.CompilerParams(vmem_limit_bytes=32 << 20),
    )(grad, weight, first, second)


def local(
    tokens,
    cotangent,
    block_order,
    attention_in,
    attention_out,
    gate_up,
    down_matrix,
    gains,
    mean_attention_in,
    mean_attention_out,
    mean_gate_up,
    mean_down,
    mean_gains,
    square_attention_in,
    square_attention_out,
    square_gate_up,
    square_down,
    square_gains,
):
    seq_count, shard_rows, width = tokens.shape
    shards = lax.axis_size("ctx")
    slow = shards // 2
    mine = lax.axis_index("dp")
    beside = lax.axis_index("ctx") % 2
    low = jnp.bfloat16
    owned = attention_in.shape[0]
    hidden_units = gate_up.shape[1] // 2
    part_hidden = hidden_units // 8
    units = down_matrix.shape[0]
    part_q = HEADS * HEAD // 8
    part_k = KV_HEADS * HEAD // 8
    part_cols = part_q + 2 * part_k
    count = seq_count * shard_rows
    together = 8 * count
    spread = shards // (4 * seq_count)
    splits = max(1, slow // 8)
    seqs = 2 // spread if spread < 2 else 1
    length = shards * shard_rows
    q_heads = HEADS // 8 // splits
    kv_heads = KV_HEADS // 8

    in_low = attention_in.astype(low)
    gains_row = jnp.pad(gains.astype(low).reshape(1, -1), ((0, 15), (0, part_cols - 2 * owned)))
    pieces = jnp.stack(
        [
            jnp.concatenate(
                [
                    jnp.concatenate(
                        [
                            in_low[:, i * part_q : (i + 1) * part_q],
                            in_low[:, 8 * part_q + i * part_k :][:, :part_k],
                            in_low[:, 8 * (part_q + part_k) + i * part_k :][:, :part_k],
                        ],
                        1,
                    ),
                    gains_row,
                ]
            )
            for i in range(8)
        ]
    )
    gate_low = gate_up.astype(low)
    gate_pieces = jnp.stack(
        [
            jnp.concatenate(
                [
                    gate_low[:, side * hidden_units + (dp * shards + 2 * s + half) * units :][
                        :, :units
                    ]
                    for side in range(2)
                    for s in range(slow)
                ],
                1,
            )
            for dp in range(4)
            for half in range(2)
        ]
    )
    tokens_all, in_all, w_out, gate_rows = first_exchange(
        tokens, pieces, attention_out.astype(low), gate_pieces, shards, spread, 1
    )
    in_all = in_all.reshape(slow, 4, 2, owned + 16, part_cols).swapaxes(0, 1)
    w_in = in_all[:, :, :, :owned].reshape(width, part_cols)
    w_out = w_out.reshape(part_q, width)
    gains_all = in_all[:, :, :, owned, : 2 * owned].reshape(-1, 2, owned)
    gains_all = gains_all.astype(jnp.float32).swapaxes(0, 1).reshape(2, width)
    gain_one, gain_two = gains_all[0], gains_all[1]
    w_gate = gather_line(gate_rows.reshape(8 * owned, 2 * part_hidden))

    normed_all, _ = norm_parts(tokens_all.reshape(together, width).astype(jnp.float32))
    input_one = (normed_all * gain_one).astype(low)
    qkv = dot_nn(input_one, w_in)
    orders = block_order.reshape(2 * splits if spread > 1 else 1, 4, -1)
    slot_order = jnp.concatenate(
        [
            orders[(2 * s + (beside ^ i)) if spread > 1 else 0, part_owner(mine ^ j)]
            for s in range(splits)
            for i in range(2 // seqs)
            for j in range(4)
        ]
    )
    tables = position_tables(slot_order.shape[0], length // slot_order.shape[0])
    groups = [
        [2 * (s * splits + g) + half for g in range(splits)]
        for s in range(slow // splits)
        for half in (0, 1)
    ]

    def split_heads(values, widths, copies):
        parts = []
        start = 0
        for each, repeat in zip(widths, copies):
            kinds = splits // repeat
            piece = values[:, start : start + kinds * each].reshape(-1, kinds, each)
            parts.append(jnp.repeat(piece.swapaxes(0, 1), repeat, axis=0))
            start += kinds * each
        sent = jnp.concatenate(parts, 2)
        got = lax.all_to_all(sent, "ctx", 0, 0, axis_index_groups=groups, tiled=True)
        return got.reshape(length, -1)

    def join_heads(values):
        sent = values.reshape(splits, together, -1)
        return lax.all_to_all(sent, "ctx", 0, 0, axis_index_groups=groups, tiled=True)

    q_width, k_width = q_heads * HEAD, kv_heads * HEAD
    if splits > 1:
        qkv = split_heads(qkv, (q_width, k_width, k_width), (1, splits, splits))
    qkv = qkv.reshape(seqs, length, -1)
    blocks = slot_order.shape[0]
    slot_where = jnp.sum(
        jnp.where(
            slot_order[None, :] == jnp.arange(blocks, dtype=jnp.int32)[:, None],
            jnp.arange(blocks, dtype=jnp.int32)[None, :],
            0,
        ),
        1,
    )
    attended, lse, kept = attend(slot_order, slot_where, qkv, tables, q_heads, kv_heads)
    if splits > 1:
        attended = join_heads(attended.reshape(length, q_width)).swapaxes(0, 1)
    attended = attended.reshape(together, part_q)

    def parts(values):
        return values.astype(low).reshape((2, 4) + tokens.shape)

    residual_rows, input_two = turn(
        parts(dot_nn(attended, w_out)), gain_two[None], [tokens_all[0, 0]], slow, False, 3
    )
    input_two = input_two.reshape(together, width)
    after = 0.0 * (residual_rows[0, 0, 0] + w_gate[0, 0].astype(jnp.float32))
    cot_rows = move_tokens(cotangent + after.astype(low), spread, 7)
    after = 0.0 * cot_rows[0, 0, 0].astype(jnp.float32)
    w_down = gather_line((down_matrix + after).astype(low))
    gate_both = dot_nn(input_two, w_gate)
    gate_part = gate_both[:, :part_hidden]
    up_part = gate_both[:, part_hidden:]
    sigmoid_gate = jax.nn.sigmoid(gate_part)
    active = gate_part * sigmoid_gate
    hidden = lax.optimization_barrier((active * up_part).astype(low))
    back_all = spread_group(cot_rows + 0.0 * hidden[0, 0], 2).reshape(together, width)
    grad_down = lax.optimization_barrier(dot_tn(hidden, back_all).astype(low))
    down_sum = sum_line(grad_down + 0.0 * w_down[0, 0]).astype(jnp.float32)
    back_hidden = dot_nt(back_all, w_down + 0.0 * hidden[0, 0])
    back_gate = back_hidden * up_part * sigmoid_gate * (1.0 + gate_part * (1.0 - sigmoid_gate))
    back_upper = back_hidden * active
    back_gate_up = jnp.concatenate([back_gate, back_upper], 1).astype(low)
    gate_low = sum_line(dot_tn(input_two, back_gate_up).astype(low))
    back_rows, grad_gain_two, back_residual_all = turn(
        parts(dot_nt(back_gate_up, w_gate)),
        gain_two[None],
        [residual_rows, cot_rows],
        slow,
        True,
        4,
    )
    back_residual_all = back_residual_all.reshape(together, width)
    grad_out = dot_tn(attended, back_residual_all).astype(low)
    back_attended = dot_nt(back_residual_all, w_out).astype(low)
    if splits > 1:
        back_attended = split_heads(back_attended, (q_width,), (1,))
    back_projected, output_rows, out_sum = attend_back(
        slot_order,
        slot_where,
        kept,
        back_attended.reshape(seqs, length, -1),
        lse,
        tables,
        parts(dot_nn(hidden, w_down)),
        residual_rows,
        grad_out.reshape(slow, owned, width),
        q_heads,
        kv_heads,
        6,
    )
    if splits > 1:
        back_projected = join_heads(back_projected.reshape(length, -1)).astype(jnp.float32)
        back_projected = jnp.concatenate(
            [
                back_projected[..., :q_width].swapaxes(0, 1).reshape(together, part_q),
                back_projected[..., q_width:].sum(0),
            ],
            1,
        ).astype(low)
    back_projected = back_projected.reshape(together, part_cols)
    grad_in = dot_tn(input_one, back_projected).astype(low)
    grad_in = grad_in.reshape(4, slow, 2 * owned, part_cols).swapaxes(0, 1)
    in_sum, out_sum, gate_sum, gains_sum, tokens_grad, block_out = last_sums(
        grad_in.reshape(slow, 8, owned, part_cols),
        out_sum,
        gate_low.reshape(8, owned, 2 * part_hidden),
        parts(dot_nt(back_projected, w_in)),
        output_rows,
        [gain_one[None], grad_gain_two, tokens_all[0, 0], back_rows],
        shards,
        spread,
        5,
    )
    tokens_grad = tokens_grad.astype(jnp.float32)
    out_sum = out_sum.astype(jnp.float32)
    gains_sum = gains_sum[:, 0, : 2 * owned].reshape(8, 2, owned).sum(0)
    cuts = ((0, part_q), (part_q, part_q + part_k), (part_q + part_k, part_cols))
    in_sum = jnp.concatenate(
        [in_sum[i, :, first:last] for first, last in cuts for i in range(8)], 1
    ).astype(jnp.float32)
    new_in = adam_update(
        attention_in,
        in_sum,
        mean_attention_in,
        square_attention_in,
        input_boost * D ** (-0.5),
        weight_decay,
    )
    new_out = adam_update(
        attention_out,
        out_sum,
        mean_attention_out,
        square_attention_out,
        (HEADS * HEAD // 32) ** (-0.5),
        weight_decay,
    )
    new_gate = gate_update(
        gate_sum, gate_up, mean_gate_up, square_gate_up, slow, D ** (-0.5)
    )
    new_down = adam_update(
        down_matrix, down_sum, mean_down, square_down, FF ** (-0.5), weight_decay
    )
    new_gain = adam_update(gains, gains_sum, mean_gains, square_gains, gain_rate, 0.0)
    return (
        block_out,
        tokens_grad,
        new_in[0],
        new_in[1],
        new_in[2],
        new_out[0],
        new_out[1],
        new_out[2],
        new_gate[0],
        new_gate[1],
        new_gate[2],
        new_down[0],
        new_down[1],
        new_down[2],
        new_gain[0],
        new_gain[1],
        new_gain[2],
    )


def solution(mesh):
    in_specs = (
        P("dp", "ctx", None),
        P("dp", "ctx", None),
        P(),
        P(("dp", "ctx"), None),
        P(("dp", "ctx"), None),
        P(("dp", "ctx"), None),
        P(("dp", "ctx"), None),
        P(None, ("dp", "ctx")),
        P(("dp", "ctx"), None),
        P(("dp", "ctx"), None),
        P(("dp", "ctx"), None),
        P(("dp", "ctx"), None),
        P(None, ("dp", "ctx")),
        P(("dp", "ctx"), None),
        P(("dp", "ctx"), None),
        P(("dp", "ctx"), None),
        P(("dp", "ctx"), None),
        P(None, ("dp", "ctx")),
    )
    out_specs = (
        P("dp", "ctx", None),
        P("dp", "ctx", None),
        P(("dp", "ctx"), None),
        P(("dp", "ctx"), None),
        P(("dp", "ctx"), None),
        P(("dp", "ctx"), None),
        P(("dp", "ctx"), None),
        P(("dp", "ctx"), None),
        P(("dp", "ctx"), None),
        P(("dp", "ctx"), None),
        P(("dp", "ctx"), None),
        P(("dp", "ctx"), None),
        P(("dp", "ctx"), None),
        P(("dp", "ctx"), None),
        P(None, ("dp", "ctx")),
        P(None, ("dp", "ctx")),
        P(None, ("dp", "ctx")),
    )
    return jax.shard_map(local, mesh=mesh, in_specs=in_specs, out_specs=out_specs, check_vma=False)
```

```python
import functools

import jax
import jax.numpy as jnp
import numpy as np
from jax import lax
from jax.experimental import pallas as pl
from jax.experimental.pallas import tpu as pltpu
from jax.sharding import PartitionSpec as P

D = 2048
HEADS = 32
KV_HEADS = 8
HEAD = 64
FF = 8192
STEP = 5


norm_eps = 1e-05
rope_base = 500000.0
beta_one = 0.9
beta_two = 0.95
gain_rate = 1.25
input_boost = 2.5
weight_decay = 0.1
adam_eps = 1e-08
masked_score = -1e30


def norm_parts(values):
    factor = lax.rsqrt(jnp.mean(values * values, -1, keepdims=True) + norm_eps)
    return (values * factor, factor)


def norm_back(back_normed, normed, factor):
    return factor * (back_normed - normed * jnp.mean(back_normed * normed, -1, keepdims=True))


def adam_update(weight, gradient, first_moment, second_moment, step_rate, decay_rate):
    first_new = beta_one * first_moment + (1.0 - beta_one) * gradient
    second_new = beta_two * second_moment + (1.0 - beta_two) * gradient * gradient
    update = (
        first_new
        / (1.0 - beta_one**STEP)
        / (jnp.sqrt(second_new / (1.0 - beta_two**STEP)) + adam_eps)
    )
    return (first_new, second_new, weight - step_rate * (update + decay_rate * weight))


def line_groups(shards):
    return [[2 * s + half for s in range(shards // 2)] for half in (0, 1)]


def gather_line(rows):
    return lax.all_gather(
        rows, "ctx", axis=0, tiled=True, axis_index_groups=line_groups(lax.axis_size("ctx"))
    )


def sum_line(gradient):
    return lax.psum_scatter(
        gradient,
        "ctx",
        scatter_dimension=0,
        tiled=True,
        axis_index_groups=line_groups(lax.axis_size("ctx")),
    )


def dot_nn(a, b):
    return lax.dot_general(a, b, (((1,), (0,)), ((), ())), preferred_element_type=jnp.float32)


def dot_nt(a, b):
    return lax.dot_general(a, b, (((1,), (1,)), ((), ())), preferred_element_type=jnp.float32)


def dot_tn(a, b):
    return lax.dot_general(a, b, (((0,), (0,)), ((), ())), preferred_element_type=jnp.float32)


def causal_keep(tile):
    keys = lax.broadcasted_iota(jnp.int32, (tile, tile), 0)
    queries = lax.broadcasted_iota(jnp.int32, (tile, tile), 1)
    return keys <= queries


def turn_group(values, cos, sin, forward):
    lanes = lax.broadcasted_iota(jnp.int32, values.shape, 1)
    other = jnp.where(
        lanes % HEAD < HEAD // 2,
        pltpu.roll(values, 2 * HEAD - HEAD // 2, 1),
        pltpu.roll(values, HEAD // 2, 1),
    )
    if forward:
        return values * cos + other * sin
    return values * cos - other * sin


def turn_columns(values, start, turned_cols, cos, sin, forward):
    if start >= turned_cols:
        return values
    turned = turn_group(values, cos, sin, forward)
    if start + 2 * HEAD <= turned_cols:
        return turned
    lanes = lax.broadcasted_iota(jnp.int32, values.shape, 1)
    return jnp.where(lanes < turned_cols - start, turned, values)


def attend_kernel(
    q_heads,
    kv_heads,
    tile,
    order_ref,
    where_ref,
    all_qkv_ref,
    cos_ref,
    sin_ref,
    all_out_ref,
    all_lse_ref,
    all_kept_ref,
    made,
):
    for sequence in range(all_qkv_ref.shape[0]):
        attend_sequence(
            q_heads,
            kv_heads,
            tile,
            order_ref,
            where_ref,
            all_qkv_ref.at[sequence],
            cos_ref,
            sin_ref,
            all_out_ref.at[sequence],
            all_lse_ref.at[sequence],
            all_kept_ref.at[sequence],
            made,
        )


def attend_sequence(
    q_heads,
    kv_heads,
    tile,
    order_ref,
    where_ref,
    qkv_ref,
    cos_ref,
    sin_ref,
    out_ref,
    lse_ref,
    kept_ref,
    made,
):
    blocks, rows, cols = qkv_ref.shape
    length = blocks * rows
    group = q_heads // kv_heads
    q_cols, k_cols = q_heads * HEAD, kv_heads * HEAD
    scale = HEAD ** (-0.5)

    def take_block(i, _):
        start = pl.multiple_of(i * rows, rows)
        cos = cos_ref[i]
        sin = sin_ref[i]
        for c in range(0, cols, 2 * HEAD):
            values = qkv_ref[where_ref[i], :, c : c + 2 * HEAD]
            values = turn_columns(values, c, q_cols + k_cols, cos, sin, True)
            kept_ref[pl.ds(start, rows), c : c + 2 * HEAD] = values.astype(jnp.bfloat16)
        return 0

    lax.fori_loop(0, blocks, take_block, 0)
    keep = causal_keep(tile)
    for kv in range(kv_heads):
        k_at = q_cols + kv * HEAD
        v_at = q_cols + k_cols + kv * HEAD

        def query_step(i, _):
            q_start = pl.multiple_of(i * tile, tile)
            queries = [
                kept_ref[
                    pl.ds(q_start, tile), (kv * group + g) * HEAD : (kv * group + g + 1) * HEAD
                ]
                for g in range(group)
            ]

            def key_tile(j, carry, masked):
                k_start = pl.multiple_of(j * tile, tile)
                keys = kept_ref[pl.ds(k_start, tile), k_at : k_at + HEAD]
                values = kept_ref[pl.ds(k_start, tile), v_at : v_at + HEAD]
                result = []
                for g in range(group):
                    peak, total, weighted = carry[g]
                    scores = dot_nt(keys, queries[g]) * scale
                    if masked:
                        scores = jnp.where(keep, scores, masked_score)
                    new_peak = jnp.maximum(peak, jnp.max(scores, 0, keepdims=True))
                    weights = jnp.exp(scores - new_peak)
                    shrink = jnp.exp(peak - new_peak)
                    total = total * shrink + jnp.sum(weights, 0, keepdims=True)
                    weighted = weighted * shrink + dot_tn(values, weights.astype(jnp.bfloat16))
                    result.append((new_peak, total, weighted))
                return tuple(result)

            start = tuple(
                (
                    jnp.full((1, tile), masked_score, jnp.float32),
                    jnp.zeros((1, tile), jnp.float32),
                    jnp.zeros((HEAD, tile), jnp.float32),
                )
                for _ in range(group)
            )
            carry = lax.fori_loop(0, i, lambda j, c: key_tile(j, c, False), start)
            carry = key_tile(i, carry, True)
            for g in range(group):
                head = kv * group + g
                peak, total, weighted = carry[g]
                lse_ref[head : head + 1, pl.ds(q_start, tile)] = peak + jnp.log(total)
                made[pl.ds(i * (tile // rows), tile // rows), :, head * HEAD : (head + 1) * HEAD] = (
                    (weighted / total).T.astype(jnp.bfloat16).reshape(-1, rows, HEAD)
                )
            return 0

        lax.fori_loop(0, length // tile, query_step, 0)

    def give_block(i, _):
        out_ref[i] = made[order_ref[i]]
        return 0

    lax.fori_loop(0, blocks, give_block, 0)


def attend_back_kernel(
    q_heads,
    kv_heads,
    tile,
    steps,
    order_ref,
    where_ref,
    all_kept_ref,
    all_back_ref,
    all_lse_ref,
    cos_ref,
    sin_ref,
    out_rows,
    residual,
    out_parts,
    all_out_ref,
    block_out,
    out_sum,
    *scratch,
):
    me = (lax.axis_index("dp"), lax.axis_index("ctx"))
    slow = out_parts.shape[0]
    line = [(me[0], me[1] ^ (2 * by)) for by in range(1, slow)]
    greet(me, [member(me, by) for by in (1, 2, 4)] + line, [])
    work, line_out, scratch = scratch[:4], scratch[4:8], scratch[8:]
    scatter = GroupScatter(me, out_rows, scratch[:7], scratch[7:], steps)
    out_line = LineSum(me, slow, out_parts, line_out[:2], line_out[2:])

    def one():
        for k in range(steps):
            scatter.send_first(k)

    def two():
        for k in range(steps):
            scatter.send_second(k)

    def three():
        for k in range(steps):
            span = scatter.window(k)
            for part in (0, 1):
                value = residual[part, span] + scatter.total(k, part)
                block_out[part, span] = value.astype(jnp.bfloat16)

    tasks = [one, two, three]

    def pause():
        if tasks:
            tasks.pop(0)()

    scatter.start()
    out_line.start()
    for sequence in range(all_kept_ref.shape[0]):
        attend_back_sequence(
            q_heads,
            kv_heads,
            tile,
            pause,
            order_ref,
            where_ref,
            all_kept_ref.at[sequence],
            all_back_ref.at[sequence],
            all_lse_ref.at[sequence],
            cos_ref,
            sin_ref,
            all_out_ref.at[sequence],
            *work,
        )
    while tasks:
        pause()
    out_sum[...] = out_line.total().astype(jnp.bfloat16)
    out_line.finish()
    scatter.finish()


def attend_back_sequence(
    q_heads,
    kv_heads,
    tile,
    pause,
    order_ref,
    where_ref,
    kept_ref,
    back_ref,
    lse_ref,
    cos_ref,
    sin_ref,
    out_ref,
    back_sorted,
    grad,
    delta_ref,
    dq_ref,
):
    length, cols = kept_ref.shape
    blocks, rows = back_ref.shape[:2]
    group = q_heads // kv_heads
    q_cols, k_cols = q_heads * HEAD, kv_heads * HEAD
    scale = HEAD ** (-0.5)
    tiles = length // tile

    def take_block(i, _):
        start = pl.multiple_of(i * rows, rows)
        back_sorted[pl.ds(start, rows), :] = back_ref[where_ref[i]]
        return 0

    lax.fori_loop(0, blocks, take_block, 0)
    keep = causal_keep(tile)
    for kv in range(kv_heads):
        k_at = q_cols + kv * HEAD
        v_at = q_cols + k_cols + kv * HEAD

        def load(i, g):
            start = pl.multiple_of(i * tile, tile)
            head = kv * group + g
            at = slice(head * HEAD, (head + 1) * HEAD)
            return (
                kept_ref[pl.ds(start, tile), at],
                back_sorted[pl.ds(start, tile), at],
                lse_ref[head : head + 1, pl.ds(start, tile)],
            )

        def load_kv(j):
            start = pl.multiple_of(j * tile, tile)
            return (
                kept_ref[pl.ds(start, tile), k_at : k_at + HEAD],
                kept_ref[pl.ds(start, tile), v_at : v_at + HEAD],
            )

        def tile_terms(keys, values, query, back, lse, masked):
            weights = jnp.exp(dot_nt(keys, query) * scale - lse)
            if masked:
                weights = jnp.where(keep, weights, 0.0)
            return weights, dot_nt(values, back)

        def delta_step(i, _):
            rows_i = [load(i, g) for g in range(group)]

            def one(j, carry, masked):
                keys, values = load_kv(j)
                result = []
                for g in range(group):
                    weights, back_weights = tile_terms(keys, values, *rows_i[g], masked)
                    result.append(carry[g] + jnp.sum(weights * back_weights, 0, keepdims=True))
                return tuple(result)

            carry = tuple(jnp.zeros((1, tile), jnp.float32) for _ in range(group))
            carry = lax.fori_loop(0, i, lambda j, c: one(j, c, False), carry)
            carry = one(i, carry, True)
            for g in range(group):
                delta_ref[g : g + 1, pl.ds(pl.multiple_of(i * tile, tile), tile)] = carry[g]
            return 0

        lax.fori_loop(0, tiles, delta_step, 0)
        if kv == 0:
            pause()
        dq_ref[...] = jnp.zeros_like(dq_ref)

        def key_step(j, _):
            keys, values = load_kv(j)

            def one(i, carry, masked):
                back_key, back_value = carry
                start = pl.multiple_of(i * tile, tile)
                for g in range(group):
                    query, back, lse = load(i, g)
                    weights, back_weights = tile_terms(keys, values, query, back, lse, masked)
                    delta = delta_ref[g : g + 1, pl.ds(start, tile)]
                    back_scores = (weights * (back_weights - delta)).astype(jnp.bfloat16)
                    back_key = back_key + dot_nn(back_scores, query)
                    back_value = back_value + dot_nn(weights.astype(jnp.bfloat16), back)
                    dq_ref[g * HEAD : (g + 1) * HEAD, pl.ds(start, tile)] += dot_tn(
                        keys, back_scores
                    )
                return back_key, back_value

            zero = jnp.zeros((tile, HEAD), jnp.float32)
            carry = one(j, (zero, zero), True)
            carry = lax.fori_loop(j + 1, tiles, lambda i, c: one(i, c, False), carry)
            span = pl.ds(j * (tile // rows), tile // rows)
            grad[span, :, k_at : k_at + HEAD] = (carry[0] * scale).reshape(-1, rows, HEAD)
            grad[span, :, v_at : v_at + HEAD] = carry[1].reshape(-1, rows, HEAD)
            return 0

        lax.fori_loop(0, tiles, key_step, 0)
        for g in range(group):
            head = kv * group + g
            turned = (dq_ref[g * HEAD : (g + 1) * HEAD, :] * scale).T
            grad[:, :, head * HEAD : (head + 1) * HEAD] = turned.reshape(-1, rows, HEAD)

    def give_block(i, _):
        cos = cos_ref[order_ref[i]]
        sin = sin_ref[order_ref[i]]
        for c in range(0, cols, 2 * HEAD):
            values = grad[order_ref[i], :, c : c + 2 * HEAD]
            values = turn_columns(values, c, q_cols + k_cols, cos, sin, False)
            out_ref[i, :, c : c + 2 * HEAD] = values.astype(jnp.bfloat16)
        return 0

    lax.fori_loop(0, blocks, give_block, 0)


MESH = pl.DeviceIdType.MESH


def part_owner(part):
    return part % 2 * 2 + part // 2


def sequence_target(group, place, second, splits):
    part = place // 2
    sequence = 2 * group + second
    held_at = sequence % 4 * 2 + sequence // 4
    target = (part_owner(part % 4), held_at * splits + part // 4)
    return target, place % 2


def token_target(group, place, half, splits):
    held_at = place // splits
    sequence = held_at % 2 * 4 + held_at // 2
    part = part_owner(group) + 4 * (place % splits)
    return (sequence // 2, 2 * part + half), sequence % 2


def remote(source, target, sems, device):
    return pltpu.make_async_remote_copy(
        src_ref=source,
        dst_ref=target,
        send_sem=sems[0],
        recv_sem=sems[1],
        device_id=device,
        device_id_type=MESH,
    )


def same(one, other):
    return jnp.logical_and(one[0] == other[0], one[1] == other[1])


def greet(me, peers, movers):
    barrier = pltpu.get_barrier_semaphore()
    for peer in peers:
        pl.semaphore_signal(barrier, inc=1, device_id=peer, device_id_type=MESH)
    expected = len(peers)
    for source, target in movers:

        @pl.when(jnp.logical_not(same(source, me)))
        def _():
            pl.semaphore_signal(barrier, inc=1, device_id=source, device_id_type=MESH)

        expected = expected + jnp.where(same(target, me), 0, 1)
    pl.semaphore_wait(barrier, expected)


def move_start(me, source, target, target_device, send, receive):
    here = same(target_device, me)

    @pl.when(here)
    def _():
        pltpu.make_async_copy(source, target, receive).start()

    @pl.when(jnp.logical_not(here))
    def _():
        remote(source, target, (send, receive), target_device).start()


def move_sent(me, source, target, target_device, send, receive):
    @pl.when(jnp.logical_not(same(target_device, me)))
    def _():
        remote(source, target, (send, receive), target_device).wait_send()


def member(me, by):
    return (me[0] ^ (by // 2), me[1] ^ (by % 2))


def group_index(device):
    return 2 * device[0] + device[1] % 2


class GroupExchange:
    def __init__(self, me, pieces, got, sems):
        self.me, self.pieces, self.got, self.sems = me, pieces, got, sems

    def hop(self, by):
        peer = member(self.me, by)
        sems = (self.sems.at[0, by - 1], self.sems.at[1, by - 1])
        return remote(
            self.pieces.at[group_index(peer)], self.got.at[group_index(self.me)], sems, peer
        )

    def own(self):
        mine = group_index(self.me)
        return pltpu.make_async_copy(self.pieces.at[mine], self.got.at[mine], self.sems.at[0, 7])

    def start(self):
        for by in range(1, 8):
            self.hop(by).start()
        self.own().start()

    def finish(self):
        self.own().wait()
        for by in range(1, 8):
            self.hop(by).wait()


class GroupGather:
    def __init__(self, me, rows, sems, own, window):
        self.rows, self.sems, self.own, self.window = rows, sems, own, window
        self.core, self.across, self.beside = member(me, 2), member(me, 4), member(me, 1)

    def hop(self, index):
        across, beside, core = self.across, self.beside, self.core
        source, i, j, half, device = (
            (None, 0, 2, 0, across),
            (None, 1, 0, 1, beside),
            (None, 1, 0, 0, beside),
            (None, 0, 2, 1, across),
            ((0, 2), 1, 2, 0, beside),
            ((1, 0), 1, 2, 1, across),
            (None, 0, 1, slice(0, 2), core),
            ((0, 2), 0, 3, slice(0, 2), core),
            ((1, 0), 1, 1, slice(0, 2), core),
            ((1, 2), 1, 3, slice(0, 2), core),
        )[index]
        if source is None:
            source = self.own.at[half, self.window]
        else:
            source = self.rows.at[source[0], source[1], half, self.window]
        target = self.rows.at[i, j, half, self.window]
        return remote(source, target, (self.sems.at[0, index], self.sems.at[1, index]), device)

    def start(self):
        for index in (0, 1, 2, 3, 6):
            self.hop(index).start()

    def pass_on(self):
        self.hop(0).wait_recv()
        self.hop(4).start()
        self.hop(1).wait_recv()
        self.hop(5).start()
        self.hop(3).wait_recv()
        self.hop(7).start()
        self.hop(2).wait_recv()
        self.hop(8).start()

    def finish(self):
        self.hop(4).wait_recv()
        self.hop(5).wait_recv()
        self.hop(9).start()
        for index in (6, 7, 8, 9):
            self.hop(index).wait_recv()
        for index in range(10):
            self.hop(index).wait_send()


class Moves:
    def __init__(self, me, splits, source, target, sems, back):
        self.me, self.splits, self.source, self.target = me, splits, source, target
        self.sems, self.back = sems, back

    def one(self, i):
        find = token_target if self.back else sequence_target
        device, place = find(self.me[0], self.me[1], i, self.splits)
        return (
            self.me,
            self.source.at[i],
            self.target.at[place],
            device,
            self.sems.at[0, i],
            self.sems.at[1, place],
        )

    def start(self):
        for i in (0, 1):
            move_start(*self.one(i))

    def wait_recv(self):
        for i in (0, 1):
            pltpu.make_async_copy(self.source.at[0], self.target.at[i], self.sems.at[1, i]).wait()

    def finish(self):
        for i in (0, 1):
            move_sent(*self.one(i))


def movers_of(me, splits, back):
    into = [sequence_target(me[0], me[1], i, splits)[0] for i in (0, 1)]
    home = [token_target(me[0], me[1], i, splits)[0] for i in (0, 1)]
    return list(zip(into, home)) if back else list(zip(home, into))


def first_kernel(shards, splits, tokens, pieces, out_own, gate_pieces, *refs):
    rows, in_all, out_all, gate_rows, held = refs[:5]
    move_sems, group_sems, piece_sems, gate_sems, own_sem, in_sems, out_sems = refs[5:]
    me = (lax.axis_index("dp"), lax.axis_index("ctx"))
    group, place = me
    slow = shards // 2
    slot = place // 2
    line = [(group, place ^ (2 * by)) for by in range(1, slow)]
    wanted, block = place // slow, place % slow
    takers = [(group, 2 * (slot ^ by) + wanted) for by in range(slow)]
    givers = [(group, place % 2 * slow + block_by) for block_by in range(slow)]
    movers = movers_of(me, splits, False) + list(zip(givers, takers))
    greet(me, [member(me, by) for by in range(1, 8)] + line, movers)
    swap = GroupExchange(me, pieces, held, piece_sems)
    gate_swap = GroupExchange(me, gate_pieces, gate_rows, gate_sems)
    move = Moves(me, splits, tokens, rows.at[0, 0], move_sems, False)

    def in_line(by):
        sems = (in_sems.at[0, by - 1], in_sems.at[1, by - 1])
        return remote(held, in_all.at[slot], sems, line[by - 1])

    def out_send(by):
        return (
            me,
            out_own,
            out_all.at[block],
            takers[by],
            out_sems.at[0, by],
            out_sems.at[1, block],
        )

    own = pltpu.make_async_copy(held, in_all.at[slot], own_sem)
    move.start()
    swap.start()
    gate_swap.start()
    swap.finish()
    move.wait_recv()
    spread = GroupGather(me, rows, group_sems, rows.at[0, 0], slice(0, tokens.shape[1]))
    spread.start()
    for by in range(1, slow):
        in_line(by).start()
    own.start()
    for by in range(slow):
        move_start(*out_send(by))
    spread.pass_on()
    for by in range(1, slow):
        in_line(by).wait()
    spread.finish()
    own.wait()
    for by in range(slow):
        pltpu.make_async_copy(out_own, out_all.at[by], out_sems.at[1, by]).wait()
    for by in range(slow):
        move_sent(*out_send(by))
    gate_swap.finish()
    move.finish()


def first_exchange(tokens, pieces, out_own, gate_pieces, shards, splits, identity):
    low = jnp.bfloat16
    slow = shards // 2
    any_space = pl.BlockSpec(memory_space=pl.ANY)
    dma = pltpu.SemaphoreType.DMA
    made = pl.pallas_call(
        functools.partial(first_kernel, shards, splits),
        out_shape=(
            jax.ShapeDtypeStruct((2, 4) + tokens.shape, low),
            jax.ShapeDtypeStruct((slow,) + pieces.shape, low),
            jax.ShapeDtypeStruct((slow,) + out_own.shape, low),
            jax.ShapeDtypeStruct(gate_pieces.shape, low),
            jax.ShapeDtypeStruct(pieces.shape, low),
        ),
        in_specs=[any_space] * 4,
        out_specs=(any_space,) * 5,
        scratch_shapes=[
            dma((2, 2)),
            dma((2, 10)),
            dma((2, 8)),
            dma((2, 8)),
            dma,
            dma((2, slow - 1)),
            dma((2, slow)),
        ],
        compiler_params=pltpu.CompilerParams(
            collective_id=identity, has_side_effects=True, vmem_limit_bytes=8 << 20
        ),
        cost_estimate=pl.CostEstimate(flops=0, bytes_accessed=200 << 20, transcendentals=0),
    )(tokens, pieces, out_own, gate_pieces)
    return made[:4]


class GroupScatter:
    def __init__(self, me, parts, buffers, sems, steps):
        self.parts = parts
        self.core_in, self.kept, self.sent, self.came, self.held = buffers[:5]
        self.sent_last, self.came_last = buffers[5:]
        self.core_sems, self.kept_sems, self.one_sems, self.last_sems = sems
        self.core, self.across, self.beside = member(me, 2), member(me, 4), member(me, 1)
        self.size = parts.shape[3] // steps
        self.steps = steps

    def window(self, k):
        return slice(k * self.size, (k + 1) * self.size)

    def to_core(self, k, j):
        return remote(
            self.parts.at[:, 2 * j + 1, :, self.window(k)],
            self.core_in.at[:, j, :, self.window(k)],
            (self.core_sems.at[0, k, j], self.core_sems.at[1, k, j]),
            self.core,
        )

    def keep(self, k, j):
        return pltpu.make_async_copy(
            self.parts.at[:, 2 * j, :, self.window(k)],
            self.kept.at[:, j, :, self.window(k)],
            self.kept_sems.at[k, j],
        )

    def first(self, k, half):
        return remote(
            self.sent.at[half, :, self.window(k)],
            self.came.at[half, :, self.window(k)],
            (self.one_sems.at[0, k, half], self.one_sems.at[1, k, half]),
            (self.beside, self.across)[half],
        )

    def second(self, k, half):
        return remote(
            self.sent_last.at[half, self.window(k)],
            self.came_last.at[half, self.window(k)],
            (self.last_sems.at[0, k, half], self.last_sems.at[1, k, half]),
            (self.across, self.beside)[half],
        )

    def start(self):
        for k in range(self.steps):
            for j in (0, 1):
                self.to_core(k, j).start()
                self.keep(k, j).start()

    def send_first(self, k):
        wide = jnp.float32
        rows = self.window(k)
        for j in (0, 1):
            self.keep(k, j).wait()
            self.to_core(k, j).wait_recv()
        for half in (0, 1):
            for other in (0, 1):
                at = (1, other) if half == 0 else (other, 1)
                both = self.kept[at[0], at[1], half, rows].astype(wide)
                both = both + self.core_in[at[0], at[1], half, rows].astype(wide)
                self.sent[half, other, rows] = both.astype(jnp.bfloat16)
            self.first(k, half).start()
        for half in (0, 1):
            for other in (0, 1):
                at = (0, other) if half == 0 else (other, 0)
                both = self.kept[at[0], at[1], half, rows].astype(wide)
                self.held[half, other, rows] = both + self.core_in[at[0], at[1], half, rows].astype(
                    wide
                )

    def send_second(self, k):
        wide = jnp.float32
        rows = self.window(k)
        for half in (0, 1):
            self.first(k, half).wait_recv()
            both = self.held[half, 1, rows] + self.came[half, 1, rows].astype(wide)
            self.sent_last[half, rows] = both.astype(jnp.bfloat16)
            self.second(k, half).start()
            self.held[half, 0, rows] = self.held[half, 0, rows] + self.came[half, 0, rows].astype(
                wide
            )

    def total(self, k, half):
        self.second(k, half).wait_recv()
        rows = self.window(k)
        return self.held[half, 0, rows] + self.came_last[half, rows].astype(jnp.float32)

    def finish(self):
        for k in range(self.steps):
            for j in (0, 1):
                self.to_core(k, j).wait_send()
            for half in (0, 1):
                self.first(k, half).wait_send()
                self.second(k, half).wait_send()


def scatter_scratch(rows, width, steps):
    low, wide = jnp.bfloat16, jnp.float32
    dma = pltpu.SemaphoreType.DMA
    return [
        pltpu.VMEM((2, 2, 2, rows, width), low),
        pltpu.VMEM((2, 2, 2, rows, width), low),
        pltpu.VMEM((2, 2, rows, width), low),
        pltpu.VMEM((2, 2, rows, width), low),
        pltpu.VMEM((2, 2, rows, width), wide),
        pltpu.VMEM((2, rows, width), low),
        pltpu.VMEM((2, rows, width), low),
        dma((2, steps, 2)),
        dma((steps, 2)),
        dma((2, steps, 2)),
        dma((2, steps, 2)),
    ]


def reordered(rows, slow, back):
    each = rows.shape[1] // (4 * slow)
    if back:
        starts = [s * 4 + dp for dp in range(4) for s in range(slow)]
    else:
        starts = [dp * slow + s for s in range(slow) for dp in range(4)]
    return jnp.concatenate([rows[:, i * each : (i + 1) * each] for i in starts], 1)


def turn_kernel(slow, steps, backward, parts, gain, *refs):
    if backward:
        residual, cot, result, gain_grad, rows = refs[:5]
        scratch = refs[5:]
    else:
        tokens, result, rows = refs[:3]
        scratch = refs[3:]
    own, own_sems, group_sems = scratch[:3]
    me = (lax.axis_index("dp"), lax.axis_index("ctx"))
    greet(me, [member(me, by) for by in (1, 2, 4)], [])
    scatter = GroupScatter(me, parts, scratch[3:10], scratch[10:], steps)
    gathers = [GroupGather(me, rows, group_sems.at[k], own, scatter.window(k)) for k in range(steps)]
    scatter.start()
    for k in range(steps):
        scatter.send_first(k)
    for k in range(steps):
        scatter.send_second(k)
    for k in range(steps):
        span = scatter.window(k)
        for half in (0, 1):
            total = scatter.total(k, half)
            if backward:
                values = residual[half, span]
                factor = lax.rsqrt(jnp.mean(values * values, -1, keepdims=True) + norm_eps)
                normed = values * factor
                total = reordered(total, slow, True)
                part = jnp.sum(total * normed, 0, keepdims=True)
                if k == 0 and half == 0:
                    gain_grad[...] = part
                else:
                    gain_grad[...] += part
                back = total * gain[...]
                back = factor * (back - normed * jnp.mean(back * normed, -1, keepdims=True))
                back = cot[half, span].astype(jnp.float32) + back
                result[half, span] = back
                own[half, span] = back.astype(jnp.bfloat16)
            else:
                values = tokens[half, span].astype(jnp.float32) + total
                factor = lax.rsqrt(jnp.mean(values * values, -1, keepdims=True) + norm_eps)
                result[half, span] = values
                own[half, span] = reordered(values * factor * gain[...], slow, False).astype(
                    jnp.bfloat16
                )
        gathers[k].start()
        keep = pltpu.make_async_copy(own.at[:, span], rows.at[0, 0, :, span], own_sems.at[k])
        keep.start()
    for k in range(steps):
        gathers[k].pass_on()
    for k in range(steps):
        gathers[k].finish()
        span = scatter.window(k)
        pltpu.make_async_copy(own.at[:, span], rows.at[0, 0, :, span], own_sems.at[k]).wait()
    scatter.finish()


def turn(parts, gain, rows_in, slow, backward, identity):
    low, wide = jnp.bfloat16, jnp.float32
    dma = pltpu.SemaphoreType.DMA
    rows, width = parts.shape[3:]
    steps = 2
    any_space = pl.BlockSpec(memory_space=pl.ANY)
    vmem = pl.BlockSpec(memory_space=pltpu.VMEM)
    shapes = [jax.ShapeDtypeStruct((2, rows, width), wide)]
    if backward:
        shapes.append(jax.ShapeDtypeStruct((1, width), wide))
    return pl.pallas_call(
        functools.partial(turn_kernel, slow, steps, backward),
        out_shape=tuple(shapes) + (jax.ShapeDtypeStruct((2, 4, 2, rows, width), low),),
        in_specs=[any_space, vmem] + [vmem] * len(rows_in),
        out_specs=tuple([vmem] * len(shapes) + [any_space]),
        scratch_shapes=[
            pltpu.VMEM((2, rows, width), low),
            dma((steps,)),
            dma((steps, 2, 10)),
        ]
        + scatter_scratch(rows, width, steps),
        compiler_params=pltpu.CompilerParams(
            collective_id=identity, has_side_effects=True, vmem_limit_bytes=48 << 20
        ),
        cost_estimate=pl.CostEstimate(flops=0, bytes_accessed=250 << 20, transcendentals=0),
    )(parts, gain, *rows_in)


def move_kernel(splits, tokens, rows, move_sems):
    me = (lax.axis_index("dp"), lax.axis_index("ctx"))
    greet(me, [], movers_of(me, splits, False))
    move = Moves(me, splits, tokens, rows, move_sems, False)
    move.start()
    move.wait_recv()
    move.finish()


def move_tokens(tokens, splits, identity):
    any_space = pl.BlockSpec(memory_space=pl.ANY)
    return pl.pallas_call(
        functools.partial(move_kernel, splits),
        out_shape=jax.ShapeDtypeStruct(tokens.shape, tokens.dtype),
        in_specs=[any_space],
        out_specs=any_space,
        scratch_shapes=[pltpu.SemaphoreType.DMA((2, 2))],
        compiler_params=pltpu.CompilerParams(
            collective_id=identity, has_side_effects=True, vmem_limit_bytes=4 << 20
        ),
        cost_estimate=pl.CostEstimate(flops=0, bytes_accessed=40 << 20, transcendentals=0),
    )(tokens)


def spread_kernel(own, rows, group_sems, own_sem):
    me = (lax.axis_index("dp"), lax.axis_index("ctx"))
    greet(me, [member(me, by) for by in (1, 2, 4)], [])
    gather = GroupGather(me, rows, group_sems, own, slice(0, own.shape[1]))
    keep = pltpu.make_async_copy(own, rows.at[0, 0], own_sem)
    gather.start()
    keep.start()
    gather.pass_on()
    gather.finish()
    keep.wait()


def spread_group(own, identity):
    any_space = pl.BlockSpec(memory_space=pl.ANY)
    dma = pltpu.SemaphoreType.DMA
    return pl.pallas_call(
        spread_kernel,
        out_shape=jax.ShapeDtypeStruct((2, 4) + own.shape, own.dtype),
        in_specs=[any_space],
        out_specs=any_space,
        scratch_shapes=[dma((2, 10)), dma],
        compiler_params=pltpu.CompilerParams(
            collective_id=identity, has_side_effects=True, vmem_limit_bytes=4 << 20
        ),
        cost_estimate=pl.CostEstimate(flops=0, bytes_accessed=100 << 20, transcendentals=0),
    )(own)


class LineSum:
    def __init__(self, me, slow, parts, buffers, sems):
        self.parts = parts
        self.kept, self.arrived = buffers
        self.sems, self.own_sem = sems
        self.slot = me[1] // 2
        self.slow = slow
        self.line = [(me[0], me[1] ^ (2 * by)) for by in range(1, slow)]

    def hop(self, by):
        sems = (self.sems.at[0, by - 1], self.sems.at[1, by - 1])
        return remote(
            self.parts.at[self.slot ^ by], self.arrived.at[by - 1], sems, self.line[by - 1]
        )

    def own(self):
        return pltpu.make_async_copy(self.parts.at[self.slot], self.kept, self.own_sem)

    def start(self):
        for by in range(1, self.slow):
            self.hop(by).start()
        self.own().start()

    def total(self):
        self.own().wait()
        value = self.kept[...].astype(jnp.float32)
        for by in range(1, self.slow):
            self.hop(by).wait_recv()
            value = value + self.arrived[by - 1].astype(jnp.float32)
        return value

    def finish(self):
        for by in range(1, self.slow):
            self.hop(by).wait_send()


def line_scratch(shape, kind, slow):
    dma = pltpu.SemaphoreType.DMA
    return [
        pltpu.VMEM(shape, kind),
        pltpu.VMEM((slow - 1,) + shape, kind),
        dma((2, slow - 1)),
        dma,
    ]


def last_kernel(shards, splits, steps, in_parts, out_done, gate_parts, in_back, made_two, *refs):
    gain, gain_two_grad, tokens, back_rows = refs[:4]
    in_total, out_total, gate_total, gains_total, tokens_grad, block_out = refs[4:10]
    scratch = list(refs[10:])

    def take(count):
        taken = scratch[:count]
        del scratch[:count]
        return taken

    me = (lax.axis_index("dp"), lax.axis_index("ctx"))
    group, place = me
    slow = shards // 2
    slot, half = place // 2, place % 2
    owned = in_parts.shape[2]
    home = (group, half * slow + slot)
    movers = movers_of(me, splits, True)
    movers.append(((group, place % slow * 2 + place // slow), home))
    line = [(group, place ^ (2 * by)) for by in range(1, slow)]
    greet(me, [member(me, by) for by in range(1, 8)] + line, movers)
    one = take(11)
    back_sum = GroupScatter(me, in_back, one[:7], one[7:], steps)
    line_in = take(4)
    line_gains = take(4)
    in_done, gains_own, gains_done, made_one, gain_grad = take(5)
    in_sems, gate_sems, gains_sems, one_sems, two_sems, home_sems = take(6)
    in_line = LineSum(me, slow, in_parts, line_in[:2], line_in[2:])
    gains_line = LineSum(me, slow, gains_own, line_gains[:2], line_gains[2:])
    in_swap = GroupExchange(me, in_done, in_total, in_sems)
    gate_swap = GroupExchange(me, gate_parts, gate_total, gate_sems)
    gains_swap = GroupExchange(me, gains_done, gains_total, gains_sems)
    move_grad = Moves(me, splits, made_one, tokens_grad, one_sems, True)
    move_out = Moves(me, splits, made_two, block_out, two_sems, True)
    back_sum.start()
    to_home = (me, out_done, out_total, home, home_sems.at[0], home_sems.at[1])
    in_line.start()
    move_start(*to_home)
    move_out.start()
    for k in range(steps):
        back_sum.send_first(k)
    for k in range(steps):
        back_sum.send_second(k)
    for k in range(steps):
        span = back_sum.window(k)
        for part in (0, 1):
            total = back_sum.total(k, part)
            values = tokens[part, span].astype(jnp.float32)
            normed, factor = norm_parts(values)
            grad = jnp.sum(total * normed, 0, keepdims=True)
            if k == 0 and part == 0:
                gain_grad[...] = grad
            else:
                gain_grad[...] += grad
            value = back_rows[part, span] + norm_back(total * gain[...], normed, factor)
            made_one[part, span] = value.astype(jnp.bfloat16)
    move_grad.start()
    gains_own[...] = jnp.zeros_like(gains_own)
    for dp in range(4):
        for s in range(slow):
            for side in range(2):
                at = ((dp * slow + s) * 2 + side) * owned
                index = 2 * dp + side
                gains_own[s, index, 0:1, 0:owned] = gain_grad[:, at : at + owned]
                gains_own[s, index, 0:1, owned : 2 * owned] = gain_two_grad[:, at : at + owned]
    gains_line.start()
    gate_swap.start()
    in_done[...] = in_line.total().astype(jnp.bfloat16)
    in_swap.start()
    gains_done[...] = gains_line.total()
    gains_swap.start()
    pltpu.make_async_copy(out_done, out_total, home_sems.at[1]).wait()
    move_sent(*to_home)
    for swap in (in_swap, gate_swap, gains_swap):
        swap.finish()
    for move in (move_out, move_grad):
        move.wait_recv()
        move.finish()
    for part in (in_line, gains_line, back_sum):
        part.finish()


def last_sums(
    in_parts, out_done, gate_parts, in_back, out_rows, others, shards, splits, identity
):
    low, wide = jnp.bfloat16, jnp.float32
    slow = shards // 2
    steps = 2
    any_space = pl.BlockSpec(memory_space=pl.ANY)
    vmem = pl.BlockSpec(memory_space=pltpu.VMEM)
    dma = pltpu.SemaphoreType.DMA
    rows, width = in_back.shape[3:]
    gains_shape = (8, 8, 128)
    moved = jax.ShapeDtypeStruct((2, rows, width), low)
    return pl.pallas_call(
        functools.partial(last_kernel, shards, splits, steps),
        out_shape=(
            jax.ShapeDtypeStruct(in_parts.shape[1:], low),
            jax.ShapeDtypeStruct(out_done.shape, low),
            jax.ShapeDtypeStruct(gate_parts.shape, low),
            jax.ShapeDtypeStruct(gains_shape, wide),
            moved,
            moved,
        ),
        in_specs=[any_space] * 5 + [vmem] * 4,
        out_specs=(any_space,) * 6,
        scratch_shapes=scatter_scratch(rows, width, steps)
        + line_scratch(in_parts.shape[1:], low, slow)
        + line_scratch(gains_shape, wide, slow)
        + [
            pltpu.VMEM(in_parts.shape[1:], low),
            pltpu.VMEM((slow,) + gains_shape, wide),
            pltpu.VMEM(gains_shape, wide),
            pltpu.VMEM(moved.shape, low),
            pltpu.VMEM((1, width), wide),
            dma((2, 8)),
            dma((2, 8)),
            dma((2, 8)),
            dma((2, 2)),
            dma((2, 2)),
            dma((2,)),
        ],
        compiler_params=pltpu.CompilerParams(
            collective_id=identity, has_side_effects=True, vmem_limit_bytes=56 << 20
        ),
        cost_estimate=pl.CostEstimate(flops=0, bytes_accessed=300 << 20, transcendentals=0),
    )(in_parts, out_done, gate_parts, in_back, out_rows, *others)


def position_tables(blocks, rows):
    frequency = rope_base ** (-(np.arange(HEAD // 2) * 2.0 / HEAD))
    angles = np.arange(blocks * rows).reshape(blocks, rows, 1) * frequency
    cos, sin = np.cos(angles), np.sin(angles)
    cosine = np.concatenate([cos, cos, cos, cos], 2)
    sines = np.concatenate([-sin, sin, -sin, sin], 2)
    return jnp.asarray(cosine, jnp.float32), jnp.asarray(sines, jnp.float32)


def attend(order, where, qkv, tables, q_heads, kv_heads):
    seqs, length, cols = qkv.shape
    blocks = order.shape[0]
    rows = length // blocks
    whole = pl.BlockSpec(memory_space=pltpu.VMEM)
    small = pl.BlockSpec(memory_space=pltpu.SMEM)
    return pl.pallas_call(
        functools.partial(attend_kernel, q_heads, kv_heads, 256),
        out_shape=(
            jax.ShapeDtypeStruct((seqs, blocks, rows, q_heads * HEAD), jnp.bfloat16),
            jax.ShapeDtypeStruct((seqs, q_heads, length), jnp.float32),
            jax.ShapeDtypeStruct((seqs, length, cols), jnp.bfloat16),
        ),
        in_specs=[small, small, whole, whole, whole],
        out_specs=(whole, whole, whole),
        scratch_shapes=[pltpu.VMEM((blocks, rows, q_heads * HEAD), jnp.bfloat16)],
        compiler_params=pltpu.CompilerParams(vmem_limit_bytes=40 << 20),
        cost_estimate=pl.CostEstimate(
            flops=2 * seqs * length * length * q_heads * HEAD,
            bytes_accessed=100 << 20,
            transcendentals=seqs * length * length * q_heads // 2,
        ),
    )(order, where, qkv.reshape(seqs, blocks, rows, cols), *tables)


def attend_back(
    order, where, kept, back, lse, tables, out_rows, residual, out_parts, q_heads, kv_heads, identity
):
    seqs, length, cols = kept.shape
    blocks = order.shape[0]
    block = length // blocks
    group = q_heads // kv_heads
    rows, width = out_rows.shape[3:]
    steps = 2
    whole = pl.BlockSpec(memory_space=pltpu.VMEM)
    small = pl.BlockSpec(memory_space=pltpu.SMEM)
    any_space = pl.BlockSpec(memory_space=pl.ANY)
    return pl.pallas_call(
        functools.partial(attend_back_kernel, q_heads, kv_heads, 256, steps),
        out_shape=(
            jax.ShapeDtypeStruct((seqs, blocks, block, cols), jnp.bfloat16),
            jax.ShapeDtypeStruct((2, rows, width), jnp.bfloat16),
            jax.ShapeDtypeStruct(out_parts.shape[1:], jnp.bfloat16),
        ),
        in_specs=[small, small] + [whole] * 5 + [any_space, whole, any_space],
        out_specs=(whole, whole, whole),
        scratch_shapes=[
            pltpu.VMEM((length, q_heads * HEAD), jnp.bfloat16),
            pltpu.VMEM((blocks, block, cols), jnp.float32),
            pltpu.VMEM((group, length), jnp.float32),
            pltpu.VMEM((group * HEAD, length), jnp.float32),
        ]
        + line_scratch(out_parts.shape[1:], jnp.bfloat16, out_parts.shape[0])
        + scatter_scratch(rows, width, steps),
        compiler_params=pltpu.CompilerParams(
            collective_id=identity, has_side_effects=True, vmem_limit_bytes=56 << 20
        ),
        cost_estimate=pl.CostEstimate(
            flops=7 * seqs * length * length * q_heads * HEAD,
            bytes_accessed=100 << 20,
            transcendentals=seqs * length * length * q_heads // 2,
        ),
    )(
        order,
        where,
        kept,
        back.reshape(seqs, blocks, block, -1),
        lse,
        *tables,
        out_rows,
        residual,
        out_parts,
    )


def gate_update_kernel(slow, step_rate, grad, weight, first, second, new_first, new_second, new):
    units = grad.shape[2] // slow
    pieces = [grad[half, :, s * units : (s + 1) * units] for s in range(slow) for half in (0, 1)]
    gradient = jnp.concatenate(pieces, 1).astype(jnp.float32)
    new_first[...], new_second[...], new[...] = adam_update(
        weight[...], gradient, first[...], second[...], step_rate, weight_decay
    )


def gate_update(grad, weight, first, second, slow, step_rate):
    rows, width = weight.shape
    block = pl.BlockSpec((rows, width // 8), lambda side, dp: (0, 4 * side + dp))
    piece = pl.BlockSpec((2, rows, width // 16), lambda side, dp: (dp, 0, side))
    return pl.pallas_call(
        functools.partial(gate_update_kernel, slow, step_rate),
        grid=(2, 4),
        out_shape=(jax.ShapeDtypeStruct(weight.shape, jnp.float32),) * 3,
        in_specs=[piece, block, block, block],
        out_specs=(block,) * 3,
        compiler_params=pltpu.CompilerParams(vmem_limit_bytes=32 << 20),
    )(grad, weight, first, second)


def local(
    tokens,
    cotangent,
    block_order,
    attention_in,
    attention_out,
    gate_up,
    down_matrix,
    gains,
    mean_attention_in,
    mean_attention_out,
    mean_gate_up,
    mean_down,
    mean_gains,
    square_attention_in,
    square_attention_out,
    square_gate_up,
    square_down,
    square_gains,
):
    seq_count, shard_rows, width = tokens.shape
    shards = lax.axis_size("ctx")
    slow = shards // 2
    mine = lax.axis_index("dp")
    beside = lax.axis_index("ctx") % 2
    low = jnp.bfloat16
    owned = attention_in.shape[0]
    hidden_units = gate_up.shape[1] // 2
    part_hidden = hidden_units // 8
    units = down_matrix.shape[0]
    part_q = HEADS * HEAD // 8
    part_k = KV_HEADS * HEAD // 8
    part_cols = part_q + 2 * part_k
    count = seq_count * shard_rows
    together = 8 * count
    spread = shards // (4 * seq_count)
    splits = max(1, slow // 8)
    seqs = 2 // spread if spread < 2 else 1
    length = shards * shard_rows
    q_heads = HEADS // 8 // splits
    kv_heads = KV_HEADS // 8

    in_low = attention_in.astype(low)
    gains_row = jnp.pad(gains.astype(low).reshape(1, -1), ((0, 15), (0, part_cols - 2 * owned)))
    pieces = jnp.stack(
        [
            jnp.concatenate(
                [
                    jnp.concatenate(
                        [
                            in_low[:, i * part_q : (i + 1) * part_q],
                            in_low[:, 8 * part_q + i * part_k :][:, :part_k],
                            in_low[:, 8 * (part_q + part_k) + i * part_k :][:, :part_k],
                        ],
                        1,
                    ),
                    gains_row,
                ]
            )
            for i in range(8)
        ]
    )
    gate_low = gate_up.astype(low)
    gate_pieces = jnp.stack(
        [
            jnp.concatenate(
                [
                    gate_low[:, side * hidden_units + (dp * shards + 2 * s + half) * units :][
                        :, :units
                    ]
                    for side in range(2)
                    for s in range(slow)
                ],
                1,
            )
            for dp in range(4)
            for half in range(2)
        ]
    )
    tokens_all, in_all, w_out, gate_rows = first_exchange(
        tokens, pieces, attention_out.astype(low), gate_pieces, shards, spread, 1
    )
    in_all = in_all.reshape(slow, 4, 2, owned + 16, part_cols).swapaxes(0, 1)
    w_in = in_all[:, :, :, :owned].reshape(width, part_cols)
    w_out = w_out.reshape(part_q, width)
    gains_all = in_all[:, :, :, owned, : 2 * owned].reshape(-1, 2, owned)
    gains_all = gains_all.astype(jnp.float32).swapaxes(0, 1).reshape(2, width)
    gain_one, gain_two = gains_all[0], gains_all[1]
    w_gate = gather_line(gate_rows.reshape(8 * owned, 2 * part_hidden))

    normed_all, _ = norm_parts(tokens_all.reshape(together, width).astype(jnp.float32))
    input_one = (normed_all * gain_one).astype(low)
    qkv = dot_nn(input_one, w_in)
    orders = block_order.reshape(2 * splits if spread > 1 else 1, 4, -1)
    slot_order = jnp.concatenate(
        [
            orders[(2 * s + (beside ^ i)) if spread > 1 else 0, part_owner(mine ^ j)]
            for s in range(splits)
            for i in range(2 // seqs)
            for j in range(4)
        ]
    )
    tables = position_tables(slot_order.shape[0], length // slot_order.shape[0])
    groups = [
        [2 * (s * splits + g) + half for g in range(splits)]
        for s in range(slow // splits)
        for half in (0, 1)
    ]

    def split_heads(values, widths, copies):
        parts = []
        start = 0
        for each, repeat in zip(widths, copies):
            kinds = splits // repeat
            piece = values[:, start : start + kinds * each].reshape(-1, kinds, each)
            parts.append(jnp.repeat(piece.swapaxes(0, 1), repeat, axis=0))
            start += kinds * each
        sent = jnp.concatenate(parts, 2)
        got = lax.all_to_all(sent, "ctx", 0, 0, axis_index_groups=groups, tiled=True)
        return got.reshape(length, -1)

    def join_heads(values):
        sent = values.reshape(splits, together, -1)
        return lax.all_to_all(sent, "ctx", 0, 0, axis_index_groups=groups, tiled=True)

    q_width, k_width = q_heads * HEAD, kv_heads * HEAD
    if splits > 1:
        qkv = split_heads(qkv, (q_width, k_width, k_width), (1, splits, splits))
    qkv = qkv.reshape(seqs, length, -1)
    blocks = slot_order.shape[0]
    slot_where = jnp.sum(
        jnp.where(
            slot_order[None, :] == jnp.arange(blocks, dtype=jnp.int32)[:, None],
            jnp.arange(blocks, dtype=jnp.int32)[None, :],
            0,
        ),
        1,
    )
    attended, lse, kept = attend(slot_order, slot_where, qkv, tables, q_heads, kv_heads)
    if splits > 1:
        attended = join_heads(attended.reshape(length, q_width)).swapaxes(0, 1)
    attended = attended.reshape(together, part_q)

    def parts(values):
        return values.astype(low).reshape((2, 4) + tokens.shape)

    residual_rows, input_two = turn(
        parts(dot_nn(attended, w_out)), gain_two[None], [tokens_all[0, 0]], slow, False, 3
    )
    input_two = input_two.reshape(together, width)
    after = 0.0 * (residual_rows[0, 0, 0] + w_gate[0, 0].astype(jnp.float32))
    cot_rows = move_tokens(cotangent + after.astype(low), spread, 7)
    after = 0.0 * cot_rows[0, 0, 0].astype(jnp.float32)
    w_down = gather_line((down_matrix + after).astype(low))
    gate_both = dot_nn(input_two, w_gate)
    gate_part = gate_both[:, :part_hidden]
    up_part = gate_both[:, part_hidden:]
    sigmoid_gate = jax.nn.sigmoid(gate_part)
    active = gate_part * sigmoid_gate
    hidden = lax.optimization_barrier((active * up_part).astype(low))
    back_all = spread_group(cot_rows + 0.0 * hidden[0, 0], 2).reshape(together, width)
    grad_down = lax.optimization_barrier(dot_tn(hidden, back_all).astype(low))
    down_sum = sum_line(grad_down + 0.0 * w_down[0, 0]).astype(jnp.float32)
    back_hidden = dot_nt(back_all, w_down + 0.0 * hidden[0, 0])
    back_gate = back_hidden * up_part * sigmoid_gate * (1.0 + gate_part * (1.0 - sigmoid_gate))
    back_upper = back_hidden * active
    back_gate_up = jnp.concatenate([back_gate, back_upper], 1).astype(low)
    gate_low = sum_line(dot_tn(input_two, back_gate_up).astype(low))
    back_rows, grad_gain_two, back_residual_all = turn(
        parts(dot_nt(back_gate_up, w_gate)),
        gain_two[None],
        [residual_rows, cot_rows],
        slow,
        True,
        4,
    )
    back_residual_all = back_residual_all.reshape(together, width)
    grad_out = dot_tn(attended, back_residual_all).astype(low)
    back_attended = dot_nt(back_residual_all, w_out).astype(low)
    if splits > 1:
        back_attended = split_heads(back_attended, (q_width,), (1,))
    back_projected, output_rows, out_sum = attend_back(
        slot_order,
        slot_where,
        kept,
        back_attended.reshape(seqs, length, -1),
        lse,
        tables,
        parts(dot_nn(hidden, w_down)),
        residual_rows,
        grad_out.reshape(slow, owned, width),
        q_heads,
        kv_heads,
        6,
    )
    if splits > 1:
        back_projected = join_heads(back_projected.reshape(length, -1)).astype(jnp.float32)
        back_projected = jnp.concatenate(
            [
                back_projected[..., :q_width].swapaxes(0, 1).reshape(together, part_q),
                back_projected[..., q_width:].sum(0),
            ],
            1,
        ).astype(low)
    back_projected = back_projected.reshape(together, part_cols)
    grad_in = dot_tn(input_one, back_projected).astype(low)
    grad_in = grad_in.reshape(4, slow, 2 * owned, part_cols).swapaxes(0, 1)
    in_sum, out_sum, gate_sum, gains_sum, tokens_grad, block_out = last_sums(
        grad_in.reshape(slow, 8, owned, part_cols),
        out_sum,
        gate_low.reshape(8, owned, 2 * part_hidden),
        parts(dot_nt(back_projected, w_in)),
        output_rows,
        [gain_one[None], grad_gain_two, tokens_all[0, 0], back_rows],
        shards,
        spread,
        5,
    )
    tokens_grad = tokens_grad.astype(jnp.float32)
    out_sum = out_sum.astype(jnp.float32)
    gains_sum = gains_sum[:, 0, : 2 * owned].reshape(8, 2, owned).sum(0)
    cuts = ((0, part_q), (part_q, part_q + part_k), (part_q + part_k, part_cols))
    in_sum = jnp.concatenate(
        [in_sum[i, :, first:last] for first, last in cuts for i in range(8)], 1
    ).astype(jnp.float32)
    new_in = adam_update(
        attention_in,
        in_sum,
        mean_attention_in,
        square_attention_in,
        input_boost * D ** (-0.5),
        weight_decay,
    )
    new_out = adam_update(
        attention_out,
        out_sum,
        mean_attention_out,
        square_attention_out,
        (HEADS * HEAD // 32) ** (-0.5),
        weight_decay,
    )
    new_gate = gate_update(
        gate_sum, gate_up, mean_gate_up, square_gate_up, slow, D ** (-0.5)
    )
    new_down = adam_update(
        down_matrix, down_sum, mean_down, square_down, FF ** (-0.5), weight_decay
    )
    new_gain = adam_update(gains, gains_sum, mean_gains, square_gains, gain_rate, 0.0)
    return (
        block_out,
        tokens_grad,
        new_in[0],
        new_in[1],
        new_in[2],
        new_out[0],
        new_out[1],
        new_out[2],
        new_gate[0],
        new_gate[1],
        new_gate[2],
        new_down[0],
        new_down[1],
        new_down[2],
        new_gain[0],
        new_gain[1],
        new_gain[2],
    )


def solution(mesh):
    in_specs = (
        P("dp", "ctx", None),
        P("dp", "ctx", None),
        P(),
        P(("dp", "ctx"), None),
        P(("dp", "ctx"), None),
        P(("dp", "ctx"), None),
        P(("dp", "ctx"), None),
        P(None, ("dp", "ctx")),
        P(("dp", "ctx"), None),
        P(("dp", "ctx"), None),
        P(("dp", "ctx"), None),
        P(("dp", "ctx"), None),
        P(None, ("dp", "ctx")),
        P(("dp", "ctx"), None),
        P(("dp", "ctx"), None),
        P(("dp", "ctx"), None),
        P(("dp", "ctx"), None),
        P(None, ("dp", "ctx")),
    )
    out_specs = (
        P("dp", "ctx", None),
        P("dp", "ctx", None),
        P(("dp", "ctx"), None),
        P(("dp", "ctx"), None),
        P(("dp", "ctx"), None),
        P(("dp", "ctx"), None),
        P(("dp", "ctx"), None),
        P(("dp", "ctx"), None),
        P(("dp", "ctx"), None),
        P(("dp", "ctx"), None),
        P(("dp", "ctx"), None),
        P(("dp", "ctx"), None),
        P(("dp", "ctx"), None),
        P(("dp", "ctx"), None),
        P(None, ("dp", "ctx")),
        P(None, ("dp", "ctx")),
        P(None, ("dp", "ctx")),
    )
    return jax.shard_map(local, mesh=mesh, in_specs=in_specs, out_specs=out_specs, check_vma=False)
```

```python
import functools

import jax
import jax.numpy as jnp
import numpy as np
from jax import lax
from jax.experimental import pallas as pl
from jax.experimental.pallas import tpu as pltpu
from jax.sharding import PartitionSpec as P

D = 2048
HEADS = 32
KV_HEADS = 8
HEAD = 64
FF = 8192
STEP = 5


norm_eps = 1e-05
rope_base = 500000.0
beta_one = 0.9
beta_two = 0.95
gain_rate = 1.25
input_boost = 2.5
weight_decay = 0.1
adam_eps = 1e-08
masked_score = -1e30


def norm_parts(values):
    factor = lax.rsqrt(jnp.mean(values * values, -1, keepdims=True) + norm_eps)
    return (values * factor, factor)


def norm_back(back_normed, normed, factor):
    return factor * (back_normed - normed * jnp.mean(back_normed * normed, -1, keepdims=True))


def adam_update(weight, gradient, first_moment, second_moment, step_rate, decay_rate):
    first_new = beta_one * first_moment + (1.0 - beta_one) * gradient
    second_new = beta_two * second_moment + (1.0 - beta_two) * gradient * gradient
    update = (
        first_new
        / (1.0 - beta_one**STEP)
        / (jnp.sqrt(second_new / (1.0 - beta_two**STEP)) + adam_eps)
    )
    return (first_new, second_new, weight - step_rate * (update + decay_rate * weight))


def line_groups(shards):
    return [[2 * s + half for s in range(shards // 2)] for half in (0, 1)]


def gather_line(rows):
    return lax.all_gather(
        rows, "ctx", axis=0, tiled=True, axis_index_groups=line_groups(lax.axis_size("ctx"))
    )


def sum_line(gradient):
    return lax.psum_scatter(
        gradient,
        "ctx",
        scatter_dimension=0,
        tiled=True,
        axis_index_groups=line_groups(lax.axis_size("ctx")),
    )


def dot_nn(a, b):
    return lax.dot_general(a, b, (((1,), (0,)), ((), ())), preferred_element_type=jnp.float32)


def dot_nt(a, b):
    return lax.dot_general(a, b, (((1,), (1,)), ((), ())), preferred_element_type=jnp.float32)


def dot_tn(a, b):
    return lax.dot_general(a, b, (((0,), (0,)), ((), ())), preferred_element_type=jnp.float32)


def causal_keep(tile):
    keys = lax.broadcasted_iota(jnp.int32, (tile, tile), 0)
    queries = lax.broadcasted_iota(jnp.int32, (tile, tile), 1)
    return keys <= queries


def turn_group(values, cos, sin, forward):
    lanes = lax.broadcasted_iota(jnp.int32, values.shape, 1)
    other = jnp.where(
        lanes % HEAD < HEAD // 2,
        pltpu.roll(values, 2 * HEAD - HEAD // 2, 1),
        pltpu.roll(values, HEAD // 2, 1),
    )
    if forward:
        return values * cos + other * sin
    return values * cos - other * sin


def turn_columns(values, start, turned_cols, cos, sin, forward):
    if start >= turned_cols:
        return values
    turned = turn_group(values, cos, sin, forward)
    if start + 2 * HEAD <= turned_cols:
        return turned
    lanes = lax.broadcasted_iota(jnp.int32, values.shape, 1)
    return jnp.where(lanes < turned_cols - start, turned, values)


def attend_kernel(
    q_heads,
    kv_heads,
    tile,
    order_ref,
    where_ref,
    all_qkv_ref,
    cos_ref,
    sin_ref,
    all_out_ref,
    all_lse_ref,
    all_kept_ref,
    made,
):
    for sequence in range(all_qkv_ref.shape[0]):
        attend_sequence(
            q_heads,
            kv_heads,
            tile,
            order_ref,
            where_ref,
            all_qkv_ref.at[sequence],
            cos_ref,
            sin_ref,
            all_out_ref.at[sequence],
            all_lse_ref.at[sequence],
            all_kept_ref.at[sequence],
            made,
        )


def attend_sequence(
    q_heads,
    kv_heads,
    tile,
    order_ref,
    where_ref,
    qkv_ref,
    cos_ref,
    sin_ref,
    out_ref,
    lse_ref,
    kept_ref,
    made,
):
    blocks, rows, cols = qkv_ref.shape
    length = blocks * rows
    group = q_heads // kv_heads
    q_cols, k_cols = q_heads * HEAD, kv_heads * HEAD
    scale = HEAD ** (-0.5)

    def take_block(i, _):
        start = pl.multiple_of(i * rows, rows)
        cos = cos_ref[i]
        sin = sin_ref[i]
        for c in range(0, cols, 2 * HEAD):
            values = qkv_ref[where_ref[i], :, c : c + 2 * HEAD]
            values = turn_columns(values, c, q_cols + k_cols, cos, sin, True)
            kept_ref[pl.ds(start, rows), c : c + 2 * HEAD] = values.astype(jnp.bfloat16)
        return 0

    lax.fori_loop(0, blocks, take_block, 0)
    keep = causal_keep(tile)
    for kv in range(kv_heads):
        k_at = q_cols + kv * HEAD
        v_at = q_cols + k_cols + kv * HEAD

        def query_step(i, _):
            q_start = pl.multiple_of(i * tile, tile)
            queries = [
                kept_ref[
                    pl.ds(q_start, tile), (kv * group + g) * HEAD : (kv * group + g + 1) * HEAD
                ]
                for g in range(group)
            ]

            def key_tile(j, carry, masked):
                k_start = pl.multiple_of(j * tile, tile)
                keys = kept_ref[pl.ds(k_start, tile), k_at : k_at + HEAD]
                values = kept_ref[pl.ds(k_start, tile), v_at : v_at + HEAD]
                result = []
                for g in range(group):
                    peak, total, weighted = carry[g]
                    scores = dot_nt(keys, queries[g]) * scale
                    if masked:
                        scores = jnp.where(keep, scores, masked_score)
                    new_peak = jnp.maximum(peak, jnp.max(scores, 0, keepdims=True))
                    weights = jnp.exp(scores - new_peak)
                    shrink = jnp.exp(peak - new_peak)
                    total = total * shrink + jnp.sum(weights, 0, keepdims=True)
                    weighted = weighted * shrink + dot_tn(values, weights.astype(jnp.bfloat16))
                    result.append((new_peak, total, weighted))
                return tuple(result)

            start = tuple(
                (
                    jnp.full((1, tile), masked_score, jnp.float32),
                    jnp.zeros((1, tile), jnp.float32),
                    jnp.zeros((HEAD, tile), jnp.float32),
                )
                for _ in range(group)
            )
            carry = lax.fori_loop(0, i, lambda j, c: key_tile(j, c, False), start)
            carry = key_tile(i, carry, True)
            for g in range(group):
                head = kv * group + g
                peak, total, weighted = carry[g]
                lse_ref[head : head + 1, pl.ds(q_start, tile)] = peak + jnp.log(total)
                made[pl.ds(i * (tile // rows), tile // rows), :, head * HEAD : (head + 1) * HEAD] = (
                    (weighted / total).T.astype(jnp.bfloat16).reshape(-1, rows, HEAD)
                )
            return 0

        lax.fori_loop(0, length // tile, query_step, 0)

    def give_block(i, _):
        out_ref[i] = made[order_ref[i]]
        return 0

    lax.fori_loop(0, blocks, give_block, 0)


def attend_back_kernel(
    q_heads,
    kv_heads,
    tile,
    steps,
    order_ref,
    where_ref,
    all_kept_ref,
    all_back_ref,
    all_lse_ref,
    cos_ref,
    sin_ref,
    out_rows,
    residual,
    out_parts,
    all_out_ref,
    block_out,
    out_sum,
    *scratch,
):
    me = (lax.axis_index("dp"), lax.axis_index("ctx"))
    slow = out_parts.shape[0]
    line = [(me[0], me[1] ^ (2 * by)) for by in range(1, slow)]
    greet(me, [member(me, by) for by in (1, 2, 4)] + line, [])
    work, line_out, scratch = scratch[:4], scratch[4:8], scratch[8:]
    scatter = GroupScatter(me, out_rows, scratch[:7], scratch[7:], steps)
    out_line = LineSum(me, slow, out_parts, line_out[:2], line_out[2:])

    def one():
        for k in range(steps):
            scatter.send_first(k)

    def two():
        for k in range(steps):
            scatter.send_second(k)

    def three():
        for k in range(steps):
            span = scatter.window(k)
            for part in (0, 1):
                value = residual[part, span] + scatter.total(k, part)
                block_out[part, span] = value.astype(jnp.bfloat16)

    tasks = [one, two, three]

    def pause():
        if tasks:
            tasks.pop(0)()

    scatter.start()
    out_line.start()
    for sequence in range(all_kept_ref.shape[0]):
        attend_back_sequence(
            q_heads,
            kv_heads,
            tile,
            pause,
            order_ref,
            where_ref,
            all_kept_ref.at[sequence],
            all_back_ref.at[sequence],
            all_lse_ref.at[sequence],
            cos_ref,
            sin_ref,
            all_out_ref.at[sequence],
            *work,
        )
    while tasks:
        pause()
    out_sum[...] = out_line.total().astype(jnp.bfloat16)
    out_line.finish()
    scatter.finish()


def attend_back_sequence(
    q_heads,
    kv_heads,
    tile,
    pause,
    order_ref,
    where_ref,
    kept_ref,
    back_ref,
    lse_ref,
    cos_ref,
    sin_ref,
    out_ref,
    back_sorted,
    grad,
    delta_ref,
    dq_ref,
):
    length, cols = kept_ref.shape
    blocks, rows = back_ref.shape[:2]
    group = q_heads // kv_heads
    q_cols, k_cols = q_heads * HEAD, kv_heads * HEAD
    scale = HEAD ** (-0.5)
    tiles = length // tile

    def take_block(i, _):
        start = pl.multiple_of(i * rows, rows)
        back_sorted[pl.ds(start, rows), :] = back_ref[where_ref[i]]
        return 0

    lax.fori_loop(0, blocks, take_block, 0)
    keep = causal_keep(tile)
    for kv in range(kv_heads):
        k_at = q_cols + kv * HEAD
        v_at = q_cols + k_cols + kv * HEAD

        def load(i, g):
            start = pl.multiple_of(i * tile, tile)
            head = kv * group + g
            at = slice(head * HEAD, (head + 1) * HEAD)
            return (
                kept_ref[pl.ds(start, tile), at],
                back_sorted[pl.ds(start, tile), at],
                lse_ref[head : head + 1, pl.ds(start, tile)],
            )

        def load_kv(j):
            start = pl.multiple_of(j * tile, tile)
            return (
                kept_ref[pl.ds(start, tile), k_at : k_at + HEAD],
                kept_ref[pl.ds(start, tile), v_at : v_at + HEAD],
            )

        def tile_terms(keys, values, query, back, lse, masked):
            weights = jnp.exp(dot_nt(keys, query) * scale - lse)
            if masked:
                weights = jnp.where(keep, weights, 0.0)
            return weights, dot_nt(values, back)

        def delta_step(i, _):
            rows_i = [load(i, g) for g in range(group)]

            def one(j, carry, masked):
                keys, values = load_kv(j)
                result = []
                for g in range(group):
                    weights, back_weights = tile_terms(keys, values, *rows_i[g], masked)
                    result.append(carry[g] + jnp.sum(weights * back_weights, 0, keepdims=True))
                return tuple(result)

            carry = tuple(jnp.zeros((1, tile), jnp.float32) for _ in range(group))
            carry = lax.fori_loop(0, i, lambda j, c: one(j, c, False), carry)
            carry = one(i, carry, True)
            for g in range(group):
                delta_ref[g : g + 1, pl.ds(pl.multiple_of(i * tile, tile), tile)] = carry[g]
            return 0

        lax.fori_loop(0, tiles, delta_step, 0)
        if kv == 0:
            pause()
        dq_ref[...] = jnp.zeros_like(dq_ref)

        def key_step(j, _):
            keys, values = load_kv(j)

            def one(i, carry, masked):
                back_key, back_value = carry
                start = pl.multiple_of(i * tile, tile)
                for g in range(group):
                    query, back, lse = load(i, g)
                    weights, back_weights = tile_terms(keys, values, query, back, lse, masked)
                    delta = delta_ref[g : g + 1, pl.ds(start, tile)]
                    back_scores = (weights * (back_weights - delta)).astype(jnp.bfloat16)
                    back_key = back_key + dot_nn(back_scores, query)
                    back_value = back_value + dot_nn(weights.astype(jnp.bfloat16), back)
                    dq_ref[g * HEAD : (g + 1) * HEAD, pl.ds(start, tile)] += dot_tn(
                        keys, back_scores
                    )
                return back_key, back_value

            zero = jnp.zeros((tile, HEAD), jnp.float32)
            carry = one(j, (zero, zero), True)
            carry = lax.fori_loop(j + 1, tiles, lambda i, c: one(i, c, False), carry)
            span = pl.ds(j * (tile // rows), tile // rows)
            grad[span, :, k_at : k_at + HEAD] = (carry[0] * scale).reshape(-1, rows, HEAD)
            grad[span, :, v_at : v_at + HEAD] = carry[1].reshape(-1, rows, HEAD)
            return 0

        lax.fori_loop(0, tiles, key_step, 0)
        for g in range(group):
            head = kv * group + g
            turned = (dq_ref[g * HEAD : (g + 1) * HEAD, :] * scale).T
            grad[:, :, head * HEAD : (head + 1) * HEAD] = turned.reshape(-1, rows, HEAD)

    def give_block(i, _):
        cos = cos_ref[order_ref[i]]
        sin = sin_ref[order_ref[i]]
        for c in range(0, cols, 2 * HEAD):
            values = grad[order_ref[i], :, c : c + 2 * HEAD]
            values = turn_columns(values, c, q_cols + k_cols, cos, sin, False)
            out_ref[i, :, c : c + 2 * HEAD] = values.astype(jnp.bfloat16)
        return 0

    lax.fori_loop(0, blocks, give_block, 0)


MESH = pl.DeviceIdType.MESH


def sequence_target(group, place, second, splits):
    sequence = 2 * group + second
    held_at = sequence % 4 * 2 + (sequence % 2 ^ sequence // 4)
    slot = place // 2
    target = (place % 2 * 2 + slot % 4 // 2, held_at * splits + slot // 4)
    return target, slot % 2


def token_target(group, place, half, splits):
    held_at = place // splits
    sequence = (held_at % 2 ^ held_at // 2 % 2) * 4 + held_at // 2
    slot = place % splits * 4 + group % 2 * 2 + half
    return (sequence // 2, 2 * slot + group // 2), sequence % 2


def remote(source, target, sems, device):
    return pltpu.make_async_remote_copy(
        src_ref=source,
        dst_ref=target,
        send_sem=sems[0],
        recv_sem=sems[1],
        device_id=device,
        device_id_type=MESH,
    )


def same(one, other):
    return jnp.logical_and(one[0] == other[0], one[1] == other[1])


def greet(me, peers, movers):
    barrier = pltpu.get_barrier_semaphore()
    for peer in peers:
        pl.semaphore_signal(barrier, inc=1, device_id=peer, device_id_type=MESH)
    expected = len(peers)
    for source, target in movers:

        @pl.when(jnp.logical_not(same(source, me)))
        def _():
            pl.semaphore_signal(barrier, inc=1, device_id=source, device_id_type=MESH)

        expected = expected + jnp.where(same(target, me), 0, 1)
    pl.semaphore_wait(barrier, expected)


def move_start(me, source, target, target_device, send, receive):
    here = same(target_device, me)

    @pl.when(here)
    def _():
        pltpu.make_async_copy(source, target, receive).start()

    @pl.when(jnp.logical_not(here))
    def _():
        remote(source, target, (send, receive), target_device).start()


def move_sent(me, source, target, target_device, send, receive):
    @pl.when(jnp.logical_not(same(target_device, me)))
    def _():
        remote(source, target, (send, receive), target_device).wait_send()


def member(me, by):
    return (me[0] ^ (by // 2), me[1] ^ (by % 2))


def group_index(device):
    return 2 * device[0] + device[1] % 2


class GroupExchange:
    def __init__(self, me, pieces, got, sems):
        self.me, self.pieces, self.got, self.sems = me, pieces, got, sems

    def hop(self, by):
        peer = member(self.me, by)
        sems = (self.sems.at[0, by - 1], self.sems.at[1, by - 1])
        return remote(
            self.pieces.at[group_index(peer)], self.got.at[group_index(self.me)], sems, peer
        )

    def own(self):
        mine = group_index(self.me)
        return pltpu.make_async_copy(self.pieces.at[mine], self.got.at[mine], self.sems.at[0, 7])

    def start(self):
        for by in range(1, 8):
            self.hop(by).start()
        self.own().start()

    def finish(self):
        self.own().wait()
        for by in range(1, 8):
            self.hop(by).wait()


class GroupGather:
    def __init__(self, me, rows, sems, own, window):
        self.rows, self.sems, self.own, self.window = rows, sems, own, window
        self.core, self.across, self.beside = member(me, 2), member(me, 4), member(me, 1)

    def hop(self, index):
        across, beside, core = self.across, self.beside, self.core
        source, i, j, half, device = (
            (None, 0, 2, 0, across),
            (None, 1, 0, 1, beside),
            (None, 1, 0, 0, beside),
            (None, 0, 2, 1, across),
            ((0, 2), 1, 2, 0, beside),
            ((1, 0), 1, 2, 1, across),
            (None, 0, 1, slice(0, 2), core),
            ((0, 2), 0, 3, slice(0, 2), core),
            ((1, 0), 1, 1, slice(0, 2), core),
            ((1, 2), 1, 3, slice(0, 2), core),
        )[index]
        if source is None:
            source = self.own.at[half, self.window]
        else:
            source = self.rows.at[source[0], source[1], half, self.window]
        target = self.rows.at[i, j, half, self.window]
        return remote(source, target, (self.sems.at[0, index], self.sems.at[1, index]), device)

    def start(self):
        for index in (0, 1, 2, 3, 6):
            self.hop(index).start()

    def pass_on(self):
        self.hop(0).wait_recv()
        self.hop(4).start()
        self.hop(1).wait_recv()
        self.hop(5).start()
        self.hop(3).wait_recv()
        self.hop(7).start()
        self.hop(2).wait_recv()
        self.hop(8).start()

    def finish(self):
        self.hop(4).wait_recv()
        self.hop(5).wait_recv()
        self.hop(9).start()
        for index in (6, 7, 8, 9):
            self.hop(index).wait_recv()
        for index in range(10):
            self.hop(index).wait_send()


class Moves:
    def __init__(self, me, splits, source, target, sems, back):
        self.me, self.splits, self.source, self.target = me, splits, source, target
        self.sems, self.back = sems, back

    def one(self, i):
        find = token_target if self.back else sequence_target
        device, place = find(self.me[0], self.me[1], i, self.splits)
        return (
            self.me,
            self.source.at[i],
            self.target.at[place],
            device,
            self.sems.at[0, i],
            self.sems.at[1, place],
        )

    def start(self):
        for i in (0, 1):
            move_start(*self.one(i))

    def wait_recv(self):
        for i in (0, 1):
            pltpu.make_async_copy(self.source.at[0], self.target.at[i], self.sems.at[1, i]).wait()

    def finish(self):
        for i in (0, 1):
            move_sent(*self.one(i))


def movers_of(me, splits, back):
    into = [sequence_target(me[0], me[1], i, splits)[0] for i in (0, 1)]
    home = [token_target(me[0], me[1], i, splits)[0] for i in (0, 1)]
    return list(zip(into, home)) if back else list(zip(home, into))


def first_kernel(shards, splits, tokens, pieces, out_own, gate_pieces, *refs):
    rows, in_all, out_all, gate_rows, held = refs[:5]
    move_sems, group_sems, piece_sems, gate_sems, own_sem, in_sems, out_sems = refs[5:]
    me = (lax.axis_index("dp"), lax.axis_index("ctx"))
    group, place = me
    slow = shards // 2
    slot = place // 2
    line = [(group, place ^ (2 * by)) for by in range(1, slow)]
    wanted, block = place // slow, place % slow
    takers = [(group, 2 * (slot ^ by) + wanted) for by in range(slow)]
    givers = [(group, place % 2 * slow + block_by) for block_by in range(slow)]
    movers = movers_of(me, splits, False) + list(zip(givers, takers))
    greet(me, [member(me, by) for by in range(1, 8)] + line, movers)
    swap = GroupExchange(me, pieces, held, piece_sems)
    gate_swap = GroupExchange(me, gate_pieces, gate_rows, gate_sems)
    move = Moves(me, splits, tokens, rows.at[0, 0], move_sems, False)

    def in_line(by):
        sems = (in_sems.at[0, by - 1], in_sems.at[1, by - 1])
        return remote(held, in_all.at[slot], sems, line[by - 1])

    def out_send(by):
        return (
            me,
            out_own,
            out_all.at[block],
            takers[by],
            out_sems.at[0, by],
            out_sems.at[1, block],
        )

    own = pltpu.make_async_copy(held, in_all.at[slot], own_sem)
    move.start()
    swap.start()
    gate_swap.start()
    swap.finish()
    move.wait_recv()
    spread = GroupGather(me, rows, group_sems, rows.at[0, 0], slice(0, tokens.shape[1]))
    spread.start()
    for by in range(1, slow):
        in_line(by).start()
    own.start()
    for by in range(slow):
        move_start(*out_send(by))
    spread.pass_on()
    for by in range(1, slow):
        in_line(by).wait()
    spread.finish()
    own.wait()
    for by in range(slow):
        pltpu.make_async_copy(out_own, out_all.at[by], out_sems.at[1, by]).wait()
    for by in range(slow):
        move_sent(*out_send(by))
    gate_swap.finish()
    move.finish()


def first_exchange(tokens, pieces, out_own, gate_pieces, shards, splits, identity):
    low = jnp.bfloat16
    slow = shards // 2
    any_space = pl.BlockSpec(memory_space=pl.ANY)
    dma = pltpu.SemaphoreType.DMA
    made = pl.pallas_call(
        functools.partial(first_kernel, shards, splits),
        out_shape=(
            jax.ShapeDtypeStruct((2, 4) + tokens.shape, low),
            jax.ShapeDtypeStruct((slow,) + pieces.shape, low),
            jax.ShapeDtypeStruct((slow,) + out_own.shape, low),
            jax.ShapeDtypeStruct(gate_pieces.shape, low),
            jax.ShapeDtypeStruct(pieces.shape, low),
        ),
        in_specs=[any_space] * 4,
        out_specs=(any_space,) * 5,
        scratch_shapes=[
            dma((2, 2)),
            dma((2, 10)),
            dma((2, 8)),
            dma((2, 8)),
            dma,
            dma((2, slow - 1)),
            dma((2, slow)),
        ],
        compiler_params=pltpu.CompilerParams(
            collective_id=identity, has_side_effects=True, vmem_limit_bytes=8 << 20
        ),
        cost_estimate=pl.CostEstimate(flops=0, bytes_accessed=200 << 20, transcendentals=0),
    )(tokens, pieces, out_own, gate_pieces)
    return made[:4]


class GroupScatter:
    def __init__(self, me, parts, buffers, sems, steps):
        self.parts = parts
        self.core_in, self.kept, self.sent, self.came, self.held = buffers[:5]
        self.sent_last, self.came_last = buffers[5:]
        self.core_sems, self.kept_sems, self.one_sems, self.last_sems = sems
        self.core, self.across, self.beside = member(me, 2), member(me, 4), member(me, 1)
        self.size = parts.shape[3] // steps
        self.steps = steps

    def window(self, k):
        return slice(k * self.size, (k + 1) * self.size)

    def to_core(self, k, j):
        return remote(
            self.parts.at[:, 2 * j + 1, :, self.window(k)],
            self.core_in.at[:, j, :, self.window(k)],
            (self.core_sems.at[0, k, j], self.core_sems.at[1, k, j]),
            self.core,
        )

    def keep(self, k, j):
        return pltpu.make_async_copy(
            self.parts.at[:, 2 * j, :, self.window(k)],
            self.kept.at[:, j, :, self.window(k)],
            self.kept_sems.at[k, j],
        )

    def first(self, k, half):
        return remote(
            self.sent.at[half, :, self.window(k)],
            self.came.at[half, :, self.window(k)],
            (self.one_sems.at[0, k, half], self.one_sems.at[1, k, half]),
            (self.beside, self.across)[half],
        )

    def second(self, k, half):
        return remote(
            self.sent_last.at[half, self.window(k)],
            self.came_last.at[half, self.window(k)],
            (self.last_sems.at[0, k, half], self.last_sems.at[1, k, half]),
            (self.across, self.beside)[half],
        )

    def start(self):
        for k in range(self.steps):
            for j in (0, 1):
                self.to_core(k, j).start()
                self.keep(k, j).start()

    def send_first(self, k):
        wide = jnp.float32
        rows = self.window(k)
        for j in (0, 1):
            self.keep(k, j).wait()
            self.to_core(k, j).wait_recv()
        for half in (0, 1):
            for other in (0, 1):
                at = (1, other) if half == 0 else (other, 1)
                both = self.kept[at[0], at[1], half, rows].astype(wide)
                both = both + self.core_in[at[0], at[1], half, rows].astype(wide)
                self.sent[half, other, rows] = both.astype(jnp.bfloat16)
            self.first(k, half).start()
        for half in (0, 1):
            for other in (0, 1):
                at = (0, other) if half == 0 else (other, 0)
                both = self.kept[at[0], at[1], half, rows].astype(wide)
                self.held[half, other, rows] = both + self.core_in[at[0], at[1], half, rows].astype(
                    wide
                )

    def send_second(self, k):
        wide = jnp.float32
        rows = self.window(k)
        for half in (0, 1):
            self.first(k, half).wait_recv()
            both = self.held[half, 1, rows] + self.came[half, 1, rows].astype(wide)
            self.sent_last[half, rows] = both.astype(jnp.bfloat16)
            self.second(k, half).start()
            self.held[half, 0, rows] = self.held[half, 0, rows] + self.came[half, 0, rows].astype(
                wide
            )

    def total(self, k, half):
        self.second(k, half).wait_recv()
        rows = self.window(k)
        return self.held[half, 0, rows] + self.came_last[half, rows].astype(jnp.float32)

    def finish(self):
        for k in range(self.steps):
            for j in (0, 1):
                self.to_core(k, j).wait_send()
            for half in (0, 1):
                self.first(k, half).wait_send()
                self.second(k, half).wait_send()


def scatter_scratch(rows, width, steps):
    low, wide = jnp.bfloat16, jnp.float32
    dma = pltpu.SemaphoreType.DMA
    return [
        pltpu.VMEM((2, 2, 2, rows, width), low),
        pltpu.VMEM((2, 2, 2, rows, width), low),
        pltpu.VMEM((2, 2, rows, width), low),
        pltpu.VMEM((2, 2, rows, width), low),
        pltpu.VMEM((2, 2, rows, width), wide),
        pltpu.VMEM((2, rows, width), low),
        pltpu.VMEM((2, rows, width), low),
        dma((2, steps, 2)),
        dma((steps, 2)),
        dma((2, steps, 2)),
        dma((2, steps, 2)),
    ]


def reordered(rows, slow, back):
    each = rows.shape[1] // (4 * slow)
    if back:
        starts = [s * 4 + dp for dp in range(4) for s in range(slow)]
    else:
        starts = [dp * slow + s for s in range(slow) for dp in range(4)]
    return jnp.concatenate([rows[:, i * each : (i + 1) * each] for i in starts], 1)


def turn_kernel(slow, steps, backward, parts, gain, *refs):
    if backward:
        residual, cot, result, gain_grad, rows = refs[:5]
        scratch = refs[5:]
    else:
        tokens, result, rows = refs[:3]
        scratch = refs[3:]
    own, own_sems, group_sems = scratch[:3]
    me = (lax.axis_index("dp"), lax.axis_index("ctx"))
    greet(me, [member(me, by) for by in (1, 2, 4)], [])
    scatter = GroupScatter(me, parts, scratch[3:10], scratch[10:], steps)
    gathers = [GroupGather(me, rows, group_sems.at[k], own, scatter.window(k)) for k in range(steps)]
    scatter.start()
    for k in range(steps):
        scatter.send_first(k)
    for k in range(steps):
        scatter.send_second(k)
    for k in range(steps):
        span = scatter.window(k)
        for half in (0, 1):
            total = scatter.total(k, half)
            if backward:
                values = residual[half, span]
                factor = lax.rsqrt(jnp.mean(values * values, -1, keepdims=True) + norm_eps)
                normed = values * factor
                total = reordered(total, slow, True)
                part = jnp.sum(total * normed, 0, keepdims=True)
                if k == 0 and half == 0:
                    gain_grad[...] = part
                else:
                    gain_grad[...] += part
                back = total * gain[...]
                back = factor * (back - normed * jnp.mean(back * normed, -1, keepdims=True))
                back = cot[half, span].astype(jnp.float32) + back
                result[half, span] = back
                own[half, span] = back.astype(jnp.bfloat16)
            else:
                values = tokens[half, span].astype(jnp.float32) + total
                factor = lax.rsqrt(jnp.mean(values * values, -1, keepdims=True) + norm_eps)
                result[half, span] = values
                own[half, span] = reordered(values * factor * gain[...], slow, False).astype(
                    jnp.bfloat16
                )
        gathers[k].start()
        keep = pltpu.make_async_copy(own.at[:, span], rows.at[0, 0, :, span], own_sems.at[k])
        keep.start()
    for k in range(steps):
        gathers[k].pass_on()
    for k in range(steps):
        gathers[k].finish()
        span = scatter.window(k)
        pltpu.make_async_copy(own.at[:, span], rows.at[0, 0, :, span], own_sems.at[k]).wait()
    scatter.finish()


def turn(parts, gain, rows_in, slow, backward, identity):
    low, wide = jnp.bfloat16, jnp.float32
    dma = pltpu.SemaphoreType.DMA
    rows, width = parts.shape[3:]
    steps = 2
    any_space = pl.BlockSpec(memory_space=pl.ANY)
    vmem = pl.BlockSpec(memory_space=pltpu.VMEM)
    shapes = [jax.ShapeDtypeStruct((2, rows, width), wide)]
    if backward:
        shapes.append(jax.ShapeDtypeStruct((1, width), wide))
    return pl.pallas_call(
        functools.partial(turn_kernel, slow, steps, backward),
        out_shape=tuple(shapes) + (jax.ShapeDtypeStruct((2, 4, 2, rows, width), low),),
        in_specs=[any_space, vmem] + [vmem] * len(rows_in),
        out_specs=tuple([vmem] * len(shapes) + [any_space]),
        scratch_shapes=[
            pltpu.VMEM((2, rows, width), low),
            dma((steps,)),
            dma((steps, 2, 10)),
        ]
        + scatter_scratch(rows, width, steps),
        compiler_params=pltpu.CompilerParams(
            collective_id=identity, has_side_effects=True, vmem_limit_bytes=48 << 20
        ),
        cost_estimate=pl.CostEstimate(flops=0, bytes_accessed=250 << 20, transcendentals=0),
    )(parts, gain, *rows_in)


def move_kernel(splits, tokens, rows, move_sems):
    me = (lax.axis_index("dp"), lax.axis_index("ctx"))
    greet(me, [], movers_of(me, splits, False))
    move = Moves(me, splits, tokens, rows, move_sems, False)
    move.start()
    move.wait_recv()
    move.finish()


def move_tokens(tokens, splits, identity):
    any_space = pl.BlockSpec(memory_space=pl.ANY)
    return pl.pallas_call(
        functools.partial(move_kernel, splits),
        out_shape=jax.ShapeDtypeStruct(tokens.shape, tokens.dtype),
        in_specs=[any_space],
        out_specs=any_space,
        scratch_shapes=[pltpu.SemaphoreType.DMA((2, 2))],
        compiler_params=pltpu.CompilerParams(
            collective_id=identity, has_side_effects=True, vmem_limit_bytes=4 << 20
        ),
        cost_estimate=pl.CostEstimate(flops=0, bytes_accessed=40 << 20, transcendentals=0),
    )(tokens)


def spread_kernel(own, rows, group_sems, own_sem):
    me = (lax.axis_index("dp"), lax.axis_index("ctx"))
    greet(me, [member(me, by) for by in (1, 2, 4)], [])
    gather = GroupGather(me, rows, group_sems, own, slice(0, own.shape[1]))
    keep = pltpu.make_async_copy(own, rows.at[0, 0], own_sem)
    gather.start()
    keep.start()
    gather.pass_on()
    gather.finish()
    keep.wait()


def spread_group(own, identity):
    any_space = pl.BlockSpec(memory_space=pl.ANY)
    dma = pltpu.SemaphoreType.DMA
    return pl.pallas_call(
        spread_kernel,
        out_shape=jax.ShapeDtypeStruct((2, 4) + own.shape, own.dtype),
        in_specs=[any_space],
        out_specs=any_space,
        scratch_shapes=[dma((2, 10)), dma],
        compiler_params=pltpu.CompilerParams(
            collective_id=identity, has_side_effects=True, vmem_limit_bytes=4 << 20
        ),
        cost_estimate=pl.CostEstimate(flops=0, bytes_accessed=100 << 20, transcendentals=0),
    )(own)


class LineSum:
    def __init__(self, me, slow, parts, buffers, sems):
        self.parts = parts
        self.kept, self.arrived = buffers
        self.sems, self.own_sem = sems
        self.slot = me[1] // 2
        self.slow = slow
        self.line = [(me[0], me[1] ^ (2 * by)) for by in range(1, slow)]

    def hop(self, by):
        sems = (self.sems.at[0, by - 1], self.sems.at[1, by - 1])
        return remote(
            self.parts.at[self.slot ^ by], self.arrived.at[by - 1], sems, self.line[by - 1]
        )

    def own(self):
        return pltpu.make_async_copy(self.parts.at[self.slot], self.kept, self.own_sem)

    def start(self):
        for by in range(1, self.slow):
            self.hop(by).start()
        self.own().start()

    def total(self):
        self.own().wait()
        value = self.kept[...].astype(jnp.float32)
        for by in range(1, self.slow):
            self.hop(by).wait_recv()
            value = value + self.arrived[by - 1].astype(jnp.float32)
        return value

    def finish(self):
        for by in range(1, self.slow):
            self.hop(by).wait_send()


def line_scratch(shape, kind, slow):
    dma = pltpu.SemaphoreType.DMA
    return [
        pltpu.VMEM(shape, kind),
        pltpu.VMEM((slow - 1,) + shape, kind),
        dma((2, slow - 1)),
        dma,
    ]


def last_kernel(shards, splits, steps, in_parts, out_done, gate_parts, in_back, made_two, *refs):
    gain, gain_two_grad, tokens, back_rows = refs[:4]
    in_total, out_total, gate_total, gains_total, tokens_grad, block_out = refs[4:10]
    scratch = list(refs[10:])

    def take(count):
        taken = scratch[:count]
        del scratch[:count]
        return taken

    me = (lax.axis_index("dp"), lax.axis_index("ctx"))
    group, place = me
    slow = shards // 2
    slot, half = place // 2, place % 2
    owned = in_parts.shape[2]
    home = (group, half * slow + slot)
    movers = movers_of(me, splits, True)
    movers.append(((group, place % slow * 2 + place // slow), home))
    line = [(group, place ^ (2 * by)) for by in range(1, slow)]
    greet(me, [member(me, by) for by in range(1, 8)] + line, movers)
    one = take(11)
    back_sum = GroupScatter(me, in_back, one[:7], one[7:], steps)
    line_in = take(4)
    line_gains = take(4)
    in_done, gains_own, gains_done, made_one, gain_grad = take(5)
    in_sems, gate_sems, gains_sems, one_sems, two_sems, home_sems = take(6)
    in_line = LineSum(me, slow, in_parts, line_in[:2], line_in[2:])
    gains_line = LineSum(me, slow, gains_own, line_gains[:2], line_gains[2:])
    in_swap = GroupExchange(me, in_done, in_total, in_sems)
    gate_swap = GroupExchange(me, gate_parts, gate_total, gate_sems)
    gains_swap = GroupExchange(me, gains_done, gains_total, gains_sems)
    move_grad = Moves(me, splits, made_one, tokens_grad, one_sems, True)
    move_out = Moves(me, splits, made_two, block_out, two_sems, True)
    back_sum.start()
    to_home = (me, out_done, out_total, home, home_sems.at[0], home_sems.at[1])
    in_line.start()
    move_start(*to_home)
    for k in range(steps):
        back_sum.send_first(k)
    move_out.start()
    for k in range(steps):
        back_sum.send_second(k)
    for k in range(steps):
        span = back_sum.window(k)
        for part in (0, 1):
            total = back_sum.total(k, part)
            values = tokens[part, span].astype(jnp.float32)
            normed, factor = norm_parts(values)
            grad = jnp.sum(total * normed, 0, keepdims=True)
            if k == 0 and part == 0:
                gain_grad[...] = grad
            else:
                gain_grad[...] += grad
            value = back_rows[part, span] + norm_back(total * gain[...], normed, factor)
            made_one[part, span] = value.astype(jnp.bfloat16)
    move_grad.start()
    gains_own[...] = jnp.zeros_like(gains_own)
    for dp in range(4):
        for s in range(slow):
            for side in range(2):
                at = ((dp * slow + s) * 2 + side) * owned
                index = 2 * dp + side
                gains_own[s, index, 0:1, 0:owned] = gain_grad[:, at : at + owned]
                gains_own[s, index, 0:1, owned : 2 * owned] = gain_two_grad[:, at : at + owned]
    gains_line.start()
    gate_swap.start()
    in_done[...] = in_line.total().astype(jnp.bfloat16)
    in_swap.start()
    gains_done[...] = gains_line.total()
    gains_swap.start()
    pltpu.make_async_copy(out_done, out_total, home_sems.at[1]).wait()
    move_sent(*to_home)
    for swap in (in_swap, gate_swap, gains_swap):
        swap.finish()
    for move in (move_out, move_grad):
        move.wait_recv()
        move.finish()
    for part in (in_line, gains_line, back_sum):
        part.finish()


def last_sums(
    in_parts, out_done, gate_parts, in_back, out_rows, others, shards, splits, identity
):
    low, wide = jnp.bfloat16, jnp.float32
    slow = shards // 2
    steps = 2
    any_space = pl.BlockSpec(memory_space=pl.ANY)
    vmem = pl.BlockSpec(memory_space=pltpu.VMEM)
    dma = pltpu.SemaphoreType.DMA
    rows, width = in_back.shape[3:]
    gains_shape = (8, 8, 128)
    moved = jax.ShapeDtypeStruct((2, rows, width), low)
    return pl.pallas_call(
        functools.partial(last_kernel, shards, splits, steps),
        out_shape=(
            jax.ShapeDtypeStruct(in_parts.shape[1:], low),
            jax.ShapeDtypeStruct(out_done.shape, low),
            jax.ShapeDtypeStruct(gate_parts.shape, low),
            jax.ShapeDtypeStruct(gains_shape, wide),
            moved,
            moved,
        ),
        in_specs=[any_space] * 5 + [vmem] * 4,
        out_specs=(any_space,) * 6,
        scratch_shapes=scatter_scratch(rows, width, steps)
        + line_scratch(in_parts.shape[1:], low, slow)
        + line_scratch(gains_shape, wide, slow)
        + [
            pltpu.VMEM(in_parts.shape[1:], low),
            pltpu.VMEM((slow,) + gains_shape, wide),
            pltpu.VMEM(gains_shape, wide),
            pltpu.VMEM(moved.shape, low),
            pltpu.VMEM((1, width), wide),
            dma((2, 8)),
            dma((2, 8)),
            dma((2, 8)),
            dma((2, 2)),
            dma((2, 2)),
            dma((2,)),
        ],
        compiler_params=pltpu.CompilerParams(
            collective_id=identity, has_side_effects=True, vmem_limit_bytes=56 << 20
        ),
        cost_estimate=pl.CostEstimate(flops=0, bytes_accessed=300 << 20, transcendentals=0),
    )(in_parts, out_done, gate_parts, in_back, out_rows, *others)


def position_tables(blocks, rows):
    frequency = rope_base ** (-(np.arange(HEAD // 2) * 2.0 / HEAD))
    angles = np.arange(blocks * rows).reshape(blocks, rows, 1) * frequency
    cos, sin = np.cos(angles), np.sin(angles)
    cosine = np.concatenate([cos, cos, cos, cos], 2)
    sines = np.concatenate([-sin, sin, -sin, sin], 2)
    return jnp.asarray(cosine, jnp.float32), jnp.asarray(sines, jnp.float32)


def attend(order, where, qkv, tables, q_heads, kv_heads):
    seqs, length, cols = qkv.shape
    blocks = order.shape[0]
    rows = length // blocks
    whole = pl.BlockSpec(memory_space=pltpu.VMEM)
    small = pl.BlockSpec(memory_space=pltpu.SMEM)
    return pl.pallas_call(
        functools.partial(attend_kernel, q_heads, kv_heads, 256),
        out_shape=(
            jax.ShapeDtypeStruct((seqs, blocks, rows, q_heads * HEAD), jnp.bfloat16),
            jax.ShapeDtypeStruct((seqs, q_heads, length), jnp.float32),
            jax.ShapeDtypeStruct((seqs, length, cols), jnp.bfloat16),
        ),
        in_specs=[small, small, whole, whole, whole],
        out_specs=(whole, whole, whole),
        scratch_shapes=[pltpu.VMEM((blocks, rows, q_heads * HEAD), jnp.bfloat16)],
        compiler_params=pltpu.CompilerParams(vmem_limit_bytes=40 << 20),
        cost_estimate=pl.CostEstimate(
            flops=2 * seqs * length * length * q_heads * HEAD,
            bytes_accessed=100 << 20,
            transcendentals=seqs * length * length * q_heads // 2,
        ),
    )(order, where, qkv.reshape(seqs, blocks, rows, cols), *tables)


def attend_back(
    order, where, kept, back, lse, tables, out_rows, residual, out_parts, q_heads, kv_heads, identity
):
    seqs, length, cols = kept.shape
    blocks = order.shape[0]
    block = length // blocks
    group = q_heads // kv_heads
    rows, width = out_rows.shape[3:]
    steps = 2
    whole = pl.BlockSpec(memory_space=pltpu.VMEM)
    small = pl.BlockSpec(memory_space=pltpu.SMEM)
    any_space = pl.BlockSpec(memory_space=pl.ANY)
    return pl.pallas_call(
        functools.partial(attend_back_kernel, q_heads, kv_heads, 256, steps),
        out_shape=(
            jax.ShapeDtypeStruct((seqs, blocks, block, cols), jnp.bfloat16),
            jax.ShapeDtypeStruct((2, rows, width), jnp.bfloat16),
            jax.ShapeDtypeStruct(out_parts.shape[1:], jnp.bfloat16),
        ),
        in_specs=[small, small] + [whole] * 5 + [any_space, whole, any_space],
        out_specs=(whole, whole, whole),
        scratch_shapes=[
            pltpu.VMEM((length, q_heads * HEAD), jnp.bfloat16),
            pltpu.VMEM((blocks, block, cols), jnp.float32),
            pltpu.VMEM((group, length), jnp.float32),
            pltpu.VMEM((group * HEAD, length), jnp.float32),
        ]
        + line_scratch(out_parts.shape[1:], jnp.bfloat16, out_parts.shape[0])
        + scatter_scratch(rows, width, steps),
        compiler_params=pltpu.CompilerParams(
            collective_id=identity, has_side_effects=True, vmem_limit_bytes=56 << 20
        ),
        cost_estimate=pl.CostEstimate(
            flops=7 * seqs * length * length * q_heads * HEAD,
            bytes_accessed=100 << 20,
            transcendentals=seqs * length * length * q_heads // 2,
        ),
    )(
        order,
        where,
        kept,
        back.reshape(seqs, blocks, block, -1),
        lse,
        *tables,
        out_rows,
        residual,
        out_parts,
    )


def gate_update_kernel(slow, step_rate, grad, weight, first, second, new_first, new_second, new):
    units = grad.shape[2] // slow
    pieces = [grad[half, :, s * units : (s + 1) * units] for s in range(slow) for half in (0, 1)]
    gradient = jnp.concatenate(pieces, 1).astype(jnp.float32)
    new_first[...], new_second[...], new[...] = adam_update(
        weight[...], gradient, first[...], second[...], step_rate, weight_decay
    )


def gate_update(grad, weight, first, second, slow, step_rate):
    rows, width = weight.shape
    block = pl.BlockSpec((rows, width // 8), lambda side, dp: (0, 4 * side + dp))
    piece = pl.BlockSpec((2, rows, width // 16), lambda side, dp: (dp, 0, side))
    return pl.pallas_call(
        functools.partial(gate_update_kernel, slow, step_rate),
        grid=(2, 4),
        out_shape=(jax.ShapeDtypeStruct(weight.shape, jnp.float32),) * 3,
        in_specs=[piece, block, block, block],
        out_specs=(block,) * 3,
        compiler_params=pltpu.CompilerParams(vmem_limit_bytes=32 << 20),
    )(grad, weight, first, second)


def local(
    tokens,
    cotangent,
    block_order,
    attention_in,
    attention_out,
    gate_up,
    down_matrix,
    gains,
    mean_attention_in,
    mean_attention_out,
    mean_gate_up,
    mean_down,
    mean_gains,
    square_attention_in,
    square_attention_out,
    square_gate_up,
    square_down,
    square_gains,
):
    seq_count, shard_rows, width = tokens.shape
    shards = lax.axis_size("ctx")
    slow = shards // 2
    mine = lax.axis_index("dp")
    beside = lax.axis_index("ctx") % 2
    low = jnp.bfloat16
    owned = attention_in.shape[0]
    hidden_units = gate_up.shape[1] // 2
    part_hidden = hidden_units // 8
    units = down_matrix.shape[0]
    part_q = HEADS * HEAD // 8
    part_k = KV_HEADS * HEAD // 8
    part_cols = part_q + 2 * part_k
    count = seq_count * shard_rows
    together = 8 * count
    spread = shards // (4 * seq_count)
    splits = max(1, slow // 8)
    seqs = 2 // spread if spread < 2 else 1
    length = shards * shard_rows
    q_heads = HEADS // 8 // splits
    kv_heads = KV_HEADS // 8

    in_low = attention_in.astype(low)
    gains_row = jnp.pad(gains.astype(low).reshape(1, -1), ((0, 15), (0, part_cols - 2 * owned)))
    pieces = jnp.stack(
        [
            jnp.concatenate(
                [
                    jnp.concatenate(
                        [
                            in_low[:, i * part_q : (i + 1) * part_q],
                            in_low[:, 8 * part_q + i * part_k :][:, :part_k],
                            in_low[:, 8 * (part_q + part_k) + i * part_k :][:, :part_k],
                        ],
                        1,
                    ),
                    gains_row,
                ]
            )
            for i in range(8)
        ]
    )
    gate_low = gate_up.astype(low)
    gate_pieces = jnp.stack(
        [
            jnp.concatenate(
                [
                    gate_low[:, side * hidden_units + (dp * shards + 2 * s + half) * units :][
                        :, :units
                    ]
                    for side in range(2)
                    for s in range(slow)
                ],
                1,
            )
            for dp in range(4)
            for half in range(2)
        ]
    )
    tokens_all, in_all, w_out, gate_rows = first_exchange(
        tokens, pieces, attention_out.astype(low), gate_pieces, shards, spread, 1
    )
    in_all = in_all.reshape(slow, 4, 2, owned + 16, part_cols).swapaxes(0, 1)
    w_in = in_all[:, :, :, :owned].reshape(width, part_cols)
    w_out = w_out.reshape(part_q, width)
    gains_all = in_all[:, :, :, owned, : 2 * owned].reshape(-1, 2, owned)
    gains_all = gains_all.astype(jnp.float32).swapaxes(0, 1).reshape(2, width)
    gain_one, gain_two = gains_all[0], gains_all[1]
    w_gate = gather_line(gate_rows.reshape(8 * owned, 2 * part_hidden))

    normed_all, _ = norm_parts(tokens_all.reshape(together, width).astype(jnp.float32))
    input_one = (normed_all * gain_one).astype(low)
    qkv = dot_nn(input_one, w_in)
    orders = block_order.reshape(spread, 2, 2, 2, -1).transpose(0, 3, 1, 2, 4)
    orders = orders.reshape(spread, 4, -1)
    slot_order = jnp.concatenate(
        [
            orders[(2 * s + (beside ^ i)) if spread > 1 else 0, mine ^ j]
            for s in range(splits)
            for i in range(2 // seqs)
            for j in range(4)
        ]
    )
    tables = position_tables(slot_order.shape[0], length // slot_order.shape[0])
    groups = [
        [2 * (s * splits + g) + half for g in range(splits)]
        for s in range(slow // splits)
        for half in (0, 1)
    ]

    def split_heads(values, widths, copies):
        parts = []
        start = 0
        for each, repeat in zip(widths, copies):
            kinds = splits // repeat
            piece = values[:, start : start + kinds * each].reshape(-1, kinds, each)
            parts.append(jnp.repeat(piece.swapaxes(0, 1), repeat, axis=0))
            start += kinds * each
        sent = jnp.concatenate(parts, 2)
        got = lax.all_to_all(sent, "ctx", 0, 0, axis_index_groups=groups, tiled=True)
        return got.reshape(length, -1)

    def join_heads(values):
        sent = values.reshape(splits, together, -1)
        return lax.all_to_all(sent, "ctx", 0, 0, axis_index_groups=groups, tiled=True)

    q_width, k_width = q_heads * HEAD, kv_heads * HEAD
    if splits > 1:
        qkv = split_heads(qkv, (q_width, k_width, k_width), (1, splits, splits))
    qkv = qkv.reshape(seqs, length, -1)
    blocks = slot_order.shape[0]
    slot_where = jnp.sum(
        jnp.where(
            slot_order[None, :] == jnp.arange(blocks, dtype=jnp.int32)[:, None],
            jnp.arange(blocks, dtype=jnp.int32)[None, :],
            0,
        ),
        1,
    )
    attended, lse, kept = attend(slot_order, slot_where, qkv, tables, q_heads, kv_heads)
    if splits > 1:
        attended = join_heads(attended.reshape(length, q_width)).swapaxes(0, 1)
    attended = attended.reshape(together, part_q)

    def parts(values):
        return values.astype(low).reshape((2, 4) + tokens.shape)

    residual_rows, input_two = turn(
        parts(dot_nn(attended, w_out)), gain_two[None], [tokens_all[0, 0]], slow, False, 3
    )
    input_two = input_two.reshape(together, width)
    after = 0.0 * (residual_rows[0, 0, 0] + w_gate[0, 0].astype(jnp.float32))
    cot_rows = move_tokens(cotangent + after.astype(low), spread, 7)
    after = 0.0 * cot_rows[0, 0, 0].astype(jnp.float32)
    w_down = gather_line((down_matrix + after).astype(low))
    gate_both = dot_nn(input_two, w_gate)
    gate_part = gate_both[:, :part_hidden]
    up_part = gate_both[:, part_hidden:]
    sigmoid_gate = jax.nn.sigmoid(gate_part)
    active = gate_part * sigmoid_gate
    hidden = lax.optimization_barrier((active * up_part).astype(low))
    back_all = spread_group(cot_rows + 0.0 * hidden[0, 0], 2).reshape(together, width)
    grad_down = lax.optimization_barrier(dot_tn(hidden, back_all).astype(low))
    down_sum = sum_line(grad_down + 0.0 * w_down[0, 0]).astype(jnp.float32)
    back_hidden = dot_nt(back_all, w_down + 0.0 * hidden[0, 0])
    back_gate = back_hidden * up_part * sigmoid_gate * (1.0 + gate_part * (1.0 - sigmoid_gate))
    back_upper = back_hidden * active
    back_gate_up = jnp.concatenate([back_gate, back_upper], 1).astype(low)
    gate_low = sum_line(dot_tn(input_two, back_gate_up).astype(low))
    back_rows, grad_gain_two, back_residual_all = turn(
        parts(dot_nt(back_gate_up, w_gate)),
        gain_two[None],
        [residual_rows, cot_rows],
        slow,
        True,
        4,
    )
    back_residual_all = back_residual_all.reshape(together, width)
    grad_out = dot_tn(attended, back_residual_all).astype(low)
    back_attended = dot_nt(back_residual_all, w_out).astype(low)
    if splits > 1:
        back_attended = split_heads(back_attended, (q_width,), (1,))
    back_projected, output_rows, out_sum = attend_back(
        slot_order,
        slot_where,
        kept,
        back_attended.reshape(seqs, length, -1),
        lse,
        tables,
        parts(dot_nn(hidden, w_down)),
        residual_rows,
        grad_out.reshape(slow, owned, width),
        q_heads,
        kv_heads,
        6,
    )
    if splits > 1:
        back_projected = join_heads(back_projected.reshape(length, -1)).astype(jnp.float32)
        back_projected = jnp.concatenate(
            [
                back_projected[..., :q_width].swapaxes(0, 1).reshape(together, part_q),
                back_projected[..., q_width:].sum(0),
            ],
            1,
        ).astype(low)
    back_projected = back_projected.reshape(together, part_cols)
    grad_in = dot_tn(input_one, back_projected).astype(low)
    grad_in = grad_in.reshape(4, slow, 2 * owned, part_cols).swapaxes(0, 1)
    in_sum, out_sum, gate_sum, gains_sum, tokens_grad, block_out = last_sums(
        grad_in.reshape(slow, 8, owned, part_cols),
        out_sum,
        gate_low.reshape(8, owned, 2 * part_hidden),
        parts(dot_nt(back_projected, w_in)),
        output_rows,
        [gain_one[None], grad_gain_two, tokens_all[0, 0], back_rows],
        shards,
        spread,
        5,
    )
    tokens_grad = tokens_grad.astype(jnp.float32)
    out_sum = out_sum.astype(jnp.float32)
    gains_sum = gains_sum[:, 0, : 2 * owned].reshape(8, 2, owned).sum(0)
    cuts = ((0, part_q), (part_q, part_q + part_k), (part_q + part_k, part_cols))
    in_sum = jnp.concatenate(
        [in_sum[i, :, first:last] for first, last in cuts for i in range(8)], 1
    ).astype(jnp.float32)
    new_in = adam_update(
        attention_in,
        in_sum,
        mean_attention_in,
        square_attention_in,
        input_boost * D ** (-0.5),
        weight_decay,
    )
    new_out = adam_update(
        attention_out,
        out_sum,
        mean_attention_out,
        square_attention_out,
        (HEADS * HEAD // 32) ** (-0.5),
        weight_decay,
    )
    new_gate = gate_update(
        gate_sum, gate_up, mean_gate_up, square_gate_up, slow, D ** (-0.5)
    )
    new_down = adam_update(
        down_matrix, down_sum, mean_down, square_down, FF ** (-0.5), weight_decay
    )
    new_gain = adam_update(gains, gains_sum, mean_gains, square_gains, gain_rate, 0.0)
    return (
        block_out,
        tokens_grad,
        new_in[0],
        new_in[1],
        new_in[2],
        new_out[0],
        new_out[1],
        new_out[2],
        new_gate[0],
        new_gate[1],
        new_gate[2],
        new_down[0],
        new_down[1],
        new_down[2],
        new_gain[0],
        new_gain[1],
        new_gain[2],
    )


def solution(mesh):
    in_specs = (
        P("dp", "ctx", None),
        P("dp", "ctx", None),
        P(),
        P(("dp", "ctx"), None),
        P(("dp", "ctx"), None),
        P(("dp", "ctx"), None),
        P(("dp", "ctx"), None),
        P(None, ("dp", "ctx")),
        P(("dp", "ctx"), None),
        P(("dp", "ctx"), None),
        P(("dp", "ctx"), None),
        P(("dp", "ctx"), None),
        P(None, ("dp", "ctx")),
        P(("dp", "ctx"), None),
        P(("dp", "ctx"), None),
        P(("dp", "ctx"), None),
        P(("dp", "ctx"), None),
        P(None, ("dp", "ctx")),
    )
    out_specs = (
        P("dp", "ctx", None),
        P("dp", "ctx", None),
        P(("dp", "ctx"), None),
        P(("dp", "ctx"), None),
        P(("dp", "ctx"), None),
        P(("dp", "ctx"), None),
        P(("dp", "ctx"), None),
        P(("dp", "ctx"), None),
        P(("dp", "ctx"), None),
        P(("dp", "ctx"), None),
        P(("dp", "ctx"), None),
        P(("dp", "ctx"), None),
        P(("dp", "ctx"), None),
        P(("dp", "ctx"), None),
        P(None, ("dp", "ctx")),
        P(None, ("dp", "ctx")),
        P(None, ("dp", "ctx")),
    )
    return jax.shard_map(local, mesh=mesh, in_specs=in_specs, out_specs=out_specs, check_vma=False)
```

```python
import functools

import jax
import jax.numpy as jnp
import numpy as np
from jax import lax
from jax.experimental import pallas as pl
from jax.experimental.pallas import tpu as pltpu
from jax.sharding import PartitionSpec as P

D = 2048
HEADS = 32
KV_HEADS = 8
HEAD = 64
FF = 8192
STEP = 5


norm_eps = 1e-05
rope_base = 500000.0
beta_one = 0.9
beta_two = 0.95
gain_rate = 1.25
input_boost = 2.5
weight_decay = 0.1
adam_eps = 1e-08
masked_score = -1e30


def norm_parts(values):
    factor = lax.rsqrt(jnp.mean(values * values, -1, keepdims=True) + norm_eps)
    return (values * factor, factor)


def norm_back(back_normed, normed, factor):
    return factor * (back_normed - normed * jnp.mean(back_normed * normed, -1, keepdims=True))


def adam_update(weight, gradient, first_moment, second_moment, step_rate, decay_rate):
    first_new = beta_one * first_moment + (1.0 - beta_one) * gradient
    second_new = beta_two * second_moment + (1.0 - beta_two) * gradient * gradient
    update = (
        first_new
        / (1.0 - beta_one**STEP)
        / (jnp.sqrt(second_new / (1.0 - beta_two**STEP)) + adam_eps)
    )
    return (first_new, second_new, weight - step_rate * (update + decay_rate * weight))


def line_groups(shards):
    return [[2 * s + half for s in range(shards // 2)] for half in (0, 1)]


def gather_line(rows):
    return lax.all_gather(
        rows, "ctx", axis=0, tiled=True, axis_index_groups=line_groups(lax.axis_size("ctx"))
    )


def sum_line(gradient):
    return lax.psum_scatter(
        gradient,
        "ctx",
        scatter_dimension=0,
        tiled=True,
        axis_index_groups=line_groups(lax.axis_size("ctx")),
    )


def dot_nn(a, b):
    return lax.dot_general(a, b, (((1,), (0,)), ((), ())), preferred_element_type=jnp.float32)


def dot_nt(a, b):
    return lax.dot_general(a, b, (((1,), (1,)), ((), ())), preferred_element_type=jnp.float32)


def dot_tn(a, b):
    return lax.dot_general(a, b, (((0,), (0,)), ((), ())), preferred_element_type=jnp.float32)


def causal_keep(tile):
    keys = lax.broadcasted_iota(jnp.int32, (tile, tile), 0)
    queries = lax.broadcasted_iota(jnp.int32, (tile, tile), 1)
    return keys <= queries


def turn_group(values, cos, sin, forward):
    lanes = lax.broadcasted_iota(jnp.int32, values.shape, 1)
    other = jnp.where(
        lanes % HEAD < HEAD // 2,
        pltpu.roll(values, 2 * HEAD - HEAD // 2, 1),
        pltpu.roll(values, HEAD // 2, 1),
    )
    if forward:
        return values * cos + other * sin
    return values * cos - other * sin


def turn_columns(values, start, turned_cols, cos, sin, forward):
    if start >= turned_cols:
        return values
    turned = turn_group(values, cos, sin, forward)
    if start + 2 * HEAD <= turned_cols:
        return turned
    lanes = lax.broadcasted_iota(jnp.int32, values.shape, 1)
    return jnp.where(lanes < turned_cols - start, turned, values)


def attend_kernel(
    q_heads,
    kv_heads,
    tile,
    order_ref,
    where_ref,
    all_qkv_ref,
    cos_ref,
    sin_ref,
    all_out_ref,
    all_lse_ref,
    all_kept_ref,
    made,
):
    for sequence in range(all_qkv_ref.shape[0]):
        attend_sequence(
            q_heads,
            kv_heads,
            tile,
            order_ref,
            where_ref,
            all_qkv_ref.at[sequence],
            cos_ref,
            sin_ref,
            all_out_ref.at[sequence],
            all_lse_ref.at[sequence],
            all_kept_ref.at[sequence],
            made,
        )


def attend_sequence(
    q_heads,
    kv_heads,
    tile,
    order_ref,
    where_ref,
    qkv_ref,
    cos_ref,
    sin_ref,
    out_ref,
    lse_ref,
    kept_ref,
    made,
):
    blocks, rows, cols = qkv_ref.shape
    length = blocks * rows
    group = q_heads // kv_heads
    q_cols, k_cols = q_heads * HEAD, kv_heads * HEAD
    scale = HEAD ** (-0.5)

    def take_block(i, _):
        start = pl.multiple_of(i * rows, rows)
        cos = cos_ref[i]
        sin = sin_ref[i]
        for c in range(0, cols, 2 * HEAD):
            values = qkv_ref[where_ref[i], :, c : c + 2 * HEAD]
            values = turn_columns(values, c, q_cols + k_cols, cos, sin, True)
            kept_ref[pl.ds(start, rows), c : c + 2 * HEAD] = values.astype(jnp.bfloat16)
        return 0

    lax.fori_loop(0, blocks, take_block, 0)
    keep = causal_keep(tile)
    for kv in range(kv_heads):
        k_at = q_cols + kv * HEAD
        v_at = q_cols + k_cols + kv * HEAD

        def query_step(i, _):
            q_start = pl.multiple_of(i * tile, tile)
            queries = [
                kept_ref[
                    pl.ds(q_start, tile), (kv * group + g) * HEAD : (kv * group + g + 1) * HEAD
                ]
                for g in range(group)
            ]

            def key_tile(j, carry, masked):
                k_start = pl.multiple_of(j * tile, tile)
                keys = kept_ref[pl.ds(k_start, tile), k_at : k_at + HEAD]
                values = kept_ref[pl.ds(k_start, tile), v_at : v_at + HEAD]
                result = []
                for g in range(group):
                    peak, total, weighted = carry[g]
                    scores = dot_nt(keys, queries[g]) * scale
                    if masked:
                        scores = jnp.where(keep, scores, masked_score)
                    new_peak = jnp.maximum(peak, jnp.max(scores, 0, keepdims=True))
                    weights = jnp.exp(scores - new_peak)
                    shrink = jnp.exp(peak - new_peak)
                    total = total * shrink + jnp.sum(weights, 0, keepdims=True)
                    weighted = weighted * shrink + dot_tn(values, weights.astype(jnp.bfloat16))
                    result.append((new_peak, total, weighted))
                return tuple(result)

            start = tuple(
                (
                    jnp.full((1, tile), masked_score, jnp.float32),
                    jnp.zeros((1, tile), jnp.float32),
                    jnp.zeros((HEAD, tile), jnp.float32),
                )
                for _ in range(group)
            )
            carry = lax.fori_loop(0, i, lambda j, c: key_tile(j, c, False), start)
            carry = key_tile(i, carry, True)
            for g in range(group):
                head = kv * group + g
                peak, total, weighted = carry[g]
                lse_ref[head : head + 1, pl.ds(q_start, tile)] = peak + jnp.log(total)
                made[pl.ds(i * (tile // rows), tile // rows), :, head * HEAD : (head + 1) * HEAD] = (
                    (weighted / total).T.astype(jnp.bfloat16).reshape(-1, rows, HEAD)
                )
            return 0

        lax.fori_loop(0, length // tile, query_step, 0)

    def give_block(i, _):
        out_ref[i] = made[order_ref[i]]
        return 0

    lax.fori_loop(0, blocks, give_block, 0)


def attend_back_kernel(
    q_heads,
    kv_heads,
    tile,
    steps,
    order_ref,
    where_ref,
    all_kept_ref,
    all_back_ref,
    all_lse_ref,
    cos_ref,
    sin_ref,
    out_rows,
    residual,
    out_parts,
    all_out_ref,
    block_out,
    out_sum,
    *scratch,
):
    me = (lax.axis_index("dp"), lax.axis_index("ctx"))
    slow = out_parts.shape[0]
    line = [(me[0], me[1] ^ (2 * by)) for by in range(1, slow)]
    greet(me, [member(me, by) for by in (1, 2, 4)] + line, [])
    work, line_out, scratch = scratch[:4], scratch[4:8], scratch[8:]
    scatter = GroupScatter(me, out_rows, scratch[:7], scratch[7:], steps)
    out_line = LineSum(me, slow, out_parts, line_out[:2], line_out[2:])

    def one():
        for k in range(steps):
            scatter.send_first(k)

    def two():
        for k in range(steps):
            scatter.send_second(k)

    def three():
        for k in range(steps):
            span = scatter.window(k)
            for part in (0, 1):
                value = residual[part, span] + scatter.total(k, part)
                block_out[part, span] = value.astype(jnp.bfloat16)

    tasks = [one, two, three]

    def pause():
        if tasks:
            tasks.pop(0)()

    scatter.start()
    out_line.start()
    for sequence in range(all_kept_ref.shape[0]):
        attend_back_sequence(
            q_heads,
            kv_heads,
            tile,
            pause,
            order_ref,
            where_ref,
            all_kept_ref.at[sequence],
            all_back_ref.at[sequence],
            all_lse_ref.at[sequence],
            cos_ref,
            sin_ref,
            all_out_ref.at[sequence],
            *work,
        )
    while tasks:
        pause()
    out_sum[...] = out_line.total().astype(jnp.bfloat16)
    out_line.finish()
    scatter.finish()


def attend_back_sequence(
    q_heads,
    kv_heads,
    tile,
    pause,
    order_ref,
    where_ref,
    kept_ref,
    back_ref,
    lse_ref,
    cos_ref,
    sin_ref,
    out_ref,
    back_sorted,
    grad,
    delta_ref,
    dq_ref,
):
    length, cols = kept_ref.shape
    blocks, rows = back_ref.shape[:2]
    group = q_heads // kv_heads
    q_cols, k_cols = q_heads * HEAD, kv_heads * HEAD
    scale = HEAD ** (-0.5)
    tiles = length // tile

    def take_block(i, _):
        start = pl.multiple_of(i * rows, rows)
        back_sorted[pl.ds(start, rows), :] = back_ref[where_ref[i]]
        return 0

    lax.fori_loop(0, blocks, take_block, 0)
    keep = causal_keep(tile)
    for kv in range(kv_heads):
        k_at = q_cols + kv * HEAD
        v_at = q_cols + k_cols + kv * HEAD

        def load(i, g):
            start = pl.multiple_of(i * tile, tile)
            head = kv * group + g
            at = slice(head * HEAD, (head + 1) * HEAD)
            return (
                kept_ref[pl.ds(start, tile), at],
                back_sorted[pl.ds(start, tile), at],
                lse_ref[head : head + 1, pl.ds(start, tile)],
            )

        def load_kv(j):
            start = pl.multiple_of(j * tile, tile)
            return (
                kept_ref[pl.ds(start, tile), k_at : k_at + HEAD],
                kept_ref[pl.ds(start, tile), v_at : v_at + HEAD],
            )

        def tile_terms(keys, values, query, back, lse, masked):
            weights = jnp.exp(dot_nt(keys, query) * scale - lse)
            if masked:
                weights = jnp.where(keep, weights, 0.0)
            return weights, dot_nt(values, back)

        def delta_step(i, _):
            rows_i = [load(i, g) for g in range(group)]

            def one(j, carry, masked):
                keys, values = load_kv(j)
                result = []
                for g in range(group):
                    weights, back_weights = tile_terms(keys, values, *rows_i[g], masked)
                    result.append(carry[g] + jnp.sum(weights * back_weights, 0, keepdims=True))
                return tuple(result)

            carry = tuple(jnp.zeros((1, tile), jnp.float32) for _ in range(group))
            carry = lax.fori_loop(0, i, lambda j, c: one(j, c, False), carry)
            carry = one(i, carry, True)
            for g in range(group):
                delta_ref[g : g + 1, pl.ds(pl.multiple_of(i * tile, tile), tile)] = carry[g]
            return 0

        lax.fori_loop(0, tiles, delta_step, 0)
        if kv == 0:
            pause()
        dq_ref[...] = jnp.zeros_like(dq_ref)

        def key_step(j, _):
            keys, values = load_kv(j)

            def one(i, carry, masked):
                back_key, back_value = carry
                start = pl.multiple_of(i * tile, tile)
                for g in range(group):
                    query, back, lse = load(i, g)
                    weights, back_weights = tile_terms(keys, values, query, back, lse, masked)
                    delta = delta_ref[g : g + 1, pl.ds(start, tile)]
                    back_scores = (weights * (back_weights - delta)).astype(jnp.bfloat16)
                    back_key = back_key + dot_nn(back_scores, query)
                    back_value = back_value + dot_nn(weights.astype(jnp.bfloat16), back)
                    dq_ref[g * HEAD : (g + 1) * HEAD, pl.ds(start, tile)] += dot_tn(
                        keys, back_scores
                    )
                return back_key, back_value

            zero = jnp.zeros((tile, HEAD), jnp.float32)
            carry = one(j, (zero, zero), True)
            carry = lax.fori_loop(j + 1, tiles, lambda i, c: one(i, c, False), carry)
            span = pl.ds(j * (tile // rows), tile // rows)
            grad[span, :, k_at : k_at + HEAD] = (carry[0] * scale).reshape(-1, rows, HEAD)
            grad[span, :, v_at : v_at + HEAD] = carry[1].reshape(-1, rows, HEAD)
            return 0

        lax.fori_loop(0, tiles, key_step, 0)
        for g in range(group):
            head = kv * group + g
            turned = (dq_ref[g * HEAD : (g + 1) * HEAD, :] * scale).T
            grad[:, :, head * HEAD : (head + 1) * HEAD] = turned.reshape(-1, rows, HEAD)

    def give_block(i, _):
        cos = cos_ref[order_ref[i]]
        sin = sin_ref[order_ref[i]]
        for c in range(0, cols, 2 * HEAD):
            values = grad[order_ref[i], :, c : c + 2 * HEAD]
            values = turn_columns(values, c, q_cols + k_cols, cos, sin, False)
            out_ref[i, :, c : c + 2 * HEAD] = values.astype(jnp.bfloat16)
        return 0

    lax.fori_loop(0, blocks, give_block, 0)


MESH = pl.DeviceIdType.MESH


def sequence_target(group, place, second, splits):
    sequence = 2 * group + second
    held_at = sequence % 4 * 2 + (sequence % 2 ^ sequence // 4)
    slot = place // 2
    target = (place % 2 * 2 + slot % 4 // 2, held_at * splits + slot // 4)
    return target, slot % 2


def token_target(group, place, half, splits):
    held_at = place // splits
    sequence = (held_at % 2 ^ held_at // 2 % 2) * 4 + held_at // 2
    slot = place % splits * 4 + group % 2 * 2 + half
    return (sequence // 2, 2 * slot + group // 2), sequence % 2


def remote(source, target, sems, device):
    return pltpu.make_async_remote_copy(
        src_ref=source,
        dst_ref=target,
        send_sem=sems[0],
        recv_sem=sems[1],
        device_id=device,
        device_id_type=MESH,
    )


def same(one, other):
    return jnp.logical_and(one[0] == other[0], one[1] == other[1])


def greet(me, peers, movers):
    barrier = pltpu.get_barrier_semaphore()
    for peer in peers:
        pl.semaphore_signal(barrier, inc=1, device_id=peer, device_id_type=MESH)
    expected = len(peers)
    for source, target in movers:

        @pl.when(jnp.logical_not(same(source, me)))
        def _():
            pl.semaphore_signal(barrier, inc=1, device_id=source, device_id_type=MESH)

        expected = expected + jnp.where(same(target, me), 0, 1)
    pl.semaphore_wait(barrier, expected)


def move_start(me, source, target, target_device, send, receive):
    here = same(target_device, me)

    @pl.when(here)
    def _():
        pltpu.make_async_copy(source, target, receive).start()

    @pl.when(jnp.logical_not(here))
    def _():
        remote(source, target, (send, receive), target_device).start()


def move_sent(me, source, target, target_device, send, receive):
    @pl.when(jnp.logical_not(same(target_device, me)))
    def _():
        remote(source, target, (send, receive), target_device).wait_send()


def member(me, by):
    return (me[0] ^ (by // 2), me[1] ^ (by % 2))


def group_index(device):
    return 2 * device[0] + device[1] % 2


class GroupExchange:
    def __init__(self, me, pieces, got, sems):
        self.me, self.pieces, self.got, self.sems = me, pieces, got, sems

    def hop(self, by):
        peer = member(self.me, by)
        sems = (self.sems.at[0, by - 1], self.sems.at[1, by - 1])
        return remote(
            self.pieces.at[group_index(peer)], self.got.at[group_index(self.me)], sems, peer
        )

    def own(self):
        mine = group_index(self.me)
        return pltpu.make_async_copy(self.pieces.at[mine], self.got.at[mine], self.sems.at[0, 7])

    def start(self):
        for by in range(1, 8):
            self.hop(by).start()
        self.own().start()

    def finish(self):
        self.own().wait()
        for by in range(1, 8):
            self.hop(by).wait()


class GroupGather:
    def __init__(self, me, rows, sems, own, window):
        self.rows, self.sems, self.own, self.window = rows, sems, own, window
        self.core, self.across, self.beside = member(me, 2), member(me, 4), member(me, 1)

    def hop(self, index):
        across, beside, core = self.across, self.beside, self.core
        source, i, j, half, device = (
            (None, 0, 2, 0, across),
            (None, 1, 0, 1, beside),
            (None, 1, 0, 0, beside),
            (None, 0, 2, 1, across),
            ((0, 2), 1, 2, 0, beside),
            ((1, 0), 1, 2, 1, across),
            (None, 0, 1, slice(0, 2), core),
            ((0, 2), 0, 3, slice(0, 2), core),
            ((1, 0), 1, 1, slice(0, 2), core),
            ((1, 2), 1, 3, slice(0, 2), core),
        )[index]
        if source is None:
            source = self.own.at[half, self.window]
        else:
            source = self.rows.at[source[0], source[1], half, self.window]
        target = self.rows.at[i, j, half, self.window]
        return remote(source, target, (self.sems.at[0, index], self.sems.at[1, index]), device)

    def start(self):
        for index in (0, 1, 2, 3, 6):
            self.hop(index).start()

    def pass_on(self):
        self.hop(0).wait_recv()
        self.hop(4).start()
        self.hop(1).wait_recv()
        self.hop(5).start()
        self.hop(3).wait_recv()
        self.hop(7).start()
        self.hop(2).wait_recv()
        self.hop(8).start()

    def finish(self):
        self.hop(4).wait_recv()
        self.hop(5).wait_recv()
        self.hop(9).start()
        for index in (6, 7, 8, 9):
            self.hop(index).wait_recv()
        for index in range(10):
            self.hop(index).wait_send()


class Moves:
    def __init__(self, me, splits, source, target, sems, back):
        self.me, self.splits, self.source, self.target = me, splits, source, target
        self.sems, self.back = sems, back

    def one(self, i):
        find = token_target if self.back else sequence_target
        device, place = find(self.me[0], self.me[1], i, self.splits)
        return (
            self.me,
            self.source.at[i],
            self.target.at[place],
            device,
            self.sems.at[0, i],
            self.sems.at[1, place],
        )

    def start(self):
        for i in (0, 1):
            move_start(*self.one(i))

    def wait_recv(self):
        for i in (0, 1):
            pltpu.make_async_copy(self.source.at[0], self.target.at[i], self.sems.at[1, i]).wait()

    def finish(self):
        for i in (0, 1):
            move_sent(*self.one(i))


def movers_of(me, splits, back):
    into = [sequence_target(me[0], me[1], i, splits)[0] for i in (0, 1)]
    home = [token_target(me[0], me[1], i, splits)[0] for i in (0, 1)]
    return list(zip(into, home)) if back else list(zip(home, into))


def first_kernel(shards, splits, tokens, pieces, out_own, gate_pieces, *refs):
    rows, in_all, out_all, gate_rows, held = refs[:5]
    move_sems, group_sems, piece_sems, gate_sems, own_sem, in_sems, out_sems = refs[5:]
    me = (lax.axis_index("dp"), lax.axis_index("ctx"))
    group, place = me
    slow = shards // 2
    slot = place // 2
    line = [(group, place ^ (2 * by)) for by in range(1, slow)]
    wanted, block = place // slow, place % slow
    takers = [(group, 2 * (slot ^ by) + wanted) for by in range(slow)]
    givers = [(group, place % 2 * slow + block_by) for block_by in range(slow)]
    movers = movers_of(me, splits, False) + list(zip(givers, takers))
    greet(me, [member(me, by) for by in range(1, 8)] + line, movers)
    swap = GroupExchange(me, pieces, held, piece_sems)
    gate_swap = GroupExchange(me, gate_pieces, gate_rows, gate_sems)
    move = Moves(me, splits, tokens, rows.at[0, 0], move_sems, False)

    def in_line(by):
        sems = (in_sems.at[0, by - 1], in_sems.at[1, by - 1])
        return remote(held, in_all.at[slot], sems, line[by - 1])

    def out_send(by):
        return (
            me,
            out_own,
            out_all.at[block],
            takers[by],
            out_sems.at[0, by],
            out_sems.at[1, block],
        )

    own = pltpu.make_async_copy(held, in_all.at[slot], own_sem)
    move.start()
    swap.start()
    gate_swap.start()
    swap.finish()
    move.wait_recv()
    spread = GroupGather(me, rows, group_sems, rows.at[0, 0], slice(0, tokens.shape[1]))
    spread.start()
    for by in range(1, slow):
        in_line(by).start()
    own.start()
    for by in range(slow):
        move_start(*out_send(by))
    spread.pass_on()
    for by in range(1, slow):
        in_line(by).wait()
    spread.finish()
    own.wait()
    for by in range(slow):
        pltpu.make_async_copy(out_own, out_all.at[by], out_sems.at[1, by]).wait()
    for by in range(slow):
        move_sent(*out_send(by))
    gate_swap.finish()
    move.finish()


def first_exchange(tokens, pieces, out_own, gate_pieces, shards, splits, identity):
    low = jnp.bfloat16
    slow = shards // 2
    any_space = pl.BlockSpec(memory_space=pl.ANY)
    dma = pltpu.SemaphoreType.DMA
    made = pl.pallas_call(
        functools.partial(first_kernel, shards, splits),
        out_shape=(
            jax.ShapeDtypeStruct((2, 4) + tokens.shape, low),
            jax.ShapeDtypeStruct((slow,) + pieces.shape, low),
            jax.ShapeDtypeStruct((slow,) + out_own.shape, low),
            jax.ShapeDtypeStruct(gate_pieces.shape, low),
            jax.ShapeDtypeStruct(pieces.shape, low),
        ),
        in_specs=[any_space] * 4,
        out_specs=(any_space,) * 5,
        scratch_shapes=[
            dma((2, 2)),
            dma((2, 10)),
            dma((2, 8)),
            dma((2, 8)),
            dma,
            dma((2, slow - 1)),
            dma((2, slow)),
        ],
        compiler_params=pltpu.CompilerParams(
            collective_id=identity, has_side_effects=True, vmem_limit_bytes=8 << 20
        ),
        cost_estimate=pl.CostEstimate(flops=0, bytes_accessed=200 << 20, transcendentals=0),
    )(tokens, pieces, out_own, gate_pieces)
    return made[:4]


class GroupScatter:
    def __init__(self, me, parts, buffers, sems, steps):
        self.parts = parts
        self.core_in, self.kept, self.sent, self.came, self.held = buffers[:5]
        self.sent_last, self.came_last = buffers[5:]
        self.core_sems, self.kept_sems, self.one_sems, self.last_sems = sems
        self.core, self.across, self.beside = member(me, 2), member(me, 4), member(me, 1)
        self.size = parts.shape[3] // steps
        self.steps = steps

    def window(self, k):
        return slice(k * self.size, (k + 1) * self.size)

    def to_core(self, k, j):
        return remote(
            self.parts.at[:, 2 * j + 1, :, self.window(k)],
            self.core_in.at[:, j, :, self.window(k)],
            (self.core_sems.at[0, k, j], self.core_sems.at[1, k, j]),
            self.core,
        )

    def keep(self, k, j):
        return pltpu.make_async_copy(
            self.parts.at[:, 2 * j, :, self.window(k)],
            self.kept.at[:, j, :, self.window(k)],
            self.kept_sems.at[k, j],
        )

    def first(self, k, half):
        return remote(
            self.sent.at[half, :, self.window(k)],
            self.came.at[half, :, self.window(k)],
            (self.one_sems.at[0, k, half], self.one_sems.at[1, k, half]),
            (self.beside, self.across)[half],
        )

    def second(self, k, half):
        return remote(
            self.sent_last.at[half, self.window(k)],
            self.came_last.at[half, self.window(k)],
            (self.last_sems.at[0, k, half], self.last_sems.at[1, k, half]),
            (self.across, self.beside)[half],
        )

    def start(self):
        for k in range(self.steps):
            for j in (0, 1):
                self.to_core(k, j).start()
                self.keep(k, j).start()

    def send_first(self, k):
        wide = jnp.float32
        rows = self.window(k)
        for j in (0, 1):
            self.keep(k, j).wait()
            self.to_core(k, j).wait_recv()
        for half in (0, 1):
            for other in (0, 1):
                at = (1, other) if half == 0 else (other, 1)
                both = self.kept[at[0], at[1], half, rows].astype(wide)
                both = both + self.core_in[at[0], at[1], half, rows].astype(wide)
                self.sent[half, other, rows] = both.astype(jnp.bfloat16)
            self.first(k, half).start()
        for half in (0, 1):
            for other in (0, 1):
                at = (0, other) if half == 0 else (other, 0)
                both = self.kept[at[0], at[1], half, rows].astype(wide)
                self.held[half, other, rows] = both + self.core_in[at[0], at[1], half, rows].astype(
                    wide
                )

    def send_second(self, k):
        wide = jnp.float32
        rows = self.window(k)
        for half in (0, 1):
            self.first(k, half).wait_recv()
            both = self.held[half, 1, rows] + self.came[half, 1, rows].astype(wide)
            self.sent_last[half, rows] = both.astype(jnp.bfloat16)
            self.second(k, half).start()
            self.held[half, 0, rows] = self.held[half, 0, rows] + self.came[half, 0, rows].astype(
                wide
            )

    def total(self, k, half):
        self.second(k, half).wait_recv()
        rows = self.window(k)
        return self.held[half, 0, rows] + self.came_last[half, rows].astype(jnp.float32)

    def finish(self):
        for k in range(self.steps):
            for j in (0, 1):
                self.to_core(k, j).wait_send()
            for half in (0, 1):
                self.first(k, half).wait_send()
                self.second(k, half).wait_send()


def scatter_scratch(rows, width, steps):
    low, wide = jnp.bfloat16, jnp.float32
    dma = pltpu.SemaphoreType.DMA
    return [
        pltpu.VMEM((2, 2, 2, rows, width), low),
        pltpu.VMEM((2, 2, 2, rows, width), low),
        pltpu.VMEM((2, 2, rows, width), low),
        pltpu.VMEM((2, 2, rows, width), low),
        pltpu.VMEM((2, 2, rows, width), wide),
        pltpu.VMEM((2, rows, width), low),
        pltpu.VMEM((2, rows, width), low),
        dma((2, steps, 2)),
        dma((steps, 2)),
        dma((2, steps, 2)),
        dma((2, steps, 2)),
    ]


def reordered(rows, slow, back):
    each = rows.shape[1] // (4 * slow)
    if back:
        starts = [s * 4 + dp for dp in range(4) for s in range(slow)]
    else:
        starts = [dp * slow + s for s in range(slow) for dp in range(4)]
    return jnp.concatenate([rows[:, i * each : (i + 1) * each] for i in starts], 1)


def turn_kernel(slow, steps, backward, parts, gain, *refs):
    if backward:
        residual, cot, result, gain_grad, rows = refs[:5]
        scratch = refs[5:]
    else:
        tokens, result, rows = refs[:3]
        scratch = refs[3:]
    own, own_sems, group_sems = scratch[:3]
    me = (lax.axis_index("dp"), lax.axis_index("ctx"))
    greet(me, [member(me, by) for by in (1, 2, 4)], [])
    scatter = GroupScatter(me, parts, scratch[3:10], scratch[10:], steps)
    gathers = [GroupGather(me, rows, group_sems.at[k], own, scatter.window(k)) for k in range(steps)]
    scatter.start()
    for k in range(steps):
        scatter.send_first(k)
    for k in range(steps):
        scatter.send_second(k)
    for k in range(steps):
        span = scatter.window(k)
        for half in (0, 1):
            total = scatter.total(k, half)
            if backward:
                values = residual[half, span]
                factor = lax.rsqrt(jnp.mean(values * values, -1, keepdims=True) + norm_eps)
                normed = values * factor
                total = reordered(total, slow, True)
                part = jnp.sum(total * normed, 0, keepdims=True)
                if k == 0 and half == 0:
                    gain_grad[...] = part
                else:
                    gain_grad[...] += part
                back = total * gain[...]
                back = factor * (back - normed * jnp.mean(back * normed, -1, keepdims=True))
                back = cot[half, span].astype(jnp.float32) + back
                result[half, span] = back
                own[half, span] = back.astype(jnp.bfloat16)
            else:
                values = tokens[half, span].astype(jnp.float32) + total
                factor = lax.rsqrt(jnp.mean(values * values, -1, keepdims=True) + norm_eps)
                result[half, span] = values
                own[half, span] = reordered(values * factor * gain[...], slow, False).astype(
                    jnp.bfloat16
                )
        gathers[k].start()
        keep = pltpu.make_async_copy(own.at[:, span], rows.at[0, 0, :, span], own_sems.at[k])
        keep.start()
    for k in range(steps):
        gathers[k].pass_on()
    for k in range(steps):
        gathers[k].finish()
        span = scatter.window(k)
        pltpu.make_async_copy(own.at[:, span], rows.at[0, 0, :, span], own_sems.at[k]).wait()
    scatter.finish()


def turn(parts, gain, rows_in, slow, backward, identity):
    low, wide = jnp.bfloat16, jnp.float32
    dma = pltpu.SemaphoreType.DMA
    rows, width = parts.shape[3:]
    steps = 2
    any_space = pl.BlockSpec(memory_space=pl.ANY)
    vmem = pl.BlockSpec(memory_space=pltpu.VMEM)
    shapes = [jax.ShapeDtypeStruct((2, rows, width), wide)]
    if backward:
        shapes.append(jax.ShapeDtypeStruct((1, width), wide))
    return pl.pallas_call(
        functools.partial(turn_kernel, slow, steps, backward),
        out_shape=tuple(shapes) + (jax.ShapeDtypeStruct((2, 4, 2, rows, width), low),),
        in_specs=[any_space, vmem] + [vmem] * len(rows_in),
        out_specs=tuple([vmem] * len(shapes) + [any_space]),
        scratch_shapes=[
            pltpu.VMEM((2, rows, width), low),
            dma((steps,)),
            dma((steps, 2, 10)),
        ]
        + scatter_scratch(rows, width, steps),
        compiler_params=pltpu.CompilerParams(
            collective_id=identity, has_side_effects=True, vmem_limit_bytes=48 << 20
        ),
        cost_estimate=pl.CostEstimate(flops=0, bytes_accessed=250 << 20, transcendentals=0),
    )(parts, gain, *rows_in)


def move_kernel(splits, tokens, rows, move_sems):
    me = (lax.axis_index("dp"), lax.axis_index("ctx"))
    greet(me, [], movers_of(me, splits, False))
    move = Moves(me, splits, tokens, rows, move_sems, False)
    move.start()
    move.wait_recv()
    move.finish()


def move_tokens(tokens, splits, identity):
    any_space = pl.BlockSpec(memory_space=pl.ANY)
    return pl.pallas_call(
        functools.partial(move_kernel, splits),
        out_shape=jax.ShapeDtypeStruct(tokens.shape, tokens.dtype),
        in_specs=[any_space],
        out_specs=any_space,
        scratch_shapes=[pltpu.SemaphoreType.DMA((2, 2))],
        compiler_params=pltpu.CompilerParams(
            collective_id=identity, has_side_effects=True, vmem_limit_bytes=4 << 20
        ),
        cost_estimate=pl.CostEstimate(flops=0, bytes_accessed=40 << 20, transcendentals=0),
    )(tokens)


def spread_kernel(own, rows, group_sems, own_sem):
    me = (lax.axis_index("dp"), lax.axis_index("ctx"))
    greet(me, [member(me, by) for by in (1, 2, 4)], [])
    gather = GroupGather(me, rows, group_sems, own, slice(0, own.shape[1]))
    keep = pltpu.make_async_copy(own, rows.at[0, 0], own_sem)
    gather.start()
    keep.start()
    gather.pass_on()
    gather.finish()
    keep.wait()


def spread_group(own, identity):
    any_space = pl.BlockSpec(memory_space=pl.ANY)
    dma = pltpu.SemaphoreType.DMA
    return pl.pallas_call(
        spread_kernel,
        out_shape=jax.ShapeDtypeStruct((2, 4) + own.shape, own.dtype),
        in_specs=[any_space],
        out_specs=any_space,
        scratch_shapes=[dma((2, 10)), dma],
        compiler_params=pltpu.CompilerParams(
            collective_id=identity, has_side_effects=True, vmem_limit_bytes=4 << 20
        ),
        cost_estimate=pl.CostEstimate(flops=0, bytes_accessed=100 << 20, transcendentals=0),
    )(own)


class LineSum:
    def __init__(self, me, slow, parts, buffers, sems):
        self.parts = parts
        self.kept, self.arrived = buffers
        self.sems, self.own_sem = sems
        self.slot = me[1] // 2
        self.slow = slow
        self.line = [(me[0], me[1] ^ (2 * by)) for by in range(1, slow)]

    def hop(self, by):
        sems = (self.sems.at[0, by - 1], self.sems.at[1, by - 1])
        return remote(
            self.parts.at[self.slot ^ by], self.arrived.at[by - 1], sems, self.line[by - 1]
        )

    def own(self):
        return pltpu.make_async_copy(self.parts.at[self.slot], self.kept, self.own_sem)

    def start(self):
        for by in range(1, self.slow):
            self.hop(by).start()
        self.own().start()

    def total(self):
        self.own().wait()
        value = self.kept[...].astype(jnp.float32)
        for by in range(1, self.slow):
            self.hop(by).wait_recv()
            value = value + self.arrived[by - 1].astype(jnp.float32)
        return value

    def finish(self):
        for by in range(1, self.slow):
            self.hop(by).wait_send()


def line_scratch(shape, kind, slow):
    dma = pltpu.SemaphoreType.DMA
    return [
        pltpu.VMEM(shape, kind),
        pltpu.VMEM((slow - 1,) + shape, kind),
        dma((2, slow - 1)),
        dma,
    ]


def last_kernel(shards, splits, steps, in_parts, out_done, gate_parts, in_back, made_two, *refs):
    gain, gain_two_grad, tokens, back_rows = refs[:4]
    in_total, out_total, gate_total, gains_total, tokens_grad, block_out = refs[4:10]
    scratch = list(refs[10:])

    def take(count):
        taken = scratch[:count]
        del scratch[:count]
        return taken

    me = (lax.axis_index("dp"), lax.axis_index("ctx"))
    group, place = me
    slow = shards // 2
    slot, half = place // 2, place % 2
    owned = in_parts.shape[2]
    home = (group, half * slow + slot)
    movers = movers_of(me, splits, True)
    movers.append(((group, place % slow * 2 + place // slow), home))
    line = [(group, place ^ (2 * by)) for by in range(1, slow)]
    greet(me, [member(me, by) for by in range(1, 8)] + line, movers)
    one = take(11)
    back_sum = GroupScatter(me, in_back, one[:7], one[7:], steps)
    line_in = take(4)
    line_gains = take(4)
    in_done, gains_own, gains_done, made_one, gain_grad = take(5)
    in_sems, gate_sems, gains_sems, one_sems, two_sems, home_sems = take(6)
    in_line = LineSum(me, slow, in_parts, line_in[:2], line_in[2:])
    gains_line = LineSum(me, slow, gains_own, line_gains[:2], line_gains[2:])
    in_swap = GroupExchange(me, in_done, in_total, in_sems)
    gate_swap = GroupExchange(me, gate_parts, gate_total, gate_sems)
    gains_swap = GroupExchange(me, gains_done, gains_total, gains_sems)
    move_grads = [
        Moves(
            me,
            splits,
            made_one.at[:, back_sum.window(k)],
            tokens_grad.at[:, back_sum.window(k)],
            one_sems.at[k],
            True,
        )
        for k in range(steps)
    ]
    move_out = Moves(me, splits, made_two, block_out, two_sems, True)
    back_sum.start()
    to_home = (me, out_done, out_total, home, home_sems.at[0], home_sems.at[1])
    in_line.start()
    move_start(*to_home)
    for k in range(steps):
        back_sum.send_first(k)
    move_out.start()
    for k in range(steps):
        back_sum.send_second(k)
    for k in range(steps):
        span = back_sum.window(k)
        for part in (0, 1):
            total = back_sum.total(k, part)
            values = tokens[part, span].astype(jnp.float32)
            normed, factor = norm_parts(values)
            grad = jnp.sum(total * normed, 0, keepdims=True)
            if k == 0 and part == 0:
                gain_grad[...] = grad
            else:
                gain_grad[...] += grad
            value = back_rows[part, span] + norm_back(total * gain[...], normed, factor)
            made_one[part, span] = value.astype(jnp.bfloat16)
        move_grads[k].start()
    gains_own[...] = jnp.zeros_like(gains_own)
    for dp in range(4):
        for s in range(slow):
            for side in range(2):
                at = ((dp * slow + s) * 2 + side) * owned
                index = 2 * dp + side
                gains_own[s, index, 0:1, 0:owned] = gain_grad[:, at : at + owned]
                gains_own[s, index, 0:1, owned : 2 * owned] = gain_two_grad[:, at : at + owned]
    gains_line.start()
    gate_swap.start()
    in_done[...] = in_line.total().astype(jnp.bfloat16)
    in_swap.start()
    gains_done[...] = gains_line.total()
    gains_swap.start()
    pltpu.make_async_copy(out_done, out_total, home_sems.at[1]).wait()
    move_sent(*to_home)
    for swap in (in_swap, gate_swap, gains_swap):
        swap.finish()
    for move in [move_out] + move_grads:
        move.wait_recv()
        move.finish()
    for part in (in_line, gains_line, back_sum):
        part.finish()


def last_sums(
    in_parts, out_done, gate_parts, in_back, out_rows, others, shards, splits, identity
):
    low, wide = jnp.bfloat16, jnp.float32
    slow = shards // 2
    steps = 2
    any_space = pl.BlockSpec(memory_space=pl.ANY)
    vmem = pl.BlockSpec(memory_space=pltpu.VMEM)
    dma = pltpu.SemaphoreType.DMA
    rows, width = in_back.shape[3:]
    gains_shape = (8, 8, 128)
    moved = jax.ShapeDtypeStruct((2, rows, width), low)
    return pl.pallas_call(
        functools.partial(last_kernel, shards, splits, steps),
        out_shape=(
            jax.ShapeDtypeStruct(in_parts.shape[1:], low),
            jax.ShapeDtypeStruct(out_done.shape, low),
            jax.ShapeDtypeStruct(gate_parts.shape, low),
            jax.ShapeDtypeStruct(gains_shape, wide),
            moved,
            moved,
        ),
        in_specs=[any_space] * 5 + [vmem] * 4,
        out_specs=(any_space,) * 6,
        scratch_shapes=scatter_scratch(rows, width, steps)
        + line_scratch(in_parts.shape[1:], low, slow)
        + line_scratch(gains_shape, wide, slow)
        + [
            pltpu.VMEM(in_parts.shape[1:], low),
            pltpu.VMEM((slow,) + gains_shape, wide),
            pltpu.VMEM(gains_shape, wide),
            pltpu.VMEM(moved.shape, low),
            pltpu.VMEM((1, width), wide),
            dma((2, 8)),
            dma((2, 8)),
            dma((2, 8)),
            dma((steps, 2, 2)),
            dma((2, 2)),
            dma((2,)),
        ],
        compiler_params=pltpu.CompilerParams(
            collective_id=identity, has_side_effects=True, vmem_limit_bytes=56 << 20
        ),
        cost_estimate=pl.CostEstimate(flops=0, bytes_accessed=300 << 20, transcendentals=0),
    )(in_parts, out_done, gate_parts, in_back, out_rows, *others)


def position_tables(blocks, rows):
    frequency = rope_base ** (-(np.arange(HEAD // 2) * 2.0 / HEAD))
    angles = np.arange(blocks * rows).reshape(blocks, rows, 1) * frequency
    cos, sin = np.cos(angles), np.sin(angles)
    cosine = np.concatenate([cos, cos, cos, cos], 2)
    sines = np.concatenate([-sin, sin, -sin, sin], 2)
    return jnp.asarray(cosine, jnp.float32), jnp.asarray(sines, jnp.float32)


def attend(order, where, qkv, tables, q_heads, kv_heads):
    seqs, length, cols = qkv.shape
    blocks = order.shape[0]
    rows = length // blocks
    whole = pl.BlockSpec(memory_space=pltpu.VMEM)
    small = pl.BlockSpec(memory_space=pltpu.SMEM)
    return pl.pallas_call(
        functools.partial(attend_kernel, q_heads, kv_heads, 256),
        out_shape=(
            jax.ShapeDtypeStruct((seqs, blocks, rows, q_heads * HEAD), jnp.bfloat16),
            jax.ShapeDtypeStruct((seqs, q_heads, length), jnp.float32),
            jax.ShapeDtypeStruct((seqs, length, cols), jnp.bfloat16),
        ),
        in_specs=[small, small, whole, whole, whole],
        out_specs=(whole, whole, whole),
        scratch_shapes=[pltpu.VMEM((blocks, rows, q_heads * HEAD), jnp.bfloat16)],
        compiler_params=pltpu.CompilerParams(vmem_limit_bytes=40 << 20),
        cost_estimate=pl.CostEstimate(
            flops=2 * seqs * length * length * q_heads * HEAD,
            bytes_accessed=100 << 20,
            transcendentals=seqs * length * length * q_heads // 2,
        ),
    )(order, where, qkv.reshape(seqs, blocks, rows, cols), *tables)


def attend_back(
    order, where, kept, back, lse, tables, out_rows, residual, out_parts, q_heads, kv_heads, identity
):
    seqs, length, cols = kept.shape
    blocks = order.shape[0]
    block = length // blocks
    group = q_heads // kv_heads
    rows, width = out_rows.shape[3:]
    steps = 2
    whole = pl.BlockSpec(memory_space=pltpu.VMEM)
    small = pl.BlockSpec(memory_space=pltpu.SMEM)
    any_space = pl.BlockSpec(memory_space=pl.ANY)
    return pl.pallas_call(
        functools.partial(attend_back_kernel, q_heads, kv_heads, 256, steps),
        out_shape=(
            jax.ShapeDtypeStruct((seqs, blocks, block, cols), jnp.bfloat16),
            jax.ShapeDtypeStruct((2, rows, width), jnp.bfloat16),
            jax.ShapeDtypeStruct(out_parts.shape[1:], jnp.bfloat16),
        ),
        in_specs=[small, small] + [whole] * 5 + [any_space, whole, any_space],
        out_specs=(whole, whole, whole),
        scratch_shapes=[
            pltpu.VMEM((length, q_heads * HEAD), jnp.bfloat16),
            pltpu.VMEM((blocks, block, cols), jnp.float32),
            pltpu.VMEM((group, length), jnp.float32),
            pltpu.VMEM((group * HEAD, length), jnp.float32),
        ]
        + line_scratch(out_parts.shape[1:], jnp.bfloat16, out_parts.shape[0])
        + scatter_scratch(rows, width, steps),
        compiler_params=pltpu.CompilerParams(
            collective_id=identity, has_side_effects=True, vmem_limit_bytes=56 << 20
        ),
        cost_estimate=pl.CostEstimate(
            flops=7 * seqs * length * length * q_heads * HEAD,
            bytes_accessed=100 << 20,
            transcendentals=seqs * length * length * q_heads // 2,
        ),
    )(
        order,
        where,
        kept,
        back.reshape(seqs, blocks, block, -1),
        lse,
        *tables,
        out_rows,
        residual,
        out_parts,
    )


def gate_update_kernel(slow, step_rate, grad, weight, first, second, new_first, new_second, new):
    units = grad.shape[2] // slow
    pieces = [grad[half, :, s * units : (s + 1) * units] for s in range(slow) for half in (0, 1)]
    gradient = jnp.concatenate(pieces, 1).astype(jnp.float32)
    new_first[...], new_second[...], new[...] = adam_update(
        weight[...], gradient, first[...], second[...], step_rate, weight_decay
    )


def gate_update(grad, weight, first, second, slow, step_rate):
    rows, width = weight.shape
    block = pl.BlockSpec((rows, width // 8), lambda side, dp: (0, 4 * side + dp))
    piece = pl.BlockSpec((2, rows, width // 16), lambda side, dp: (dp, 0, side))
    return pl.pallas_call(
        functools.partial(gate_update_kernel, slow, step_rate),
        grid=(2, 4),
        out_shape=(jax.ShapeDtypeStruct(weight.shape, jnp.float32),) * 3,
        in_specs=[piece, block, block, block],
        out_specs=(block,) * 3,
        compiler_params=pltpu.CompilerParams(vmem_limit_bytes=32 << 20),
    )(grad, weight, first, second)


def local(
    tokens,
    cotangent,
    block_order,
    attention_in,
    attention_out,
    gate_up,
    down_matrix,
    gains,
    mean_attention_in,
    mean_attention_out,
    mean_gate_up,
    mean_down,
    mean_gains,
    square_attention_in,
    square_attention_out,
    square_gate_up,
    square_down,
    square_gains,
):
    seq_count, shard_rows, width = tokens.shape
    shards = lax.axis_size("ctx")
    slow = shards // 2
    mine = lax.axis_index("dp")
    beside = lax.axis_index("ctx") % 2
    low = jnp.bfloat16
    owned = attention_in.shape[0]
    hidden_units = gate_up.shape[1] // 2
    part_hidden = hidden_units // 8
    units = down_matrix.shape[0]
    part_q = HEADS * HEAD // 8
    part_k = KV_HEADS * HEAD // 8
    part_cols = part_q + 2 * part_k
    count = seq_count * shard_rows
    together = 8 * count
    spread = shards // (4 * seq_count)
    splits = max(1, slow // 8)
    seqs = 2 // spread if spread < 2 else 1
    length = shards * shard_rows
    q_heads = HEADS // 8 // splits
    kv_heads = KV_HEADS // 8

    in_low = attention_in.astype(low)
    gains_row = jnp.pad(gains.astype(low).reshape(1, -1), ((0, 15), (0, part_cols - 2 * owned)))
    pieces = jnp.stack(
        [
            jnp.concatenate(
                [
                    jnp.concatenate(
                        [
                            in_low[:, i * part_q : (i + 1) * part_q],
                            in_low[:, 8 * part_q + i * part_k :][:, :part_k],
                            in_low[:, 8 * (part_q + part_k) + i * part_k :][:, :part_k],
                        ],
                        1,
                    ),
                    gains_row,
                ]
            )
            for i in range(8)
        ]
    )
    gate_low = gate_up.astype(low)
    gate_pieces = jnp.stack(
        [
            jnp.concatenate(
                [
                    gate_low[:, side * hidden_units + (dp * shards + 2 * s + half) * units :][
                        :, :units
                    ]
                    for side in range(2)
                    for s in range(slow)
                ],
                1,
            )
            for dp in range(4)
            for half in range(2)
        ]
    )
    tokens_all, in_all, w_out, gate_rows = first_exchange(
        tokens, pieces, attention_out.astype(low), gate_pieces, shards, spread, 1
    )
    in_all = in_all.reshape(slow, 4, 2, owned + 16, part_cols).swapaxes(0, 1)
    w_in = in_all[:, :, :, :owned].reshape(width, part_cols)
    w_out = w_out.reshape(part_q, width)
    gains_all = in_all[:, :, :, owned, : 2 * owned].reshape(-1, 2, owned)
    gains_all = gains_all.astype(jnp.float32).swapaxes(0, 1).reshape(2, width)
    gain_one, gain_two = gains_all[0], gains_all[1]
    w_gate = gather_line(gate_rows.reshape(8 * owned, 2 * part_hidden))

    normed_all, _ = norm_parts(tokens_all.reshape(together, width).astype(jnp.float32))
    input_one = (normed_all * gain_one).astype(low)
    qkv = dot_nn(input_one, w_in)
    orders = block_order.reshape(spread, 2, 2, 2, -1).transpose(0, 3, 1, 2, 4)
    orders = orders.reshape(spread, 4, -1)
    slot_order = jnp.concatenate(
        [
            orders[(2 * s + (beside ^ i)) if spread > 1 else 0, mine ^ j]
            for s in range(splits)
            for i in range(2 // seqs)
            for j in range(4)
        ]
    )
    tables = position_tables(slot_order.shape[0], length // slot_order.shape[0])
    groups = [
        [2 * (s * splits + g) + half for g in range(splits)]
        for s in range(slow // splits)
        for half in (0, 1)
    ]

    def split_heads(values, widths, copies):
        parts = []
        start = 0
        for each, repeat in zip(widths, copies):
            kinds = splits // repeat
            piece = values[:, start : start + kinds * each].reshape(-1, kinds, each)
            parts.append(jnp.repeat(piece.swapaxes(0, 1), repeat, axis=0))
            start += kinds * each
        sent = jnp.concatenate(parts, 2)
        got = lax.all_to_all(sent, "ctx", 0, 0, axis_index_groups=groups, tiled=True)
        return got.reshape(length, -1)

    def join_heads(values):
        sent = values.reshape(splits, together, -1)
        return lax.all_to_all(sent, "ctx", 0, 0, axis_index_groups=groups, tiled=True)

    q_width, k_width = q_heads * HEAD, kv_heads * HEAD
    if splits > 1:
        qkv = split_heads(qkv, (q_width, k_width, k_width), (1, splits, splits))
    qkv = qkv.reshape(seqs, length, -1)
    blocks = slot_order.shape[0]
    slot_where = jnp.sum(
        jnp.where(
            slot_order[None, :] == jnp.arange(blocks, dtype=jnp.int32)[:, None],
            jnp.arange(blocks, dtype=jnp.int32)[None, :],
            0,
        ),
        1,
    )
    attended, lse, kept = attend(slot_order, slot_where, qkv, tables, q_heads, kv_heads)
    if splits > 1:
        attended = join_heads(attended.reshape(length, q_width)).swapaxes(0, 1)
    attended = attended.reshape(together, part_q)

    def parts(values):
        return values.astype(low).reshape((2, 4) + tokens.shape)

    residual_rows, input_two = turn(
        parts(dot_nn(attended, w_out)), gain_two[None], [tokens_all[0, 0]], slow, False, 3
    )
    input_two = input_two.reshape(together, width)
    after = 0.0 * (residual_rows[0, 0, 0] + w_gate[0, 0].astype(jnp.float32))
    cot_rows = move_tokens(cotangent + after.astype(low), spread, 7)
    after = 0.0 * cot_rows[0, 0, 0].astype(jnp.float32)
    w_down = gather_line((down_matrix + after).astype(low))
    gate_both = dot_nn(input_two, w_gate)
    gate_part = gate_both[:, :part_hidden]
    up_part = gate_both[:, part_hidden:]
    sigmoid_gate = jax.nn.sigmoid(gate_part)
    active = gate_part * sigmoid_gate
    hidden = lax.optimization_barrier((active * up_part).astype(low))
    back_all = spread_group(cot_rows + 0.0 * hidden[0, 0], 2).reshape(together, width)
    grad_down = lax.optimization_barrier(dot_tn(hidden, back_all).astype(low))
    down_sum = sum_line(grad_down + 0.0 * w_down[0, 0]).astype(jnp.float32)
    back_hidden = dot_nt(back_all, w_down + 0.0 * hidden[0, 0])
    back_gate = back_hidden * up_part * sigmoid_gate * (1.0 + gate_part * (1.0 - sigmoid_gate))
    back_upper = back_hidden * active
    back_gate_up = jnp.concatenate([back_gate, back_upper], 1).astype(low)
    gate_low = sum_line(dot_tn(input_two, back_gate_up).astype(low))
    back_rows, grad_gain_two, back_residual_all = turn(
        parts(dot_nt(back_gate_up, w_gate)),
        gain_two[None],
        [residual_rows, cot_rows],
        slow,
        True,
        4,
    )
    back_residual_all = back_residual_all.reshape(together, width)
    grad_out = dot_tn(attended, back_residual_all).astype(low)
    back_attended = dot_nt(back_residual_all, w_out).astype(low)
    if splits > 1:
        back_attended = split_heads(back_attended, (q_width,), (1,))
    back_projected, output_rows, out_sum = attend_back(
        slot_order,
        slot_where,
        kept,
        back_attended.reshape(seqs, length, -1),
        lse,
        tables,
        parts(dot_nn(hidden, w_down)),
        residual_rows,
        grad_out.reshape(slow, owned, width),
        q_heads,
        kv_heads,
        6,
    )
    if splits > 1:
        back_projected = join_heads(back_projected.reshape(length, -1)).astype(jnp.float32)
        back_projected = jnp.concatenate(
            [
                back_projected[..., :q_width].swapaxes(0, 1).reshape(together, part_q),
                back_projected[..., q_width:].sum(0),
            ],
            1,
        ).astype(low)
    back_projected = back_projected.reshape(together, part_cols)
    grad_in = dot_tn(input_one, back_projected).astype(low)
    grad_in = grad_in.reshape(4, slow, 2 * owned, part_cols).swapaxes(0, 1)
    in_sum, out_sum, gate_sum, gains_sum, tokens_grad, block_out = last_sums(
        grad_in.reshape(slow, 8, owned, part_cols),
        out_sum,
        gate_low.reshape(8, owned, 2 * part_hidden),
        parts(dot_nt(back_projected, w_in)),
        output_rows,
        [gain_one[None], grad_gain_two, tokens_all[0, 0], back_rows],
        shards,
        spread,
        5,
    )
    tokens_grad = tokens_grad.astype(jnp.float32)
    out_sum = out_sum.astype(jnp.float32)
    gains_sum = gains_sum[:, 0, : 2 * owned].reshape(8, 2, owned).sum(0)
    cuts = ((0, part_q), (part_q, part_q + part_k), (part_q + part_k, part_cols))
    in_sum = jnp.concatenate(
        [in_sum[i, :, first:last] for first, last in cuts for i in range(8)], 1
    ).astype(jnp.float32)
    new_in = adam_update(
        attention_in,
        in_sum,
        mean_attention_in,
        square_attention_in,
        input_boost * D ** (-0.5),
        weight_decay,
    )
    new_out = adam_update(
        attention_out,
        out_sum,
        mean_attention_out,
        square_attention_out,
        (HEADS * HEAD // 32) ** (-0.5),
        weight_decay,
    )
    new_gate = gate_update(
        gate_sum, gate_up, mean_gate_up, square_gate_up, slow, D ** (-0.5)
    )
    new_down = adam_update(
        down_matrix, down_sum, mean_down, square_down, FF ** (-0.5), weight_decay
    )
    new_gain = adam_update(gains, gains_sum, mean_gains, square_gains, gain_rate, 0.0)
    return (
        block_out,
        tokens_grad,
        new_in[0],
        new_in[1],
        new_in[2],
        new_out[0],
        new_out[1],
        new_out[2],
        new_gate[0],
        new_gate[1],
        new_gate[2],
        new_down[0],
        new_down[1],
        new_down[2],
        new_gain[0],
        new_gain[1],
        new_gain[2],
    )


def solution(mesh):
    in_specs = (
        P("dp", "ctx", None),
        P("dp", "ctx", None),
        P(),
        P(("dp", "ctx"), None),
        P(("dp", "ctx"), None),
        P(("dp", "ctx"), None),
        P(("dp", "ctx"), None),
        P(None, ("dp", "ctx")),
        P(("dp", "ctx"), None),
        P(("dp", "ctx"), None),
        P(("dp", "ctx"), None),
        P(("dp", "ctx"), None),
        P(None, ("dp", "ctx")),
        P(("dp", "ctx"), None),
        P(("dp", "ctx"), None),
        P(("dp", "ctx"), None),
        P(("dp", "ctx"), None),
        P(None, ("dp", "ctx")),
    )
    out_specs = (
        P("dp", "ctx", None),
        P("dp", "ctx", None),
        P(("dp", "ctx"), None),
        P(("dp", "ctx"), None),
        P(("dp", "ctx"), None),
        P(("dp", "ctx"), None),
        P(("dp", "ctx"), None),
        P(("dp", "ctx"), None),
        P(("dp", "ctx"), None),
        P(("dp", "ctx"), None),
        P(("dp", "ctx"), None),
        P(("dp", "ctx"), None),
        P(("dp", "ctx"), None),
        P(("dp", "ctx"), None),
        P(None, ("dp", "ctx")),
        P(None, ("dp", "ctx")),
        P(None, ("dp", "ctx")),
    )
    return jax.shard_map(local, mesh=mesh, in_specs=in_specs, out_specs=out_specs, check_vma=False)
```
